32 devices in a mesh: parts: 2 (over y), frame: 4 (over z), head: 4 (over x, core).
Axes of the slice: x: 2, y: 2, z: 4, core: 2. Of those that a mesh axis runs over, the one named last changes fastest.
Arguments:
- queries: bfloat16 [4096, 2560], P(('parts', 'frame', 'head')), parts along dimension 0, may hold values from -108 to 108
- keys: bfloat16 [4096, 2560], P(('parts', 'frame', 'head')), parts along dimension 0, may hold values from -4 to 4
- values: bfloat16 [4096, 2560], P(('parts', 'frame', 'head')), parts along dimension 0, may hold values from -6 to 6
- pair_mask: int32 [8, 4], P(('parts', 'frame')), parts along dimension 0, may hold values 0 or 1
- tile_offset: int32 [8], P(('parts', 'frame')), parts along dimension 0, may hold values from 0 to 1
Outputs:
- attended: bfloat16 [4096, 2560], P(('parts', 'frame', 'head')), parts along dimension 0
The draws below stay inside these ranges and needn't reach their ends.
There are 2 independent parts, one for each index of `parts`. The reference program is written for one: setup_inputs(seed, part) draws one part's arguments, and reference() takes and returns one part's arrays. A program takes and returns all parts, laid end to end along the dimension named above; each array names one. Nothing has to cross between parts.
All inputs are finite; a program needn't handle non-finite values. No bound on the sum of `pair_mask` on one device may be relied on, other than what follows from the above.
Results may differ from the reference program's by a relative error of at most 0.003.
Values may be sent and summed in bfloat16 or wider, within the bound.
No kernel may reach another device: no remote copies, remote signals or barrier semaphores. Data moves between devices by JAX's collectives and lax.ppermute only.
A program may use at most 128 MiB of HBM per device.

```python
from functools import partial
import jax
import jax.numpy as jnp
from jax import lax

HEAD_DIM = 128
FRAME_TOK = 512
FRAMES = 4
TOKENS = 2048
CH = 2560
TILES = 2
TILE = 256
LOG_FRAME = 2


def shared_keys(key):
    base = jax.random.normal(key, (TOKENS, CH), jnp.float32)
    return jnp.clip(base, -4.0, 4.0)


def draw_keys(key, part):
    return shared_keys(key).astype(jnp.bfloat16)


def draw_queries(key, part):
    key = jax.random.fold_in(key, 5)
    own = jnp.clip(jax.random.normal(key, (TOKENS, CH), jnp.float32), -4.0, 4.0) * 3.0
    return own.astype(jnp.bfloat16)


def set_ends(result, rng, least, largest):
    longest = result.shape.index(max(result.shape))
    spots = []
    for shift in (0, 1):
        where = [jax.random.randint(jax.random.fold_in(rng, axis), (), 0, length) for axis, length in enumerate(result.shape)]
        where[longest] = (where[longest] + shift) % result.shape[longest]
        spots.append(tuple(where))
    return result.at[spots[0]].set(least).at[spots[1]].set(largest)


def block_levels(stream_key, extent, cuts, low, top_value):
    def one(axis_at, shards_of):
        heights = jax.random.uniform(jax.random.fold_in(jax.random.fold_in(stream_key, 6), axis_at), (shards_of,), jnp.float32, low / len(cuts), top_value / len(cuts))
        return jnp.repeat(jnp.exp(heights), extent[axis_at] // shards_of).reshape((-1,) + (1,) * (len(extent) - axis_at - 1))

    level = one(*cuts[0])
    for cut in cuts[1:]:
        level = level * one(*cut)
    return level


def centred(own_key, shape, scale, most, split=(), held_as=jnp.bfloat16):
    result = jax.random.normal(own_key, shape, jnp.float32) * scale
    if len(split) > 0:
        result = block_levels(own_key, shape, split, -0.22, 0.18) * result
    return jnp.clip(result, min=-most, max=most).astype(held_as)


def setup_inputs(seed: int = 0, part: int = 0) -> dict:
    key_list = jax.random.split(jax.random.key(seed), 6)
    part_keys = jax.random.split(jax.random.fold_in(key_list[5], part), 6)
    queries = draw_queries(jax.random.fold_in(jax.random.fold_in(key_list[5], part), 71), part)
    keys = draw_keys(jax.random.fold_in(jax.random.fold_in(key_list[5], part), 71), part)
    values = centred(part_keys[2], (TOKENS, CH), 1.0, 6.0, ((0, 16),))
    pair_mask = set_ends((jax.random.randint(part_keys[3], (FRAMES, FRAMES), 0, 4) < 3).astype(jnp.int32), jax.random.fold_in(part_keys[3], 1), 0, 1)
    tile_offset = set_ends(jax.random.randint(part_keys[4], (FRAMES,), 0, TILES), jax.random.fold_in(part_keys[4], 1), 0, TILES - 1).astype(jnp.int32)
    return dict(queries=queries, keys=keys, values=values, pair_mask=pair_mask, tile_offset=tile_offset)


def subsample(frame_rows, offset, level):
    step = 2 ** level
    width = frame_rows.shape[-1]
    grouped = frame_rows.reshape(TILES // step, step, TILE, width)
    picked = lax.dynamic_index_in_dim(grouped, (offset % step).astype(jnp.int32), 1, keepdims=False)
    return picked.reshape(-1, width)


def attend(query_rows, key_rows, value_rows, valid):
    count = query_rows.shape[0]
    heads = query_rows.shape[1] // HEAD_DIM
    q_three = query_rows.reshape(count, heads, HEAD_DIM).transpose(1, 0, 2)
    k_three = key_rows.reshape(-1, heads, HEAD_DIM).transpose(1, 0, 2)
    v_three = value_rows.reshape(-1, heads, HEAD_DIM).transpose(1, 0, 2)
    scale = 1.0 / (HEAD_DIM ** 0.5)

    def one_head(operands):
        q_head, k_head, v_head = operands
        scores = jnp.dot(q_head, k_head.T, preferred_element_type=jnp.float32) * scale
        scores = jnp.where(valid[None, :] > 0, scores, -1e30)
        top = jnp.max(scores, axis=1, keepdims=True)
        weights = jnp.exp(scores - top) * valid[None, :]
        total = jnp.sum(weights, axis=1, keepdims=True)
        mixed = jnp.dot(weights.astype(jnp.bfloat16), v_head, preferred_element_type=jnp.float32)
        return mixed / total

    outcome = lax.map(one_head, (q_three, k_three, v_three))
    return outcome.transpose(1, 0, 2).reshape(count, heads * HEAD_DIM).astype(jnp.bfloat16)


def reference(queries, keys, values, pair_mask, tile_offset):
    q_frames = queries.reshape(FRAMES, FRAME_TOK, CH)
    k_frames = keys.reshape(FRAMES, FRAME_TOK, CH)
    v_frames = values.reshape(FRAMES, FRAME_TOK, CH)

    def frame_out(current):
        near_index = current - 1 + jnp.arange(3, dtype=jnp.int32)
        near_good = ((near_index >= 0) & (near_index < FRAMES)).astype(jnp.float32)
        clamped = jnp.clip(near_index, 0, FRAMES - 1)
        key_parts = [k_frames[clamped].reshape(-1, CH)]
        value_parts = [v_frames[clamped].reshape(-1, CH)]
        valid_parts = [jnp.repeat(near_good, FRAME_TOK)]
        mask_row = pair_mask[current]
        for level in range(1, LOG_FRAME):
            step = 2 ** level
            start = jnp.bitwise_xor(current // step, 1) * step
            frame_ids = start + jnp.arange(step, dtype=jnp.int32)
            offsets = tile_offset[frame_ids]
            pick = jax.vmap(partial(subsample, level=level))
            k_sel = pick(k_frames[frame_ids].reshape(step, TILES, TILE, CH), offsets)
            v_sel = pick(v_frames[frame_ids].reshape(step, TILES, TILE, CH), offsets)
            rows = k_sel.shape[1]
            allowed = lax.dynamic_slice_in_dim(mask_row, start, step, 0)
            good = ((jnp.abs(frame_ids - current) >= 2) & (allowed == 1)).astype(jnp.float32)
            key_parts.append(k_sel.reshape(-1, CH))
            value_parts.append(v_sel.reshape(-1, CH))
            valid_parts.append(jnp.repeat(good, rows))
        return attend(q_frames[current], jnp.concatenate(key_parts), jnp.concatenate(value_parts), jnp.concatenate(valid_parts))

    outcome = lax.map(frame_out, jnp.arange(FRAMES, dtype=jnp.int32))
    return outcome.reshape(TOKENS, CH)
```

```python
import math

import jax
import jax.numpy as jnp
from jax import lax
from jax.experimental import pallas as pl
from jax.experimental.pallas import tpu as pltpu
from jax.sharding import PartitionSpec as P

HEAD_DIM = 128
SCALE = 1.0 / HEAD_DIM**0.5
LOG2E = math.log2(math.e)


def padded(x, sides, width):
    for axis, dim in sides:
        peers, length = (lax.axis_size(axis), x.shape[dim])
        up = [(i, (i + 1) % peers) for i in range(peers - 1)]
        down = [(j, i) for i, j in up]
        last = lax.slice_in_dim(x, length - width, length, axis=dim)
        leading = lax.slice_in_dim(x, 0, width, axis=dim)
        before = lax.ppermute(last, axis, up)
        after = lax.ppermute(leading, axis, down)
        x = jnp.concatenate([before, x, after], axis=dim)
    return x


def from_partner(x, axis, bit):
    return lax.ppermute(x, axis, [(i, i ^ 1 << bit) for i in range(lax.axis_size(axis))])


def subsample(frame_rows, offset, level, tiles, tile):
    step = 2**level
    width = frame_rows.shape[-1]
    grouped = frame_rows.reshape(tiles // step, step, tile, width)
    picked = lax.dynamic_index_in_dim(grouped, offset % step, 1, keepdims=False)
    return picked.reshape(-1, width)


def attend(query_rows, key_rows, value_rows, valid):
    count = query_rows.shape[0]
    heads = query_rows.shape[1] // HEAD_DIM
    q_three = query_rows.reshape(count, heads, HEAD_DIM).transpose(1, 0, 2)
    k_three = key_rows.reshape(-1, heads, HEAD_DIM).transpose(1, 0, 2)
    v_three = value_rows.reshape(-1, heads, HEAD_DIM).transpose(1, 0, 2)

    def one_head(operands):
        q_head, k_head, v_head = operands
        scores = jnp.dot(q_head, k_head.T, preferred_element_type=jnp.float32) * SCALE
        scores = jnp.where(valid[None, :] > 0, scores, -1e30)
        top = jnp.max(scores, axis=1, keepdims=True)
        weights = jnp.exp(scores - top) * valid[None, :]
        total = jnp.sum(weights, axis=1, keepdims=True)
        mixed = jnp.dot(weights.astype(jnp.bfloat16), v_head, preferred_element_type=jnp.float32)
        return mixed / total

    outcome = lax.map(one_head, (q_three, k_three, v_three))
    return outcome.transpose(1, 0, 2).reshape(count, heads * HEAD_DIM).astype(jnp.bfloat16)


def ordered(mine, theirs, upper):
    return jnp.where(upper == 1, jnp.concatenate([theirs, mine]), jnp.concatenate([mine, theirs]))


def general(queries, keys, values, pair_mask, tile_offset):
    frames_n = lax.axis_size("frame")
    current = lax.axis_index("frame")
    q_rows, k_rows, v_rows = (
        lax.all_to_all(queries, "head", split_axis=1, concat_axis=0, tiled=True),
        lax.all_to_all(keys, "head", split_axis=1, concat_axis=0, tiled=True),
        lax.all_to_all(values, "head", split_axis=1, concat_axis=0, tiled=True),
    )
    count = q_rows.shape[0]
    width = q_rows.shape[1]
    tiles = frames_n // 2
    tile = count // tiles
    depth = frames_n.bit_length() - 1
    stacked = jnp.stack([k_rows, v_rows])
    near = padded(stacked, (("frame", 1),), count)
    near_index = current - 1 + jnp.arange(3, dtype=jnp.int32)
    near_good = ((near_index >= 0) & (near_index < frames_n)).astype(jnp.float32)
    key_parts = [near[0]]
    value_parts = [near[1]]
    valid_parts = [jnp.repeat(near_good, count)]
    mask_row = pair_mask[0]
    offset = tile_offset[0]
    k_tiles = k_rows.reshape(tiles, tile, width)
    v_tiles = v_rows.reshape(tiles, tile, width)
    own = {}
    for level in range(1, depth):
        own[level] = (
            subsample(k_tiles, offset, level, tiles, tile)[None],
            subsample(v_tiles, offset, level, tiles, tile)[None],
        )
    sibling = {}
    cut = max(1, depth - 2)
    upper_levels = [level for level in range(1, depth) if level >= cut]
    k_pack = jnp.concatenate([own[level][0].reshape(-1, width) for level in upper_levels])
    v_pack = jnp.concatenate([own[level][1].reshape(-1, width) for level in upper_levels])
    k_every, v_every = (
        lax.all_gather(k_pack, "frame", axis=0, tiled=True),
        lax.all_gather(v_pack, "frame", axis=0, tiled=True),
    )
    k_every = k_every.reshape(frames_n, -1, width)
    v_every = v_every.reshape(frames_n, -1, width)
    position = 0
    for level in upper_levels:
        step = 2**level
        rows = count // step
        start = jnp.bitwise_xor(current // step, 1) * step
        block_k = lax.dynamic_slice_in_dim(k_every[:, position : position + rows], start, step, 0)
        block_v = lax.dynamic_slice_in_dim(v_every[:, position : position + rows], start, step, 0)
        sibling[level] = (block_k, block_v)
        position = position + rows
    swap_levels = [level for level in range(1, depth) if level < cut]
    growing = {level: own[level] for level in swap_levels}
    sections = cut if swap_levels else 0
    for bit in range(sections):
        active = [level for level in swap_levels if level >= bit]
        k_pack = jnp.concatenate([growing[level][0].reshape(-1, width) for level in active])
        v_pack = jnp.concatenate([growing[level][1].reshape(-1, width) for level in active])
        k_in, v_in = (from_partner(k_pack, "frame", bit), from_partner(v_pack, "frame", bit))
        upper = current // 2**bit % 2
        position = 0
        for level in active:
            shape = growing[level][0].shape
            size = shape[0] * shape[1]
            theirs_k = k_in[position : position + size].reshape(shape)
            theirs_v = v_in[position : position + size].reshape(shape)
            position = position + size
            if level == bit:
                sibling[level] = (theirs_k, theirs_v)
            else:
                growing[level] = (
                    ordered(growing[level][0], theirs_k, upper),
                    ordered(growing[level][1], theirs_v, upper),
                )
    for level in range(1, depth):
        step = 2**level
        start = jnp.bitwise_xor(current // step, 1) * step
        frame_ids = start + jnp.arange(step, dtype=jnp.int32)
        allowed = lax.dynamic_slice_in_dim(mask_row, start, step, 0)
        good = ((jnp.abs(frame_ids - current) >= 2) & (allowed == 1)).astype(jnp.float32)
        block_k, block_v = sibling[level]
        key_parts.append(block_k.reshape(-1, width))
        value_parts.append(block_v.reshape(-1, width))
        valid_parts.append(jnp.repeat(good, block_k.shape[1]))
    result = attend(
        q_rows,
        jnp.concatenate(key_parts),
        jnp.concatenate(value_parts),
        jnp.concatenate(valid_parts),
    )
    return lax.all_to_all(result, "head", split_axis=0, concat_axis=1, tiled=True)


def attention_kernel(info, q0, q1, q2, q3, own_s, own_u, n1_s, n1_u, n2_s, n2_u, r1, r2, r3, o0, o1, o2, o3, held):
    tile = own_s.shape[1]
    rows = q0.shape[0]
    factor = SCALE * LOG2E

    def body(slots):
        for pair in ((q0, q1, o0, o1), (q2, q3, o2, o3)):
            q = jnp.concatenate([pair[0][...], pair[1][...]], axis=0)
            top = None
            for at, (ref, valid) in enumerate(slots):
                s = lax.dot_general(q, ref[0], (((1,), (1,)), ((), ())), preferred_element_type=jnp.float32)
                held[:, at * tile : (at + 1) * tile] = s
                best = jnp.max(s, axis=1, keepdims=True)
                if valid is not None:
                    best = jnp.where(valid == 1, best, -1e30)
                top = best if top is None else jnp.maximum(top, best)
            total, mixed = None, None
            for at, (ref, valid) in enumerate(slots):
                level = top if valid is None else jnp.where(valid == 1, top, 1e30)
                w = jnp.exp2((held[:, at * tile : (at + 1) * tile] - level) * factor)
                part = jnp.sum(w, axis=1, keepdims=True)
                mix = jnp.dot(w.astype(jnp.bfloat16), ref[1], preferred_element_type=jnp.float32)
                total = part if total is None else total + part
                mixed = mix if mixed is None else mixed + mix
            result = (mixed / total).astype(jnp.bfloat16)
            pair[2][...] = result[:rows]
            pair[3][...] = result[rows:]

    always = [(own_s, None), (own_u, None), (n1_s, None), (n1_u, None)]

    @pl.when(info[1] == 1)
    def _():
        body(always + [(n2_s, None), (n2_u, None), (r1, info[2])])

    @pl.when(info[1] == 0)
    def _():
        body(always + [(r2, info[2]), (r3, info[3])])


def attention(info, q_own, q_in, slots, heads):
    rows = q_in[0].shape[0]
    tile = slots[0].shape[1]
    q_own_spec = pl.BlockSpec((rows, HEAD_DIM), lambda i, info: (0, info[0] * heads + i))
    q_spec = pl.BlockSpec((rows, HEAD_DIM), lambda i, info: (0, i))
    kv_spec = pl.BlockSpec((2, tile, HEAD_DIM), lambda i, info: (0, 0, i))
    flops = heads * 4 * rows * 7 * tile * HEAD_DIM * 4
    return pl.pallas_call(
        attention_kernel,
        grid_spec=pltpu.PrefetchScalarGridSpec(
            num_scalar_prefetch=1,
            grid=(heads,),
            in_specs=[q_own_spec] + [q_spec] * 3 + [kv_spec] * len(slots),
            out_specs=[q_spec] * 4,
            scratch_shapes=[pltpu.VMEM((2 * rows, 7 * tile), jnp.float32)],
        ),
        out_shape=[jax.ShapeDtypeStruct((rows, heads * HEAD_DIM), jnp.bfloat16)] * 4,
        compiler_params=pltpu.CompilerParams(vmem_limit_bytes=32 * 1024 * 1024),
        cost_estimate=pl.CostEstimate(
            flops=flops, bytes_accessed=heads * HEAD_DIM * 2 * (8 * rows + 18 * tile), transcendentals=heads * 28 * rows * tile
        ),
    )(info, q_own, *q_in, *slots)


def four_frames(queries, keys, values, pair_mask, tile_offset):
    z = lax.axis_index("frame")
    h = lax.axis_index("head")
    rows, features = queries.shape
    width = features // 4
    heads = width // HEAD_DIM

    def columns(x, j):
        return lax.dynamic_slice_in_dim(x, j * width, width, axis=1)

    def to_head(x, d):
        return lax.ppermute(x, "head", [(i, i ^ d) for i in range(4)])

    def along(x, pairs):
        return lax.ppermute(x, "frame", pairs)

    kv = [jnp.stack([columns(keys, h ^ d), columns(values, h ^ d)]) for d in range(4)]
    kv = [kv[0]] + [to_head(kv[d], d) for d in (1, 2, 3)]
    mine = jnp.concatenate(kv[:2], axis=1)
    other = jnp.concatenate(kv[2:], axis=1)
    here = h // 2 == tile_offset[0]
    own_s = jnp.where(here, mine, other)
    own_u = jnp.where(here, other, mine)

    outer = [(0, 1), (1, 0), (2, 3), (3, 2)]
    inner = [(1, 2), (2, 1)]
    outward = [(1, 0), (2, 3)]
    n1_s = along(own_s, outer)
    n2_s = along(own_s, inner)
    r1 = along(n1_s, inner)
    r2 = along(n2_s, outward)
    n1_u = along(own_u, outer)
    n2_u = along(own_u, inner)
    r3 = along(r1, outward)

    q_in = [to_head(columns(queries, h ^ d), d) for d in (1, 2, 3)]

    mask_row = pair_mask[0]
    info = jnp.stack([h, ((z == 1) | (z == 2)).astype(jnp.int32), mask_row[z ^ 2], mask_row[z ^ 3]]).astype(jnp.int32)
    out = attention(info, queries, q_in, [own_s, own_u, n1_s, n1_u, n2_s, n2_u, r1, r2, r3], heads)
    out = [out[0]] + [to_head(out[d], d) for d in (1, 2, 3)]
    result = jnp.zeros((rows, features), jnp.bfloat16)
    for d in range(4):
        result = lax.dynamic_update_slice_in_dim(result, out[d], (h ^ d) * width, axis=1)
    return result


def solution(mesh):
    sizes = dict(mesh.shape)
    per_device = four_frames if sizes["frame"] == 4 and sizes["head"] == 4 else general
    return jax.shard_map(
        per_device,
        mesh=mesh,
        in_specs=(
            P(("parts", "frame", "head"), None),
            P(("parts", "frame", "head"), None),
            P(("parts", "frame", "head"), None),
            P(("parts", "frame"), None),
            P(("parts", "frame")),
        ),
        out_specs=P(("parts", "frame", "head"), None),
        check_vma=False,
    )
```

```python
import math

import jax
import jax.numpy as jnp
from jax import lax
from jax.experimental import pallas as pl
from jax.experimental.pallas import tpu as pltpu
from jax.sharding import PartitionSpec as P

HEAD_DIM = 128
SCALE = 1.0 / HEAD_DIM**0.5
LOG2E = math.log2(math.e)


def padded(x, sides, width):
    for axis, dim in sides:
        peers, length = (lax.axis_size(axis), x.shape[dim])
        up = [(i, (i + 1) % peers) for i in range(peers - 1)]
        down = [(j, i) for i, j in up]
        last = lax.slice_in_dim(x, length - width, length, axis=dim)
        leading = lax.slice_in_dim(x, 0, width, axis=dim)
        before = lax.ppermute(last, axis, up)
        after = lax.ppermute(leading, axis, down)
        x = jnp.concatenate([before, x, after], axis=dim)
    return x


def from_partner(x, axis, bit):
    return lax.ppermute(x, axis, [(i, i ^ 1 << bit) for i in range(lax.axis_size(axis))])


def subsample(frame_rows, offset, level, tiles, tile):
    step = 2**level
    width = frame_rows.shape[-1]
    grouped = frame_rows.reshape(tiles // step, step, tile, width)
    picked = lax.dynamic_index_in_dim(grouped, offset % step, 1, keepdims=False)
    return picked.reshape(-1, width)


def attend(query_rows, key_rows, value_rows, valid):
    count = query_rows.shape[0]
    heads = query_rows.shape[1] // HEAD_DIM
    q_three = query_rows.reshape(count, heads, HEAD_DIM).transpose(1, 0, 2)
    k_three = key_rows.reshape(-1, heads, HEAD_DIM).transpose(1, 0, 2)
    v_three = value_rows.reshape(-1, heads, HEAD_DIM).transpose(1, 0, 2)

    def one_head(operands):
        q_head, k_head, v_head = operands
        scores = jnp.dot(q_head, k_head.T, preferred_element_type=jnp.float32) * SCALE
        scores = jnp.where(valid[None, :] > 0, scores, -1e30)
        top = jnp.max(scores, axis=1, keepdims=True)
        weights = jnp.exp(scores - top) * valid[None, :]
        total = jnp.sum(weights, axis=1, keepdims=True)
        mixed = jnp.dot(weights.astype(jnp.bfloat16), v_head, preferred_element_type=jnp.float32)
        return mixed / total

    outcome = lax.map(one_head, (q_three, k_three, v_three))
    return outcome.transpose(1, 0, 2).reshape(count, heads * HEAD_DIM).astype(jnp.bfloat16)


def ordered(mine, theirs, upper):
    return jnp.where(upper == 1, jnp.concatenate([theirs, mine]), jnp.concatenate([mine, theirs]))


def general(queries, keys, values, pair_mask, tile_offset):
    frames_n = lax.axis_size("frame")
    current = lax.axis_index("frame")
    q_rows, k_rows, v_rows = (
        lax.all_to_all(queries, "head", split_axis=1, concat_axis=0, tiled=True),
        lax.all_to_all(keys, "head", split_axis=1, concat_axis=0, tiled=True),
        lax.all_to_all(values, "head", split_axis=1, concat_axis=0, tiled=True),
    )
    count = q_rows.shape[0]
    width = q_rows.shape[1]
    tiles = frames_n // 2
    tile = count // tiles
    depth = frames_n.bit_length() - 1
    stacked = jnp.stack([k_rows, v_rows])
    near = padded(stacked, (("frame", 1),), count)
    near_index = current - 1 + jnp.arange(3, dtype=jnp.int32)
    near_good = ((near_index >= 0) & (near_index < frames_n)).astype(jnp.float32)
    key_parts = [near[0]]
    value_parts = [near[1]]
    valid_parts = [jnp.repeat(near_good, count)]
    mask_row = pair_mask[0]
    offset = tile_offset[0]
    k_tiles = k_rows.reshape(tiles, tile, width)
    v_tiles = v_rows.reshape(tiles, tile, width)
    own = {}
    for level in range(1, depth):
        own[level] = (
            subsample(k_tiles, offset, level, tiles, tile)[None],
            subsample(v_tiles, offset, level, tiles, tile)[None],
        )
    sibling = {}
    cut = max(1, depth - 2)
    upper_levels = [level for level in range(1, depth) if level >= cut]
    k_pack = jnp.concatenate([own[level][0].reshape(-1, width) for level in upper_levels])
    v_pack = jnp.concatenate([own[level][1].reshape(-1, width) for level in upper_levels])
    k_every, v_every = (
        lax.all_gather(k_pack, "frame", axis=0, tiled=True),
        lax.all_gather(v_pack, "frame", axis=0, tiled=True),
    )
    k_every = k_every.reshape(frames_n, -1, width)
    v_every = v_every.reshape(frames_n, -1, width)
    position = 0
    for level in upper_levels:
        step = 2**level
        rows = count // step
        start = jnp.bitwise_xor(current // step, 1) * step
        block_k = lax.dynamic_slice_in_dim(k_every[:, position : position + rows], start, step, 0)
        block_v = lax.dynamic_slice_in_dim(v_every[:, position : position + rows], start, step, 0)
        sibling[level] = (block_k, block_v)
        position = position + rows
    swap_levels = [level for level in range(1, depth) if level < cut]
    growing = {level: own[level] for level in swap_levels}
    sections = cut if swap_levels else 0
    for bit in range(sections):
        active = [level for level in swap_levels if level >= bit]
        k_pack = jnp.concatenate([growing[level][0].reshape(-1, width) for level in active])
        v_pack = jnp.concatenate([growing[level][1].reshape(-1, width) for level in active])
        k_in, v_in = (from_partner(k_pack, "frame", bit), from_partner(v_pack, "frame", bit))
        upper = current // 2**bit % 2
        position = 0
        for level in active:
            shape = growing[level][0].shape
            size = shape[0] * shape[1]
            theirs_k = k_in[position : position + size].reshape(shape)
            theirs_v = v_in[position : position + size].reshape(shape)
            position = position + size
            if level == bit:
                sibling[level] = (theirs_k, theirs_v)
            else:
                growing[level] = (
                    ordered(growing[level][0], theirs_k, upper),
                    ordered(growing[level][1], theirs_v, upper),
                )
    for level in range(1, depth):
        step = 2**level
        start = jnp.bitwise_xor(current // step, 1) * step
        frame_ids = start + jnp.arange(step, dtype=jnp.int32)
        allowed = lax.dynamic_slice_in_dim(mask_row, start, step, 0)
        good = ((jnp.abs(frame_ids - current) >= 2) & (allowed == 1)).astype(jnp.float32)
        block_k, block_v = sibling[level]
        key_parts.append(block_k.reshape(-1, width))
        value_parts.append(block_v.reshape(-1, width))
        valid_parts.append(jnp.repeat(good, block_k.shape[1]))
    result = attend(
        q_rows,
        jnp.concatenate(key_parts),
        jnp.concatenate(value_parts),
        jnp.concatenate(valid_parts),
    )
    return lax.all_to_all(result, "head", split_axis=0, concat_axis=1, tiled=True)


STAGES = (3, 2)
OUTER = [(0, 1), (1, 0), (2, 3), (3, 2)]
INNER = [(1, 2), (2, 1)]
INWARD = [(0, 1), (3, 2)]
OUTWARD = [(1, 0), (2, 3)]


def attend_rows(q, slots, held):
    factor = SCALE * LOG2E
    top = None
    spans = []
    for k, v, valid in slots:
        begin = spans[-1][1] if spans else 0
        spans.append((begin, begin + k.shape[0]))
        s = lax.dot_general(q, k, (((1,), (1,)), ((), ())), preferred_element_type=jnp.float32)
        held[:, spans[-1][0] : spans[-1][1]] = s
        best = jnp.max(s, axis=1, keepdims=True)
        if valid is not None:
            best = jnp.where(valid, best, -1e30)
        top = best if top is None else jnp.maximum(top, best)
    total, mixed = None, None
    for (k, v, valid), (begin, end) in zip(slots, spans):
        level = top if valid is None else jnp.where(valid, top, 1e30)
        w = jnp.exp2((held[:, begin:end] - level) * factor)
        part = jnp.sum(w, axis=1, keepdims=True)
        mix = jnp.dot(w.astype(jnp.bfloat16), v, preferred_element_type=jnp.float32)
        total = part if total is None else total + part
        mixed = mix if mixed is None else mixed + mix
    return (mixed / total).astype(jnp.bfloat16)


def attention_kernel(guest, scalars, refs):
    mask, off2 = scalars
    z = lax.axis_index("frame")
    x = lax.axis_index("head") // 2
    qs, kvs, outs, held = refs

    @pl.when((z == 1) | (z == 2))
    def _():
        tiles = []
        for k, v in kvs:
            for begin in range(0, k.shape[0], held.shape[2] // 7):
                span = slice(begin, begin + held.shape[2] // 7)
                tiles.append((k[span], v[span]))
        if guest:
            far = mask[0, z ^ 3] == 1
            picked = off2[0] == x
            valid = [None] * 4 + [far & picked, far & jnp.logical_not(picked), mask[0, z ^ 2] == 1]
        else:
            valid = [None] * 6 + [mask[0, z ^ 2] == 1]
        slots = [(k, v, ok) for (k, v), ok in zip(tiles, valid)]
        rows = held.shape[1]
        for half, q in enumerate(qs):
            for begin in range(0, q.shape[0], rows):
                out = attend_rows(q[begin : begin + rows], slots, held.at[half + begin // rows])
                at = half * q.shape[0] + begin
                for ref, first in outs:
                    if first <= at < first + ref.shape[0] or at <= first < at + rows:
                        low, high = max(at, first), min(at + rows, first + ref.shape[0])
                        ref[low - first : high - first] = out[low - at : high - at]


def attention(guest, mask, off2, q, first, kv, heads, outs):
    n_q, n_kv, n_out = len(q), len(kv), len(outs)
    tile = kv[0].shape[0]
    half = sum(outs) // 2

    def body(*refs):
        kvs = refs[2 + n_q : 2 + n_q + 2 * n_kv]
        placed, at = [], 0
        for ref in refs[2 + n_q + 2 * n_kv : 2 + n_q + 2 * n_kv + n_out]:
            placed.append((ref, at))
            at += ref.shape[0]
        attention_kernel(
            guest, refs[:2], (refs[2 : 2 + n_q], list(zip(kvs[::2], kvs[1::2])), placed, refs[-1])
        )

    def spec(x, at):
        return pl.BlockSpec((x.shape[0], HEAD_DIM), lambda i: (0, at + i))

    blocks = [(x, first) for x in q]
    for x in kv:
        blocks += [(x, 0), (x, heads)]
    return pl.pallas_call(
        body,
        grid=(heads,),
        in_specs=[pl.BlockSpec(memory_space=pltpu.SMEM)] * 2 + [spec(x, at) for x, at in blocks],
        out_specs=[pl.BlockSpec((rows, HEAD_DIM), lambda i: (0, i)) for rows in outs],
        out_shape=[jax.ShapeDtypeStruct((rows, heads * HEAD_DIM), jnp.bfloat16) for rows in outs],
        scratch_shapes=[pltpu.VMEM((2, half, 7 * tile), jnp.float32)],
        compiler_params=pltpu.CompilerParams(vmem_limit_bytes=32 * 1024 * 1024),
        cost_estimate=pl.CostEstimate(
            flops=heads * 2 * half * 7 * tile * HEAD_DIM * 4,
            bytes_accessed=heads * HEAD_DIM * 2 * (4 * half + 14 * tile),
            transcendentals=heads * 2 * half * 7 * tile,
        ),
    )(mask, off2, *[x for x, _ in blocks])


def four_frames(queries, keys, values, pair_mask, tile_offset):
    z = lax.axis_index("frame")
    h = lax.axis_index("head")
    rows, features = queries.shape
    width = features // 4
    heads = width // HEAD_DIM
    stages, begin = [], 0
    for count in STAGES[:-1]:
        stages.append((begin, begin + count))
        begin += count
    stages.append((begin, heads))

    def columns(x, d, begin, end):
        return lax.dynamic_slice_in_dim(x, (h ^ d) * width + begin * HEAD_DIM, (end - begin) * HEAD_DIM, axis=1)

    def to_head(x, d):
        return lax.ppermute(x, "head", [(i, i ^ d) for i in range(4)])

    def along(x, pairs):
        return lax.ppermute(x, "frame", pairs)

    def after(x, earlier):
        return lax.optimization_barrier((x, earlier))[0]

    def kv_columns(d, stage):
        return [columns(keys, d, *stage), columns(values, d, *stage)]

    mask1 = along(pair_mask, INWARD)
    off1 = along(tile_offset, INWARD)
    off2 = along(tile_offset, INNER)
    x = h // 2

    width1 = 2 * (stages[0][1] - stages[0][0]) * HEAD_DIM
    got = to_head(jnp.concatenate(kv_columns(1, stages[0]) + kv_columns(3, stages[0]), axis=1), 1)
    mine = jnp.concatenate([jnp.concatenate(kv_columns(0, stages[0]), axis=1), got[:, :width1]], axis=0)
    pay = jnp.concatenate([jnp.concatenate(kv_columns(2, stages[0]), axis=1), got[:, width1:]], axis=0)
    other = to_head(pay, 2)
    n1 = [along(mine, INWARD)]
    n2 = [along(mine, INNER)]
    n1.append(along(other, INWARD))
    n2.append(along(other, INNER))
    r1 = along(jnp.where(x == off1[0], n1[0], n1[1]), INNER)
    kv = [[mine, other, *n1, *n2, r1]]

    width2 = 2 * (stages[1][1] - stages[1][0]) * HEAD_DIM
    pieces = [columns(queries, 1, 0, heads), columns(queries, 3, 0, heads)] + kv_columns(1, stages[1]) + kv_columns(3, stages[1])
    got = to_head(after(jnp.concatenate(pieces, axis=1), mine), 1)
    q_mine = jnp.concatenate([columns(queries, 0, 0, heads), got[:, :width]], axis=0)
    pay = jnp.concatenate([columns(queries, 2, 0, heads), got[:, width : 2 * width]], axis=0)
    q_other = to_head(after(pay, other), 2)
    mine = jnp.concatenate([jnp.concatenate(kv_columns(0, stages[1]), axis=1), got[:, 2 * width : 2 * width + width2]], axis=0)
    pay = jnp.concatenate([jnp.concatenate(kv_columns(2, stages[1]), axis=1), got[:, 2 * width + width2 :]], axis=0)
    other = to_head(after(pay, q_other), 2)
    guests = []
    for begin, end in stages:
        span = slice(begin * HEAD_DIM, end * HEAD_DIM)
        guests.append(along(jnp.concatenate([q_mine[:, span], q_other[:, span]], axis=0), INWARD))
    whole = jnp.concatenate([mine, other], axis=0)
    n1 = along(whole, INWARD)
    n2 = along(whole, INNER)
    r1 = along(lax.dynamic_slice_in_dim(n1, jnp.where(x == off1[0], 0, 2 * rows), 2 * rows, axis=0), INNER)
    kv.append([mine, other, n1, n2, r1])

    end_frame = (z == 0) | (z == 3)
    result = jnp.zeros((rows, features), jnp.bfloat16)
    for (begin, end), guest, arrays in zip(stages, guests, kv):
        (far,) = attention(True, mask1, off2, [guest], 0, arrays, end - begin, [4 * rows])
        back = along(far, OUTWARD)
        own = attention(False, pair_mask, off2, [q_mine, q_other], begin, arrays, end - begin, [rows] * 4)
        out = [jnp.where(end_frame, back[d * rows : (d + 1) * rows], own[d]) for d in range(4)]
        out = [out[0]] + [to_head(out[d], d) for d in (1, 2, 3)]
        for d in range(4):
            result = lax.dynamic_update_slice_in_dim(result, out[d], (h ^ d) * width + begin * HEAD_DIM, axis=1)
    return result


def solution(mesh):
    sizes = dict(mesh.shape)
    per_device = four_frames if sizes["frame"] == 4 and sizes["head"] == 4 else general
    return jax.shard_map(
        per_device,
        mesh=mesh,
        in_specs=(
            P(("parts", "frame", "head"), None),
            P(("parts", "frame", "head"), None),
            P(("parts", "frame", "head"), None),
            P(("parts", "frame"), None),
            P(("parts", "frame")),
        ),
        out_specs=P(("parts", "frame", "head"), None),
        check_vma=False,
    )
```

```python
import math

import jax
import jax.numpy as jnp
from jax import lax
from jax.experimental import pallas as pl
from jax.experimental.pallas import tpu as pltpu
from jax.sharding import PartitionSpec as P

HEAD_DIM = 128
SCALE = 1.0 / HEAD_DIM**0.5
LOG2E = math.log2(math.e)


def padded(x, sides, width):
    for axis, dim in sides:
        peers, length = (lax.axis_size(axis), x.shape[dim])
        up = [(i, (i + 1) % peers) for i in range(peers - 1)]
        down = [(j, i) for i, j in up]
        last = lax.slice_in_dim(x, length - width, length, axis=dim)
        leading = lax.slice_in_dim(x, 0, width, axis=dim)
        before = lax.ppermute(last, axis, up)
        after = lax.ppermute(leading, axis, down)
        x = jnp.concatenate([before, x, after], axis=dim)
    return x


def from_partner(x, axis, bit):
    return lax.ppermute(x, axis, [(i, i ^ 1 << bit) for i in range(lax.axis_size(axis))])


def subsample(frame_rows, offset, level, tiles, tile):
    step = 2**level
    width = frame_rows.shape[-1]
    grouped = frame_rows.reshape(tiles // step, step, tile, width)
    picked = lax.dynamic_index_in_dim(grouped, offset % step, 1, keepdims=False)
    return picked.reshape(-1, width)


def attend(query_rows, key_rows, value_rows, valid):
    count = query_rows.shape[0]
    heads = query_rows.shape[1] // HEAD_DIM
    q_three = query_rows.reshape(count, heads, HEAD_DIM).transpose(1, 0, 2)
    k_three = key_rows.reshape(-1, heads, HEAD_DIM).transpose(1, 0, 2)
    v_three = value_rows.reshape(-1, heads, HEAD_DIM).transpose(1, 0, 2)

    def one_head(operands):
        q_head, k_head, v_head = operands
        scores = jnp.dot(q_head, k_head.T, preferred_element_type=jnp.float32) * SCALE
        scores = jnp.where(valid[None, :] > 0, scores, -1e30)
        top = jnp.max(scores, axis=1, keepdims=True)
        weights = jnp.exp(scores - top) * valid[None, :]
        total = jnp.sum(weights, axis=1, keepdims=True)
        mixed = jnp.dot(weights.astype(jnp.bfloat16), v_head, preferred_element_type=jnp.float32)
        return mixed / total

    outcome = lax.map(one_head, (q_three, k_three, v_three))
    return outcome.transpose(1, 0, 2).reshape(count, heads * HEAD_DIM).astype(jnp.bfloat16)


def ordered(mine, theirs, upper):
    return jnp.where(upper == 1, jnp.concatenate([theirs, mine]), jnp.concatenate([mine, theirs]))


def general(queries, keys, values, pair_mask, tile_offset):
    frames_n = lax.axis_size("frame")
    current = lax.axis_index("frame")
    q_rows, k_rows, v_rows = (
        lax.all_to_all(queries, "head", split_axis=1, concat_axis=0, tiled=True),
        lax.all_to_all(keys, "head", split_axis=1, concat_axis=0, tiled=True),
        lax.all_to_all(values, "head", split_axis=1, concat_axis=0, tiled=True),
    )
    count = q_rows.shape[0]
    width = q_rows.shape[1]
    tiles = frames_n // 2
    tile = count // tiles
    depth = frames_n.bit_length() - 1
    stacked = jnp.stack([k_rows, v_rows])
    near = padded(stacked, (("frame", 1),), count)
    near_index = current - 1 + jnp.arange(3, dtype=jnp.int32)
    near_good = ((near_index >= 0) & (near_index < frames_n)).astype(jnp.float32)
    key_parts = [near[0]]
    value_parts = [near[1]]
    valid_parts = [jnp.repeat(near_good, count)]
    mask_row = pair_mask[0]
    offset = tile_offset[0]
    k_tiles = k_rows.reshape(tiles, tile, width)
    v_tiles = v_rows.reshape(tiles, tile, width)
    own = {}
    for level in range(1, depth):
        own[level] = (
            subsample(k_tiles, offset, level, tiles, tile)[None],
            subsample(v_tiles, offset, level, tiles, tile)[None],
        )
    sibling = {}
    cut = max(1, depth - 2)
    upper_levels = [level for level in range(1, depth) if level >= cut]
    k_pack = jnp.concatenate([own[level][0].reshape(-1, width) for level in upper_levels])
    v_pack = jnp.concatenate([own[level][1].reshape(-1, width) for level in upper_levels])
    k_every, v_every = (
        lax.all_gather(k_pack, "frame", axis=0, tiled=True),
        lax.all_gather(v_pack, "frame", axis=0, tiled=True),
    )
    k_every = k_every.reshape(frames_n, -1, width)
    v_every = v_every.reshape(frames_n, -1, width)
    position = 0
    for level in upper_levels:
        step = 2**level
        rows = count // step
        start = jnp.bitwise_xor(current // step, 1) * step
        block_k = lax.dynamic_slice_in_dim(k_every[:, position : position + rows], start, step, 0)
        block_v = lax.dynamic_slice_in_dim(v_every[:, position : position + rows], start, step, 0)
        sibling[level] = (block_k, block_v)
        position = position + rows
    swap_levels = [level for level in range(1, depth) if level < cut]
    growing = {level: own[level] for level in swap_levels}
    sections = cut if swap_levels else 0
    for bit in range(sections):
        active = [level for level in swap_levels if level >= bit]
        k_pack = jnp.concatenate([growing[level][0].reshape(-1, width) for level in active])
        v_pack = jnp.concatenate([growing[level][1].reshape(-1, width) for level in active])
        k_in, v_in = (from_partner(k_pack, "frame", bit), from_partner(v_pack, "frame", bit))
        upper = current // 2**bit % 2
        position = 0
        for level in active:
            shape = growing[level][0].shape
            size = shape[0] * shape[1]
            theirs_k = k_in[position : position + size].reshape(shape)
            theirs_v = v_in[position : position + size].reshape(shape)
            position = position + size
            if level == bit:
                sibling[level] = (theirs_k, theirs_v)
            else:
                growing[level] = (
                    ordered(growing[level][0], theirs_k, upper),
                    ordered(growing[level][1], theirs_v, upper),
                )
    for level in range(1, depth):
        step = 2**level
        start = jnp.bitwise_xor(current // step, 1) * step
        frame_ids = start + jnp.arange(step, dtype=jnp.int32)
        allowed = lax.dynamic_slice_in_dim(mask_row, start, step, 0)
        good = ((jnp.abs(frame_ids - current) >= 2) & (allowed == 1)).astype(jnp.float32)
        block_k, block_v = sibling[level]
        key_parts.append(block_k.reshape(-1, width))
        value_parts.append(block_v.reshape(-1, width))
        valid_parts.append(jnp.repeat(good, block_k.shape[1]))
    result = attend(
        q_rows,
        jnp.concatenate(key_parts),
        jnp.concatenate(value_parts),
        jnp.concatenate(valid_parts),
    )
    return lax.all_to_all(result, "head", split_axis=0, concat_axis=1, tiled=True)


FIRST = 3
INFO_ROWS = 16
OUTER = [(0, 1), (1, 0), (2, 3), (3, 2)]
INNER = [(0, 0), (1, 2), (2, 1), (3, 3)]
OUTWARD = [(1, 0), (2, 3)]


def fold(x):
    parts = [x[:, at : at + 128] for at in range(0, x.shape[1], 128)]
    best = parts[0]
    for part in parts[1:]:
        best = jnp.maximum(best, part)
    return best


def scores_of(q, slots, held):
    free, top = None, None
    for at, (k, _, valid) in enumerate(slots):
        s = lax.dot_general(q, k(), (((1,), (1,)), ((), ())), preferred_element_type=jnp.float32)
        held[:, at * s.shape[1] : (at + 1) * s.shape[1]] = s
        best = fold(s)
        if valid is None:
            free = best if free is None else jnp.maximum(free, best)
        else:
            best = jnp.where(valid, jnp.max(best, axis=1, keepdims=True), -1e30)
            top = best if top is None else jnp.maximum(top, best)
    free = jnp.max(free, axis=1, keepdims=True)
    return free if top is None else jnp.maximum(free, top)


def mixed_of(top, slots, held):
    factor = SCALE * LOG2E
    total, mixed = None, None
    for at, (_, v, valid) in enumerate(slots):
        values = v()
        tile = values.shape[0]
        level = top if valid is None else jnp.where(valid, top, 1e30)
        w = jnp.exp2((held[:, at * tile : (at + 1) * tile] - level) * factor)
        mix = jnp.dot(w.astype(jnp.bfloat16), values, preferred_element_type=jnp.float32)
        mixed = mix if mixed is None else mixed + mix
        for begin in range(0, tile, 128):
            part = w[:, begin : begin + 128]
            total = part if total is None else total + part
    return (mixed * (1.0 / jnp.sum(total, axis=1, keepdims=True))).astype(jnp.bfloat16)


def tiles_of(ref, i, tile):
    half = ref.shape[1] // 2

    def load(begin, at):
        return lambda: ref[begin : begin + tile, pl.ds(pl.multiple_of(at + i * HEAD_DIM, HEAD_DIM), HEAD_DIM)]

    return [(load(begin, 0), load(begin, half)) for begin in range(0, ref.shape[0] - tile + 1, tile)]


def with_valid(pairs, valid):
    return [(k, v, ok) for (k, v), ok in zip(pairs, valid)]


def run_chunks(chunks):
    tops = []
    for q, slots, held, _ in chunks:
        tops.append(scores_of(q(), slots, held))
    for top, (_, slots, held, store) in zip(tops, chunks):
        store(mixed_of(top, slots, held))


def first_kernel(mask, q_mine, q_other, q_guest, mine, other, n1_mine, n1_other, n2_mine, n2_other, r1, *rest):
    outs, guest_out, held = rest[:4], rest[4], rest[5:]
    z = lax.axis_index("frame")
    x = (lax.axis_index("head") // 2).astype(jnp.float32)
    tile = r1.shape[0]
    rows = tile // 2
    heads = r1.shape[1] // (2 * HEAD_DIM)

    @pl.when((z == 1) | (z == 2))
    def _():
        def told(ref, group):
            return ref[tile : tile + 1, group * 128 : (group + 1) * 128][:, :1].astype(jnp.float32)

        near2 = jnp.where(z == 1, told(n1_mine, 2), told(n1_mine, 1)) > 0.5
        near1 = jnp.where(z == 1, told(n1_mine, 3), told(n1_mine, 0)) > 0.5
        picked = told(n2_mine, 4) == x
        own_valid = [None] * 6 + [mask[0, z ^ 2] == 1]
        guest_valid = [None] * 4 + [near2 & picked, near2 & jnp.logical_not(picked), near1]

        def one_head(i, carry):
            lanes = pl.ds(pl.multiple_of(i * HEAD_DIM, HEAD_DIM), HEAD_DIM)
            pairs = []
            for ref in (mine, other, n1_mine, n1_other, n2_mine, n2_other, r1):
                pairs += tiles_of(ref, i, tile)
            own, guest = with_valid(pairs, own_valid), with_valid(pairs, guest_valid)

            def keep_own(half):
                def store(value):
                    outs[2 * half][:, lanes] = value[:rows]
                    outs[2 * half + 1][:, lanes] = value[rows:]

                return store

            def keep_guest(half):
                def store(value):
                    guest_out[half * tile : (half + 1) * tile, lanes] = value

                return store

            chunks = [
                (lambda: q_guest[:tile, lanes], guest, held[0], keep_guest(0)),
                (lambda: q_guest[tile:, lanes], guest, held[1], keep_guest(1)),
                (lambda: q_mine[:, lanes], own, held[2], keep_own(0)),
                (lambda: q_other[:, lanes], own, held[3], keep_own(1)),
            ]
            run_chunks(chunks)
            return carry

        lax.fori_loop(0, heads, one_head, 0)


def second_kernel(mask, q_mine, q_other, whole, n1, n2, r1, r2, r3, *rest):
    outs, held = rest[:4], rest[4:]
    z = lax.axis_index("frame")
    tile = r1.shape[0]
    rows = tile // 2
    heads = r1.shape[1] // (2 * HEAD_DIM)
    skip = q_mine.shape[1] - heads * HEAD_DIM

    def body(refs, valid):
        def one_head(i, carry):
            lanes = pl.ds(pl.multiple_of(i * HEAD_DIM, HEAD_DIM), HEAD_DIM)
            q_lanes = pl.ds(pl.multiple_of(skip + i * HEAD_DIM, HEAD_DIM), HEAD_DIM)
            pairs = []
            for ref in refs:
                pairs += tiles_of(ref, i, tile)
            slots = with_valid(pairs, valid)

            def keep(half):
                def store(value):
                    outs[2 * half][:, lanes] = value[:rows]
                    outs[2 * half + 1][:, lanes] = value[rows:]

                return store

            run_chunks(
                [
                    (lambda: q_mine[:, q_lanes], slots, held[0], keep(0)),
                    (lambda: q_other[:, q_lanes], slots, held[1], keep(1)),
                ]
            )
            return carry

        lax.fori_loop(0, heads, one_head, 0)

    inner = (z == 1) | (z == 2)

    @pl.when(inner)
    def _():
        body([whole, n1, n2, r1], [None] * 6 + [mask[0, z ^ 2] == 1])

    @pl.when(jnp.logical_not(inner))
    def _():
        body([whole, n1, r2, r3], [None] * 4 + [mask[0, z ^ 2] == 1, mask[0, z ^ 3] == 1])


def run_kernel(kernel, mask, arrays, outs, chunks, tile, heads):
    return pl.pallas_call(
        kernel,
        in_specs=[pl.BlockSpec(memory_space=pltpu.SMEM)] + [pl.BlockSpec(memory_space=pltpu.VMEM)] * len(arrays),
        out_specs=[pl.BlockSpec(memory_space=pltpu.VMEM)] * len(outs),
        out_shape=[jax.ShapeDtypeStruct((rows, heads * HEAD_DIM), jnp.bfloat16) for rows in outs],
        scratch_shapes=[pltpu.VMEM((tile, 7 * tile), jnp.float32) for _ in range(chunks)],
        compiler_params=pltpu.CompilerParams(vmem_limit_bytes=20 * 1024 * 1024),
        cost_estimate=pl.CostEstimate(
            flops=heads * chunks * tile * 7 * tile * HEAD_DIM * 4,
            bytes_accessed=sum(x.size * 2 for x in arrays),
            transcendentals=heads * chunks * tile * 7 * tile,
        ),
    )(mask, *arrays)


def four_frames(queries, keys, values, pair_mask, tile_offset):
    z = lax.axis_index("frame")
    h = lax.axis_index("head")
    x = h // 2
    rows, features = queries.shape
    tile = 2 * rows
    width = features // 4
    heads = width // HEAD_DIM
    cut = FIRST * HEAD_DIM

    def columns(array, d, begin, end):
        return lax.dynamic_slice_in_dim(array, (h ^ d) * width + begin, end - begin, axis=1)

    def to_head(array, d):
        return lax.ppermute(array, "head", [(i, i ^ d) for i in range(4)])

    def along(array, pairs):
        return lax.ppermute(array, "frame", pairs)

    def after(array, earlier):
        return lax.optimization_barrier((array, earlier))[0]

    def beside(*arrays):
        return jnp.concatenate(arrays, axis=1)

    def below(*arrays):
        return jnp.concatenate(arrays, axis=0)

    k = [columns(keys, d, 0, cut) for d in range(4)]
    v = [columns(values, d, 0, cut) for d in range(4)]
    k, v = lax.optimization_barrier((k, v))
    got = to_head(beside(k[1], v[1], k[3], v[3]), 1)
    told = [pair_mask[0, g] for g in range(4)] + [tile_offset[0]] + [0] * (2 * FIRST - 5)
    told = beside(*[jnp.broadcast_to(jnp.asarray(t).astype(jnp.bfloat16), (INFO_ROWS, 128)) for t in told])
    mine = below(beside(k[0], v[0]), got[:, : 2 * cut], told)
    other = to_head(below(beside(k[2], v[2]), got[:, 2 * cut :]), 2)
    n1_mine = along(mine, OUTER)
    n2_mine = along(mine, INNER)
    n1_other = along(other, OUTER)
    n2_other = along(other, INNER)
    picked = n1_mine[tile, 4 * 128] == x.astype(jnp.bfloat16)
    r1 = along(jnp.where(picked, n1_mine[:tile], n1_other), INNER)
    first = [mine, other, n1_mine, n1_other, n2_mine, n2_other, r1]

    q = [columns(queries, d, 0, width) for d in range(4)]
    k = [columns(keys, d, cut, width) for d in range(4)]
    v = [columns(values, d, cut, width) for d in range(4)]
    q, k, v = lax.optimization_barrier((q, k, v))
    got = to_head(after(beside(q[1], q[3], k[1], v[1], k[3], v[3]), mine), 1)
    q_mine = below(q[0], got[:, :width])
    q_other = to_head(after(below(q[2], got[:, width : 2 * width]), other), 2)
    split = 2 * width + 2 * (width - cut)
    mine2 = below(beside(k[0], v[0]), got[:, 2 * width : split])
    other2 = to_head(after(below(beside(k[2], v[2]), got[:, split:]), q_other), 2)
    q_guest = along(below(q_mine[:, :cut], q_other[:, :cut]), OUTER)
    whole = jnp.where(x == tile_offset[0], below(mine2, other2), below(other2, mine2))
    n1 = along(whole, OUTER)
    n2 = along(whole, INNER)
    r1 = along(n1[:tile], INNER)
    r2 = along(n2[:tile], OUTER)
    r3 = along(r1, OUTER)

    *own, guest = run_kernel(
        first_kernel, pair_mask, [q_mine, q_other, q_guest, *first], [rows] * 4 + [2 * tile], 4, tile, FIRST
    )
    back = along(guest, OUTWARD)
    end_frame = (z == 0) | (z == 3)
    out = [jnp.where(end_frame, back[d * rows : (d + 1) * rows], own[d]) for d in range(4)]
    out = [out[0]] + [to_head(out[d], d) for d in (1, 2, 3)]
    late = run_kernel(
        second_kernel, pair_mask, [q_mine, q_other, whole, n1, n2, r1, r2, r3], [rows] * 4, 2, tile, heads - FIRST
    )
    late = [late[0]] + [to_head(late[d], d) for d in (1, 2, 3)]
    result = jnp.zeros((rows, features), jnp.bfloat16)
    for d in range(4):
        result = lax.dynamic_update_slice_in_dim(result, out[d], (h ^ d) * width, axis=1)
    for d in range(4):
        result = lax.dynamic_update_slice_in_dim(result, late[d], (h ^ d) * width + cut, axis=1)
    return result


def solution(mesh):
    sizes = dict(mesh.shape)
    per_device = four_frames if sizes["frame"] == 4 and sizes["head"] == 4 else general
    return jax.shard_map(
        per_device,
        mesh=mesh,
        in_specs=(
            P(("parts", "frame", "head"), None),
            P(("parts", "frame", "head"), None),
            P(("parts", "frame", "head"), None),
            P(("parts", "frame"), None),
            P(("parts", "frame")),
        ),
        out_specs=P(("parts", "frame", "head"), None),
        check_vma=False,
    )
```

```python
import functools
import math

import jax
import jax.numpy as jnp
from jax import lax
from jax.experimental import pallas as pl
from jax.experimental.pallas import tpu as pltpu
from jax.sharding import PartitionSpec as P

HEAD_DIM = 128
SCALE = 1.0 / HEAD_DIM**0.5
LOG2E = math.log2(math.e)


def padded(x, sides, width):
    for axis, dim in sides:
        peers, length = (lax.axis_size(axis), x.shape[dim])
        up = [(i, (i + 1) % peers) for i in range(peers - 1)]
        down = [(j, i) for i, j in up]
        last = lax.slice_in_dim(x, length - width, length, axis=dim)
        leading = lax.slice_in_dim(x, 0, width, axis=dim)
        before = lax.ppermute(last, axis, up)
        after = lax.ppermute(leading, axis, down)
        x = jnp.concatenate([before, x, after], axis=dim)
    return x


def from_partner(x, axis, bit):
    return lax.ppermute(x, axis, [(i, i ^ 1 << bit) for i in range(lax.axis_size(axis))])


def subsample(frame_rows, offset, level, tiles, tile):
    step = 2**level
    width = frame_rows.shape[-1]
    grouped = frame_rows.reshape(tiles // step, step, tile, width)
    picked = lax.dynamic_index_in_dim(grouped, offset % step, 1, keepdims=False)
    return picked.reshape(-1, width)


def attend(query_rows, key_rows, value_rows, valid):
    count = query_rows.shape[0]
    heads = query_rows.shape[1] // HEAD_DIM
    q_three = query_rows.reshape(count, heads, HEAD_DIM).transpose(1, 0, 2)
    k_three = key_rows.reshape(-1, heads, HEAD_DIM).transpose(1, 0, 2)
    v_three = value_rows.reshape(-1, heads, HEAD_DIM).transpose(1, 0, 2)

    def one_head(operands):
        q_head, k_head, v_head = operands
        scores = jnp.dot(q_head, k_head.T, preferred_element_type=jnp.float32) * SCALE
        scores = jnp.where(valid[None, :] > 0, scores, -1e30)
        top = jnp.max(scores, axis=1, keepdims=True)
        weights = jnp.exp(scores - top) * valid[None, :]
        total = jnp.sum(weights, axis=1, keepdims=True)
        mixed = jnp.dot(weights.astype(jnp.bfloat16), v_head, preferred_element_type=jnp.float32)
        return mixed / total

    outcome = lax.map(one_head, (q_three, k_three, v_three))
    return outcome.transpose(1, 0, 2).reshape(count, heads * HEAD_DIM).astype(jnp.bfloat16)


def ordered(mine, theirs, upper):
    return jnp.where(upper == 1, jnp.concatenate([theirs, mine]), jnp.concatenate([mine, theirs]))


def general(queries, keys, values, pair_mask, tile_offset):
    frames_n = lax.axis_size("frame")
    current = lax.axis_index("frame")
    q_rows, k_rows, v_rows = (
        lax.all_to_all(queries, "head", split_axis=1, concat_axis=0, tiled=True),
        lax.all_to_all(keys, "head", split_axis=1, concat_axis=0, tiled=True),
        lax.all_to_all(values, "head", split_axis=1, concat_axis=0, tiled=True),
    )
    count = q_rows.shape[0]
    width = q_rows.shape[1]
    tiles = frames_n // 2
    tile = count // tiles
    depth = frames_n.bit_length() - 1
    stacked = jnp.stack([k_rows, v_rows])
    near = padded(stacked, (("frame", 1),), count)
    near_index = current - 1 + jnp.arange(3, dtype=jnp.int32)
    near_good = ((near_index >= 0) & (near_index < frames_n)).astype(jnp.float32)
    key_parts = [near[0]]
    value_parts = [near[1]]
    valid_parts = [jnp.repeat(near_good, count)]
    mask_row = pair_mask[0]
    offset = tile_offset[0]
    k_tiles = k_rows.reshape(tiles, tile, width)
    v_tiles = v_rows.reshape(tiles, tile, width)
    own = {}
    for level in range(1, depth):
        own[level] = (
            subsample(k_tiles, offset, level, tiles, tile)[None],
            subsample(v_tiles, offset, level, tiles, tile)[None],
        )
    sibling = {}
    cut = max(1, depth - 2)
    upper_levels = [level for level in range(1, depth) if level >= cut]
    k_pack = jnp.concatenate([own[level][0].reshape(-1, width) for level in upper_levels])
    v_pack = jnp.concatenate([own[level][1].reshape(-1, width) for level in upper_levels])
    k_every, v_every = (
        lax.all_gather(k_pack, "frame", axis=0, tiled=True),
        lax.all_gather(v_pack, "frame", axis=0, tiled=True),
    )
    k_every = k_every.reshape(frames_n, -1, width)
    v_every = v_every.reshape(frames_n, -1, width)
    position = 0
    for level in upper_levels:
        step = 2**level
        rows = count // step
        start = jnp.bitwise_xor(current // step, 1) * step
        block_k = lax.dynamic_slice_in_dim(k_every[:, position : position + rows], start, step, 0)
        block_v = lax.dynamic_slice_in_dim(v_every[:, position : position + rows], start, step, 0)
        sibling[level] = (block_k, block_v)
        position = position + rows
    swap_levels = [level for level in range(1, depth) if level < cut]
    growing = {level: own[level] for level in swap_levels}
    sections = cut if swap_levels else 0
    for bit in range(sections):
        active = [level for level in swap_levels if level >= bit]
        k_pack = jnp.concatenate([growing[level][0].reshape(-1, width) for level in active])
        v_pack = jnp.concatenate([growing[level][1].reshape(-1, width) for level in active])
        k_in, v_in = (from_partner(k_pack, "frame", bit), from_partner(v_pack, "frame", bit))
        upper = current // 2**bit % 2
        position = 0
        for level in active:
            shape = growing[level][0].shape
            size = shape[0] * shape[1]
            theirs_k = k_in[position : position + size].reshape(shape)
            theirs_v = v_in[position : position + size].reshape(shape)
            position = position + size
            if level == bit:
                sibling[level] = (theirs_k, theirs_v)
            else:
                growing[level] = (
                    ordered(growing[level][0], theirs_k, upper),
                    ordered(growing[level][1], theirs_v, upper),
                )
    for level in range(1, depth):
        step = 2**level
        start = jnp.bitwise_xor(current // step, 1) * step
        frame_ids = start + jnp.arange(step, dtype=jnp.int32)
        allowed = lax.dynamic_slice_in_dim(mask_row, start, step, 0)
        good = ((jnp.abs(frame_ids - current) >= 2) & (allowed == 1)).astype(jnp.float32)
        block_k, block_v = sibling[level]
        key_parts.append(block_k.reshape(-1, width))
        value_parts.append(block_v.reshape(-1, width))
        valid_parts.append(jnp.repeat(good, block_k.shape[1]))
    result = attend(
        q_rows,
        jnp.concatenate(key_parts),
        jnp.concatenate(value_parts),
        jnp.concatenate(valid_parts),
    )
    return lax.all_to_all(result, "head", split_axis=0, concat_axis=1, tiled=True)


FIRST = 3
INFO_ROWS = 16
OUTER = [(0, 1), (1, 0), (2, 3), (3, 2)]
INNER = [(0, 0), (1, 2), (2, 1), (3, 3)]
OUTWARD = [(1, 0), (2, 3)]


def fold(x):
    parts = [x[:, at : at + 128] for at in range(0, x.shape[1], 128)]
    best = parts[0]
    for part in parts[1:]:
        best = jnp.maximum(best, part)
    return best


def scores_of(q, slots, held):
    free, top = None, None
    for at, (k, _, valid) in enumerate(slots):
        s = lax.dot_general(q, k(), (((1,), (1,)), ((), ())), preferred_element_type=jnp.float32)
        held[:, at * s.shape[1] : (at + 1) * s.shape[1]] = s
        best = fold(s)
        if valid is None:
            free = best if free is None else jnp.maximum(free, best)
        else:
            best = jnp.where(valid, jnp.max(best, axis=1, keepdims=True), -1e30)
            top = best if top is None else jnp.maximum(top, best)
    free = jnp.max(free, axis=1, keepdims=True)
    return free if top is None else jnp.maximum(free, top)


def mixed_of(top, slots, held):
    factor = SCALE * LOG2E
    total, mixed = None, None
    for at, (_, v, valid) in enumerate(slots):
        values = v()
        tile = values.shape[0]
        level = top if valid is None else jnp.where(valid, top, 1e30)
        w = jnp.exp2((held[:, at * tile : (at + 1) * tile] - level) * factor)
        mix = jnp.dot(w.astype(jnp.bfloat16), values, preferred_element_type=jnp.float32)
        mixed = mix if mixed is None else mixed + mix
        for begin in range(0, tile, 128):
            part = w[:, begin : begin + 128]
            total = part if total is None else total + part
    return (mixed * (1.0 / jnp.sum(total, axis=1, keepdims=True))).astype(jnp.bfloat16)


def tiles_of(ref, i, tile):
    half = ref.shape[1] // 2

    def load(begin, at):
        return lambda: ref[begin : begin + tile, pl.ds(pl.multiple_of(at + i * HEAD_DIM, HEAD_DIM), HEAD_DIM)]

    return [(load(begin, 0), load(begin, half)) for begin in range(0, ref.shape[0] - tile + 1, tile)]


def with_valid(pairs, valid):
    return [(k, v, ok) for (k, v), ok in zip(pairs, valid)]


def run_chunks(chunks):
    tops = []
    for q, slots, held, _ in chunks:
        tops.append(scores_of(q(), slots, held))
    for top, (_, slots, held, store) in zip(tops, chunks):
        store(mixed_of(top, slots, held))


def first_kernel(mask, q_mine, q_other, q_guest, mine, other, n1_mine, n1_other, n2_mine, n2_other, r1, *rest):
    outs, guest_out, held = rest[:4], rest[4], rest[5:]
    z = lax.axis_index("frame")
    x = (lax.axis_index("head") // 2).astype(jnp.float32)
    tile = r1.shape[0]
    rows = tile // 2
    heads = r1.shape[1] // (2 * HEAD_DIM)

    @pl.when((z == 1) | (z == 2))
    def _():
        def told(ref, group):
            return ref[tile : tile + 1, group * 128 : (group + 1) * 128][:, :1].astype(jnp.float32)

        near2 = jnp.where(z == 1, told(n1_mine, 2), told(n1_mine, 1)) > 0.5
        near1 = jnp.where(z == 1, told(n1_mine, 3), told(n1_mine, 0)) > 0.5
        picked = told(n2_mine, 4) == x
        own_valid = [None] * 6 + [mask[0, z ^ 2] == 1]
        guest_valid = [None] * 4 + [near2 & picked, near2 & jnp.logical_not(picked), near1]

        def one_head(i, carry):
            lanes = pl.ds(pl.multiple_of(i * HEAD_DIM, HEAD_DIM), HEAD_DIM)
            pairs = []
            for ref in (mine, other, n1_mine, n1_other, n2_mine, n2_other, r1):
                pairs += tiles_of(ref, i, tile)
            own, guest = with_valid(pairs, own_valid), with_valid(pairs, guest_valid)

            def keep_own(half):
                def store(value):
                    outs[2 * half][:, lanes] = value[:rows]
                    outs[2 * half + 1][:, lanes] = value[rows:]

                return store

            def keep_guest(half):
                def store(value):
                    guest_out[half * tile : (half + 1) * tile, lanes] = value

                return store

            chunks = [
                (lambda: q_guest[:tile, lanes], guest, held[0], keep_guest(0)),
                (lambda: q_guest[tile:, lanes], guest, held[1], keep_guest(1)),
                (lambda: q_mine[:, lanes], own, held[2], keep_own(0)),
                (lambda: q_other[:, lanes], own, held[3], keep_own(1)),
            ]
            run_chunks(chunks)
            return carry

        lax.fori_loop(0, heads, one_head, 0)


def second_kernel(mask, q_mine, q_other, whole, n1, n2, r1, r2, r3, *rest):
    outs, held = rest[:4], rest[4:]
    z = lax.axis_index("frame")
    tile = r1.shape[0]
    rows = tile // 2
    heads = r1.shape[1] // (2 * HEAD_DIM)
    skip = q_mine.shape[1] - heads * HEAD_DIM

    def body(refs, valid):
        def one_head(i, carry):
            lanes = pl.ds(pl.multiple_of(i * HEAD_DIM, HEAD_DIM), HEAD_DIM)
            q_lanes = pl.ds(pl.multiple_of(skip + i * HEAD_DIM, HEAD_DIM), HEAD_DIM)
            pairs = []
            for ref in refs:
                pairs += tiles_of(ref, i, tile)
            slots = with_valid(pairs, valid)

            def keep(half):
                def store(value):
                    outs[2 * half][:, lanes] = value[:rows]
                    outs[2 * half + 1][:, lanes] = value[rows:]

                return store

            run_chunks(
                [
                    (lambda: q_mine[:, q_lanes], slots, held[0], keep(0)),
                    (lambda: q_other[:, q_lanes], slots, held[1], keep(1)),
                ]
            )
            return carry

        lax.fori_loop(0, heads, one_head, 0)

    inner = (z == 1) | (z == 2)

    @pl.when(inner)
    def _():
        body([whole, n1, n2, r1], [None] * 6 + [mask[0, z ^ 2] == 1])

    @pl.when(jnp.logical_not(inner))
    def _():
        body([whole, n1, r2, r3], [None] * 4 + [mask[0, z ^ 2] == 1, mask[0, z ^ 3] == 1])


def pack_kernel(copies, width, mask, offset, *refs):
    ins, outs, sems = refs[:3], refs[3:-1], refs[-1]
    h = lax.axis_index("head")
    started = []
    for n, (operand, d, begin, result, at, lanes) in enumerate(copies):
        source = ins[operand].at[:, pl.ds(pl.multiple_of((h ^ d) * width + begin, HEAD_DIM), lanes)]
        copy = pltpu.make_async_copy(source, outs[result].at[:, at : at + lanes], sems.at[n])
        copy.start()
        started.append(copy)
    if len(outs) > 1 + max(copy[3] for copy in copies):
        told = outs[-1]
        for group in range(told.shape[1] // 128):
            value = mask[0, group] if group < 4 else offset[0]
            rows = jnp.full((told.shape[0], 128), value, jnp.int32).astype(jnp.float32)
            told[:, group * 128 : (group + 1) * 128] = rows.astype(told.dtype)
    for copy in started:
        copy.wait()


def packed(operands, mask, offset, results, width, told):
    rows = operands[0].shape[0]
    copies, shapes = [], []
    for n, parts in enumerate(results):
        at = 0
        for operand, d, begin, lanes in parts:
            copies.append((operand, d, begin, n, at, lanes))
            at += lanes
        shapes.append(jax.ShapeDtypeStruct((rows, at), jnp.bfloat16))
    if told:
        shapes.append(jax.ShapeDtypeStruct((INFO_ROWS, told), jnp.bfloat16))
    return pl.pallas_call(
        functools.partial(pack_kernel, copies, width),
        in_specs=[pl.BlockSpec(memory_space=pltpu.SMEM)] * 2 + [pl.BlockSpec(memory_space=pltpu.HBM)] * 3,
        out_specs=[pl.BlockSpec(memory_space=pltpu.VMEM)] * len(shapes),
        out_shape=shapes,
        scratch_shapes=[pltpu.SemaphoreType.DMA((len(copies),))],
        compiler_params=pltpu.CompilerParams(vmem_limit_bytes=4 * 1024 * 1024),
    )(mask, offset, *operands)


def relayed_kernel(mine, other, out):
    tile = out.shape[0]
    offset = jnp.max(mine[tile : tile + INFO_ROWS, 4 * 128 : 5 * 128].astype(jnp.float32))
    here = offset == (lax.axis_index("head") // 2).astype(jnp.float32)

    @pl.when(here)
    def _():
        out[...] = mine[:tile]

    @pl.when(jnp.logical_not(here))
    def _():
        out[...] = other[...]


def relayed(mine, other):
    return pl.pallas_call(
        relayed_kernel,
        in_specs=[pl.BlockSpec(memory_space=pltpu.VMEM)] * 2,
        out_specs=pl.BlockSpec(memory_space=pltpu.VMEM),
        out_shape=jax.ShapeDtypeStruct(other.shape, other.dtype),
    )(mine, other)


def run_kernel(kernel, mask, arrays, outs, chunks, tile, heads):
    return pl.pallas_call(
        kernel,
        in_specs=[pl.BlockSpec(memory_space=pltpu.SMEM)] + [pl.BlockSpec(memory_space=pltpu.VMEM)] * len(arrays),
        out_specs=[pl.BlockSpec(memory_space=pltpu.VMEM)] * len(outs),
        out_shape=[jax.ShapeDtypeStruct((rows, heads * HEAD_DIM), jnp.bfloat16) for rows in outs],
        scratch_shapes=[pltpu.VMEM((tile, 7 * tile), jnp.float32) for _ in range(chunks)],
        compiler_params=pltpu.CompilerParams(vmem_limit_bytes=(4 + 2 * chunks) * 1024 * 1024),
        cost_estimate=pl.CostEstimate(
            flops=heads * chunks * tile * 7 * tile * HEAD_DIM * 4,
            bytes_accessed=sum(x.size * 2 for x in arrays),
            transcendentals=heads * chunks * tile * 7 * tile,
        ),
    )(mask, *arrays)


def four_frames(queries, keys, values, pair_mask, tile_offset):
    z = lax.axis_index("frame")
    h = lax.axis_index("head")
    x = h // 2
    rows, features = queries.shape
    tile = 2 * rows
    width = features // 4
    heads = width // HEAD_DIM
    cut = FIRST * HEAD_DIM

    def columns(array, d, begin, end):
        return lax.dynamic_slice_in_dim(array, (h ^ d) * width + begin, end - begin, axis=1)

    def beside(*arrays):
        return jnp.concatenate(arrays, axis=1)

    def to_head(array, d):
        return lax.ppermute(array, "head", [(i, i ^ d) for i in range(4)])

    def along(array, pairs):
        return lax.ppermute(array, "frame", pairs)

    def after(array, earlier):
        return lax.optimization_barrier((array, earlier))[0]

    def below(*arrays):
        return jnp.concatenate(arrays, axis=0)

    operands = (queries, keys, values)

    def keys_values(d, begin, end):
        return [(1, d, begin, end - begin), (2, d, begin, end - begin)]

    first = [[columns(array, d, 0, cut) for array in (keys, values)] for d in range(4)]
    first = lax.optimization_barrier(first)
    got = to_head(beside(*first[1], *first[3]), 1)
    pay, q_own, q_far, own, far, told = packed(
        operands,
        pair_mask,
        tile_offset,
        [
            [(0, 1, 0, width), (0, 3, 0, width)] + keys_values(1, cut, width) + keys_values(3, cut, width),
            [(0, 0, 0, width)],
            [(0, 2, 0, width)],
            keys_values(0, cut, width),
            keys_values(2, cut, width),
        ],
        width,
        2 * cut,
    )
    mine = below(beside(*first[0]), got[:, : 2 * cut], told)
    other = to_head(below(beside(*first[2]), got[:, 2 * cut :]), 2)
    n1_mine = along(mine, OUTER)
    n2_mine = along(mine, INNER)
    n1_other = along(other, OUTER)
    n2_other = along(other, INNER)
    r1 = along(after(relayed(n1_mine, n1_other), n2_mine), INNER)
    first = [mine, other, n1_mine, n1_other, n2_mine, n2_other, r1]

    got = to_head(after(pay, got), 1)
    q_mine = below(q_own, got[:, :width])
    q_other = to_head(after(below(q_far, got[:, width : 2 * width]), other), 2)
    split = 2 * width + 2 * (width - cut)
    mine2 = below(own, got[:, 2 * width : split])
    other2 = to_head(after(below(far, got[:, split:]), q_other), 2)
    q_guest = along(below(q_mine[:, :cut], q_other[:, :cut]), OUTER)
    whole = jnp.where(x == tile_offset[0], below(mine2, other2), below(other2, mine2))
    whole = after(whole, n2_other)
    n1 = along(whole, OUTER)
    n2 = along(whole, INNER)
    r1 = along(n1[:tile], INNER)
    r2 = along(n2[:tile], OUTER)
    r3 = along(r1, OUTER)

    *own, guest = run_kernel(
        first_kernel, pair_mask, [q_mine, q_other, q_guest, *first], [rows] * 4 + [2 * tile], 4, tile, FIRST
    )
    back = along(after(guest, n2), OUTWARD)
    end_frame = (z == 0) | (z == 3)
    out = [jnp.where(end_frame, back[d * rows : (d + 1) * rows], own[d]) for d in range(4)]
    out = [out[0]] + [to_head(out[d], d) for d in (1, 2, 3)]
    late = run_kernel(
        second_kernel, pair_mask, [q_mine, q_other, whole, n1, n2, r1, r2, r3], [rows] * 4, 2, tile, heads - FIRST
    )
    late = [late[0]] + [to_head(late[d], d) for d in (1, 2, 3)]
    result = jnp.zeros((rows, features), jnp.bfloat16)
    for d in range(4):
        result = lax.dynamic_update_slice_in_dim(result, out[d], (h ^ d) * width, axis=1)
    for d in range(4):
        result = lax.dynamic_update_slice_in_dim(result, late[d], (h ^ d) * width + cut, axis=1)
    return result


def solution(mesh):
    sizes = dict(mesh.shape)
    per_device = four_frames if sizes["frame"] == 4 and sizes["head"] == 4 else general
    return jax.shard_map(
        per_device,
        mesh=mesh,
        in_specs=(
            P(("parts", "frame", "head"), None),
            P(("parts", "frame", "head"), None),
            P(("parts", "frame", "head"), None),
            P(("parts", "frame"), None),
            P(("parts", "frame")),
        ),
        out_specs=P(("parts", "frame", "head"), None),
        check_vma=False,
    )
```

```python
import functools
import math

import jax
import jax.numpy as jnp
from jax import lax
from jax.experimental import pallas as pl
from jax.experimental.pallas import tpu as pltpu
from jax.sharding import PartitionSpec as P

HEAD_DIM = 128
SCALE = 1.0 / HEAD_DIM**0.5
LOG2E = math.log2(math.e)


def padded(x, sides, width):
    for axis, dim in sides:
        peers, length = (lax.axis_size(axis), x.shape[dim])
        up = [(i, (i + 1) % peers) for i in range(peers - 1)]
        down = [(j, i) for i, j in up]
        last = lax.slice_in_dim(x, length - width, length, axis=dim)
        leading = lax.slice_in_dim(x, 0, width, axis=dim)
        before = lax.ppermute(last, axis, up)
        after = lax.ppermute(leading, axis, down)
        x = jnp.concatenate([before, x, after], axis=dim)
    return x


def from_partner(x, axis, bit):
    return lax.ppermute(x, axis, [(i, i ^ 1 << bit) for i in range(lax.axis_size(axis))])


def subsample(frame_rows, offset, level, tiles, tile):
    step = 2**level
    width = frame_rows.shape[-1]
    grouped = frame_rows.reshape(tiles // step, step, tile, width)
    picked = lax.dynamic_index_in_dim(grouped, offset % step, 1, keepdims=False)
    return picked.reshape(-1, width)


def attend(query_rows, key_rows, value_rows, valid):
    count = query_rows.shape[0]
    heads = query_rows.shape[1] // HEAD_DIM
    q_three = query_rows.reshape(count, heads, HEAD_DIM).transpose(1, 0, 2)
    k_three = key_rows.reshape(-1, heads, HEAD_DIM).transpose(1, 0, 2)
    v_three = value_rows.reshape(-1, heads, HEAD_DIM).transpose(1, 0, 2)

    def one_head(operands):
        q_head, k_head, v_head = operands
        scores = jnp.dot(q_head, k_head.T, preferred_element_type=jnp.float32) * SCALE
        scores = jnp.where(valid[None, :] > 0, scores, -1e30)
        top = jnp.max(scores, axis=1, keepdims=True)
        weights = jnp.exp(scores - top) * valid[None, :]
        total = jnp.sum(weights, axis=1, keepdims=True)
        mixed = jnp.dot(weights.astype(jnp.bfloat16), v_head, preferred_element_type=jnp.float32)
        return mixed / total

    outcome = lax.map(one_head, (q_three, k_three, v_three))
    return outcome.transpose(1, 0, 2).reshape(count, heads * HEAD_DIM).astype(jnp.bfloat16)


def ordered(mine, theirs, upper):
    return jnp.where(upper == 1, jnp.concatenate([theirs, mine]), jnp.concatenate([mine, theirs]))


def general(queries, keys, values, pair_mask, tile_offset):
    frames_n = lax.axis_size("frame")
    current = lax.axis_index("frame")
    q_rows, k_rows, v_rows = (
        lax.all_to_all(queries, "head", split_axis=1, concat_axis=0, tiled=True),
        lax.all_to_all(keys, "head", split_axis=1, concat_axis=0, tiled=True),
        lax.all_to_all(values, "head", split_axis=1, concat_axis=0, tiled=True),
    )
    count = q_rows.shape[0]
    width = q_rows.shape[1]
    tiles = frames_n // 2
    tile = count // tiles
    depth = frames_n.bit_length() - 1
    stacked = jnp.stack([k_rows, v_rows])
    near = padded(stacked, (("frame", 1),), count)
    near_index = current - 1 + jnp.arange(3, dtype=jnp.int32)
    near_good = ((near_index >= 0) & (near_index < frames_n)).astype(jnp.float32)
    key_parts = [near[0]]
    value_parts = [near[1]]
    valid_parts = [jnp.repeat(near_good, count)]
    mask_row = pair_mask[0]
    offset = tile_offset[0]
    k_tiles = k_rows.reshape(tiles, tile, width)
    v_tiles = v_rows.reshape(tiles, tile, width)
    own = {}
    for level in range(1, depth):
        own[level] = (
            subsample(k_tiles, offset, level, tiles, tile)[None],
            subsample(v_tiles, offset, level, tiles, tile)[None],
        )
    sibling = {}
    cut = max(1, depth - 2)
    upper_levels = [level for level in range(1, depth) if level >= cut]
    k_pack = jnp.concatenate([own[level][0].reshape(-1, width) for level in upper_levels])
    v_pack = jnp.concatenate([own[level][1].reshape(-1, width) for level in upper_levels])
    k_every, v_every = (
        lax.all_gather(k_pack, "frame", axis=0, tiled=True),
        lax.all_gather(v_pack, "frame", axis=0, tiled=True),
    )
    k_every = k_every.reshape(frames_n, -1, width)
    v_every = v_every.reshape(frames_n, -1, width)
    position = 0
    for level in upper_levels:
        step = 2**level
        rows = count // step
        start = jnp.bitwise_xor(current // step, 1) * step
        block_k = lax.dynamic_slice_in_dim(k_every[:, position : position + rows], start, step, 0)
        block_v = lax.dynamic_slice_in_dim(v_every[:, position : position + rows], start, step, 0)
        sibling[level] = (block_k, block_v)
        position = position + rows
    swap_levels = [level for level in range(1, depth) if level < cut]
    growing = {level: own[level] for level in swap_levels}
    sections = cut if swap_levels else 0
    for bit in range(sections):
        active = [level for level in swap_levels if level >= bit]
        k_pack = jnp.concatenate([growing[level][0].reshape(-1, width) for level in active])
        v_pack = jnp.concatenate([growing[level][1].reshape(-1, width) for level in active])
        k_in, v_in = (from_partner(k_pack, "frame", bit), from_partner(v_pack, "frame", bit))
        upper = current // 2**bit % 2
        position = 0
        for level in active:
            shape = growing[level][0].shape
            size = shape[0] * shape[1]
            theirs_k = k_in[position : position + size].reshape(shape)
            theirs_v = v_in[position : position + size].reshape(shape)
            position = position + size
            if level == bit:
                sibling[level] = (theirs_k, theirs_v)
            else:
                growing[level] = (
                    ordered(growing[level][0], theirs_k, upper),
                    ordered(growing[level][1], theirs_v, upper),
                )
    for level in range(1, depth):
        step = 2**level
        start = jnp.bitwise_xor(current // step, 1) * step
        frame_ids = start + jnp.arange(step, dtype=jnp.int32)
        allowed = lax.dynamic_slice_in_dim(mask_row, start, step, 0)
        good = ((jnp.abs(frame_ids - current) >= 2) & (allowed == 1)).astype(jnp.float32)
        block_k, block_v = sibling[level]
        key_parts.append(block_k.reshape(-1, width))
        value_parts.append(block_v.reshape(-1, width))
        valid_parts.append(jnp.repeat(good, block_k.shape[1]))
    result = attend(
        q_rows,
        jnp.concatenate(key_parts),
        jnp.concatenate(value_parts),
        jnp.concatenate(valid_parts),
    )
    return lax.all_to_all(result, "head", split_axis=0, concat_axis=1, tiled=True)


INFO_ROWS = 16
OUTER = [(0, 1), (1, 0), (2, 3), (3, 2)]
INNER = [(1, 2), (2, 1)]
OUTWARD = [(1, 0), (2, 3)]


def fold(x):
    parts = [x[:, at : at + 128] for at in range(0, x.shape[1], 128)]
    best = parts[0]
    for part in parts[1:]:
        best = jnp.maximum(best, part)
    return best


def scores_of(q, slots, held):
    free, top = None, None
    for at, (k, valid) in enumerate(slots):
        s = lax.dot_general(q, k[...], (((1,), (1,)), ((), ())), preferred_element_type=jnp.float32)
        held[:, at * s.shape[1] : (at + 1) * s.shape[1]] = s
        best = fold(s)
        if valid is None:
            free = best if free is None else jnp.maximum(free, best)
        else:
            best = jnp.where(valid, jnp.max(best, axis=1, keepdims=True), -1e30)
            top = best if top is None else jnp.maximum(top, best)
    free = jnp.max(free, axis=1, keepdims=True)
    return free if top is None else jnp.maximum(free, top)


def weights_of(top, slots, held, out):
    factor = SCALE * LOG2E
    total = None
    for at, (k, valid) in enumerate(slots):
        tile = k.shape[0]
        level = top if valid is None else jnp.where(valid, top, 1e30)
        w = jnp.exp2((held[:, at * tile : (at + 1) * tile] - level) * factor)
        out[:, at * tile : (at + 1) * tile] = w.astype(jnp.bfloat16)
        for begin in range(0, tile, 128):
            part = w[:, begin : begin + 128]
            total = part if total is None else total + part
    return jnp.sum(total, axis=1, keepdims=True)


def inner_frame():
    z = lax.axis_index("frame")
    return (z == 1) | (z == 2)


def weights_kernel(mask, q_mine, q_other, mine, other, n1m, n1o, n2m, n2o, r1, r2, r3, weights, totals, held0, held1):
    z = lax.axis_index("frame")
    tile = r1.shape[0]
    near = mask[0, z ^ 2] == 1
    always = [(mine, None), (other, None), (n1m, None), (n1o, None)]

    def body(slots):
        rooms = (held0, held1)
        tops = [scores_of(q[...], slots, held) for q, held in zip((q_mine, q_other), rooms)]
        for half, (top, held) in enumerate(zip(tops, rooms)):
            rows = slice(half * tile, (half + 1) * tile)
            total = weights_of(top, slots, held, weights.at[rows])
            totals[rows] = jnp.broadcast_to(total, (tile, totals.shape[1]))

    @pl.when(inner_frame())
    def _():
        body(always + [(n2m, None), (n2o, None), (r1, near)])

    @pl.when(jnp.logical_not(inner_frame()))
    def _():
        body(always + [(r2, near), (r3, mask[0, z ^ 3] == 1)])


def values_kernel(weights, totals, mine, other, n1m, n1o, n2m, n2o, r1, r2, r3, *outs):
    tile = r1.shape[0]
    rows = outs[0].shape[0]
    always = [mine, other, n1m, n1o]

    def body(slots):
        for d, out in enumerate(outs):
            span = slice(d * rows, (d + 1) * rows)
            mixed = None
            for at, v in enumerate(slots):
                w = weights[span, at * tile : (at + 1) * tile]
                mix = jnp.dot(w, v[...], preferred_element_type=jnp.float32)
                mixed = mix if mixed is None else mixed + mix
            out[...] = (mixed / totals[span]).astype(jnp.bfloat16)

    @pl.when(inner_frame())
    def _():
        body(always + [n2m, n2o, r1])

    @pl.when(jnp.logical_not(inner_frame()))
    def _():
        body(always + [r2, r3])


def by_head(x, rows, first=0):
    return x, pl.BlockSpec((rows, HEAD_DIM), lambda i: (0, first + i))


def find_weights(mask, q_mine, q_other, keys, heads):
    tile = q_mine.shape[0]
    blocks = [by_head(q_mine, tile), by_head(q_other, tile)] + [by_head(k, tile) for k in keys]
    shapes = [(2 * tile, 7 * tile, jnp.bfloat16), (2 * tile, HEAD_DIM, jnp.float32)]
    return pl.pallas_call(
        weights_kernel,
        grid=(heads,),
        in_specs=[pl.BlockSpec(memory_space=pltpu.SMEM)] + [spec for _, spec in blocks],
        out_specs=[pl.BlockSpec((rows, lanes), lambda i: (i, 0)) for rows, lanes, _ in shapes],
        out_shape=[jax.ShapeDtypeStruct((heads * rows, lanes), dtype) for rows, lanes, dtype in shapes],
        scratch_shapes=[pltpu.VMEM((tile, 7 * tile), jnp.float32)] * 2,
        compiler_params=pltpu.CompilerParams(vmem_limit_bytes=16 * 1024 * 1024),
        cost_estimate=pl.CostEstimate(
            flops=heads * 28 * tile * tile * HEAD_DIM,
            bytes_accessed=heads * 28 * tile * tile,
            transcendentals=heads * 14 * tile * tile,
        ),
    )(mask, *[x for x, _ in blocks])


def mix_values(weights, totals, values, heads):
    rows, lanes = weights.shape[0] // heads, weights.shape[1]
    tile = lanes // 7
    blocks = [by_head(v, tile, first) for v, first in values]
    return pl.pallas_call(
        values_kernel,
        grid=(heads,),
        in_specs=[pl.BlockSpec((rows, lanes), lambda i: (i, 0)), pl.BlockSpec((rows, HEAD_DIM), lambda i: (i, 0))]
        + [spec for _, spec in blocks],
        out_specs=[pl.BlockSpec((rows // 4, HEAD_DIM), lambda i: (0, i))] * 4,
        out_shape=[jax.ShapeDtypeStruct((rows // 4, heads * HEAD_DIM), jnp.bfloat16)] * 4,
        compiler_params=pltpu.CompilerParams(vmem_limit_bytes=16 * 1024 * 1024),
        cost_estimate=pl.CostEstimate(
            flops=heads * 2 * rows * lanes * HEAD_DIM, bytes_accessed=heads * 2 * rows * lanes, transcendentals=0
        ),
    )(weights, totals, *[x for x, _ in blocks])


def pack_kernel(copies, width, mask, offset, *refs):
    ins, outs, sems = refs[:3], refs[3:-1], refs[-1]
    h = lax.axis_index("head")
    started = []
    for n, (operand, d, begin, result, at, lanes) in enumerate(copies):
        source = ins[operand].at[:, pl.ds(pl.multiple_of((h ^ d) * width + begin, HEAD_DIM), lanes)]
        copy = pltpu.make_async_copy(source, outs[result].at[:, at : at + lanes], sems.at[n])
        copy.start()
        started.append(copy)
    if len(outs) > 1 + max(copy[3] for copy in copies):
        told = outs[-1]
        for group in range(told.shape[1] // 128):
            value = mask[0, group] if group < 4 else offset[0]
            rows = jnp.full((told.shape[0], 128), value, jnp.int32).astype(jnp.float32)
            told[:, group * 128 : (group + 1) * 128] = rows.astype(told.dtype)
    for copy in started:
        copy.wait()


def packed(operands, mask, offset, results, width, told):
    rows = operands[0].shape[0]
    copies, shapes = [], []
    for n, parts in enumerate(results):
        at = 0
        for operand, d, begin, lanes in parts:
            copies.append((operand, d, begin, n, at, lanes))
            at += lanes
        shapes.append(jax.ShapeDtypeStruct((rows, at), jnp.bfloat16))
    if told:
        shapes.append(jax.ShapeDtypeStruct((INFO_ROWS, told), jnp.bfloat16))
    return pl.pallas_call(
        functools.partial(pack_kernel, copies, width),
        in_specs=[pl.BlockSpec(memory_space=pltpu.SMEM)] * 2 + [pl.BlockSpec(memory_space=pltpu.HBM)] * 3,
        out_specs=[pl.BlockSpec(memory_space=pltpu.VMEM)] * len(shapes),
        out_shape=shapes,
        scratch_shapes=[pltpu.SemaphoreType.DMA((len(copies),))],
        compiler_params=pltpu.CompilerParams(vmem_limit_bytes=4 * 1024 * 1024),
    )(mask, offset, *operands)


def relayed_kernel(mine, other, k_out, v_out):
    tile, width = k_out.shape
    offset = jnp.max(mine[tile : tile + INFO_ROWS, 4 * 128 : 5 * 128].astype(jnp.float32))
    here = offset == (lax.axis_index("head") // 2).astype(jnp.float32)

    def take(ref):
        k_out[...] = ref[:tile, :width]
        v_out[...] = ref[:tile, width:]

    @pl.when(here)
    def _():
        take(mine)

    @pl.when(jnp.logical_not(here))
    def _():
        take(other)


def relayed(mine, other):
    tile, lanes = other.shape
    return pl.pallas_call(
        relayed_kernel,
        in_specs=[pl.BlockSpec(memory_space=pltpu.VMEM)] * 2,
        out_specs=[pl.BlockSpec(memory_space=pltpu.VMEM)] * 2,
        out_shape=[jax.ShapeDtypeStruct((tile, lanes // 2), other.dtype)] * 2,
        compiler_params=pltpu.CompilerParams(vmem_limit_bytes=4 * 1024 * 1024),
    )(mine, other)


def four_frames(queries, keys, values, pair_mask, tile_offset):
    h = lax.axis_index("head")
    rows, features = queries.shape
    width = features // 4
    heads = width // HEAD_DIM

    def columns(array, d):
        return lax.dynamic_slice_in_dim(array, (h ^ d) * width, width, axis=1)

    def beside(*arrays):
        return jnp.concatenate(arrays, axis=1)

    def below(*arrays):
        return jnp.concatenate(arrays, axis=0)

    def to_head(array, d):
        return lax.ppermute(array, "head", [(i, i ^ d) for i in range(4)])

    def along(array, pairs):
        return lax.ppermute(array, "frame", pairs)

    def after(array, earlier):
        return lax.optimization_barrier((array, earlier))[0]

    kv = [[columns(array, d) for array in (keys, values)] for d in range(4)]
    kv = lax.optimization_barrier(kv)
    got = to_head(beside(*kv[1], *kv[3]), 1)
    pay, q_own, q_far, told = packed(
        (queries, keys, values),
        pair_mask,
        tile_offset,
        [[(0, 1, 0, width), (0, 3, 0, width)], [(0, 0, 0, width)], [(0, 2, 0, width)]],
        width,
        2 * width,
    )
    mine = below(beside(*kv[0]), got[:, : 2 * width], told)
    other = to_head(below(beside(*kv[2]), got[:, 2 * width :]), 2)
    n1m = along(mine, OUTER)
    n2m = along(mine, INNER)
    n1o = along(other, OUTER)
    n2o = along(other, INNER)

    got = to_head(after(pay, got), 1)
    q_mine = below(q_own, got[:, :width])
    q_other = to_head(after(below(q_far, got[:, width:]), other), 2)

    r1k, r1v = after(relayed(n1m, n1o), n2m)
    r1k = along(r1k, INNER)
    r1v = along(r1v, INNER)
    r2k, r2v = relayed(n2m, n2o)
    r2k = along(r2k, OUTWARD)
    r3k = along(r1k, OUTWARD)
    r2v = along(after(r2v, r1k), OUTWARD)
    r3v = along(r1v, OUTWARD)

    near = [mine, other, n1m, n1o, n2m, n2o]
    weights, totals = find_weights(pair_mask, q_mine, q_other, [*near, r1k, r2k, r3k], heads)
    out = mix_values(weights, totals, [(x, heads) for x in near] + [(x, 0) for x in (r1v, r2v, r3v)], heads)
    out = [out[0]] + [to_head(out[d], d) for d in (1, 2, 3)]
    result = jnp.zeros((rows, features), jnp.bfloat16)
    for d in range(4):
        result = lax.dynamic_update_slice_in_dim(result, out[d], (h ^ d) * width, axis=1)
    return result


def solution(mesh):
    sizes = dict(mesh.shape)
    per_device = four_frames if sizes["frame"] == 4 and sizes["head"] == 4 else general
    return jax.shard_map(
        per_device,
        mesh=mesh,
        in_specs=(
            P(("parts", "frame", "head"), None),
            P(("parts", "frame", "head"), None),
            P(("parts", "frame", "head"), None),
            P(("parts", "frame"), None),
            P(("parts", "frame")),
        ),
        out_specs=P(("parts", "frame", "head"), None),
        check_vma=False,
    )
```

```python
import functools
import math

import jax
import jax.numpy as jnp
from jax import lax
from jax.experimental import pallas as pl
from jax.experimental.pallas import tpu as pltpu
from jax.sharding import PartitionSpec as P

HEAD_DIM = 128
SCALE = 1.0 / HEAD_DIM**0.5
LOG2E = math.log2(math.e)


def padded(x, sides, width):
    for axis, dim in sides:
        peers, length = (lax.axis_size(axis), x.shape[dim])
        up = [(i, (i + 1) % peers) for i in range(peers - 1)]
        down = [(j, i) for i, j in up]
        last = lax.slice_in_dim(x, length - width, length, axis=dim)
        leading = lax.slice_in_dim(x, 0, width, axis=dim)
        before = lax.ppermute(last, axis, up)
        after = lax.ppermute(leading, axis, down)
        x = jnp.concatenate([before, x, after], axis=dim)
    return x


def from_partner(x, axis, bit):
    return lax.ppermute(x, axis, [(i, i ^ 1 << bit) for i in range(lax.axis_size(axis))])


def subsample(frame_rows, offset, level, tiles, tile):
    step = 2**level
    width = frame_rows.shape[-1]
    grouped = frame_rows.reshape(tiles // step, step, tile, width)
    picked = lax.dynamic_index_in_dim(grouped, offset % step, 1, keepdims=False)
    return picked.reshape(-1, width)


def attend(query_rows, key_rows, value_rows, valid):
    count = query_rows.shape[0]
    heads = query_rows.shape[1] // HEAD_DIM
    q_three = query_rows.reshape(count, heads, HEAD_DIM).transpose(1, 0, 2)
    k_three = key_rows.reshape(-1, heads, HEAD_DIM).transpose(1, 0, 2)
    v_three = value_rows.reshape(-1, heads, HEAD_DIM).transpose(1, 0, 2)

    def one_head(operands):
        q_head, k_head, v_head = operands
        scores = jnp.dot(q_head, k_head.T, preferred_element_type=jnp.float32) * SCALE
        scores = jnp.where(valid[None, :] > 0, scores, -1e30)
        top = jnp.max(scores, axis=1, keepdims=True)
        weights = jnp.exp(scores - top) * valid[None, :]
        total = jnp.sum(weights, axis=1, keepdims=True)
        mixed = jnp.dot(weights.astype(jnp.bfloat16), v_head, preferred_element_type=jnp.float32)
        return mixed / total

    outcome = lax.map(one_head, (q_three, k_three, v_three))
    return outcome.transpose(1, 0, 2).reshape(count, heads * HEAD_DIM).astype(jnp.bfloat16)


def ordered(mine, theirs, upper):
    return jnp.where(upper == 1, jnp.concatenate([theirs, mine]), jnp.concatenate([mine, theirs]))


def general(queries, keys, values, pair_mask, tile_offset):
    frames_n = lax.axis_size("frame")
    current = lax.axis_index("frame")
    q_rows, k_rows, v_rows = (
        lax.all_to_all(queries, "head", split_axis=1, concat_axis=0, tiled=True),
        lax.all_to_all(keys, "head", split_axis=1, concat_axis=0, tiled=True),
        lax.all_to_all(values, "head", split_axis=1, concat_axis=0, tiled=True),
    )
    count = q_rows.shape[0]
    width = q_rows.shape[1]
    tiles = frames_n // 2
    tile = count // tiles
    depth = frames_n.bit_length() - 1
    stacked = jnp.stack([k_rows, v_rows])
    near = padded(stacked, (("frame", 1),), count)
    near_index = current - 1 + jnp.arange(3, dtype=jnp.int32)
    near_good = ((near_index >= 0) & (near_index < frames_n)).astype(jnp.float32)
    key_parts = [near[0]]
    value_parts = [near[1]]
    valid_parts = [jnp.repeat(near_good, count)]
    mask_row = pair_mask[0]
    offset = tile_offset[0]
    k_tiles = k_rows.reshape(tiles, tile, width)
    v_tiles = v_rows.reshape(tiles, tile, width)
    own = {}
    for level in range(1, depth):
        own[level] = (
            subsample(k_tiles, offset, level, tiles, tile)[None],
            subsample(v_tiles, offset, level, tiles, tile)[None],
        )
    sibling = {}
    cut = max(1, depth - 2)
    upper_levels = [level for level in range(1, depth) if level >= cut]
    k_pack = jnp.concatenate([own[level][0].reshape(-1, width) for level in upper_levels])
    v_pack = jnp.concatenate([own[level][1].reshape(-1, width) for level in upper_levels])
    k_every, v_every = (
        lax.all_gather(k_pack, "frame", axis=0, tiled=True),
        lax.all_gather(v_pack, "frame", axis=0, tiled=True),
    )
    k_every = k_every.reshape(frames_n, -1, width)
    v_every = v_every.reshape(frames_n, -1, width)
    position = 0
    for level in upper_levels:
        step = 2**level
        rows = count // step
        start = jnp.bitwise_xor(current // step, 1) * step
        block_k = lax.dynamic_slice_in_dim(k_every[:, position : position + rows], start, step, 0)
        block_v = lax.dynamic_slice_in_dim(v_every[:, position : position + rows], start, step, 0)
        sibling[level] = (block_k, block_v)
        position = position + rows
    swap_levels = [level for level in range(1, depth) if level < cut]
    growing = {level: own[level] for level in swap_levels}
    sections = cut if swap_levels else 0
    for bit in range(sections):
        active = [level for level in swap_levels if level >= bit]
        k_pack = jnp.concatenate([growing[level][0].reshape(-1, width) for level in active])
        v_pack = jnp.concatenate([growing[level][1].reshape(-1, width) for level in active])
        k_in, v_in = (from_partner(k_pack, "frame", bit), from_partner(v_pack, "frame", bit))
        upper = current // 2**bit % 2
        position = 0
        for level in active:
            shape = growing[level][0].shape
            size = shape[0] * shape[1]
            theirs_k = k_in[position : position + size].reshape(shape)
            theirs_v = v_in[position : position + size].reshape(shape)
            position = position + size
            if level == bit:
                sibling[level] = (theirs_k, theirs_v)
            else:
                growing[level] = (
                    ordered(growing[level][0], theirs_k, upper),
                    ordered(growing[level][1], theirs_v, upper),
                )
    for level in range(1, depth):
        step = 2**level
        start = jnp.bitwise_xor(current // step, 1) * step
        frame_ids = start + jnp.arange(step, dtype=jnp.int32)
        allowed = lax.dynamic_slice_in_dim(mask_row, start, step, 0)
        good = ((jnp.abs(frame_ids - current) >= 2) & (allowed == 1)).astype(jnp.float32)
        block_k, block_v = sibling[level]
        key_parts.append(block_k.reshape(-1, width))
        value_parts.append(block_v.reshape(-1, width))
        valid_parts.append(jnp.repeat(good, block_k.shape[1]))
    result = attend(
        q_rows,
        jnp.concatenate(key_parts),
        jnp.concatenate(value_parts),
        jnp.concatenate(valid_parts),
    )
    return lax.all_to_all(result, "head", split_axis=0, concat_axis=1, tiled=True)


INFO_ROWS = 16
OUTER = [(0, 1), (1, 0), (2, 3), (3, 2)]
INNER = [(1, 2), (2, 1)]
OUTWARD = [(1, 0), (2, 3)]


def fold(x):
    parts = [x[:, at : at + 128] for at in range(0, x.shape[1], 128)]
    best = parts[0]
    for part in parts[1:]:
        best = jnp.maximum(best, part)
    return best


def scores_of(q, slots, held):
    free, top = None, None
    for at, (k, valid) in enumerate(slots):
        s = lax.dot_general(q, k[...], (((1,), (1,)), ((), ())), preferred_element_type=jnp.float32)
        held[:, at * s.shape[1] : (at + 1) * s.shape[1]] = s
        best = fold(s)
        if valid is None:
            free = best if free is None else jnp.maximum(free, best)
        else:
            best = jnp.where(valid, jnp.max(best, axis=1, keepdims=True), -1e30)
            top = best if top is None else jnp.maximum(top, best)
    free = jnp.max(free, axis=1, keepdims=True)
    return free if top is None else jnp.maximum(free, top)


def weights_of(top, slots, held, out):
    factor = SCALE * LOG2E
    total = None
    for at, (k, valid) in enumerate(slots):
        tile = k.shape[0]
        level = top if valid is None else jnp.where(valid, top, 1e30)
        w = jnp.exp2((held[:, at * tile : (at + 1) * tile] - level) * factor)
        out[:, at * tile : (at + 1) * tile] = w.astype(jnp.bfloat16)
        for begin in range(0, tile, 128):
            part = w[:, begin : begin + 128]
            total = part if total is None else total + part
    return jnp.sum(total, axis=1, keepdims=True)


def inner_frame():
    z = lax.axis_index("frame")
    return (z == 1) | (z == 2)


def weights_kernel(mask, q_mine, q_other, mine, other, n1m, n1o, n2m, n2o, r1, r2, r3, weights, totals, held0, held1):
    z = lax.axis_index("frame")
    tile = r1.shape[0]
    near = mask[0, z ^ 2] == 1
    always = [(mine, None), (other, None), (n1m, None), (n1o, None)]

    def body(slots):
        rooms = (held0, held1)
        tops = [scores_of(q[...], slots, held) for q, held in zip((q_mine, q_other), rooms)]
        for half, (top, held) in enumerate(zip(tops, rooms)):
            rows = slice(half * tile, (half + 1) * tile)
            total = weights_of(top, slots, held, weights.at[rows])
            totals[rows] = jnp.broadcast_to(total, (tile, totals.shape[1]))

    @pl.when(inner_frame())
    def _():
        body(always + [(n2m, None), (n2o, None), (r1, near)])

    @pl.when(jnp.logical_not(inner_frame()))
    def _():
        body(always + [(r2, near), (r3, mask[0, z ^ 3] == 1)])


def values_kernel(weights, totals, mine, other, n1m, n1o, n2m, n2o, r1, r2, r3, *outs):
    tile = r1.shape[0]
    rows = outs[0].shape[0]
    always = [mine, other, n1m, n1o]

    def body(slots):
        for d, out in enumerate(outs):
            span = slice(d * rows, (d + 1) * rows)
            mixed = None
            for at, v in enumerate(slots):
                w = weights[span, at * tile : (at + 1) * tile]
                mix = jnp.dot(w, v[...], preferred_element_type=jnp.float32)
                mixed = mix if mixed is None else mixed + mix
            out[...] = (mixed / totals[span]).astype(jnp.bfloat16)

    @pl.when(inner_frame())
    def _():
        body(always + [n2m, n2o, r1])

    @pl.when(jnp.logical_not(inner_frame()))
    def _():
        body(always + [r2, r3])


def by_head(x, rows, first=0):
    return x, pl.BlockSpec((rows, HEAD_DIM), lambda i: (0, first + i))


def find_weights(mask, q_mine, q_other, keys, heads):
    tile = q_mine.shape[0]
    blocks = [by_head(q_mine, tile), by_head(q_other, tile)] + [by_head(k, tile) for k in keys]
    shapes = [(2 * tile, 7 * tile, jnp.bfloat16), (2 * tile, HEAD_DIM, jnp.float32)]
    return pl.pallas_call(
        weights_kernel,
        grid=(heads,),
        in_specs=[pl.BlockSpec(memory_space=pltpu.SMEM)] + [spec for _, spec in blocks],
        out_specs=[pl.BlockSpec((rows, lanes), lambda i: (i, 0)) for rows, lanes, _ in shapes],
        out_shape=[jax.ShapeDtypeStruct((heads * rows, lanes), dtype) for rows, lanes, dtype in shapes],
        scratch_shapes=[pltpu.VMEM((tile, 7 * tile), jnp.float32)] * 2,
        compiler_params=pltpu.CompilerParams(vmem_limit_bytes=16 * 1024 * 1024),
        cost_estimate=pl.CostEstimate(
            flops=heads * 28 * tile * tile * HEAD_DIM,
            bytes_accessed=heads * 28 * tile * tile,
            transcendentals=heads * 14 * tile * tile,
        ),
    )(mask, *[x for x, _ in blocks])


def mix_values(weights, totals, values, skip, heads):
    tile = weights.shape[1] // 7
    rows, lanes = 2 * tile, weights.shape[1]
    blocks = [by_head(v, tile, first) for v, first in values]
    return pl.pallas_call(
        values_kernel,
        grid=(heads,),
        in_specs=[
            pl.BlockSpec((rows, lanes), lambda i: (skip + i, 0)),
            pl.BlockSpec((rows, HEAD_DIM), lambda i: (skip + i, 0)),
        ]
        + [spec for _, spec in blocks],
        out_specs=[pl.BlockSpec((rows // 4, HEAD_DIM), lambda i: (0, i))] * 4,
        out_shape=[jax.ShapeDtypeStruct((rows // 4, heads * HEAD_DIM), jnp.bfloat16)] * 4,
        compiler_params=pltpu.CompilerParams(vmem_limit_bytes=16 * 1024 * 1024),
        cost_estimate=pl.CostEstimate(
            flops=heads * 2 * rows * lanes * HEAD_DIM, bytes_accessed=heads * 2 * rows * lanes, transcendentals=0
        ),
    )(weights, totals, *[x for x, _ in blocks])


def pack_kernel(copies, width, mask, offset, *refs):
    ins, outs, sems = refs[:3], refs[3:-1], refs[-1]
    h = lax.axis_index("head")
    started = []
    for n, (operand, d, begin, result, at, lanes) in enumerate(copies):
        source = ins[operand].at[:, pl.ds(pl.multiple_of((h ^ d) * width + begin, HEAD_DIM), lanes)]
        copy = pltpu.make_async_copy(source, outs[result].at[:, at : at + lanes], sems.at[n])
        copy.start()
        started.append(copy)
    if len(outs) > 1 + max(copy[3] for copy in copies):
        told = outs[-1]
        for group in range(told.shape[1] // 128):
            value = mask[0, group] if group < 4 else offset[0]
            rows = jnp.full((told.shape[0], 128), value, jnp.int32).astype(jnp.float32)
            told[:, group * 128 : (group + 1) * 128] = rows.astype(told.dtype)
    for copy in started:
        copy.wait()


def packed(operands, mask, offset, results, width, told):
    rows = operands[0].shape[0]
    copies, shapes = [], []
    for n, parts in enumerate(results):
        at = 0
        for operand, d, begin, lanes in parts:
            copies.append((operand, d, begin, n, at, lanes))
            at += lanes
        shapes.append(jax.ShapeDtypeStruct((rows, at), jnp.bfloat16))
    if told:
        shapes.append(jax.ShapeDtypeStruct((INFO_ROWS, told), jnp.bfloat16))
    return pl.pallas_call(
        functools.partial(pack_kernel, copies, width),
        in_specs=[pl.BlockSpec(memory_space=pltpu.SMEM)] * 2 + [pl.BlockSpec(memory_space=pltpu.HBM)] * 3,
        out_specs=[pl.BlockSpec(memory_space=pltpu.VMEM)] * len(shapes),
        out_shape=shapes,
        scratch_shapes=[pltpu.SemaphoreType.DMA((len(copies),))],
        compiler_params=pltpu.CompilerParams(vmem_limit_bytes=4 * 1024 * 1024),
    )(mask, offset, *operands)


def relayed_kernel(at, mine, other, out):
    tile, width = out.shape
    offset = jnp.max(mine[tile : tile + INFO_ROWS, 4 * 128 : 5 * 128].astype(jnp.float32))
    here = offset == (lax.axis_index("head") // 2).astype(jnp.float32)

    @pl.when(here)
    def _():
        out[...] = mine[:tile, at : at + width]

    @pl.when(jnp.logical_not(here))
    def _():
        out[...] = other[...]


def relayed(mine, other, at):
    return pl.pallas_call(
        functools.partial(relayed_kernel, at),
        in_specs=[pl.BlockSpec(memory_space=pltpu.VMEM)] * 2,
        out_specs=pl.BlockSpec(memory_space=pltpu.VMEM),
        out_shape=jax.ShapeDtypeStruct(other.shape, other.dtype),
        compiler_params=pltpu.CompilerParams(vmem_limit_bytes=4 * 1024 * 1024),
    )(mine, other)


def four_frames(queries, keys, values, pair_mask, tile_offset):
    h = lax.axis_index("head")
    rows, features = queries.shape
    width = features // 4
    heads = width // HEAD_DIM

    def columns(array, d):
        return lax.dynamic_slice_in_dim(array, (h ^ d) * width, width, axis=1)

    def beside(*arrays):
        return jnp.concatenate(arrays, axis=1)

    def below(*arrays):
        return jnp.concatenate(arrays, axis=0)

    def to_head(array, d):
        return lax.ppermute(array, "head", [(i, i ^ d) for i in range(4)])

    def along(array, pairs):
        return lax.ppermute(array, "frame", pairs)

    def after(array, earlier):
        return lax.optimization_barrier((array, earlier))[0]

    kv = [[columns(array, d) for array in (keys, values)] for d in range(4)]
    kv = lax.optimization_barrier(kv)
    got = to_head(beside(*kv[1], *kv[3]), 1)
    pay, q_own, q_far, told = packed(
        (queries, keys, values),
        pair_mask,
        tile_offset,
        [[(0, 1, 0, width), (0, 3, 0, width)], [(0, 0, 0, width)], [(0, 2, 0, width)]],
        width,
        2 * width,
    )
    mine = below(beside(*kv[0]), got[:, : 2 * width], told)
    other_k = to_head(below(kv[2][0], got[:, 2 * width : 3 * width]), 2)
    other_v = to_head(below(kv[2][1], got[:, 3 * width :]), 2)
    n1m = along(mine, OUTER)
    n2m = along(mine, INNER)
    n1k = along(other_k, OUTER)
    n2k = along(other_k, INNER)
    n1v = along(other_v, OUTER)
    n2v = along(other_v, INNER)

    got = to_head(after(pay, got), 1)
    q_mine = below(q_own, got[:, :width])
    q_other = to_head(after(below(q_far, got[:, width:]), other_v), 2)

    r1k = along(after(relayed(n1m, n1k, 0), (n2m, n2k)), INNER)
    r1v = along(after(relayed(n1m, n1v, width), n2v), INNER)
    r2k = along(relayed(n2m, n2k, 0), OUTWARD)
    r3k = along(r1k, OUTWARD)
    r2v = along(after(relayed(n2m, n2v, width), r1k), OUTWARD)

    weights, totals = find_weights(
        pair_mask, q_mine, q_other, [mine, other_k, n1m, n1k, n2m, n2k, r1k, r2k, r3k], heads
    )
    result = jnp.zeros((rows, features), jnp.bfloat16)
    cut = (heads + 1) // 2
    for begin, end in ((0, cut), (cut, heads)):
        r3v = along(r1v[:, begin * HEAD_DIM : end * HEAD_DIM], OUTWARD)
        whole = [(x, heads + begin) for x in (mine, n1m, n2m)]
        part = [(x, begin) for x in (other_v, n1v, n2v, r1v, r2v)]
        slots = [whole[0], part[0], whole[1], part[1], whole[2], part[2], part[3], part[4], (r3v, 0)]
        out = mix_values(weights, totals, slots, begin, end - begin)
        out = [out[0]] + [to_head(out[d], d) for d in (1, 2, 3)]
        for d in range(4):
            result = lax.dynamic_update_slice_in_dim(result, out[d], (h ^ d) * width + begin * HEAD_DIM, axis=1)
    return result


def solution(mesh):
    sizes = dict(mesh.shape)
    per_device = four_frames if sizes["frame"] == 4 and sizes["head"] == 4 else general
    return jax.shard_map(
        per_device,
        mesh=mesh,
        in_specs=(
            P(("parts", "frame", "head"), None),
            P(("parts", "frame", "head"), None),
            P(("parts", "frame", "head"), None),
            P(("parts", "frame"), None),
            P(("parts", "frame")),
        ),
        out_specs=P(("parts", "frame", "head"), None),
        check_vma=False,
    )
```

```python
import functools
import math

import jax
import jax.numpy as jnp
from jax import lax
from jax.experimental import pallas as pl
from jax.experimental.pallas import tpu as pltpu
from jax.sharding import PartitionSpec as P

HEAD_DIM = 128
SCALE = 1.0 / HEAD_DIM**0.5
LOG2E = math.log2(math.e)


def padded(x, sides, width):
    for axis, dim in sides:
        peers, length = (lax.axis_size(axis), x.shape[dim])
        up = [(i, (i + 1) % peers) for i in range(peers - 1)]
        down = [(j, i) for i, j in up]
        last = lax.slice_in_dim(x, length - width, length, axis=dim)
        leading = lax.slice_in_dim(x, 0, width, axis=dim)
        before = lax.ppermute(last, axis, up)
        after = lax.ppermute(leading, axis, down)
        x = jnp.concatenate([before, x, after], axis=dim)
    return x


def from_partner(x, axis, bit):
    return lax.ppermute(x, axis, [(i, i ^ 1 << bit) for i in range(lax.axis_size(axis))])


def subsample(frame_rows, offset, level, tiles, tile):
    step = 2**level
    width = frame_rows.shape[-1]
    grouped = frame_rows.reshape(tiles // step, step, tile, width)
    picked = lax.dynamic_index_in_dim(grouped, offset % step, 1, keepdims=False)
    return picked.reshape(-1, width)


def attend(query_rows, key_rows, value_rows, valid):
    count = query_rows.shape[0]
    heads = query_rows.shape[1] // HEAD_DIM
    q_three = query_rows.reshape(count, heads, HEAD_DIM).transpose(1, 0, 2)
    k_three = key_rows.reshape(-1, heads, HEAD_DIM).transpose(1, 0, 2)
    v_three = value_rows.reshape(-1, heads, HEAD_DIM).transpose(1, 0, 2)

    def one_head(operands):
        q_head, k_head, v_head = operands
        scores = jnp.dot(q_head, k_head.T, preferred_element_type=jnp.float32) * SCALE
        scores = jnp.where(valid[None, :] > 0, scores, -1e30)
        top = jnp.max(scores, axis=1, keepdims=True)
        weights = jnp.exp(scores - top) * valid[None, :]
        total = jnp.sum(weights, axis=1, keepdims=True)
        mixed = jnp.dot(weights.astype(jnp.bfloat16), v_head, preferred_element_type=jnp.float32)
        return mixed / total

    outcome = lax.map(one_head, (q_three, k_three, v_three))
    return outcome.transpose(1, 0, 2).reshape(count, heads * HEAD_DIM).astype(jnp.bfloat16)


def ordered(mine, theirs, upper):
    return jnp.where(upper == 1, jnp.concatenate([theirs, mine]), jnp.concatenate([mine, theirs]))


def general(queries, keys, values, pair_mask, tile_offset):
    frames_n = lax.axis_size("frame")
    current = lax.axis_index("frame")
    q_rows, k_rows, v_rows = (
        lax.all_to_all(queries, "head", split_axis=1, concat_axis=0, tiled=True),
        lax.all_to_all(keys, "head", split_axis=1, concat_axis=0, tiled=True),
        lax.all_to_all(values, "head", split_axis=1, concat_axis=0, tiled=True),
    )
    count = q_rows.shape[0]
    width = q_rows.shape[1]
    tiles = frames_n // 2
    tile = count // tiles
    depth = frames_n.bit_length() - 1
    stacked = jnp.stack([k_rows, v_rows])
    near = padded(stacked, (("frame", 1),), count)
    near_index = current - 1 + jnp.arange(3, dtype=jnp.int32)
    near_good = ((near_index >= 0) & (near_index < frames_n)).astype(jnp.float32)
    key_parts = [near[0]]
    value_parts = [near[1]]
    valid_parts = [jnp.repeat(near_good, count)]
    mask_row = pair_mask[0]
    offset = tile_offset[0]
    k_tiles = k_rows.reshape(tiles, tile, width)
    v_tiles = v_rows.reshape(tiles, tile, width)
    own = {}
    for level in range(1, depth):
        own[level] = (
            subsample(k_tiles, offset, level, tiles, tile)[None],
            subsample(v_tiles, offset, level, tiles, tile)[None],
        )
    sibling = {}
    cut = max(1, depth - 2)
    upper_levels = [level for level in range(1, depth) if level >= cut]
    k_pack = jnp.concatenate([own[level][0].reshape(-1, width) for level in upper_levels])
    v_pack = jnp.concatenate([own[level][1].reshape(-1, width) for level in upper_levels])
    k_every, v_every = (
        lax.all_gather(k_pack, "frame", axis=0, tiled=True),
        lax.all_gather(v_pack, "frame", axis=0, tiled=True),
    )
    k_every = k_every.reshape(frames_n, -1, width)
    v_every = v_every.reshape(frames_n, -1, width)
    position = 0
    for level in upper_levels:
        step = 2**level
        rows = count // step
        start = jnp.bitwise_xor(current // step, 1) * step
        block_k = lax.dynamic_slice_in_dim(k_every[:, position : position + rows], start, step, 0)
        block_v = lax.dynamic_slice_in_dim(v_every[:, position : position + rows], start, step, 0)
        sibling[level] = (block_k, block_v)
        position = position + rows
    swap_levels = [level for level in range(1, depth) if level < cut]
    growing = {level: own[level] for level in swap_levels}
    sections = cut if swap_levels else 0
    for bit in range(sections):
        active = [level for level in swap_levels if level >= bit]
        k_pack = jnp.concatenate([growing[level][0].reshape(-1, width) for level in active])
        v_pack = jnp.concatenate([growing[level][1].reshape(-1, width) for level in active])
        k_in, v_in = (from_partner(k_pack, "frame", bit), from_partner(v_pack, "frame", bit))
        upper = current // 2**bit % 2
        position = 0
        for level in active:
            shape = growing[level][0].shape
            size = shape[0] * shape[1]
            theirs_k = k_in[position : position + size].reshape(shape)
            theirs_v = v_in[position : position + size].reshape(shape)
            position = position + size
            if level == bit:
                sibling[level] = (theirs_k, theirs_v)
            else:
                growing[level] = (
                    ordered(growing[level][0], theirs_k, upper),
                    ordered(growing[level][1], theirs_v, upper),
                )
    for level in range(1, depth):
        step = 2**level
        start = jnp.bitwise_xor(current // step, 1) * step
        frame_ids = start + jnp.arange(step, dtype=jnp.int32)
        allowed = lax.dynamic_slice_in_dim(mask_row, start, step, 0)
        good = ((jnp.abs(frame_ids - current) >= 2) & (allowed == 1)).astype(jnp.float32)
        block_k, block_v = sibling[level]
        key_parts.append(block_k.reshape(-1, width))
        value_parts.append(block_v.reshape(-1, width))
        valid_parts.append(jnp.repeat(good, block_k.shape[1]))
    result = attend(
        q_rows,
        jnp.concatenate(key_parts),
        jnp.concatenate(value_parts),
        jnp.concatenate(valid_parts),
    )
    return lax.all_to_all(result, "head", split_axis=0, concat_axis=1, tiled=True)


INFO_ROWS = 16
OUTER = [(0, 1), (1, 0), (2, 3), (3, 2)]


def fold(x):
    parts = [x[:, at : at + 128] for at in range(0, x.shape[1], 128)]
    best = parts[0]
    for part in parts[1:]:
        best = jnp.maximum(best, part)
    return best


def scores_of(q, slots, held):
    free, top = None, None
    for at, (k, valid) in enumerate(slots):
        s = lax.dot_general(q, k[...], (((1,), (1,)), ((), ())), preferred_element_type=jnp.float32)
        held[:, at * s.shape[1] : (at + 1) * s.shape[1]] = s
        best = fold(s)
        if valid is None:
            free = best if free is None else jnp.maximum(free, best)
        else:
            best = jnp.where(valid, jnp.max(best, axis=1, keepdims=True), -1e30)
            top = best if top is None else jnp.maximum(top, best)
    free = jnp.max(free, axis=1, keepdims=True)
    return free if top is None else jnp.maximum(free, top)


def weights_of(top, slots, held, out):
    factor = SCALE * LOG2E
    total = None
    for at, (k, valid) in enumerate(slots):
        tile = k.shape[0]
        level = top if valid is None else jnp.where(valid, top, 1e30)
        w = jnp.exp2((held[:, at * tile : (at + 1) * tile] - level) * factor)
        out[:, at * tile : (at + 1) * tile] = w.astype(jnp.bfloat16)
        for begin in range(0, tile, 128):
            part = w[:, begin : begin + 128]
            total = part if total is None else total + part
    return jnp.sum(total, axis=1, keepdims=True)


def inner_frame():
    z = lax.axis_index("frame")
    return (z == 1) | (z == 2)


def weights_kernel(mask, q_mine, q_other, mine, other, n1m, n1o, n2m, n2o, r1, r2, r3, weights, totals, held0, held1):
    z = lax.axis_index("frame")
    tile = r1.shape[0]
    near = mask[0, z ^ 2] == 1
    always = [(mine, None), (other, None), (n1m, None), (n1o, None)]

    def body(slots):
        rooms = (held0, held1)
        tops = [scores_of(q[...], slots, held) for q, held in zip((q_mine, q_other), rooms)]
        for half, (top, held) in enumerate(zip(tops, rooms)):
            rows = slice(half * tile, (half + 1) * tile)
            total = weights_of(top, slots, held, weights.at[rows])
            totals[rows] = jnp.broadcast_to(total, (tile, totals.shape[1]))

    @pl.when(inner_frame())
    def _():
        body(always + [(n2m, None), (n2o, None), (r1, near)])

    @pl.when(jnp.logical_not(inner_frame()))
    def _():
        body(always + [(r2, near), (r3, mask[0, z ^ 3] == 1)])


def mixed_tiles(weights, at, values):
    mixed = None
    for n, v in enumerate(values):
        tile = v.shape[0]
        mix = jnp.dot(weights[:, (at + n) * tile : (at + n + 1) * tile], v[...], preferred_element_type=jnp.float32)
        mixed = mix if mixed is None else mixed + mix
    return mixed


def values_kernel(weights, mine, other, n1m, n1o, n2m, n2o, r2, out):
    tile = r2.shape[0]
    always = [mine, other, n1m, n1o]
    for half in range(2):
        rows = slice(half * tile, (half + 1) * tile)

        @pl.when(inner_frame())
        def _():
            out[rows] = mixed_tiles(weights.at[rows], 0, always + [n2m, n2o])

        @pl.when(jnp.logical_not(inner_frame()))
        def _():
            out[rows] = mixed_tiles(weights.at[rows], 0, always + [r2])


def last_kernel(weights, totals, partial, r1, r3, *outs):
    rows = outs[0].shape[0]
    tile = r1.shape[0]

    def body(at, value):
        for d, out in enumerate(outs):
            span = slice(d * rows, (d + 1) * rows)
            mix = jnp.dot(weights[span, at * tile : (at + 1) * tile], value[...], preferred_element_type=jnp.float32)
            out[...] = ((partial[span] + mix) / totals[span]).astype(jnp.bfloat16)

    @pl.when(inner_frame())
    def _():
        body(6, r1)

    @pl.when(jnp.logical_not(inner_frame()))
    def _():
        body(5, r3)


def by_head(x, rows, first=0):
    return x, pl.BlockSpec((rows, HEAD_DIM), lambda i: (0, first + i))


def find_weights(mask, q_mine, q_other, keys, heads):
    tile = q_mine.shape[0]
    blocks = [by_head(q_mine, tile), by_head(q_other, tile)] + [by_head(k, tile) for k in keys]
    shapes = [(2 * tile, 7 * tile, jnp.bfloat16), (2 * tile, HEAD_DIM, jnp.float32)]
    return pl.pallas_call(
        weights_kernel,
        grid=(heads,),
        in_specs=[pl.BlockSpec(memory_space=pltpu.SMEM)] + [spec for _, spec in blocks],
        out_specs=[pl.BlockSpec((rows, lanes), lambda i: (i, 0)) for rows, lanes, _ in shapes],
        out_shape=[jax.ShapeDtypeStruct((heads * rows, lanes), dtype) for rows, lanes, dtype in shapes],
        scratch_shapes=[pltpu.VMEM((tile, 7 * tile), jnp.float32)] * 2,
        compiler_params=pltpu.CompilerParams(vmem_limit_bytes=16 * 1024 * 1024),
        cost_estimate=pl.CostEstimate(
            flops=heads * 28 * tile * tile * HEAD_DIM,
            bytes_accessed=heads * 28 * tile * tile,
            transcendentals=heads * 14 * tile * tile,
        ),
    )(mask, *[x for x, _ in blocks])


def mix_values(weights, totals, near, r1, r2, r3, heads):
    rows, lanes = weights.shape[0] // heads, weights.shape[1]
    tile = lanes // 7
    whole = weights, pl.BlockSpec((rows, lanes), lambda i: (i, 0))
    blocks = [whole] + [by_head(v, tile, heads) for v in near] + [by_head(r2, tile)]
    partial = pl.pallas_call(
        values_kernel,
        grid=(heads,),
        in_specs=[spec for _, spec in blocks],
        out_specs=pl.BlockSpec((rows, HEAD_DIM), lambda i: (i, 0)),
        out_shape=jax.ShapeDtypeStruct((heads * rows, HEAD_DIM), jnp.float32),
        compiler_params=pltpu.CompilerParams(vmem_limit_bytes=12 * 1024 * 1024),
        cost_estimate=pl.CostEstimate(
            flops=heads * 2 * rows * lanes * HEAD_DIM, bytes_accessed=heads * 2 * rows * lanes, transcendentals=0
        ),
    )(*[x for x, _ in blocks])
    sums = [(x, pl.BlockSpec((rows, HEAD_DIM), lambda i: (i, 0))) for x in (totals, partial)]
    blocks = [whole] + sums + [by_head(r1, tile), by_head(r3, tile)]
    return pl.pallas_call(
        last_kernel,
        grid=(heads,),
        in_specs=[spec for _, spec in blocks],
        out_specs=[pl.BlockSpec((rows // 4, HEAD_DIM), lambda i: (0, i))] * 4,
        out_shape=[jax.ShapeDtypeStruct((rows // 4, heads * HEAD_DIM), jnp.bfloat16)] * 4,
        compiler_params=pltpu.CompilerParams(vmem_limit_bytes=12 * 1024 * 1024),
        cost_estimate=pl.CostEstimate(
            flops=heads * 2 * rows * tile * HEAD_DIM, bytes_accessed=heads * 2 * rows * lanes, transcendentals=0
        ),
    )(*[x for x, _ in blocks])


def pack_kernel(copies, width, mask, offset, *refs):
    ins, outs, sems = refs[:3], refs[3:-1], refs[-1]
    h = lax.axis_index("head")
    started = []
    for n, (operand, d, begin, result, at, lanes) in enumerate(copies):
        source = ins[operand].at[:, pl.ds(pl.multiple_of((h ^ d) * width + begin, HEAD_DIM), lanes)]
        copy = pltpu.make_async_copy(source, outs[result].at[:, at : at + lanes], sems.at[n])
        copy.start()
        started.append(copy)
    if len(outs) > 1 + max(copy[3] for copy in copies):
        told = outs[-1]
        for group in range(told.shape[1] // 128):
            value = mask[0, group] if group < 4 else offset[0]
            rows = jnp.full((told.shape[0], 128), value, jnp.int32).astype(jnp.float32)
            told[:, group * 128 : (group + 1) * 128] = rows.astype(told.dtype)
    for copy in started:
        copy.wait()


def packed(operands, mask, offset, results, width, told):
    rows = operands[0].shape[0]
    copies, shapes = [], []
    for n, parts in enumerate(results):
        at = 0
        for operand, d, begin, lanes in parts:
            copies.append((operand, d, begin, n, at, lanes))
            at += lanes
        shapes.append(jax.ShapeDtypeStruct((rows, at), jnp.bfloat16))
    if told:
        shapes.append(jax.ShapeDtypeStruct((INFO_ROWS, told), jnp.bfloat16))
    return pl.pallas_call(
        functools.partial(pack_kernel, copies, width),
        in_specs=[pl.BlockSpec(memory_space=pltpu.SMEM)] * 2 + [pl.BlockSpec(memory_space=pltpu.HBM)] * 3,
        out_specs=[pl.BlockSpec(memory_space=pltpu.VMEM)] * len(shapes),
        out_shape=shapes,
        scratch_shapes=[pltpu.SemaphoreType.DMA((len(copies),))],
        compiler_params=pltpu.CompilerParams(vmem_limit_bytes=4 * 1024 * 1024),
    )(mask, offset, *operands)


def relayed_kernel(mine, other, k_out, v_out):
    tile, width = k_out.shape
    offset = jnp.max(mine[tile : tile + INFO_ROWS, 4 * 128 : 5 * 128].astype(jnp.float32))
    here = offset == (lax.axis_index("head") // 2).astype(jnp.float32)

    def take(ref):
        k_out[...] = ref[:tile, :width]
        v_out[...] = ref[:tile, width:]

    @pl.when(here)
    def _():
        take(mine)

    @pl.when(jnp.logical_not(here))
    def _():
        take(other)


def relayed(mine, other):
    tile, lanes = other.shape
    return pl.pallas_call(
        relayed_kernel,
        in_specs=[pl.BlockSpec(memory_space=pltpu.VMEM)] * 2,
        out_specs=[pl.BlockSpec(memory_space=pltpu.VMEM)] * 2,
        out_shape=[jax.ShapeDtypeStruct((tile, lanes // 2), other.dtype)] * 2,
        compiler_params=pltpu.CompilerParams(vmem_limit_bytes=4 * 1024 * 1024),
    )(mine, other)


def four_frames(queries, keys, values, pair_mask, tile_offset):
    h = lax.axis_index("head")
    rows, features = queries.shape
    width = features // 4
    heads = width // HEAD_DIM

    def columns(array, d):
        return lax.dynamic_slice_in_dim(array, (h ^ d) * width, width, axis=1)

    def beside(*arrays):
        return jnp.concatenate(arrays, axis=1)

    def below(*arrays):
        return jnp.concatenate(arrays, axis=0)

    def to_head(array, d):
        return lax.ppermute(array, "head", [(i, i ^ d) for i in range(4)])

    def along(array, pairs):
        return lax.ppermute(array, "frame", pairs)

    def across(array):
        pairs = [(4 * z + j, 4 * (3 - z) + j if z in (1, 2) else 4 * z + (j ^ 1)) for z in range(4) for j in range(4)]
        return lax.ppermute(array, ("frame", "head"), pairs)

    def after(array, earlier):
        return lax.optimization_barrier((array, earlier))[0]

    kv = [[columns(array, d) for array in (keys, values)] for d in range(4)]
    kv = lax.optimization_barrier(kv)
    got = to_head(beside(*kv[1], *kv[3]), 1)
    pay, q_own, q_far, told = packed(
        (queries, keys, values),
        pair_mask,
        tile_offset,
        [[(0, 1, 0, width), (0, 3, 0, width)], [(0, 0, 0, width)], [(0, 2, 0, width)]],
        width,
        2 * width,
    )
    mine = below(beside(*kv[0]), got[:, : 2 * width], told)
    other = to_head(below(beside(*kv[2]), got[:, 2 * width :]), 2)
    n1m = along(mine, OUTER)
    n2m = across(mine)
    n1o = along(other, OUTER)
    n2o = across(other)

    got = to_head(after(pay, got), 1)
    q_mine = below(q_own, got[:, :width])
    q_other = to_head(after(below(q_far, got[:, width:]), other), 2)

    r1k, r1v = after(relayed(n1m, n1o), n2m)
    r1k = across(r1k)
    r1v = across(r1v)
    r2k, r2v = relayed(n2m, n2o)
    r2k = along(r2k, OUTER)
    r3k = along(r1k, OUTER)
    r2v = along(after(r2v, r1k), OUTER)
    r3v = along(r1v, OUTER)

    near = [mine, other, n1m, n1o, n2m, n2o]
    weights, totals = find_weights(pair_mask, q_mine, q_other, [*near, r1k, r2k, r3k], heads)
    out = mix_values(weights, totals, near, r1v, r2v, r3v, heads)
    out = [out[0]] + [to_head(out[d], d) for d in (1, 2, 3)]
    result = jnp.zeros((rows, features), jnp.bfloat16)
    for d in range(4):
        result = lax.dynamic_update_slice_in_dim(result, out[d], (h ^ d) * width, axis=1)
    return result


def solution(mesh):
    sizes = dict(mesh.shape)
    per_device = four_frames if sizes["frame"] == 4 and sizes["head"] == 4 else general
    return jax.shard_map(
        per_device,
        mesh=mesh,
        in_specs=(
            P(("parts", "frame", "head"), None),
            P(("parts", "frame", "head"), None),
            P(("parts", "frame", "head"), None),
            P(("parts", "frame"), None),
            P(("parts", "frame")),
        ),
        out_specs=P(("parts", "frame", "head"), None),
        check_vma=False,
    )
```

```python
import functools
import math

import jax
import jax.numpy as jnp
from jax import lax
from jax.experimental import pallas as pl
from jax.experimental.pallas import tpu as pltpu
from jax.sharding import PartitionSpec as P

HEAD_DIM = 128
SCALE = 1.0 / HEAD_DIM**0.5
LOG2E = math.log2(math.e)


def padded(x, sides, width):
    for axis, dim in sides:
        peers, length = (lax.axis_size(axis), x.shape[dim])
        up = [(i, (i + 1) % peers) for i in range(peers - 1)]
        down = [(j, i) for i, j in up]
        last = lax.slice_in_dim(x, length - width, length, axis=dim)
        leading = lax.slice_in_dim(x, 0, width, axis=dim)
        before = lax.ppermute(last, axis, up)
        after = lax.ppermute(leading, axis, down)
        x = jnp.concatenate([before, x, after], axis=dim)
    return x


def from_partner(x, axis, bit):
    return lax.ppermute(x, axis, [(i, i ^ 1 << bit) for i in range(lax.axis_size(axis))])


def subsample(frame_rows, offset, level, tiles, tile):
    step = 2**level
    width = frame_rows.shape[-1]
    grouped = frame_rows.reshape(tiles // step, step, tile, width)
    picked = lax.dynamic_index_in_dim(grouped, offset % step, 1, keepdims=False)
    return picked.reshape(-1, width)


def attend(query_rows, key_rows, value_rows, valid):
    count = query_rows.shape[0]
    heads = query_rows.shape[1] // HEAD_DIM
    q_three = query_rows.reshape(count, heads, HEAD_DIM).transpose(1, 0, 2)
    k_three = key_rows.reshape(-1, heads, HEAD_DIM).transpose(1, 0, 2)
    v_three = value_rows.reshape(-1, heads, HEAD_DIM).transpose(1, 0, 2)

    def one_head(operands):
        q_head, k_head, v_head = operands
        scores = jnp.dot(q_head, k_head.T, preferred_element_type=jnp.float32) * SCALE
        scores = jnp.where(valid[None, :] > 0, scores, -1e30)
        top = jnp.max(scores, axis=1, keepdims=True)
        weights = jnp.exp(scores - top) * valid[None, :]
        total = jnp.sum(weights, axis=1, keepdims=True)
        mixed = jnp.dot(weights.astype(jnp.bfloat16), v_head, preferred_element_type=jnp.float32)
        return mixed / total

    outcome = lax.map(one_head, (q_three, k_three, v_three))
    return outcome.transpose(1, 0, 2).reshape(count, heads * HEAD_DIM).astype(jnp.bfloat16)


def ordered(mine, theirs, upper):
    return jnp.where(upper == 1, jnp.concatenate([theirs, mine]), jnp.concatenate([mine, theirs]))


def general(queries, keys, values, pair_mask, tile_offset):
    frames_n = lax.axis_size("frame")
    current = lax.axis_index("frame")
    q_rows, k_rows, v_rows = (
        lax.all_to_all(queries, "head", split_axis=1, concat_axis=0, tiled=True),
        lax.all_to_all(keys, "head", split_axis=1, concat_axis=0, tiled=True),
        lax.all_to_all(values, "head", split_axis=1, concat_axis=0, tiled=True),
    )
    count = q_rows.shape[0]
    width = q_rows.shape[1]
    tiles = frames_n // 2
    tile = count // tiles
    depth = frames_n.bit_length() - 1
    stacked = jnp.stack([k_rows, v_rows])
    near = padded(stacked, (("frame", 1),), count)
    near_index = current - 1 + jnp.arange(3, dtype=jnp.int32)
    near_good = ((near_index >= 0) & (near_index < frames_n)).astype(jnp.float32)
    key_parts = [near[0]]
    value_parts = [near[1]]
    valid_parts = [jnp.repeat(near_good, count)]
    mask_row = pair_mask[0]
    offset = tile_offset[0]
    k_tiles = k_rows.reshape(tiles, tile, width)
    v_tiles = v_rows.reshape(tiles, tile, width)
    own = {}
    for level in range(1, depth):
        own[level] = (
            subsample(k_tiles, offset, level, tiles, tile)[None],
            subsample(v_tiles, offset, level, tiles, tile)[None],
        )
    sibling = {}
    cut = max(1, depth - 2)
    upper_levels = [level for level in range(1, depth) if level >= cut]
    k_pack = jnp.concatenate([own[level][0].reshape(-1, width) for level in upper_levels])
    v_pack = jnp.concatenate([own[level][1].reshape(-1, width) for level in upper_levels])
    k_every, v_every = (
        lax.all_gather(k_pack, "frame", axis=0, tiled=True),
        lax.all_gather(v_pack, "frame", axis=0, tiled=True),
    )
    k_every = k_every.reshape(frames_n, -1, width)
    v_every = v_every.reshape(frames_n, -1, width)
    position = 0
    for level in upper_levels:
        step = 2**level
        rows = count // step
        start = jnp.bitwise_xor(current // step, 1) * step
        block_k = lax.dynamic_slice_in_dim(k_every[:, position : position + rows], start, step, 0)
        block_v = lax.dynamic_slice_in_dim(v_every[:, position : position + rows], start, step, 0)
        sibling[level] = (block_k, block_v)
        position = position + rows
    swap_levels = [level for level in range(1, depth) if level < cut]
    growing = {level: own[level] for level in swap_levels}
    sections = cut if swap_levels else 0
    for bit in range(sections):
        active = [level for level in swap_levels if level >= bit]
        k_pack = jnp.concatenate([growing[level][0].reshape(-1, width) for level in active])
        v_pack = jnp.concatenate([growing[level][1].reshape(-1, width) for level in active])
        k_in, v_in = (from_partner(k_pack, "frame", bit), from_partner(v_pack, "frame", bit))
        upper = current // 2**bit % 2
        position = 0
        for level in active:
            shape = growing[level][0].shape
            size = shape[0] * shape[1]
            theirs_k = k_in[position : position + size].reshape(shape)
            theirs_v = v_in[position : position + size].reshape(shape)
            position = position + size
            if level == bit:
                sibling[level] = (theirs_k, theirs_v)
            else:
                growing[level] = (
                    ordered(growing[level][0], theirs_k, upper),
                    ordered(growing[level][1], theirs_v, upper),
                )
    for level in range(1, depth):
        step = 2**level
        start = jnp.bitwise_xor(current // step, 1) * step
        frame_ids = start + jnp.arange(step, dtype=jnp.int32)
        allowed = lax.dynamic_slice_in_dim(mask_row, start, step, 0)
        good = ((jnp.abs(frame_ids - current) >= 2) & (allowed == 1)).astype(jnp.float32)
        block_k, block_v = sibling[level]
        key_parts.append(block_k.reshape(-1, width))
        value_parts.append(block_v.reshape(-1, width))
        valid_parts.append(jnp.repeat(good, block_k.shape[1]))
    result = attend(
        q_rows,
        jnp.concatenate(key_parts),
        jnp.concatenate(value_parts),
        jnp.concatenate(valid_parts),
    )
    return lax.all_to_all(result, "head", split_axis=0, concat_axis=1, tiled=True)


INFO_ROWS = 16
OUTER = [(0, 1), (1, 0), (2, 3), (3, 2)]


def fold(x):
    parts = [x[:, at : at + 128] for at in range(0, x.shape[1], 128)]
    best = parts[0]
    for part in parts[1:]:
        best = jnp.maximum(best, part)
    return best


def scores_of(q, slots, held):
    free, top = None, None
    for at, (k, valid) in enumerate(slots):
        s = lax.dot_general(q, k[...], (((1,), (1,)), ((), ())), preferred_element_type=jnp.float32)
        held[:, at * s.shape[1] : (at + 1) * s.shape[1]] = s
        best = fold(s)
        if valid is None:
            free = best if free is None else jnp.maximum(free, best)
        else:
            best = jnp.where(valid, jnp.max(best, axis=1, keepdims=True), -1e30)
            top = best if top is None else jnp.maximum(top, best)
    free = jnp.max(free, axis=1, keepdims=True)
    return free if top is None else jnp.maximum(free, top)


def weights_of(top, slots, held, out):
    factor = SCALE * LOG2E
    total = None
    for at, (k, valid) in enumerate(slots):
        tile = k.shape[0]
        level = top if valid is None else jnp.where(valid, top, 1e30)
        w = jnp.exp2((held[:, at * tile : (at + 1) * tile] - level) * factor)
        out[:, at * tile : (at + 1) * tile] = w.astype(jnp.bfloat16)
        for begin in range(0, tile, 128):
            part = w[:, begin : begin + 128]
            total = part if total is None else total + part
    return jnp.sum(total, axis=1, keepdims=True)


def inner_frame():
    z = lax.axis_index("frame")
    return (z == 1) | (z == 2)


def weights_kernel(mask, q_mine, q_other, mine, other, n1m, n1o, n2m, n2o, r1, r2, r3, weights, totals, held0, held1):
    z = lax.axis_index("frame")
    tile = r1.shape[0]
    near = mask[0, z ^ 2] == 1
    always = [(mine, None), (other, None), (n1m, None), (n1o, None)]

    def body(slots):
        rooms = (held0, held1)
        tops = [scores_of(q[...], slots, held) for q, held in zip((q_mine, q_other), rooms)]
        for half, (top, held) in enumerate(zip(tops, rooms)):
            rows = slice(half * tile, (half + 1) * tile)
            total = weights_of(top, slots, held, weights.at[rows])
            totals[rows] = jnp.broadcast_to(total, (tile, totals.shape[1]))

    @pl.when(inner_frame())
    def _():
        body(always + [(n2m, None), (n2o, None), (r1, near)])

    @pl.when(jnp.logical_not(inner_frame()))
    def _():
        body(always + [(r2, near), (r3, mask[0, z ^ 3] == 1)])


def mixed_tiles(weights, at, values):
    mixed = None
    for n, v in enumerate(values):
        tile = v.shape[0]
        mix = jnp.dot(weights[:, (at + n) * tile : (at + n + 1) * tile], v[...], preferred_element_type=jnp.float32)
        mixed = mix if mixed is None else mixed + mix
    return mixed


def near_kernel(weights, mine, other, n1m, n1o, n2m, n2o, out):
    tile = n1o.shape[0]
    near = [mine, other, n1m, n1o]
    for half in range(2):
        rows = slice(half * tile, (half + 1) * tile)

        @pl.when(inner_frame())
        def _():
            out[rows] = mixed_tiles(weights.at[rows], 0, near + [n2m, n2o])

        @pl.when(jnp.logical_not(inner_frame()))
        def _():
            out[rows] = mixed_tiles(weights.at[rows], 0, near)


def far_kernel(weights, totals, near, r1, r2, r3, *outs):
    rows = outs[0].shape[0]

    def body(at, values):
        for d, out in enumerate(outs):
            span = slice(d * rows, (d + 1) * rows)
            mixed = near[span] + mixed_tiles(weights.at[span], at, values)
            out[...] = (mixed / totals[span]).astype(jnp.bfloat16)

    @pl.when(inner_frame())
    def _():
        body(6, [r1])

    @pl.when(jnp.logical_not(inner_frame()))
    def _():
        body(4, [r2, r3])


def by_head(x, rows, first=0):
    return x, pl.BlockSpec((rows, HEAD_DIM), lambda i: (0, first + i))


def find_weights(mask, q_mine, q_other, keys, heads):
    tile = q_mine.shape[0]
    blocks = [by_head(q_mine, tile), by_head(q_other, tile)] + [by_head(k, tile) for k in keys]
    shapes = [(2 * tile, 7 * tile, jnp.bfloat16), (2 * tile, HEAD_DIM, jnp.float32)]
    return pl.pallas_call(
        weights_kernel,
        grid=(heads,),
        in_specs=[pl.BlockSpec(memory_space=pltpu.SMEM)] + [spec for _, spec in blocks],
        out_specs=[pl.BlockSpec((rows, lanes), lambda i: (i, 0)) for rows, lanes, _ in shapes],
        out_shape=[jax.ShapeDtypeStruct((heads * rows, lanes), dtype) for rows, lanes, dtype in shapes],
        scratch_shapes=[pltpu.VMEM((tile, 7 * tile), jnp.float32)] * 2,
        compiler_params=pltpu.CompilerParams(vmem_limit_bytes=16 * 1024 * 1024),
        cost_estimate=pl.CostEstimate(
            flops=heads * 28 * tile * tile * HEAD_DIM,
            bytes_accessed=heads * 28 * tile * tile,
            transcendentals=heads * 14 * tile * tile,
        ),
    )(mask, *[x for x, _ in blocks])


def mix_near(weights, near, heads):
    rows, lanes = weights.shape[0] // heads, weights.shape[1]
    blocks = [(weights, pl.BlockSpec((rows, lanes), lambda i: (i, 0)))] + [by_head(v, rows // 2, heads) for v in near]
    return pl.pallas_call(
        near_kernel,
        grid=(heads,),
        in_specs=[spec for _, spec in blocks],
        out_specs=pl.BlockSpec((rows, HEAD_DIM), lambda i: (i, 0)),
        out_shape=jax.ShapeDtypeStruct((heads * rows, HEAD_DIM), jnp.float32),
        compiler_params=pltpu.CompilerParams(vmem_limit_bytes=12 * 1024 * 1024),
        cost_estimate=pl.CostEstimate(
            flops=heads * 2 * rows * lanes * HEAD_DIM, bytes_accessed=heads * 2 * rows * lanes, transcendentals=0
        ),
    )(*[x for x, _ in blocks])


def add_far(weights, totals, mixed, r1, r2, r3, begin, end):
    lanes = weights.shape[1]
    tile = r1.shape[0]
    rows = 2 * tile
    heads = end - begin
    blocks = [
        (x, pl.BlockSpec((rows, width), lambda i: (begin + i, 0)))
        for x, width in ((weights, lanes), (totals, HEAD_DIM), (mixed, HEAD_DIM))
    ]
    blocks += [by_head(r1, tile, begin), by_head(r2, tile), by_head(r3, tile)]
    return pl.pallas_call(
        far_kernel,
        grid=(heads,),
        in_specs=[spec for _, spec in blocks],
        out_specs=[pl.BlockSpec((rows // 4, HEAD_DIM), lambda i: (0, i))] * 4,
        out_shape=[jax.ShapeDtypeStruct((rows // 4, heads * HEAD_DIM), jnp.bfloat16)] * 4,
        compiler_params=pltpu.CompilerParams(vmem_limit_bytes=12 * 1024 * 1024),
        cost_estimate=pl.CostEstimate(
            flops=heads * 4 * rows * tile * HEAD_DIM, bytes_accessed=heads * 2 * rows * lanes, transcendentals=0
        ),
    )(*[x for x, _ in blocks])


def pack_kernel(copies, width, mask, offset, *refs):
    ins, outs, sems = refs[:3], refs[3:-1], refs[-1]
    h = lax.axis_index("head")
    started = []
    for n, (operand, d, begin, result, at, lanes) in enumerate(copies):
        source = ins[operand].at[:, pl.ds(pl.multiple_of((h ^ d) * width + begin, HEAD_DIM), lanes)]
        copy = pltpu.make_async_copy(source, outs[result].at[:, at : at + lanes], sems.at[n])
        copy.start()
        started.append(copy)
    if len(outs) > 1 + max(copy[3] for copy in copies):
        told = outs[-1]
        for group in range(told.shape[1] // 128):
            value = mask[0, group] if group < 4 else offset[0]
            rows = jnp.full((told.shape[0], 128), value, jnp.int32).astype(jnp.float32)
            told[:, group * 128 : (group + 1) * 128] = rows.astype(told.dtype)
    for copy in started:
        copy.wait()


def packed(operands, mask, offset, results, width, told):
    rows = operands[0].shape[0]
    copies, shapes = [], []
    for n, parts in enumerate(results):
        at = 0
        for operand, d, begin, lanes in parts:
            copies.append((operand, d, begin, n, at, lanes))
            at += lanes
        shapes.append(jax.ShapeDtypeStruct((rows, at), jnp.bfloat16))
    if told:
        shapes.append(jax.ShapeDtypeStruct((INFO_ROWS, told), jnp.bfloat16))
    return pl.pallas_call(
        functools.partial(pack_kernel, copies, width),
        in_specs=[pl.BlockSpec(memory_space=pltpu.SMEM)] * 2 + [pl.BlockSpec(memory_space=pltpu.HBM)] * 3,
        out_specs=[pl.BlockSpec(memory_space=pltpu.VMEM)] * len(shapes),
        out_shape=shapes,
        scratch_shapes=[pltpu.SemaphoreType.DMA((len(copies),))],
        compiler_params=pltpu.CompilerParams(vmem_limit_bytes=4 * 1024 * 1024),
    )(mask, offset, *operands)


def relayed_kernel(mine, other, k_out, v_out):
    tile, width = k_out.shape
    offset = jnp.max(mine[tile : tile + INFO_ROWS, 4 * 128 : 5 * 128].astype(jnp.float32))
    here = offset == (lax.axis_index("head") // 2).astype(jnp.float32)

    def take(ref):
        k_out[...] = ref[:tile, :width]
        v_out[...] = ref[:tile, width:]

    @pl.when(here)
    def _():
        take(mine)

    @pl.when(jnp.logical_not(here))
    def _():
        take(other)


def relayed(mine, other):
    tile, lanes = other.shape
    return pl.pallas_call(
        relayed_kernel,
        in_specs=[pl.BlockSpec(memory_space=pltpu.VMEM)] * 2,
        out_specs=[pl.BlockSpec(memory_space=pltpu.VMEM)] * 2,
        out_shape=[jax.ShapeDtypeStruct((tile, lanes // 2), other.dtype)] * 2,
        compiler_params=pltpu.CompilerParams(vmem_limit_bytes=4 * 1024 * 1024),
    )(mine, other)


def four_frames(queries, keys, values, pair_mask, tile_offset):
    h = lax.axis_index("head")
    rows, features = queries.shape
    width = features // 4
    heads = width // HEAD_DIM

    def columns(array, d):
        return lax.dynamic_slice_in_dim(array, (h ^ d) * width, width, axis=1)

    def beside(*arrays):
        return jnp.concatenate(arrays, axis=1)

    def below(*arrays):
        return jnp.concatenate(arrays, axis=0)

    def to_head(array, d):
        return lax.ppermute(array, "head", [(i, i ^ d) for i in range(4)])

    def along(array, pairs):
        return lax.ppermute(array, "frame", pairs)

    def across(array):
        pairs = [(4 * z + j, 4 * (3 - z) + j if z in (1, 2) else 4 * z + (j ^ 1)) for z in range(4) for j in range(4)]
        return lax.ppermute(array, ("frame", "head"), pairs)

    def after(array, earlier):
        return lax.optimization_barrier((array, earlier))[0]

    kv = [[columns(array, d) for array in (keys, values)] for d in range(4)]
    kv = lax.optimization_barrier(kv)
    got = to_head(beside(*kv[1], *kv[3]), 1)
    pay, q_own, q_far, told = packed(
        (queries, keys, values),
        pair_mask,
        tile_offset,
        [[(0, 1, 0, width), (0, 3, 0, width)], [(0, 0, 0, width)], [(0, 2, 0, width)]],
        width,
        2 * width,
    )
    mine = below(beside(*kv[0]), got[:, : 2 * width], told)
    other = to_head(below(beside(*kv[2]), got[:, 2 * width :]), 2)
    n1m = along(mine, OUTER)
    n2m = across(mine)
    n1o = along(other, OUTER)
    n2o = across(other)

    got = to_head(after(pay, got), 1)
    q_mine = below(q_own, got[:, :width])
    q_other = to_head(after(below(q_far, got[:, width:]), other), 2)

    r1k, r1v = after(relayed(n1m, n1o), n2m)
    r1k = across(r1k)
    r1v = across(after(r1v, n2o))
    r2k, r2v = relayed(n2m, n2o)
    r2k = along(r2k, OUTER)
    r3k = along(after(r1k, r2k), OUTER)

    cut = (heads + 1) // 2
    groups = [slice(0, cut * HEAD_DIM), slice(cut * HEAD_DIM, width)]
    far2 = along(r2v[:, groups[0]], OUTER)
    far3 = along(r1v[:, groups[0]], OUTER)
    near = [mine, other, n1m, n1o, n2m, n2o]
    weights, totals = find_weights(
        pair_mask, q_mine, q_other, [*near, r1k, r2k, after(r3k, far2)], heads
    )
    both = along(after(below(r2v[:, groups[1]], r1v[:, groups[1]]), totals), OUTER)
    mixed = mix_near(after(weights, far3), near, heads)
    result = jnp.zeros((rows, features), jnp.bfloat16)
    pieces = []
    for begin, end, tiles in ((0, cut, (far2, far3)), (cut, heads, (both[: 2 * rows], both[2 * rows :]))):
        out = add_far(weights, totals, mixed, r1v, *tiles, begin, end)
        moved = [out[0]] + [to_head(out[d], d) for d in (1, 2, 3)]
        pieces = [(after(piece, moved[1]) if d else piece, d, at) for piece, d, at in pieces]
        pieces += [(piece, d, begin) for d, piece in enumerate(moved)]
    for piece, d, begin in pieces:
        result = lax.dynamic_update_slice_in_dim(result, piece, (h ^ d) * width + begin * HEAD_DIM, axis=1)
    return result


def solution(mesh):
    sizes = dict(mesh.shape)
    per_device = four_frames if sizes["frame"] == 4 and sizes["head"] == 4 else general
    return jax.shard_map(
        per_device,
        mesh=mesh,
        in_specs=(
            P(("parts", "frame", "head"), None),
            P(("parts", "frame", "head"), None),
            P(("parts", "frame", "head"), None),
            P(("parts", "frame"), None),
            P(("parts", "frame")),
        ),
        out_specs=P(("parts", "frame", "head"), None),
        check_vma=False,
    )
```

```python
import functools
import math

import jax
import jax.numpy as jnp
from jax import lax
from jax.experimental import pallas as pl
from jax.experimental.pallas import tpu as pltpu
from jax.sharding import PartitionSpec as P

HEAD_DIM = 128
SCALE = 1.0 / HEAD_DIM**0.5
LOG2E = math.log2(math.e)


def padded(x, sides, width):
    for axis, dim in sides:
        peers, length = (lax.axis_size(axis), x.shape[dim])
        up = [(i, (i + 1) % peers) for i in range(peers - 1)]
        down = [(j, i) for i, j in up]
        last = lax.slice_in_dim(x, length - width, length, axis=dim)
        leading = lax.slice_in_dim(x, 0, width, axis=dim)
        before = lax.ppermute(last, axis, up)
        after = lax.ppermute(leading, axis, down)
        x = jnp.concatenate([before, x, after], axis=dim)
    return x


def from_partner(x, axis, bit):
    return lax.ppermute(x, axis, [(i, i ^ 1 << bit) for i in range(lax.axis_size(axis))])


def subsample(frame_rows, offset, level, tiles, tile):
    step = 2**level
    width = frame_rows.shape[-1]
    grouped = frame_rows.reshape(tiles // step, step, tile, width)
    picked = lax.dynamic_index_in_dim(grouped, offset % step, 1, keepdims=False)
    return picked.reshape(-1, width)


def attend(query_rows, key_rows, value_rows, valid):
    count = query_rows.shape[0]
    heads = query_rows.shape[1] // HEAD_DIM
    q_three = query_rows.reshape(count, heads, HEAD_DIM).transpose(1, 0, 2)
    k_three = key_rows.reshape(-1, heads, HEAD_DIM).transpose(1, 0, 2)
    v_three = value_rows.reshape(-1, heads, HEAD_DIM).transpose(1, 0, 2)

    def one_head(operands):
        q_head, k_head, v_head = operands
        scores = jnp.dot(q_head, k_head.T, preferred_element_type=jnp.float32) * SCALE
        scores = jnp.where(valid[None, :] > 0, scores, -1e30)
        top = jnp.max(scores, axis=1, keepdims=True)
        weights = jnp.exp(scores - top) * valid[None, :]
        total = jnp.sum(weights, axis=1, keepdims=True)
        mixed = jnp.dot(weights.astype(jnp.bfloat16), v_head, preferred_element_type=jnp.float32)
        return mixed / total

    outcome = lax.map(one_head, (q_three, k_three, v_three))
    return outcome.transpose(1, 0, 2).reshape(count, heads * HEAD_DIM).astype(jnp.bfloat16)


def ordered(mine, theirs, upper):
    return jnp.where(upper == 1, jnp.concatenate([theirs, mine]), jnp.concatenate([mine, theirs]))


def general(queries, keys, values, pair_mask, tile_offset):
    frames_n = lax.axis_size("frame")
    current = lax.axis_index("frame")
    q_rows, k_rows, v_rows = (
        lax.all_to_all(queries, "head", split_axis=1, concat_axis=0, tiled=True),
        lax.all_to_all(keys, "head", split_axis=1, concat_axis=0, tiled=True),
        lax.all_to_all(values, "head", split_axis=1, concat_axis=0, tiled=True),
    )
    count = q_rows.shape[0]
    width = q_rows.shape[1]
    tiles = frames_n // 2
    tile = count // tiles
    depth = frames_n.bit_length() - 1
    stacked = jnp.stack([k_rows, v_rows])
    near = padded(stacked, (("frame", 1),), count)
    near_index = current - 1 + jnp.arange(3, dtype=jnp.int32)
    near_good = ((near_index >= 0) & (near_index < frames_n)).astype(jnp.float32)
    key_parts = [near[0]]
    value_parts = [near[1]]
    valid_parts = [jnp.repeat(near_good, count)]
    mask_row = pair_mask[0]
    offset = tile_offset[0]
    k_tiles = k_rows.reshape(tiles, tile, width)
    v_tiles = v_rows.reshape(tiles, tile, width)
    own = {}
    for level in range(1, depth):
        own[level] = (
            subsample(k_tiles, offset, level, tiles, tile)[None],
            subsample(v_tiles, offset, level, tiles, tile)[None],
        )
    sibling = {}
    cut = max(1, depth - 2)
    upper_levels = [level for level in range(1, depth) if level >= cut]
    k_pack = jnp.concatenate([own[level][0].reshape(-1, width) for level in upper_levels])
    v_pack = jnp.concatenate([own[level][1].reshape(-1, width) for level in upper_levels])
    k_every, v_every = (
        lax.all_gather(k_pack, "frame", axis=0, tiled=True),
        lax.all_gather(v_pack, "frame", axis=0, tiled=True),
    )
    k_every = k_every.reshape(frames_n, -1, width)
    v_every = v_every.reshape(frames_n, -1, width)
    position = 0
    for level in upper_levels:
        step = 2**level
        rows = count // step
        start = jnp.bitwise_xor(current // step, 1) * step
        block_k = lax.dynamic_slice_in_dim(k_every[:, position : position + rows], start, step, 0)
        block_v = lax.dynamic_slice_in_dim(v_every[:, position : position + rows], start, step, 0)
        sibling[level] = (block_k, block_v)
        position = position + rows
    swap_levels = [level for level in range(1, depth) if level < cut]
    growing = {level: own[level] for level in swap_levels}
    sections = cut if swap_levels else 0
    for bit in range(sections):
        active = [level for level in swap_levels if level >= bit]
        k_pack = jnp.concatenate([growing[level][0].reshape(-1, width) for level in active])
        v_pack = jnp.concatenate([growing[level][1].reshape(-1, width) for level in active])
        k_in, v_in = (from_partner(k_pack, "frame", bit), from_partner(v_pack, "frame", bit))
        upper = current // 2**bit % 2
        position = 0
        for level in active:
            shape = growing[level][0].shape
            size = shape[0] * shape[1]
            theirs_k = k_in[position : position + size].reshape(shape)
            theirs_v = v_in[position : position + size].reshape(shape)
            position = position + size
            if level == bit:
                sibling[level] = (theirs_k, theirs_v)
            else:
                growing[level] = (
                    ordered(growing[level][0], theirs_k, upper),
                    ordered(growing[level][1], theirs_v, upper),
                )
    for level in range(1, depth):
        step = 2**level
        start = jnp.bitwise_xor(current // step, 1) * step
        frame_ids = start + jnp.arange(step, dtype=jnp.int32)
        allowed = lax.dynamic_slice_in_dim(mask_row, start, step, 0)
        good = ((jnp.abs(frame_ids - current) >= 2) & (allowed == 1)).astype(jnp.float32)
        block_k, block_v = sibling[level]
        key_parts.append(block_k.reshape(-1, width))
        value_parts.append(block_v.reshape(-1, width))
        valid_parts.append(jnp.repeat(good, block_k.shape[1]))
    result = attend(
        q_rows,
        jnp.concatenate(key_parts),
        jnp.concatenate(value_parts),
        jnp.concatenate(valid_parts),
    )
    return lax.all_to_all(result, "head", split_axis=0, concat_axis=1, tiled=True)


INFO_ROWS = 16
OUTER = [(0, 1), (1, 0), (2, 3), (3, 2)]


def fold(x):
    parts = [x[:, at : at + 128] for at in range(0, x.shape[1], 128)]
    best = parts[0]
    for part in parts[1:]:
        best = jnp.maximum(best, part)
    return best


def scores_of(q, slots, held):
    free, top = None, None
    for at, (k, valid) in enumerate(slots):
        s = lax.dot_general(q, k[...], (((1,), (1,)), ((), ())), preferred_element_type=jnp.float32)
        held[:, at * s.shape[1] : (at + 1) * s.shape[1]] = s
        best = fold(s)
        if valid is None:
            free = best if free is None else jnp.maximum(free, best)
        else:
            best = jnp.where(valid, jnp.max(best, axis=1, keepdims=True), -1e30)
            top = best if top is None else jnp.maximum(top, best)
    free = jnp.max(free, axis=1, keepdims=True)
    return free if top is None else jnp.maximum(free, top)


def attention_kernel(mask, q_mine, q_other, km, ko, n1km, n1ko, n2km, n2ko, r1, r2, r3, v, n1v, n2v, *rest):
    mixed_out, totals, far_weights, held0, held1 = rest
    factor = SCALE * LOG2E
    z = lax.axis_index("frame")
    tile = r1.shape[0]
    near2 = mask[0, z ^ 2] == 1

    def body(near, values, far):
        rooms = (held0, held1)
        slots = [(k, None) for k in near] + far
        tops = [scores_of(q[...], slots, held) for q, held in zip((q_mine, q_other), rooms)]
        for half, (top, held) in enumerate(zip(tops, rooms)):
            rows = slice(half * tile, (half + 1) * tile)
            total, mixed = None, None
            for at, (_, valid) in enumerate(slots):
                level = top if valid is None else jnp.where(valid, top, 1e30)
                w = jnp.exp2((held[:, at * tile : (at + 1) * tile] - level) * factor)
                rounded = w.astype(jnp.bfloat16)
                if at < len(near):
                    value = values[at // 2][(at % 2) * tile : (at % 2 + 1) * tile]
                    mix = jnp.dot(rounded, value, preferred_element_type=jnp.float32)
                    mixed = mix if mixed is None else mixed + mix
                else:
                    begin = (at - len(near)) * tile
                    far_weights[rows, begin : begin + tile] = rounded
                for begin in range(0, tile, 128):
                    part = w[:, begin : begin + 128]
                    total = part if total is None else total + part
            mixed_out[rows] = mixed
            totals[rows] = jnp.broadcast_to(jnp.sum(total, axis=1, keepdims=True), (tile, totals.shape[1]))

    inner = (z == 1) | (z == 2)

    @pl.when(inner)
    def _():
        body([km, ko, n1km, n1ko, n2km, n2ko], [v, n1v, n2v], [(r1, near2)])

    @pl.when(jnp.logical_not(inner))
    def _():
        body([km, ko, n1km, n1ko], [v, n1v], [(r2, near2), (r3, mask[0, z ^ 3] == 1)])


def far_kernel(mixed, totals, far_weights, r1, r2, r3, *outs):
    rows, tile = outs[0].shape[0], r1.shape[0]

    def body(values):
        for d, out in enumerate(outs):
            span = slice(d * rows, (d + 1) * rows)
            total = mixed[span]
            for at, value in enumerate(values):
                w = far_weights[span, at * tile : (at + 1) * tile]
                total = total + jnp.dot(w, value[...], preferred_element_type=jnp.float32)
            out[...] = (total / totals[span]).astype(jnp.bfloat16)

    z = lax.axis_index("frame")
    inner = (z == 1) | (z == 2)

    @pl.when(inner)
    def _():
        body([r1])

    @pl.when(jnp.logical_not(inner))
    def _():
        body([r2, r3])


def by_head(x, rows, first=0):
    return x, pl.BlockSpec((rows, HEAD_DIM), lambda i: (0, first + i))


def by_rows(rows, lanes, first=0):
    return pl.BlockSpec((rows, lanes), lambda i: (first + i, 0))


def attend_near(mask, q, keys, values, heads):
    tile = q[0].shape[0]
    blocks = [by_head(x, tile) for x in [*q, *keys]] + [by_head(x, 2 * tile) for x in values]
    shapes = [(HEAD_DIM, jnp.float32), (HEAD_DIM, jnp.float32), (2 * tile, jnp.bfloat16)]
    return pl.pallas_call(
        attention_kernel,
        grid=(heads,),
        in_specs=[pl.BlockSpec(memory_space=pltpu.SMEM)] + [spec for _, spec in blocks],
        out_specs=[by_rows(2 * tile, lanes) for lanes, _ in shapes],
        out_shape=[jax.ShapeDtypeStruct((heads * 2 * tile, lanes), dtype) for lanes, dtype in shapes],
        scratch_shapes=[pltpu.VMEM((tile, 7 * tile), jnp.float32)] * 2,
        compiler_params=pltpu.CompilerParams(vmem_limit_bytes=16 * 1024 * 1024),
        cost_estimate=pl.CostEstimate(
            flops=heads * 56 * tile * tile * HEAD_DIM,
            bytes_accessed=heads * 20 * tile * tile,
            transcendentals=heads * 14 * tile * tile,
        ),
    )(mask, *[x for x, _ in blocks])


def add_far(mixed, totals, far_weights, r1, r2, r3, begin, end):
    tile = r1.shape[0]
    rows, heads = 2 * tile, end - begin
    blocks = [(x, by_rows(rows, x.shape[1], begin)) for x in (mixed, totals, far_weights)]
    blocks += [by_head(r1, tile, begin), by_head(r2, tile, begin), by_head(r3, tile)]
    return pl.pallas_call(
        far_kernel,
        grid=(heads,),
        in_specs=[spec for _, spec in blocks],
        out_specs=[pl.BlockSpec((rows // 4, HEAD_DIM), lambda i: (0, i))] * 4,
        out_shape=[jax.ShapeDtypeStruct((rows // 4, heads * HEAD_DIM), jnp.bfloat16)] * 4,
        compiler_params=pltpu.CompilerParams(vmem_limit_bytes=8 * 1024 * 1024),
        cost_estimate=pl.CostEstimate(
            flops=heads * 4 * rows * tile * HEAD_DIM, bytes_accessed=heads * 12 * rows * tile, transcendentals=0
        ),
    )(*[x for x, _ in blocks])


def pack_kernel(copies, width, mask, offset, *refs):
    ins, outs, sems = refs[:3], refs[3:-1], refs[-1]
    h = lax.axis_index("head")
    started = []
    for n, (operand, d, begin, result, at, lanes) in enumerate(copies):
        source = ins[operand].at[:, pl.ds(pl.multiple_of((h ^ d) * width + begin, HEAD_DIM), lanes)]
        copy = pltpu.make_async_copy(source, outs[result].at[:, at : at + lanes], sems.at[n])
        copy.start()
        started.append(copy)
    if len(outs) > 1 + max(copy[3] for copy in copies):
        told = outs[-1]
        for group in range(told.shape[1] // 128):
            value = mask[0, group] if group < 4 else offset[0]
            rows = jnp.full((told.shape[0], 128), value, jnp.int32).astype(jnp.float32)
            told[:, group * 128 : (group + 1) * 128] = rows.astype(told.dtype)
    for copy in started:
        copy.wait()


def packed(operands, mask, offset, results, width, told):
    rows = operands[0].shape[0]
    copies, shapes = [], []
    for n, parts in enumerate(results):
        at = 0
        for operand, d, begin, lanes in parts:
            copies.append((operand, d, begin, n, at, lanes))
            at += lanes
        shapes.append(jax.ShapeDtypeStruct((rows, at), jnp.bfloat16))
    if told:
        shapes.append(jax.ShapeDtypeStruct((INFO_ROWS, told), jnp.bfloat16))
    return pl.pallas_call(
        functools.partial(pack_kernel, copies, width),
        in_specs=[pl.BlockSpec(memory_space=pltpu.SMEM)] * 2 + [pl.BlockSpec(memory_space=pltpu.HBM)] * 3,
        out_specs=[pl.BlockSpec(memory_space=pltpu.VMEM)] * len(shapes),
        out_shape=shapes,
        scratch_shapes=[pltpu.SemaphoreType.DMA((len(copies),))],
        compiler_params=pltpu.CompilerParams(vmem_limit_bytes=4 * 1024 * 1024),
    )(mask, offset, *operands)


def relayed_kernel(told, *refs):
    out = refs[-1]
    tile = out.shape[0]
    group = told[told.shape[0] - INFO_ROWS :, 4 * 128 : 5 * 128]
    here = jnp.max(group.astype(jnp.float32)) == (lax.axis_index("head") // 2).astype(jnp.float32)
    whole = refs[0].shape[0] == 2 * tile

    @pl.when(here)
    def _():
        out[...] = refs[0][:tile] if whole else told[:tile]

    @pl.when(jnp.logical_not(here))
    def _():
        out[...] = refs[0][tile:] if whole else refs[0][...]


def relayed(told, array, tile):
    return pl.pallas_call(
        relayed_kernel,
        in_specs=[pl.BlockSpec(memory_space=pltpu.VMEM)] * 2,
        out_specs=pl.BlockSpec(memory_space=pltpu.VMEM),
        out_shape=jax.ShapeDtypeStruct((tile, array.shape[1]), array.dtype),
        compiler_params=pltpu.CompilerParams(vmem_limit_bytes=4 * 1024 * 1024),
    )(told, array)


def four_frames(queries, keys, values, pair_mask, tile_offset):
    h = lax.axis_index("head")
    rows, features = queries.shape
    width = features // 4
    heads = width // HEAD_DIM

    def columns(array, d):
        return lax.dynamic_slice_in_dim(array, (h ^ d) * width, width, axis=1)

    def beside(*arrays):
        return jnp.concatenate(arrays, axis=1)

    def below(*arrays):
        return jnp.concatenate(arrays, axis=0)

    def to_head(array, d):
        return lax.ppermute(array, "head", [(i, i ^ d) for i in range(4)])

    def along(array, pairs):
        return lax.ppermute(array, "frame", pairs)

    def across(array):
        pairs = [(4 * z + j, 4 * (3 - z) + j if z in (1, 2) else 4 * z + (j ^ 1)) for z in range(4) for j in range(4)]
        return lax.ppermute(array, ("frame", "head"), pairs)

    def after(array, earlier):
        return lax.optimization_barrier((array, earlier))[0]

    tile = 2 * rows
    kv = [[columns(array, d) for array in (keys, values)] for d in range(4)]
    kv = lax.optimization_barrier(kv)
    got = to_head(beside(*kv[1], *kv[3]), 1)
    got = [got[:, n * width : (n + 1) * width] for n in range(4)]
    ko = to_head(below(kv[2][0], got[2]), 2)
    pay, q_own, q_far, told = packed(
        (queries, keys, values),
        after(pair_mask, got[0]),
        tile_offset,
        [[(0, 1, 0, width), (0, 3, 0, width)], [(0, 0, 0, width)], [(0, 2, 0, width)]],
        width,
        width,
    )

    km = below(kv[0][0], got[0], told)
    n1km = along(km, OUTER)
    n2km = across(km)
    vo = to_head(after(below(kv[2][1], got[3]), (n1km, n2km)), 2)
    n1ko = along(ko, OUTER)
    n2ko = across(ko)
    v = below(kv[0][1], got[1], vo)
    n1v = along(v, OUTER)
    n2v = across(v)

    got = to_head(pay, 1)
    q_mine = below(q_own, got[:, :width])
    q_other = to_head(after(below(q_far, got[:, width:]), vo), 2)

    r1k = across(after(relayed(n1km, n1ko, tile), (n2km, n2ko)))
    r2k = along(relayed(n2km, n2ko, tile), OUTER)
    r3k = along(after(r1k, r2k), OUTER)
    r1v = across(relayed(n1km, n1v, tile))
    r2v = along(relayed(n2km, n2v, tile), OUTER)
    mixed, totals, far_weights = attend_near(
        pair_mask, [q_mine, q_other], [km, ko, n1km, n1ko, n2km, n2ko, r1k, r2k, r3k], [v, n1v, n2v], heads
    )
    result = jnp.zeros((rows, features), jnp.bfloat16)
    cut = (heads + 1) // 2
    for begin, end in ((0, cut), (cut, heads)):
        r3v = r1v[:, begin * HEAD_DIM : end * HEAD_DIM]
        r3v = along(r3v if begin == 0 else after(r3v, totals), OUTER)
        r3v = r3v if begin == 0 else after(r3v, out[1])
        out = add_far(mixed, totals, far_weights, r1v, r2v, r3v, begin, end)
        out = [out[0]] + [to_head(out[d], d) for d in (1, 2, 3)]
        for d in range(4):
            result = lax.dynamic_update_slice_in_dim(result, out[d], (h ^ d) * width + begin * HEAD_DIM, axis=1)
    return result


def solution(mesh):
    sizes = dict(mesh.shape)
    per_device = four_frames if sizes["frame"] == 4 and sizes["head"] == 4 else general
    return jax.shard_map(
        per_device,
        mesh=mesh,
        in_specs=(
            P(("parts", "frame", "head"), None),
            P(("parts", "frame", "head"), None),
            P(("parts", "frame", "head"), None),
            P(("parts", "frame"), None),
            P(("parts", "frame")),
        ),
        out_specs=P(("parts", "frame", "head"), None),
        check_vma=False,
    )
```

```python
import functools
import math

import jax
import jax.numpy as jnp
from jax import lax
from jax.experimental import pallas as pl
from jax.experimental.pallas import tpu as pltpu
from jax.sharding import PartitionSpec as P

HEAD_DIM = 128
SCALE = 1.0 / HEAD_DIM**0.5
LOG2E = math.log2(math.e)


def padded(x, sides, width):
    for axis, dim in sides:
        peers, length = (lax.axis_size(axis), x.shape[dim])
        up = [(i, (i + 1) % peers) for i in range(peers - 1)]
        down = [(j, i) for i, j in up]
        last = lax.slice_in_dim(x, length - width, length, axis=dim)
        leading = lax.slice_in_dim(x, 0, width, axis=dim)
        before = lax.ppermute(last, axis, up)
        after = lax.ppermute(leading, axis, down)
        x = jnp.concatenate([before, x, after], axis=dim)
    return x


def from_partner(x, axis, bit):
    return lax.ppermute(x, axis, [(i, i ^ 1 << bit) for i in range(lax.axis_size(axis))])


def subsample(frame_rows, offset, level, tiles, tile):
    step = 2**level
    width = frame_rows.shape[-1]
    grouped = frame_rows.reshape(tiles // step, step, tile, width)
    picked = lax.dynamic_index_in_dim(grouped, offset % step, 1, keepdims=False)
    return picked.reshape(-1, width)


def attend(query_rows, key_rows, value_rows, valid):
    count = query_rows.shape[0]
    heads = query_rows.shape[1] // HEAD_DIM
    q_three = query_rows.reshape(count, heads, HEAD_DIM).transpose(1, 0, 2)
    k_three = key_rows.reshape(-1, heads, HEAD_DIM).transpose(1, 0, 2)
    v_three = value_rows.reshape(-1, heads, HEAD_DIM).transpose(1, 0, 2)

    def one_head(operands):
        q_head, k_head, v_head = operands
        scores = jnp.dot(q_head, k_head.T, preferred_element_type=jnp.float32) * SCALE
        scores = jnp.where(valid[None, :] > 0, scores, -1e30)
        top = jnp.max(scores, axis=1, keepdims=True)
        weights = jnp.exp(scores - top) * valid[None, :]
        total = jnp.sum(weights, axis=1, keepdims=True)
        mixed = jnp.dot(weights.astype(jnp.bfloat16), v_head, preferred_element_type=jnp.float32)
        return mixed / total

    outcome = lax.map(one_head, (q_three, k_three, v_three))
    return outcome.transpose(1, 0, 2).reshape(count, heads * HEAD_DIM).astype(jnp.bfloat16)


def ordered(mine, theirs, upper):
    return jnp.where(upper == 1, jnp.concatenate([theirs, mine]), jnp.concatenate([mine, theirs]))


def general(queries, keys, values, pair_mask, tile_offset):
    frames_n = lax.axis_size("frame")
    current = lax.axis_index("frame")
    q_rows, k_rows, v_rows = (
        lax.all_to_all(queries, "head", split_axis=1, concat_axis=0, tiled=True),
        lax.all_to_all(keys, "head", split_axis=1, concat_axis=0, tiled=True),
        lax.all_to_all(values, "head", split_axis=1, concat_axis=0, tiled=True),
    )
    count = q_rows.shape[0]
    width = q_rows.shape[1]
    tiles = frames_n // 2
    tile = count // tiles
    depth = frames_n.bit_length() - 1
    stacked = jnp.stack([k_rows, v_rows])
    near = padded(stacked, (("frame", 1),), count)
    near_index = current - 1 + jnp.arange(3, dtype=jnp.int32)
    near_good = ((near_index >= 0) & (near_index < frames_n)).astype(jnp.float32)
    key_parts = [near[0]]
    value_parts = [near[1]]
    valid_parts = [jnp.repeat(near_good, count)]
    mask_row = pair_mask[0]
    offset = tile_offset[0]
    k_tiles = k_rows.reshape(tiles, tile, width)
    v_tiles = v_rows.reshape(tiles, tile, width)
    own = {}
    for level in range(1, depth):
        own[level] = (
            subsample(k_tiles, offset, level, tiles, tile)[None],
            subsample(v_tiles, offset, level, tiles, tile)[None],
        )
    sibling = {}
    cut = max(1, depth - 2)
    upper_levels = [level for level in range(1, depth) if level >= cut]
    k_pack = jnp.concatenate([own[level][0].reshape(-1, width) for level in upper_levels])
    v_pack = jnp.concatenate([own[level][1].reshape(-1, width) for level in upper_levels])
    k_every, v_every = (
        lax.all_gather(k_pack, "frame", axis=0, tiled=True),
        lax.all_gather(v_pack, "frame", axis=0, tiled=True),
    )
    k_every = k_every.reshape(frames_n, -1, width)
    v_every = v_every.reshape(frames_n, -1, width)
    position = 0
    for level in upper_levels:
        step = 2**level
        rows = count // step
        start = jnp.bitwise_xor(current // step, 1) * step
        block_k = lax.dynamic_slice_in_dim(k_every[:, position : position + rows], start, step, 0)
        block_v = lax.dynamic_slice_in_dim(v_every[:, position : position + rows], start, step, 0)
        sibling[level] = (block_k, block_v)
        position = position + rows
    swap_levels = [level for level in range(1, depth) if level < cut]
    growing = {level: own[level] for level in swap_levels}
    sections = cut if swap_levels else 0
    for bit in range(sections):
        active = [level for level in swap_levels if level >= bit]
        k_pack = jnp.concatenate([growing[level][0].reshape(-1, width) for level in active])
        v_pack = jnp.concatenate([growing[level][1].reshape(-1, width) for level in active])
        k_in, v_in = (from_partner(k_pack, "frame", bit), from_partner(v_pack, "frame", bit))
        upper = current // 2**bit % 2
        position = 0
        for level in active:
            shape = growing[level][0].shape
            size = shape[0] * shape[1]
            theirs_k = k_in[position : position + size].reshape(shape)
            theirs_v = v_in[position : position + size].reshape(shape)
            position = position + size
            if level == bit:
                sibling[level] = (theirs_k, theirs_v)
            else:
                growing[level] = (
                    ordered(growing[level][0], theirs_k, upper),
                    ordered(growing[level][1], theirs_v, upper),
                )
    for level in range(1, depth):
        step = 2**level
        start = jnp.bitwise_xor(current // step, 1) * step
        frame_ids = start + jnp.arange(step, dtype=jnp.int32)
        allowed = lax.dynamic_slice_in_dim(mask_row, start, step, 0)
        good = ((jnp.abs(frame_ids - current) >= 2) & (allowed == 1)).astype(jnp.float32)
        block_k, block_v = sibling[level]
        key_parts.append(block_k.reshape(-1, width))
        value_parts.append(block_v.reshape(-1, width))
        valid_parts.append(jnp.repeat(good, block_k.shape[1]))
    result = attend(
        q_rows,
        jnp.concatenate(key_parts),
        jnp.concatenate(value_parts),
        jnp.concatenate(valid_parts),
    )
    return lax.all_to_all(result, "head", split_axis=0, concat_axis=1, tiled=True)


INFO_ROWS = 16
OUTER = [(0, 1), (1, 0), (2, 3), (3, 2)]


def fold(x):
    parts = [x[:, at : at + 128] for at in range(0, x.shape[1], 128)]
    best = parts[0]
    for part in parts[1:]:
        best = jnp.maximum(best, part)
    return best


def scores_of(q, slots, held):
    free, top = None, None
    for at, (k, valid) in enumerate(slots):
        s = lax.dot_general(q, k[...], (((1,), (1,)), ((), ())), preferred_element_type=jnp.float32)
        held[:, at * s.shape[1] : (at + 1) * s.shape[1]] = s
        best = fold(s)
        if valid is None:
            free = best if free is None else jnp.maximum(free, best)
        else:
            best = jnp.where(valid, jnp.max(best, axis=1, keepdims=True), -1e30)
            top = best if top is None else jnp.maximum(top, best)
    free = jnp.max(free, axis=1, keepdims=True)
    return free if top is None else jnp.maximum(free, top)


def attention_kernel(mask, q_mine, q_other, *rest):
    keys, (r1, r2, r3), values = rest[:6], rest[6:9], rest[9:15]
    mixed_out, totals, far_weights, held0, held1 = rest[15:]
    factor = SCALE * LOG2E
    z = lax.axis_index("frame")
    tile = r1.shape[0]
    near2 = mask[0, z ^ 2] == 1

    def body(near, values, far):
        rooms = (held0, held1)
        slots = [(k, None) for k in near] + far
        tops = [scores_of(q[...], slots, held) for q, held in zip((q_mine, q_other), rooms)]
        for half, (top, held) in enumerate(zip(tops, rooms)):
            rows = slice(half * tile, (half + 1) * tile)
            total, mixed = None, None
            for at, (_, valid) in enumerate(slots):
                level = top if valid is None else jnp.where(valid, top, 1e30)
                w = jnp.exp2((held[:, at * tile : (at + 1) * tile] - level) * factor)
                rounded = w.astype(jnp.bfloat16)
                if at < len(near):
                    mix = jnp.dot(rounded, values[at][...], preferred_element_type=jnp.float32)
                    mixed = mix if mixed is None else mixed + mix
                else:
                    begin = (at - len(near)) * tile
                    far_weights[rows, begin : begin + tile] = rounded
                for begin in range(0, tile, 128):
                    part = w[:, begin : begin + 128]
                    total = part if total is None else total + part
            mixed_out[rows] = mixed
            totals[rows] = jnp.broadcast_to(jnp.sum(total, axis=1, keepdims=True), (tile, totals.shape[1]))

    inner = (z == 1) | (z == 2)

    @pl.when(inner)
    def _():
        body(keys, values, [(r1, near2)])

    @pl.when(jnp.logical_not(inner))
    def _():
        body(keys[:4], values[:4], [(r2, near2), (r3, mask[0, z ^ 3] == 1)])


def far_kernel(mixed, totals, far_weights, r1, r2, r3, *outs):
    rows, tile = outs[0].shape[0], r1.shape[0]

    def body(values):
        for d, out in enumerate(outs):
            span = slice(d * rows, (d + 1) * rows)
            total = mixed[span]
            for at, value in enumerate(values):
                w = far_weights[span, at * tile : (at + 1) * tile]
                total = total + jnp.dot(w, value[...], preferred_element_type=jnp.float32)
            out[...] = (total / totals[span]).astype(jnp.bfloat16)

    z = lax.axis_index("frame")
    inner = (z == 1) | (z == 2)

    @pl.when(inner)
    def _():
        body([r1])

    @pl.when(jnp.logical_not(inner))
    def _():
        body([r2, r3])


def by_head(x, rows, first=0):
    return x, pl.BlockSpec((rows, HEAD_DIM), lambda i: (0, first + i))


def by_rows(rows, lanes, first=0):
    return pl.BlockSpec((rows, lanes), lambda i: (first + i, 0))


def attend_near(mask, q, near, far, begin, end, heads):
    tile = q[0].shape[0]
    count = end - begin
    blocks = [by_head(x, tile, begin) for x in [*q, *near, *far]] + [by_head(x, tile, heads + begin) for x in near]
    shapes = [(HEAD_DIM, jnp.float32), (HEAD_DIM, jnp.float32), (2 * tile, jnp.bfloat16)]
    return pl.pallas_call(
        attention_kernel,
        grid=(count,),
        in_specs=[pl.BlockSpec(memory_space=pltpu.SMEM)] + [spec for _, spec in blocks],
        out_specs=[by_rows(2 * tile, lanes) for lanes, _ in shapes],
        out_shape=[jax.ShapeDtypeStruct((count * 2 * tile, lanes), dtype) for lanes, dtype in shapes],
        scratch_shapes=[pltpu.VMEM((tile, 7 * tile), jnp.float32)] * 2,
        compiler_params=pltpu.CompilerParams(vmem_limit_bytes=16 * 1024 * 1024),
        cost_estimate=pl.CostEstimate(
            flops=count * 56 * tile * tile * HEAD_DIM,
            bytes_accessed=count * 20 * tile * tile,
            transcendentals=count * 14 * tile * tile,
        ),
    )(mask, *[x for x, _ in blocks])


def add_far(mixed, totals, far_weights, r1, r2, r3, begin, end):
    tile = r1.shape[0]
    rows, heads = 2 * tile, end - begin
    blocks = [(x, by_rows(rows, x.shape[1])) for x in (mixed, totals, far_weights)]
    blocks += [by_head(r1, tile, begin), by_head(r2, tile), by_head(r3, tile)]
    return pl.pallas_call(
        far_kernel,
        grid=(heads,),
        in_specs=[spec for _, spec in blocks],
        out_specs=[pl.BlockSpec((rows // 4, HEAD_DIM), lambda i: (0, i))] * 4,
        out_shape=[jax.ShapeDtypeStruct((rows // 4, heads * HEAD_DIM), jnp.bfloat16)] * 4,
        compiler_params=pltpu.CompilerParams(vmem_limit_bytes=8 * 1024 * 1024),
        cost_estimate=pl.CostEstimate(
            flops=heads * 4 * rows * tile * HEAD_DIM, bytes_accessed=heads * 12 * rows * tile, transcendentals=0
        ),
    )(*[x for x, _ in blocks])


def pack_kernel(copies, width, mask, offset, *refs):
    ins, outs, sems = refs[:3], refs[3:-1], refs[-1]
    h = lax.axis_index("head")
    started = []
    for n, (operand, d, begin, result, at, lanes) in enumerate(copies):
        source = ins[operand].at[:, pl.ds(pl.multiple_of((h ^ d) * width + begin, HEAD_DIM), lanes)]
        copy = pltpu.make_async_copy(source, outs[result].at[:, at : at + lanes], sems.at[n])
        copy.start()
        started.append(copy)
    if len(outs) > 1 + max(copy[3] for copy in copies):
        told = outs[-1]
        for group in range(told.shape[1] // 128):
            value = mask[0, group] if group < 4 else offset[0]
            rows = jnp.full((told.shape[0], 128), value, jnp.int32).astype(jnp.float32)
            told[:, group * 128 : (group + 1) * 128] = rows.astype(told.dtype)
    for copy in started:
        copy.wait()


def packed(operands, mask, offset, results, width, told):
    rows = operands[0].shape[0]
    copies, shapes = [], []
    for n, parts in enumerate(results):
        at = 0
        for operand, d, begin, lanes in parts:
            copies.append((operand, d, begin, n, at, lanes))
            at += lanes
        shapes.append(jax.ShapeDtypeStruct((rows, at), jnp.bfloat16))
    if told:
        shapes.append(jax.ShapeDtypeStruct((INFO_ROWS, told), jnp.bfloat16))
    return pl.pallas_call(
        functools.partial(pack_kernel, copies, width),
        in_specs=[pl.BlockSpec(memory_space=pltpu.SMEM)] * 2 + [pl.BlockSpec(memory_space=pltpu.HBM)] * 3,
        out_specs=[pl.BlockSpec(memory_space=pltpu.VMEM)] * len(shapes),
        out_shape=shapes,
        scratch_shapes=[pltpu.SemaphoreType.DMA((len(copies),))],
        compiler_params=pltpu.CompilerParams(vmem_limit_bytes=4 * 1024 * 1024),
    )(mask, offset, *operands)


def relayed_kernel(mine, other, k_out, v_out):
    tile, width = k_out.shape
    offset = jnp.max(mine[tile : tile + INFO_ROWS, 4 * 128 : 5 * 128].astype(jnp.float32))
    here = offset == (lax.axis_index("head") // 2).astype(jnp.float32)

    def take(ref):
        k_out[...] = ref[:tile, :width]
        v_out[...] = ref[:tile, width:]

    @pl.when(here)
    def _():
        take(mine)

    @pl.when(jnp.logical_not(here))
    def _():
        take(other)


def relayed(mine, other):
    tile, lanes = other.shape
    return pl.pallas_call(
        relayed_kernel,
        in_specs=[pl.BlockSpec(memory_space=pltpu.VMEM)] * 2,
        out_specs=[pl.BlockSpec(memory_space=pltpu.VMEM)] * 2,
        out_shape=[jax.ShapeDtypeStruct((tile, lanes // 2), other.dtype)] * 2,
        compiler_params=pltpu.CompilerParams(vmem_limit_bytes=4 * 1024 * 1024),
    )(mine, other)


def four_frames(queries, keys, values, pair_mask, tile_offset):
    h = lax.axis_index("head")
    rows, features = queries.shape
    width = features // 4
    heads = width // HEAD_DIM

    def columns(array, d):
        return lax.dynamic_slice_in_dim(array, (h ^ d) * width, width, axis=1)

    def beside(*arrays):
        return jnp.concatenate(arrays, axis=1)

    def below(*arrays):
        return jnp.concatenate(arrays, axis=0)

    def to_head(array, d):
        return lax.ppermute(array, "head", [(i, i ^ d) for i in range(4)])

    def along(array, pairs):
        return lax.ppermute(array, "frame", pairs)

    def across(array):
        pairs = [(4 * z + j, 4 * (3 - z) + j if z in (1, 2) else 4 * z + (j ^ 1)) for z in range(4) for j in range(4)]
        return lax.ppermute(array, ("frame", "head"), pairs)

    def after(array, earlier):
        return lax.optimization_barrier((array, earlier))[0]

    kv = [[columns(array, d) for array in (keys, values)] for d in range(4)]
    kv = lax.optimization_barrier(kv)
    got = to_head(beside(*kv[1], *kv[3]), 1)
    pay, q_own, q_far, told = packed(
        (queries, keys, values),
        pair_mask,
        tile_offset,
        [[(0, 1, 0, width), (0, 3, 0, width)], [(0, 0, 0, width)], [(0, 2, 0, width)]],
        width,
        2 * width,
    )
    mine = below(beside(*kv[0]), got[:, : 2 * width], told)
    other = to_head(below(beside(*kv[2]), got[:, 2 * width :]), 2)
    n1m = along(mine, OUTER)
    n2m = across(mine)
    n1o = along(other, OUTER)
    n2o = across(other)

    got = to_head(after(pay, got), 1)
    q_mine = below(q_own, got[:, :width])
    q_other = to_head(after(below(q_far, got[:, width:]), other), 2)

    cut = (heads + 1) // 2
    first, second = slice(0, cut * HEAD_DIM), slice(cut * HEAD_DIM, width)
    r1k, r1v = after(relayed(n1m, n1o), n2m)
    r1k = across(r1k)
    r2k, r2v = relayed(n2m, n2o)
    r1v = across(after(r1v, r2v))
    r2k = along(r2k, OUTER)
    r3k = along(after(r1k, (r2k, q_other)), OUTER)
    first_r2v = along(after(r2v[:, first], r3k), OUTER)
    first_r3v = along(after(r1v[:, first], r3k), OUTER)
    far = [r1k, r2k, r3k]
    near = [mine, other, n1m, n1o, n2m, n2o]
    q = [q_mine, q_other]
    first_parts = attend_near(pair_mask, q, near, far, 0, cut, heads)
    both = along(after(below(r2v[:, second], r1v[:, second]), first_parts[1]), OUTER)
    second_parts = attend_near(pair_mask, q, near, far, cut, heads, heads)
    out = add_far(*first_parts, r1v, first_r2v, first_r3v, 0, cut)
    pieces = [(to_head(out[d], d) if d else out[0], d, 0) for d in range(4)]
    both = after(both, out[1])
    out = add_far(*second_parts, r1v, both[: 2 * rows], both[2 * rows :], cut, heads)
    pieces += [(to_head(out[d], d) if d else out[0], d, cut) for d in range(4)]
    result = jnp.zeros((rows, features), jnp.bfloat16)
    for piece, d, begin in pieces:
        result = lax.dynamic_update_slice_in_dim(result, piece, (h ^ d) * width + begin * HEAD_DIM, axis=1)
    return result


def solution(mesh):
    sizes = dict(mesh.shape)
    per_device = four_frames if sizes["frame"] == 4 and sizes["head"] == 4 else general
    return jax.shard_map(
        per_device,
        mesh=mesh,
        in_specs=(
            P(("parts", "frame", "head"), None),
            P(("parts", "frame", "head"), None),
            P(("parts", "frame", "head"), None),
            P(("parts", "frame"), None),
            P(("parts", "frame")),
        ),
        out_specs=P(("parts", "frame", "head"), None),
        check_vma=False,
    )
```

```python
import functools
import math

import jax
import jax.numpy as jnp
from jax import lax
from jax.experimental import pallas as pl
from jax.experimental.pallas import tpu as pltpu
from jax.sharding import PartitionSpec as P

HEAD_DIM = 128
SCALE = 1.0 / HEAD_DIM**0.5
LOG2E = math.log2(math.e)


def padded(x, sides, width):
    for axis, dim in sides:
        peers, length = (lax.axis_size(axis), x.shape[dim])
        up = [(i, (i + 1) % peers) for i in range(peers - 1)]
        down = [(j, i) for i, j in up]
        last = lax.slice_in_dim(x, length - width, length, axis=dim)
        leading = lax.slice_in_dim(x, 0, width, axis=dim)
        before = lax.ppermute(last, axis, up)
        after = lax.ppermute(leading, axis, down)
        x = jnp.concatenate([before, x, after], axis=dim)
    return x


def from_partner(x, axis, bit):
    return lax.ppermute(x, axis, [(i, i ^ 1 << bit) for i in range(lax.axis_size(axis))])


def subsample(frame_rows, offset, level, tiles, tile):
    step = 2**level
    width = frame_rows.shape[-1]
    grouped = frame_rows.reshape(tiles // step, step, tile, width)
    picked = lax.dynamic_index_in_dim(grouped, offset % step, 1, keepdims=False)
    return picked.reshape(-1, width)


def attend(query_rows, key_rows, value_rows, valid):
    count = query_rows.shape[0]
    heads = query_rows.shape[1] // HEAD_DIM
    q_three = query_rows.reshape(count, heads, HEAD_DIM).transpose(1, 0, 2)
    k_three = key_rows.reshape(-1, heads, HEAD_DIM).transpose(1, 0, 2)
    v_three = value_rows.reshape(-1, heads, HEAD_DIM).transpose(1, 0, 2)

    def one_head(operands):
        q_head, k_head, v_head = operands
        scores = jnp.dot(q_head, k_head.T, preferred_element_type=jnp.float32) * SCALE
        scores = jnp.where(valid[None, :] > 0, scores, -1e30)
        top = jnp.max(scores, axis=1, keepdims=True)
        weights = jnp.exp(scores - top) * valid[None, :]
        total = jnp.sum(weights, axis=1, keepdims=True)
        mixed = jnp.dot(weights.astype(jnp.bfloat16), v_head, preferred_element_type=jnp.float32)
        return mixed / total

    outcome = lax.map(one_head, (q_three, k_three, v_three))
    return outcome.transpose(1, 0, 2).reshape(count, heads * HEAD_DIM).astype(jnp.bfloat16)


def ordered(mine, theirs, upper):
    return jnp.where(upper == 1, jnp.concatenate([theirs, mine]), jnp.concatenate([mine, theirs]))


def general(queries, keys, values, pair_mask, tile_offset):
    frames_n = lax.axis_size("frame")
    current = lax.axis_index("frame")
    q_rows, k_rows, v_rows = (
        lax.all_to_all(queries, "head", split_axis=1, concat_axis=0, tiled=True),
        lax.all_to_all(keys, "head", split_axis=1, concat_axis=0, tiled=True),
        lax.all_to_all(values, "head", split_axis=1, concat_axis=0, tiled=True),
    )
    count = q_rows.shape[0]
    width = q_rows.shape[1]
    tiles = frames_n // 2
    tile = count // tiles
    depth = frames_n.bit_length() - 1
    stacked = jnp.stack([k_rows, v_rows])
    near = padded(stacked, (("frame", 1),), count)
    near_index = current - 1 + jnp.arange(3, dtype=jnp.int32)
    near_good = ((near_index >= 0) & (near_index < frames_n)).astype(jnp.float32)
    key_parts = [near[0]]
    value_parts = [near[1]]
    valid_parts = [jnp.repeat(near_good, count)]
    mask_row = pair_mask[0]
    offset = tile_offset[0]
    k_tiles = k_rows.reshape(tiles, tile, width)
    v_tiles = v_rows.reshape(tiles, tile, width)
    own = {}
    for level in range(1, depth):
        own[level] = (
            subsample(k_tiles, offset, level, tiles, tile)[None],
            subsample(v_tiles, offset, level, tiles, tile)[None],
        )
    sibling = {}
    cut = max(1, depth - 2)
    upper_levels = [level for level in range(1, depth) if level >= cut]
    k_pack = jnp.concatenate([own[level][0].reshape(-1, width) for level in upper_levels])
    v_pack = jnp.concatenate([own[level][1].reshape(-1, width) for level in upper_levels])
    k_every, v_every = (
        lax.all_gather(k_pack, "frame", axis=0, tiled=True),
        lax.all_gather(v_pack, "frame", axis=0, tiled=True),
    )
    k_every = k_every.reshape(frames_n, -1, width)
    v_every = v_every.reshape(frames_n, -1, width)
    position = 0
    for level in upper_levels:
        step = 2**level
        rows = count // step
        start = jnp.bitwise_xor(current // step, 1) * step
        block_k = lax.dynamic_slice_in_dim(k_every[:, position : position + rows], start, step, 0)
        block_v = lax.dynamic_slice_in_dim(v_every[:, position : position + rows], start, step, 0)
        sibling[level] = (block_k, block_v)
        position = position + rows
    swap_levels = [level for level in range(1, depth) if level < cut]
    growing = {level: own[level] for level in swap_levels}
    sections = cut if swap_levels else 0
    for bit in range(sections):
        active = [level for level in swap_levels if level >= bit]
        k_pack = jnp.concatenate([growing[level][0].reshape(-1, width) for level in active])
        v_pack = jnp.concatenate([growing[level][1].reshape(-1, width) for level in active])
        k_in, v_in = (from_partner(k_pack, "frame", bit), from_partner(v_pack, "frame", bit))
        upper = current // 2**bit % 2
        position = 0
        for level in active:
            shape = growing[level][0].shape
            size = shape[0] * shape[1]
            theirs_k = k_in[position : position + size].reshape(shape)
            theirs_v = v_in[position : position + size].reshape(shape)
            position = position + size
            if level == bit:
                sibling[level] = (theirs_k, theirs_v)
            else:
                growing[level] = (
                    ordered(growing[level][0], theirs_k, upper),
                    ordered(growing[level][1], theirs_v, upper),
                )
    for level in range(1, depth):
        step = 2**level
        start = jnp.bitwise_xor(current // step, 1) * step
        frame_ids = start + jnp.arange(step, dtype=jnp.int32)
        allowed = lax.dynamic_slice_in_dim(mask_row, start, step, 0)
        good = ((jnp.abs(frame_ids - current) >= 2) & (allowed == 1)).astype(jnp.float32)
        block_k, block_v = sibling[level]
        key_parts.append(block_k.reshape(-1, width))
        value_parts.append(block_v.reshape(-1, width))
        valid_parts.append(jnp.repeat(good, block_k.shape[1]))
    result = attend(
        q_rows,
        jnp.concatenate(key_parts),
        jnp.concatenate(value_parts),
        jnp.concatenate(valid_parts),
    )
    return lax.all_to_all(result, "head", split_axis=0, concat_axis=1, tiled=True)


HOME = 3
INFO_ROWS = 16
OUTER = [(0, 1), (1, 0), (2, 3), (3, 2)]
FACTOR = SCALE * LOG2E


def inner_frame():
    z = lax.axis_index("frame")
    return (z == 1) | (z == 2)


def head_lanes(first, i):
    return pl.ds(pl.multiple_of((first + i) * HEAD_DIM, HEAD_DIM), HEAD_DIM)


def keys_of(ref, first, i, rows):
    return ref[:rows, head_lanes(first, i)]


def values_of(ref, first, i, rows):
    return ref[:rows, head_lanes(ref.shape[1] // (2 * HEAD_DIM) + first, i)]


def dot_keys(q, k):
    return lax.dot_general(q, k, (((1,), (1,)), ((), ())), preferred_element_type=jnp.float32)


def fold(x, op):
    result = x[:, :128]
    for at in range(128, x.shape[1], 128):
        result = op(result, x[:, at : at + 128])
    return result


def near_kernel(first, skip, counts, q_mine, q_other, *refs):
    tiles, (mixed_out, tops, totals, done), rooms = refs[:-6], refs[-6:-2], refs[-2:]
    done[...] = jnp.zeros_like(done)
    rows = q_mine.shape[0]

    def one_head(used, i):
        found = []
        for q, held in zip((q_mine, q_other), rooms):
            best = None
            for at, ref in enumerate(used):
                s = dot_keys(q[:, head_lanes(skip, i)], keys_of(ref, first, i, rows))
                held[:, at * rows : (at + 1) * rows] = s
                part = fold(s, jnp.maximum)
                best = part if best is None else jnp.maximum(best, part)
            found.append(jnp.max(best, axis=1, keepdims=True))
        for half, (top, held) in enumerate(zip(found, rooms)):
            total, mixed = None, None
            for at, ref in enumerate(used):
                w = jnp.exp2((held[:, at * rows : (at + 1) * rows] - top) * FACTOR)
                mix = jnp.dot(w.astype(jnp.bfloat16), values_of(ref, first, i, rows), preferred_element_type=jnp.float32)
                part = fold(w, jnp.add)
                mixed = mix if mixed is None else mixed + mix
                total = part if total is None else total + part
            span = pl.ds(pl.multiple_of((2 * i + half) * rows, rows), rows)
            mixed_out[span] = mixed
            tops[span] = jnp.broadcast_to(top, (rows, HEAD_DIM))
            totals[span] = jnp.broadcast_to(jnp.sum(total, axis=1, keepdims=True), (rows, HEAD_DIM))

    for wanted, (n_tiles, n_heads) in zip((True, False), counts):
        if n_heads:

            @pl.when(inner_frame() == wanted)
            def _():
                def step(i, carry):
                    one_head(tiles[:n_tiles], i)
                    return carry

                lax.fori_loop(0, n_heads, step, 0)


def add_far(q, state, slots, i, row, held):
    rows = q.shape[0]
    span = pl.ds(pl.multiple_of(row, rows), rows)
    near_top = state[1][span][:, :1]
    top = near_top
    for at, (ref, first, valid) in enumerate(slots):
        s = dot_keys(q, keys_of(ref, first, i, rows))
        held[:, at * rows : (at + 1) * rows] = s
        best = jnp.max(fold(s, jnp.maximum), axis=1, keepdims=True)
        top = jnp.maximum(top, best if valid is None else jnp.where(valid, best, -1e30))
    shrink = jnp.exp2((near_top - top) * FACTOR)
    mixed = state[0][span] * shrink
    total = None
    for at, (ref, first, valid) in enumerate(slots):
        level = top if valid is None else jnp.where(valid, top, 1e30)
        w = jnp.exp2((held[:, at * rows : (at + 1) * rows] - level) * FACTOR)
        mixed += jnp.dot(w.astype(jnp.bfloat16), values_of(ref, first, i, rows), preferred_element_type=jnp.float32)
        part = fold(w, jnp.add)
        total = part if total is None else total + part
    total = jnp.sum(total, axis=1, keepdims=True) + state[2][span][:, :1] * shrink
    return (mixed * (1.0 / total)).astype(jnp.bfloat16)


def write_pieces(outs, half, lanes, value):
    rows = outs[0].shape[0]
    outs[2 * half][:, lanes] = value[:rows]
    outs[2 * half + 1][:, lanes] = value[rows:]


def home_kernel(mask, q_mine, q_other, mixed, tops, totals, r1, r2, r3, *rest):
    outs, rooms = rest[:4], rest[4:]
    z = lax.axis_index("frame")
    near2 = mask[0, z ^ 2] == 1
    rows = q_mine.shape[0]

    def body(slots):
        def step(i, carry):
            for half, (q, held) in enumerate(zip((q_mine, q_other), rooms)):
                value = add_far(q[:, head_lanes(0, i)], (mixed, tops, totals), slots, i, (2 * i + half) * rows, held)
                write_pieces(outs, half, head_lanes(0, i), value)
            return carry

        lax.fori_loop(0, outs[0].shape[1] // HEAD_DIM, step, 0)

    @pl.when(inner_frame())
    def _():
        body([(r1, 0, near2)])

    @pl.when(jnp.logical_not(inner_frame()))
    def _():
        body([(r2, 0, near2), (r3, 0, mask[0, z ^ 3] == 1)])


def guest_kernel(first, q, mixed, tops, totals, n1m, n2m, n2o, r1, out, *rooms):
    rows = r1.shape[0]
    z = lax.axis_index("frame")

    def told(ref, group):
        return ref[rows : rows + 1, group * 128 : (group + 1) * 128][:, :1].astype(jnp.float32)

    @pl.when(inner_frame())
    def _():
        near2 = jnp.where(z == 1, told(n1m, 2), told(n1m, 1)) > 0.5
        near1 = jnp.where(z == 1, told(n1m, 3), told(n1m, 0)) > 0.5
        picked = told(n2m, 4) == (lax.axis_index("head") // 2).astype(jnp.float32)
        slots = [(n2m, first, near2 & picked), (n2o, first, near2 & jnp.logical_not(picked)), (r1, 0, near1)]

        def step(i, carry):
            for half, held in enumerate(rooms):
                span = slice(half * rows, (half + 1) * rows)
                value = add_far(q[span, head_lanes(0, i)], (mixed, tops, totals), slots, i, (2 * i + half) * rows, held)
                out[span, head_lanes(0, i)] = value
            return carry

        lax.fori_loop(0, out.shape[1] // HEAD_DIM, step, 0)


def rest_kernel(first, mask, q_mine, q_other, mixed, tops, totals, r1, back, *rest):
    outs, rooms = rest[:4], rest[4:]
    z = lax.axis_index("frame")
    rows = q_mine.shape[0]

    @pl.when(inner_frame())
    def _():
        def step(i, carry):
            for half, (q, held) in enumerate(zip((q_mine, q_other), rooms)):
                slots = [(r1, 0, mask[0, z ^ 2] == 1)]
                row = (2 * i + half) * rows
                value = add_far(q[:, head_lanes(first, i)], (mixed, tops, totals), slots, i, row, held)
                write_pieces(outs, half, head_lanes(0, i), value)
            return carry

        lax.fori_loop(0, outs[0].shape[1] // HEAD_DIM, step, 0)

    @pl.when(jnp.logical_not(inner_frame()))
    def _():
        for d, out in enumerate(outs):
            out[...] = back[d * out.shape[0] : (d + 1) * out.shape[0]]


def pass_kernel(done, x, out):
    out[...] = x[...]


def passed(x, done):
    return pl.pallas_call(
        pass_kernel,
        in_specs=[pl.BlockSpec(memory_space=pltpu.VMEM)] * 2,
        out_specs=pl.BlockSpec(memory_space=pltpu.VMEM),
        out_shape=jax.ShapeDtypeStruct(x.shape, x.dtype),
        compiler_params=pltpu.CompilerParams(vmem_limit_bytes=4 * 1024 * 1024),
    )(done, x)


def run_kernel(kernel, mask, arrays, outs, rooms, flops):
    scalars = [] if mask is None else [mask]
    return pl.pallas_call(
        kernel,
        in_specs=[pl.BlockSpec(memory_space=pltpu.SMEM)] * len(scalars)
        + [pl.BlockSpec(memory_space=pltpu.VMEM)] * len(arrays),
        out_specs=[pl.BlockSpec(memory_space=pltpu.VMEM)] * len(outs),
        out_shape=[jax.ShapeDtypeStruct(shape, dtype) for shape, dtype in outs],
        scratch_shapes=[pltpu.VMEM(rooms, jnp.float32)] * 2,
        compiler_params=pltpu.CompilerParams(vmem_limit_bytes=12 * 1024 * 1024),
        cost_estimate=pl.CostEstimate(
            flops=flops, bytes_accessed=sum(x.size * 2 for x in arrays), transcendentals=flops // (4 * HEAD_DIM)
        ),
    )(*scalars, *arrays)


def pack_kernel(copies, width, mask, offset, *refs):
    ins, outs, sems = refs[:3], refs[3:-1], refs[-1]
    h = lax.axis_index("head")
    started = []
    for n, (operand, d, begin, result, at, lanes) in enumerate(copies):
        source = ins[operand].at[:, pl.ds(pl.multiple_of((h ^ d) * width + begin, HEAD_DIM), lanes)]
        copy = pltpu.make_async_copy(source, outs[result].at[:, at : at + lanes], sems.at[n])
        copy.start()
        started.append(copy)
    if len(outs) > 1 + max(copy[3] for copy in copies):
        told = outs[-1]
        for group in range(told.shape[1] // 128):
            value = mask[0, group] if group < 4 else offset[0]
            rows = jnp.full((told.shape[0], 128), value, jnp.int32).astype(jnp.float32)
            told[:, group * 128 : (group + 1) * 128] = rows.astype(told.dtype)
    for copy in started:
        copy.wait()


def packed(operands, mask, offset, results, width, told):
    rows = operands[0].shape[0]
    copies, shapes = [], []
    for n, parts in enumerate(results):
        at = 0
        for operand, d, begin, lanes in parts:
            copies.append((operand, d, begin, n, at, lanes))
            at += lanes
        shapes.append(jax.ShapeDtypeStruct((rows, at), jnp.bfloat16))
    if told:
        shapes.append(jax.ShapeDtypeStruct((INFO_ROWS, told), jnp.bfloat16))
    return pl.pallas_call(
        functools.partial(pack_kernel, copies, width),
        in_specs=[pl.BlockSpec(memory_space=pltpu.SMEM)] * 2 + [pl.BlockSpec(memory_space=pltpu.HBM)] * 3,
        out_specs=[pl.BlockSpec(memory_space=pltpu.VMEM)] * len(shapes),
        out_shape=shapes,
        scratch_shapes=[pltpu.SemaphoreType.DMA((len(copies),))],
        compiler_params=pltpu.CompilerParams(vmem_limit_bytes=4 * 1024 * 1024),
    )(mask, offset, *operands)


def relayed_kernel(parts, mine, other, *outs):
    tile = other.shape[0]
    half = other.shape[1] // 2
    offset = jnp.max(mine[tile : tile + INFO_ROWS, 4 * 128 : 5 * 128].astype(jnp.float32))
    here = offset == (lax.axis_index("head") // 2).astype(jnp.float32)

    def take(ref):
        for (begin, end), out in zip(parts, outs):
            out[:, : end - begin] = ref[:tile, begin:end]
            out[:, end - begin :] = ref[:tile, half + begin : half + end]

    @pl.when(here)
    def _():
        take(mine)

    @pl.when(jnp.logical_not(here))
    def _():
        take(other)


def relayed(mine, other, parts):
    return pl.pallas_call(
        functools.partial(relayed_kernel, parts),
        in_specs=[pl.BlockSpec(memory_space=pltpu.VMEM)] * 2,
        out_specs=[pl.BlockSpec(memory_space=pltpu.VMEM)] * len(parts),
        out_shape=[jax.ShapeDtypeStruct((other.shape[0], 2 * (end - begin)), other.dtype) for begin, end in parts],
        compiler_params=pltpu.CompilerParams(vmem_limit_bytes=4 * 1024 * 1024),
    )(mine, other)


def four_frames(queries, keys, values, pair_mask, tile_offset):
    h = lax.axis_index("head")
    rows, features = queries.shape
    width = features // 4
    heads = width // HEAD_DIM

    def columns(array, d):
        return lax.dynamic_slice_in_dim(array, (h ^ d) * width, width, axis=1)

    def beside(*arrays):
        return jnp.concatenate(arrays, axis=1)

    def below(*arrays):
        return jnp.concatenate(arrays, axis=0)

    def to_head(array, d):
        return lax.ppermute(array, "head", [(i, i ^ d) for i in range(4)])

    def along(array, pairs):
        return lax.ppermute(array, "frame", pairs)

    def across(array):
        pairs = [(4 * z + j, 4 * (3 - z) + j if z in (1, 2) else 4 * z + (j ^ 1)) for z in range(4) for j in range(4)]
        return lax.ppermute(array, ("frame", "head"), pairs)

    def after(array, earlier):
        return lax.optimization_barrier((array, earlier))[0]

    kv = [[columns(array, d) for array in (keys, values)] for d in range(4)]
    kv = lax.optimization_barrier(kv)
    got = to_head(beside(*kv[1], *kv[3]), 1)
    pay, q_own, q_far, told = packed(
        (queries, keys, values),
        pair_mask,
        tile_offset,
        [[(0, 1, 0, width), (0, 3, 0, width)], [(0, 0, 0, width)], [(0, 2, 0, width)]],
        width,
        2 * width,
    )
    mine = below(beside(*kv[0]), got[:, : 2 * width], told)
    other = to_head(below(beside(*kv[2]), got[:, 2 * width :]), 2)
    n1m = along(mine, OUTER)
    n2m = across(mine)
    n1o = along(other, OUTER)
    n2o = across(other)

    got = to_head(after(pay, got), 1)
    q_mine = below(q_own, got[:, :width])
    q_other = to_head(after(below(q_far, got[:, width:]), other), 2)

    tile = 2 * rows
    cut = HOME * HEAD_DIM
    guests = heads - HOME
    q_guest = along(below(q_mine[:, cut:], q_other[:, cut:]), OUTER)
    r1_home, r1_rest = after(relayed(n1m, n1o, [(0, cut), (cut, width)]), n2m)
    r1_home = across(r1_home)
    (r2,) = relayed(n2m, n2o, [(0, cut)])
    r1_rest = across(after(r1_rest, r2))
    r2 = along(r2, OUTER)

    def state(count):
        return [((count * 2 * tile, HEAD_DIM), jnp.float32)] * 3 + [((8, 128), jnp.float32)]

    def flops(chunks, tiles):
        return 4 * chunks * tiles * tile * tile * HEAD_DIM

    bf16 = jnp.bfloat16
    q = [q_mine, q_other]
    around = [mine, other, n1m, n1o, n2m, n2o]
    *near, done = run_kernel(
        functools.partial(near_kernel, 0, 0, ((6, HOME), (4, HOME))),
        None,
        [*q, *around],
        state(HOME),
        (tile, 6 * tile),
        flops(2 * HOME, 6),
    )
    r3 = along(after(passed(r1_home, done), r2), OUTER)
    q_halves = [q_guest[:tile], q_guest[tile:]]
    *guest_near, _ = run_kernel(
        functools.partial(near_kernel, HOME, 0, ((4, guests), (0, 0))),
        None,
        [*q_halves, mine, other, n1m, n1o],
        state(guests),
        (tile, 4 * tile),
        flops(2 * guests, 4),
    )
    (back,) = run_kernel(
        functools.partial(guest_kernel, HOME),
        None,
        [q_guest, *guest_near, n1m, n2m, n2o, r1_rest],
        [((2 * tile, width - cut), bf16)],
        (tile, 3 * tile),
        flops(2 * guests, 3),
    )
    back = along(back, OUTER)
    out = run_kernel(
        home_kernel, pair_mask, [*q, *near, r1_home, r2, r3], [((rows, cut), bf16)] * 4, (tile, 2 * tile), flops(2 * HOME, 2)
    )
    pieces = [(to_head(out[d], d) if d else out[0], d, 0) for d in range(4)]
    *rest_near, _ = run_kernel(
        functools.partial(near_kernel, HOME, HOME, ((6, guests), (0, 0))),
        None,
        [*q, *around],
        state(guests),
        (tile, 6 * tile),
        flops(2 * guests, 6),
    )
    out = run_kernel(
        functools.partial(rest_kernel, HOME),
        pair_mask,
        [*q, *rest_near, r1_rest, after(back, out[1])],
        [((rows, width - cut), bf16)] * 4,
        (tile, tile),
        flops(2 * guests, 1),
    )
    pieces += [(to_head(out[d], d) if d else out[0], d, cut) for d in range(4)]
    result = jnp.zeros((rows, features), jnp.bfloat16)
    for piece, d, begin in pieces:
        result = lax.dynamic_update_slice_in_dim(result, piece, (h ^ d) * width + begin, axis=1)
    return result


def solution(mesh):
    sizes = dict(mesh.shape)
    per_device = four_frames if sizes["frame"] == 4 and sizes["head"] == 4 else general
    return jax.shard_map(
        per_device,
        mesh=mesh,
        in_specs=(
            P(("parts", "frame", "head"), None),
            P(("parts", "frame", "head"), None),
            P(("parts", "frame", "head"), None),
            P(("parts", "frame"), None),
            P(("parts", "frame")),
        ),
        out_specs=P(("parts", "frame", "head"), None),
        check_vma=False,
    )
```

```python
import functools
import math

import jax
import jax.numpy as jnp
from jax import lax
from jax.experimental import pallas as pl
from jax.experimental.pallas import tpu as pltpu
from jax.sharding import PartitionSpec as P

HEAD_DIM = 128
SCALE = 1.0 / HEAD_DIM**0.5
LOG2E = math.log2(math.e)


def padded(x, sides, width):
    for axis, dim in sides:
        peers, length = (lax.axis_size(axis), x.shape[dim])
        up = [(i, (i + 1) % peers) for i in range(peers - 1)]
        down = [(j, i) for i, j in up]
        last = lax.slice_in_dim(x, length - width, length, axis=dim)
        leading = lax.slice_in_dim(x, 0, width, axis=dim)
        before = lax.ppermute(last, axis, up)
        after = lax.ppermute(leading, axis, down)
        x = jnp.concatenate([before, x, after], axis=dim)
    return x


def from_partner(x, axis, bit):
    return lax.ppermute(x, axis, [(i, i ^ 1 << bit) for i in range(lax.axis_size(axis))])


def subsample(frame_rows, offset, level, tiles, tile):
    step = 2**level
    width = frame_rows.shape[-1]
    grouped = frame_rows.reshape(tiles // step, step, tile, width)
    picked = lax.dynamic_index_in_dim(grouped, offset % step, 1, keepdims=False)
    return picked.reshape(-1, width)


def attend(query_rows, key_rows, value_rows, valid):
    count = query_rows.shape[0]
    heads = query_rows.shape[1] // HEAD_DIM
    q_three = query_rows.reshape(count, heads, HEAD_DIM).transpose(1, 0, 2)
    k_three = key_rows.reshape(-1, heads, HEAD_DIM).transpose(1, 0, 2)
    v_three = value_rows.reshape(-1, heads, HEAD_DIM).transpose(1, 0, 2)

    def one_head(operands):
        q_head, k_head, v_head = operands
        scores = jnp.dot(q_head, k_head.T, preferred_element_type=jnp.float32) * SCALE
        scores = jnp.where(valid[None, :] > 0, scores, -1e30)
        top = jnp.max(scores, axis=1, keepdims=True)
        weights = jnp.exp(scores - top) * valid[None, :]
        total = jnp.sum(weights, axis=1, keepdims=True)
        mixed = jnp.dot(weights.astype(jnp.bfloat16), v_head, preferred_element_type=jnp.float32)
        return mixed / total

    outcome = lax.map(one_head, (q_three, k_three, v_three))
    return outcome.transpose(1, 0, 2).reshape(count, heads * HEAD_DIM).astype(jnp.bfloat16)


def ordered(mine, theirs, upper):
    return jnp.where(upper == 1, jnp.concatenate([theirs, mine]), jnp.concatenate([mine, theirs]))


def general(queries, keys, values, pair_mask, tile_offset):
    frames_n = lax.axis_size("frame")
    current = lax.axis_index("frame")
    q_rows, k_rows, v_rows = (
        lax.all_to_all(queries, "head", split_axis=1, concat_axis=0, tiled=True),
        lax.all_to_all(keys, "head", split_axis=1, concat_axis=0, tiled=True),
        lax.all_to_all(values, "head", split_axis=1, concat_axis=0, tiled=True),
    )
    count = q_rows.shape[0]
    width = q_rows.shape[1]
    tiles = frames_n // 2
    tile = count // tiles
    depth = frames_n.bit_length() - 1
    stacked = jnp.stack([k_rows, v_rows])
    near = padded(stacked, (("frame", 1),), count)
    near_index = current - 1 + jnp.arange(3, dtype=jnp.int32)
    near_good = ((near_index >= 0) & (near_index < frames_n)).astype(jnp.float32)
    key_parts = [near[0]]
    value_parts = [near[1]]
    valid_parts = [jnp.repeat(near_good, count)]
    mask_row = pair_mask[0]
    offset = tile_offset[0]
    k_tiles = k_rows.reshape(tiles, tile, width)
    v_tiles = v_rows.reshape(tiles, tile, width)
    own = {}
    for level in range(1, depth):
        own[level] = (
            subsample(k_tiles, offset, level, tiles, tile)[None],
            subsample(v_tiles, offset, level, tiles, tile)[None],
        )
    sibling = {}
    cut = max(1, depth - 2)
    upper_levels = [level for level in range(1, depth) if level >= cut]
    k_pack = jnp.concatenate([own[level][0].reshape(-1, width) for level in upper_levels])
    v_pack = jnp.concatenate([own[level][1].reshape(-1, width) for level in upper_levels])
    k_every, v_every = (
        lax.all_gather(k_pack, "frame", axis=0, tiled=True),
        lax.all_gather(v_pack, "frame", axis=0, tiled=True),
    )
    k_every = k_every.reshape(frames_n, -1, width)
    v_every = v_every.reshape(frames_n, -1, width)
    position = 0
    for level in upper_levels:
        step = 2**level
        rows = count // step
        start = jnp.bitwise_xor(current // step, 1) * step
        block_k = lax.dynamic_slice_in_dim(k_every[:, position : position + rows], start, step, 0)
        block_v = lax.dynamic_slice_in_dim(v_every[:, position : position + rows], start, step, 0)
        sibling[level] = (block_k, block_v)
        position = position + rows
    swap_levels = [level for level in range(1, depth) if level < cut]
    growing = {level: own[level] for level in swap_levels}
    sections = cut if swap_levels else 0
    for bit in range(sections):
        active = [level for level in swap_levels if level >= bit]
        k_pack = jnp.concatenate([growing[level][0].reshape(-1, width) for level in active])
        v_pack = jnp.concatenate([growing[level][1].reshape(-1, width) for level in active])
        k_in, v_in = (from_partner(k_pack, "frame", bit), from_partner(v_pack, "frame", bit))
        upper = current // 2**bit % 2
        position = 0
        for level in active:
            shape = growing[level][0].shape
            size = shape[0] * shape[1]
            theirs_k = k_in[position : position + size].reshape(shape)
            theirs_v = v_in[position : position + size].reshape(shape)
            position = position + size
            if level == bit:
                sibling[level] = (theirs_k, theirs_v)
            else:
                growing[level] = (
                    ordered(growing[level][0], theirs_k, upper),
                    ordered(growing[level][1], theirs_v, upper),
                )
    for level in range(1, depth):
        step = 2**level
        start = jnp.bitwise_xor(current // step, 1) * step
        frame_ids = start + jnp.arange(step, dtype=jnp.int32)
        allowed = lax.dynamic_slice_in_dim(mask_row, start, step, 0)
        good = ((jnp.abs(frame_ids - current) >= 2) & (allowed == 1)).astype(jnp.float32)
        block_k, block_v = sibling[level]
        key_parts.append(block_k.reshape(-1, width))
        value_parts.append(block_v.reshape(-1, width))
        valid_parts.append(jnp.repeat(good, block_k.shape[1]))
    result = attend(
        q_rows,
        jnp.concatenate(key_parts),
        jnp.concatenate(value_parts),
        jnp.concatenate(valid_parts),
    )
    return lax.all_to_all(result, "head", split_axis=0, concat_axis=1, tiled=True)


HOME = 3
INFO_ROWS = 16
OUTER = [(0, 1), (1, 0), (2, 3), (3, 2)]
FACTOR = SCALE * LOG2E


def inner_frame():
    z = lax.axis_index("frame")
    return (z == 1) | (z == 2)


def head_lanes(first, i):
    return pl.ds(pl.multiple_of((first + i) * HEAD_DIM, HEAD_DIM), HEAD_DIM)


def keys_of(ref, first, i, rows):
    return ref[:rows, head_lanes(first, i)]


def values_of(ref, first, i, rows):
    return ref[:rows, head_lanes(ref.shape[1] // (2 * HEAD_DIM) + first, i)]


def dot_keys(q, k):
    return lax.dot_general(q, k, (((1,), (1,)), ((), ())), preferred_element_type=jnp.float32)


def fold(x, op):
    result = x[:, :128]
    for at in range(128, x.shape[1], 128):
        result = op(result, x[:, at : at + 128])
    return result


def near_kernel(first, counts, queries_of, n_queries, *refs):
    queries, tiles, (mixed_out, stats, done), rooms = refs[:n_queries], refs[n_queries:-5], refs[-5:-2], refs[-2:]
    rows = rooms[0].shape[0]
    done[...] = jnp.zeros_like(done)

    def one_head(used, i):
        found = []
        for half, held in enumerate(rooms):
            q = queries_of(queries, half, i)
            best = None
            for at, ref in enumerate(used):
                s = dot_keys(q, keys_of(ref, first, i, rows))
                held[:, at * rows : (at + 1) * rows] = s
                part = fold(s, jnp.maximum)
                best = part if best is None else jnp.maximum(best, part)
            found.append(jnp.max(best, axis=1, keepdims=True))
        for half, (top, held) in enumerate(zip(found, rooms)):
            total, mixed = None, None
            for at, ref in enumerate(used):
                w = jnp.exp2((held[:, at * rows : (at + 1) * rows] - top) * FACTOR)
                mix = jnp.dot(w.astype(jnp.bfloat16), values_of(ref, first, i, rows), preferred_element_type=jnp.float32)
                part = fold(w, jnp.add)
                mixed = mix if mixed is None else mixed + mix
                total = part if total is None else total + part
            span = pl.ds(pl.multiple_of((2 * i + half) * rows, rows), rows)
            mixed_out[span] = mixed
            half_lanes = (rows, HEAD_DIM // 2)
            stats[span, : HEAD_DIM // 2] = jnp.broadcast_to(top, half_lanes)
            stats[span, HEAD_DIM // 2 :] = jnp.broadcast_to(jnp.sum(total, axis=1, keepdims=True), half_lanes)

    for wanted, (n_tiles, n_heads) in zip((True, False), counts):
        if n_heads:

            @pl.when(inner_frame() == wanted)
            def _():
                def step(i, carry):
                    one_head(tiles[:n_tiles], i)
                    return carry

                lax.fori_loop(0, n_heads, step, 0)


def own_queries(refs, half, i):
    return refs[half][:, head_lanes(0, i)]


def guest_queries(refs, half, i):
    return refs[0][:, head_lanes(half * HOME, i)]


def add_far(q, state, slots, i, begin, held):
    rows = q.shape[0]
    span = slice(begin, begin + rows)
    near_top = state[1][span, :1]
    top = near_top
    for at, (ref, first, valid) in enumerate(slots):
        s = dot_keys(q, keys_of(ref, first, i, rows))
        held[:, at * rows : (at + 1) * rows] = s
        best = jnp.max(fold(s, jnp.maximum), axis=1, keepdims=True)
        top = jnp.maximum(top, best if valid is None else jnp.where(valid, best, -1e30))
    shrink = jnp.exp2((near_top - top) * FACTOR)
    mixed = state[0][span] * shrink
    total = None
    for at, (ref, first, valid) in enumerate(slots):
        level = top if valid is None else jnp.where(valid, top, 1e30)
        w = jnp.exp2((held[:, at * rows : (at + 1) * rows] - level) * FACTOR)
        mixed += jnp.dot(w.astype(jnp.bfloat16), values_of(ref, first, i, rows), preferred_element_type=jnp.float32)
        part = fold(w, jnp.add)
        total = part if total is None else total + part
    total = jnp.sum(total, axis=1, keepdims=True) + state[1][span, HEAD_DIM // 2 : HEAD_DIM // 2 + 1] * shrink
    return (mixed * (1.0 / total)).astype(jnp.bfloat16)


def lanes_of(i):
    return slice(i * HEAD_DIM, (i + 1) * HEAD_DIM)


def finish_own(first, queries, state, slots, outs, rooms):
    rows, piece = queries[0].shape[0], outs[0].shape[0]
    for i in range(outs[0].shape[1] // HEAD_DIM):
        for half, q in enumerate(queries):
            begin = (2 * (first + i) + half) * rows
            value = add_far(q[:, lanes_of(first + i)], state, slots, i, begin, rooms[2 * i + half])
            outs[2 * half][:, lanes_of(i)] = value[:piece]
            outs[2 * half + 1][:, lanes_of(i)] = value[piece:]


def home_kernel(mask, q_mine, q_other, mixed, stats, r1, r2, r3, *rest):
    outs, rooms = rest[:4], rest[4:]
    z = lax.axis_index("frame")
    near2 = mask[0, z ^ 2] == 1

    @pl.when(inner_frame())
    def _():
        finish_own(0, (q_mine, q_other), (mixed, stats), [(r1, 0, near2)], outs, rooms)

    @pl.when(jnp.logical_not(inner_frame()))
    def _():
        slots = [(r2, 0, near2), (r3, 0, mask[0, z ^ 3] == 1)]
        finish_own(0, (q_mine, q_other), (mixed, stats), slots, outs, rooms)


def guest_kernel(q, mixed, stats, n1m, n2m, n2o, r1, out, *rooms):
    rows = r1.shape[0]
    z = lax.axis_index("frame")

    def told(ref, group):
        return ref[rows : rows + 1, group * 128 : (group + 1) * 128][:, :1].astype(jnp.float32)

    @pl.when(inner_frame())
    def _():
        near2 = jnp.where(z == 1, told(n1m, 2), told(n1m, 1)) > 0.5
        near1 = jnp.where(z == 1, told(n1m, 3), told(n1m, 0)) > 0.5
        picked = told(n2m, 4) == (lax.axis_index("head") // 2).astype(jnp.float32)
        slots = [(n2m, HOME, near2 & picked), (n2o, HOME, near2 & jnp.logical_not(picked)), (r1, 0, near1)]
        for i in range(out.shape[1] // HEAD_DIM):
            for half in range(2):
                begin = (2 * i + half) * rows
                value = add_far(guest_queries((q,), half, i), (mixed, stats), slots, i, begin, rooms[2 * i + half])
                out[half * rows : (half + 1) * rows, lanes_of(i)] = value


def rest_kernel(mask, q_mine, q_other, mixed, stats, r1, back, *rest):
    outs, rooms = rest[:4], rest[4:]
    z = lax.axis_index("frame")

    @pl.when(inner_frame())
    def _():
        finish_own(HOME, (q_mine, q_other), (mixed, stats), [(r1, 0, mask[0, z ^ 2] == 1)], outs, rooms)

    @pl.when(jnp.logical_not(inner_frame()))
    def _():
        for d, out in enumerate(outs):
            out[...] = back[d * out.shape[0] : (d + 1) * out.shape[0]]


def pass_kernel(done, x, out):
    out[...] = x[...]


def passed(x, done):
    return pl.pallas_call(
        pass_kernel,
        in_specs=[pl.BlockSpec(memory_space=pltpu.VMEM)] * 2,
        out_specs=pl.BlockSpec(memory_space=pltpu.VMEM),
        out_shape=jax.ShapeDtypeStruct(x.shape, x.dtype),
        compiler_params=pltpu.CompilerParams(vmem_limit_bytes=4 * 1024 * 1024),
    )(done, x)


def run_kernel(kernel, mask, arrays, outs, rooms, flops):
    scalars = [] if mask is None else [mask]
    return pl.pallas_call(
        kernel,
        in_specs=[pl.BlockSpec(memory_space=pltpu.SMEM)] * len(scalars)
        + [pl.BlockSpec(memory_space=pltpu.VMEM)] * len(arrays),
        out_specs=[pl.BlockSpec(memory_space=pltpu.VMEM)] * len(outs),
        out_shape=[jax.ShapeDtypeStruct(shape, dtype) for shape, dtype in outs],
        scratch_shapes=[pltpu.VMEM(rooms[1], jnp.float32)] * rooms[0],
        compiler_params=pltpu.CompilerParams(vmem_limit_bytes=10 * 1024 * 1024),
        cost_estimate=pl.CostEstimate(
            flops=flops, bytes_accessed=sum(x.size * 2 for x in arrays), transcendentals=flops // (4 * HEAD_DIM)
        ),
    )(*scalars, *arrays)


def pack_kernel(copies, width, mask, offset, *refs):
    ins, outs, sems = refs[:3], refs[3:-1], refs[-1]
    h = lax.axis_index("head")
    started = []
    for n, (operand, d, begin, result, at, lanes) in enumerate(copies):
        source = ins[operand].at[:, pl.ds(pl.multiple_of((h ^ d) * width + begin, HEAD_DIM), lanes)]
        copy = pltpu.make_async_copy(source, outs[result].at[:, at : at + lanes], sems.at[n])
        copy.start()
        started.append(copy)
    if len(outs) > 1 + max(copy[3] for copy in copies):
        told = outs[-1]
        for group in range(told.shape[1] // 128):
            value = mask[0, group] if group < 4 else offset[0]
            rows = jnp.full((told.shape[0], 128), value, jnp.int32).astype(jnp.float32)
            told[:, group * 128 : (group + 1) * 128] = rows.astype(told.dtype)
    for copy in started:
        copy.wait()


def packed(operands, mask, offset, results, width, told):
    rows = operands[0].shape[0]
    copies, shapes = [], []
    for n, parts in enumerate(results):
        at = 0
        for operand, d, begin, lanes in parts:
            copies.append((operand, d, begin, n, at, lanes))
            at += lanes
        shapes.append(jax.ShapeDtypeStruct((rows, at), jnp.bfloat16))
    if told:
        shapes.append(jax.ShapeDtypeStruct((INFO_ROWS, told), jnp.bfloat16))
    return pl.pallas_call(
        functools.partial(pack_kernel, copies, width),
        in_specs=[pl.BlockSpec(memory_space=pltpu.SMEM)] * 2 + [pl.BlockSpec(memory_space=pltpu.HBM)] * 3,
        out_specs=[pl.BlockSpec(memory_space=pltpu.VMEM)] * len(shapes),
        out_shape=shapes,
        scratch_shapes=[pltpu.SemaphoreType.DMA((len(copies),))],
        compiler_params=pltpu.CompilerParams(vmem_limit_bytes=4 * 1024 * 1024),
    )(mask, offset, *operands)


def relayed_kernel(parts, mine, other, *outs):
    tile = other.shape[0]
    half = other.shape[1] // 2
    offset = jnp.max(mine[tile : tile + INFO_ROWS, 4 * 128 : 5 * 128].astype(jnp.float32))
    here = offset == (lax.axis_index("head") // 2).astype(jnp.float32)

    def take(ref):
        for (begin, end), out in zip(parts, outs):
            out[:, : end - begin] = ref[:tile, begin:end]
            out[:, end - begin :] = ref[:tile, half + begin : half + end]

    @pl.when(here)
    def _():
        take(mine)

    @pl.when(jnp.logical_not(here))
    def _():
        take(other)


def relayed(mine, other, parts):
    return pl.pallas_call(
        functools.partial(relayed_kernel, parts),
        in_specs=[pl.BlockSpec(memory_space=pltpu.VMEM)] * 2,
        out_specs=[pl.BlockSpec(memory_space=pltpu.VMEM)] * len(parts),
        out_shape=[jax.ShapeDtypeStruct((other.shape[0], 2 * (end - begin)), other.dtype) for begin, end in parts],
        compiler_params=pltpu.CompilerParams(vmem_limit_bytes=4 * 1024 * 1024),
    )(mine, other)


def swap_kernel(mine, other, q_mine, q_other, out):
    cut = HOME * HEAD_DIM

    @pl.when(inner_frame())
    def _():
        relayed_kernel([(0, cut)], mine, other, out)

    @pl.when(jnp.logical_not(inner_frame()))
    def _():
        count = q_mine.shape[1] - cut
        out[...] = jnp.zeros_like(out)
        out[:, :count] = q_mine[:, cut:]
        out[:, cut : cut + count] = q_other[:, cut:]


def swapped(mine, other, q_mine, q_other):
    return pl.pallas_call(
        swap_kernel,
        in_specs=[pl.BlockSpec(memory_space=pltpu.VMEM)] * 4,
        out_specs=pl.BlockSpec(memory_space=pltpu.VMEM),
        out_shape=jax.ShapeDtypeStruct((other.shape[0], 2 * HOME * HEAD_DIM), other.dtype),
        compiler_params=pltpu.CompilerParams(vmem_limit_bytes=4 * 1024 * 1024),
    )(mine, other, q_mine, q_other)


def four_frames(queries, keys, values, pair_mask, tile_offset):
    h = lax.axis_index("head")
    rows, features = queries.shape
    width = features // 4
    heads = width // HEAD_DIM

    def columns(array, d):
        return lax.dynamic_slice_in_dim(array, (h ^ d) * width, width, axis=1)

    def beside(*arrays):
        return jnp.concatenate(arrays, axis=1)

    def below(*arrays):
        return jnp.concatenate(arrays, axis=0)

    def to_head(array, d):
        return lax.ppermute(array, "head", [(i, i ^ d) for i in range(4)])

    def along(array, pairs):
        return lax.ppermute(array, "frame", pairs)

    def across(array):
        pairs = [(4 * z + j, 4 * (3 - z) + j if z in (1, 2) else 4 * z + (j ^ 1)) for z in range(4) for j in range(4)]
        return lax.ppermute(array, ("frame", "head"), pairs)

    def after(array, earlier):
        return lax.optimization_barrier((array, earlier))[0]

    kv = [[columns(array, d) for array in (keys, values)] for d in range(4)]
    kv = lax.optimization_barrier(kv)
    got = to_head(beside(*kv[1], *kv[3]), 1)
    pay, q_own, q_far, told = packed(
        (queries, keys, values),
        pair_mask,
        tile_offset,
        [[(0, 1, 0, width), (0, 3, 0, width)], [(0, 0, 0, width)], [(0, 2, 0, width)]],
        width,
        2 * width,
    )
    mine = below(beside(*kv[0]), got[:, : 2 * width], told)
    other = to_head(below(beside(*kv[2]), got[:, 2 * width :]), 2)
    n1m = along(mine, OUTER)
    n2m = across(mine)
    n1o = along(other, OUTER)
    n2o = across(other)

    got = to_head(after(pay, got), 1)
    q_mine = below(q_own, got[:, :width])
    q_other = to_head(after(below(q_far, got[:, width:]), other), 2)

    tile = 2 * rows
    cut = HOME * HEAD_DIM
    guests = heads - HOME
    r1_home, r1_rest = after(relayed(n1m, n1o, [(0, cut), (cut, width)]), n2m)
    r1_home = across(r1_home)
    swap = along(swapped(n2m, n2o, q_mine, q_other), OUTER)
    r1_rest = across(after(r1_rest, n2o))

    def state(count):
        return [((count * 2 * tile, HEAD_DIM), jnp.float32)] * 2 + [((8, 128), jnp.float32)]

    def flops(chunks, tiles):
        return 4 * chunks * tiles * tile * tile * HEAD_DIM

    bf16 = jnp.bfloat16
    q = [q_mine, q_other]
    *near, done = run_kernel(
        functools.partial(near_kernel, 0, ((6, heads), (4, HOME)), own_queries, 2),
        None,
        [*q, mine, other, n1m, n1o, n2m, n2o],
        state(heads),
        (2, (tile, 6 * tile)),
        flops(2 * heads, 6),
    )
    r3 = along(after(passed(r1_home, done), swap), OUTER)
    *guest_near, _ = run_kernel(
        functools.partial(near_kernel, HOME, ((4, guests), (0, 0)), guest_queries, 1),
        None,
        [swap, mine, other, n1m, n1o],
        state(guests),
        (2, (tile, 4 * tile)),
        flops(2 * guests, 4),
    )
    (back,) = run_kernel(
        guest_kernel,
        None,
        [swap, *guest_near, n1m, n2m, n2o, r1_rest],
        [((2 * tile, width - cut), bf16)],
        (2 * guests, (tile, 3 * tile)),
        flops(2 * guests, 3),
    )
    back = along(back, OUTER)
    out = run_kernel(
        home_kernel,
        pair_mask,
        [*q, *near, r1_home, swap, r3],
        [((rows, cut), bf16)] * 4,
        (2 * HOME, (tile, 2 * tile)),
        flops(2 * HOME, 2),
    )
    pieces = [(to_head(out[d], d) if d else out[0], d, 0) for d in range(4)]
    out = run_kernel(
        rest_kernel,
        pair_mask,
        [*q, *near, r1_rest, after(back, out[1])],
        [((rows, width - cut), bf16)] * 4,
        (2 * guests, (tile, tile)),
        flops(2 * guests, 1),
    )
    pieces += [(to_head(out[d], d) if d else out[0], d, cut) for d in range(4)]
    result = jnp.zeros((rows, features), jnp.bfloat16)
    for piece, d, begin in pieces:
        result = lax.dynamic_update_slice_in_dim(result, piece, (h ^ d) * width + begin, axis=1)
    return result


def solution(mesh):
    sizes = dict(mesh.shape)
    per_device = four_frames if sizes["frame"] == 4 and sizes["head"] == 4 else general
    return jax.shard_map(
        per_device,
        mesh=mesh,
        in_specs=(
            P(("parts", "frame", "head"), None),
            P(("parts", "frame", "head"), None),
            P(("parts", "frame", "head"), None),
            P(("parts", "frame"), None),
            P(("parts", "frame")),
        ),
        out_specs=P(("parts", "frame", "head"), None),
        check_vma=False,
    )
```

```python
import functools
import math

import jax
import jax.numpy as jnp
from jax import lax
from jax.experimental import pallas as pl
from jax.experimental.pallas import tpu as pltpu
from jax.sharding import PartitionSpec as P

HEAD_DIM = 128
SCALE = 1.0 / HEAD_DIM**0.5
LOG2E = math.log2(math.e)


def padded(x, sides, width):
    for axis, dim in sides:
        peers, length = (lax.axis_size(axis), x.shape[dim])
        up = [(i, (i + 1) % peers) for i in range(peers - 1)]
        down = [(j, i) for i, j in up]
        last = lax.slice_in_dim(x, length - width, length, axis=dim)
        leading = lax.slice_in_dim(x, 0, width, axis=dim)
        before = lax.ppermute(last, axis, up)
        after = lax.ppermute(leading, axis, down)
        x = jnp.concatenate([before, x, after], axis=dim)
    return x


def from_partner(x, axis, bit):
    return lax.ppermute(x, axis, [(i, i ^ 1 << bit) for i in range(lax.axis_size(axis))])


def subsample(frame_rows, offset, level, tiles, tile):
    step = 2**level
    width = frame_rows.shape[-1]
    grouped = frame_rows.reshape(tiles // step, step, tile, width)
    picked = lax.dynamic_index_in_dim(grouped, offset % step, 1, keepdims=False)
    return picked.reshape(-1, width)


def attend(query_rows, key_rows, value_rows, valid):
    count = query_rows.shape[0]
    heads = query_rows.shape[1] // HEAD_DIM
    q_three = query_rows.reshape(count, heads, HEAD_DIM).transpose(1, 0, 2)
    k_three = key_rows.reshape(-1, heads, HEAD_DIM).transpose(1, 0, 2)
    v_three = value_rows.reshape(-1, heads, HEAD_DIM).transpose(1, 0, 2)

    def one_head(operands):
        q_head, k_head, v_head = operands
        scores = jnp.dot(q_head, k_head.T, preferred_element_type=jnp.float32) * SCALE
        scores = jnp.where(valid[None, :] > 0, scores, -1e30)
        top = jnp.max(scores, axis=1, keepdims=True)
        weights = jnp.exp(scores - top) * valid[None, :]
        total = jnp.sum(weights, axis=1, keepdims=True)
        mixed = jnp.dot(weights.astype(jnp.bfloat16), v_head, preferred_element_type=jnp.float32)
        return mixed / total

    outcome = lax.map(one_head, (q_three, k_three, v_three))
    return outcome.transpose(1, 0, 2).reshape(count, heads * HEAD_DIM).astype(jnp.bfloat16)


def ordered(mine, theirs, upper):
    return jnp.where(upper == 1, jnp.concatenate([theirs, mine]), jnp.concatenate([mine, theirs]))


def general(queries, keys, values, pair_mask, tile_offset):
    frames_n = lax.axis_size("frame")
    current = lax.axis_index("frame")
    q_rows, k_rows, v_rows = (
        lax.all_to_all(queries, "head", split_axis=1, concat_axis=0, tiled=True),
        lax.all_to_all(keys, "head", split_axis=1, concat_axis=0, tiled=True),
        lax.all_to_all(values, "head", split_axis=1, concat_axis=0, tiled=True),
    )
    count = q_rows.shape[0]
    width = q_rows.shape[1]
    tiles = frames_n // 2
    tile = count // tiles
    depth = frames_n.bit_length() - 1
    stacked = jnp.stack([k_rows, v_rows])
    near = padded(stacked, (("frame", 1),), count)
    near_index = current - 1 + jnp.arange(3, dtype=jnp.int32)
    near_good = ((near_index >= 0) & (near_index < frames_n)).astype(jnp.float32)
    key_parts = [near[0]]
    value_parts = [near[1]]
    valid_parts = [jnp.repeat(near_good, count)]
    mask_row = pair_mask[0]
    offset = tile_offset[0]
    k_tiles = k_rows.reshape(tiles, tile, width)
    v_tiles = v_rows.reshape(tiles, tile, width)
    own = {}
    for level in range(1, depth):
        own[level] = (
            subsample(k_tiles, offset, level, tiles, tile)[None],
            subsample(v_tiles, offset, level, tiles, tile)[None],
        )
    sibling = {}
    cut = max(1, depth - 2)
    upper_levels = [level for level in range(1, depth) if level >= cut]
    k_pack = jnp.concatenate([own[level][0].reshape(-1, width) for level in upper_levels])
    v_pack = jnp.concatenate([own[level][1].reshape(-1, width) for level in upper_levels])
    k_every, v_every = (
        lax.all_gather(k_pack, "frame", axis=0, tiled=True),
        lax.all_gather(v_pack, "frame", axis=0, tiled=True),
    )
    k_every = k_every.reshape(frames_n, -1, width)
    v_every = v_every.reshape(frames_n, -1, width)
    position = 0
    for level in upper_levels:
        step = 2**level
        rows = count // step
        start = jnp.bitwise_xor(current // step, 1) * step
        block_k = lax.dynamic_slice_in_dim(k_every[:, position : position + rows], start, step, 0)
        block_v = lax.dynamic_slice_in_dim(v_every[:, position : position + rows], start, step, 0)
        sibling[level] = (block_k, block_v)
        position = position + rows
    swap_levels = [level for level in range(1, depth) if level < cut]
    growing = {level: own[level] for level in swap_levels}
    sections = cut if swap_levels else 0
    for bit in range(sections):
        active = [level for level in swap_levels if level >= bit]
        k_pack = jnp.concatenate([growing[level][0].reshape(-1, width) for level in active])
        v_pack = jnp.concatenate([growing[level][1].reshape(-1, width) for level in active])
        k_in, v_in = (from_partner(k_pack, "frame", bit), from_partner(v_pack, "frame", bit))
        upper = current // 2**bit % 2
        position = 0
        for level in active:
            shape = growing[level][0].shape
            size = shape[0] * shape[1]
            theirs_k = k_in[position : position + size].reshape(shape)
            theirs_v = v_in[position : position + size].reshape(shape)
            position = position + size
            if level == bit:
                sibling[level] = (theirs_k, theirs_v)
            else:
                growing[level] = (
                    ordered(growing[level][0], theirs_k, upper),
                    ordered(growing[level][1], theirs_v, upper),
                )
    for level in range(1, depth):
        step = 2**level
        start = jnp.bitwise_xor(current // step, 1) * step
        frame_ids = start + jnp.arange(step, dtype=jnp.int32)
        allowed = lax.dynamic_slice_in_dim(mask_row, start, step, 0)
        good = ((jnp.abs(frame_ids - current) >= 2) & (allowed == 1)).astype(jnp.float32)
        block_k, block_v = sibling[level]
        key_parts.append(block_k.reshape(-1, width))
        value_parts.append(block_v.reshape(-1, width))
        valid_parts.append(jnp.repeat(good, block_k.shape[1]))
    result = attend(
        q_rows,
        jnp.concatenate(key_parts),
        jnp.concatenate(value_parts),
        jnp.concatenate(valid_parts),
    )
    return lax.all_to_all(result, "head", split_axis=0, concat_axis=1, tiled=True)


HOME = 3
INFO_ROWS = 16
OUTER = [(0, 1), (1, 0), (2, 3), (3, 2)]
FACTOR = SCALE * LOG2E


def inner_frame():
    z = lax.axis_index("frame")
    return (z == 1) | (z == 2)


def head_lanes(first, i):
    return pl.ds(pl.multiple_of((first + i) * HEAD_DIM, HEAD_DIM), HEAD_DIM)


def keys_of(ref, first, i, rows):
    return ref[:rows, head_lanes(first, i)]


def values_of(ref, first, i, rows):
    return ref[:rows, head_lanes(ref.shape[1] // (2 * HEAD_DIM) + first, i)]


def dot_keys(q, k):
    return lax.dot_general(q, k, (((1,), (1,)), ((), ())), preferred_element_type=jnp.float32)


def fold(x, op):
    result = x[:, :128]
    for at in range(128, x.shape[1], 128):
        result = op(result, x[:, at : at + 128])
    return result


def near_kernel(first, counts, queries_of, n_queries, *refs):
    queries, tiles, (mixed_out, stats, done), rooms = refs[:n_queries], refs[n_queries:-5], refs[-5:-2], refs[-2:]
    rows = rooms[0].shape[0]
    done[...] = jnp.zeros_like(done)

    def one_head(used, i):
        found = []
        for half, held in enumerate(rooms):
            q = queries_of(queries, half, i)
            best = None
            for at, ref in enumerate(used):
                s = dot_keys(q, keys_of(ref, first, i, rows))
                held[:, at * rows : (at + 1) * rows] = s
                part = fold(s, jnp.maximum)
                best = part if best is None else jnp.maximum(best, part)
            found.append(jnp.max(best, axis=1, keepdims=True))
        for half, (top, held) in enumerate(zip(found, rooms)):
            total, mixed = None, None
            for at, ref in enumerate(used):
                w = jnp.exp2((held[:, at * rows : (at + 1) * rows] - top) * FACTOR)
                mix = jnp.dot(w.astype(jnp.bfloat16), values_of(ref, first, i, rows), preferred_element_type=jnp.float32)
                part = fold(w, jnp.add)
                mixed = mix if mixed is None else mixed + mix
                total = part if total is None else total + part
            span = pl.ds(pl.multiple_of((2 * i + half) * rows, rows), rows)
            mixed_out[span] = mixed
            half_lanes = (rows, HEAD_DIM // 2)
            stats[span, : HEAD_DIM // 2] = jnp.broadcast_to(top, half_lanes)
            stats[span, HEAD_DIM // 2 :] = jnp.broadcast_to(jnp.sum(total, axis=1, keepdims=True), half_lanes)

    for wanted, (n_tiles, n_heads) in zip((True, False), counts):
        if n_heads:

            @pl.when(inner_frame() == wanted)
            def _():
                def step(i, carry):
                    one_head(tiles[:n_tiles], i)
                    return carry

                lax.fori_loop(0, n_heads, step, 0)


def own_queries(refs, half, i):
    rows = refs[0].shape[0] // 2
    return refs[0][half * rows : (half + 1) * rows, head_lanes(0, i)]


def guest_queries(refs, half, i):
    return refs[0][:, head_lanes(half * HOME, i)]


def add_far(q, state, slots, i, begin, held):
    rows = q.shape[0]
    span = pl.ds(pl.multiple_of(begin, rows), rows)
    stats = state[1][span]
    near_top = stats[:, :1]
    top = near_top
    for at, (ref, first, valid) in enumerate(slots):
        s = dot_keys(q, keys_of(ref, first, i, rows))
        held[:, at * rows : (at + 1) * rows] = s
        best = jnp.max(fold(s, jnp.maximum), axis=1, keepdims=True)
        top = jnp.maximum(top, best if valid is None else jnp.where(valid, best, -1e30))
    shrink = jnp.exp2((near_top - top) * FACTOR)
    mixed = state[0][span] * shrink
    total = None
    for at, (ref, first, valid) in enumerate(slots):
        level = top if valid is None else jnp.where(valid, top, 1e30)
        w = jnp.exp2((held[:, at * rows : (at + 1) * rows] - level) * FACTOR)
        mixed += jnp.dot(w.astype(jnp.bfloat16), values_of(ref, first, i, rows), preferred_element_type=jnp.float32)
        part = fold(w, jnp.add)
        total = part if total is None else total + part
    total = jnp.sum(total, axis=1, keepdims=True) + stats[:, HEAD_DIM // 2 : HEAD_DIM // 2 + 1] * shrink
    return (mixed * (1.0 / total)).astype(jnp.bfloat16)


def each_half(heads, body):
    def step(n, carry):
        body(lax.shift_right_logical(n, 1), lax.bitwise_and(n, 1))
        return carry

    lax.fori_loop(0, 2 * heads, step, 0)


def finish_own(first, queries, state, slots, outs, held):
    piece = outs[0].shape[0]
    rows = 2 * piece

    def body(i, half):
        q = queries[pl.ds(pl.multiple_of(half * rows, rows), rows), head_lanes(first, i)]
        value = add_far(q, state, slots, i, (2 * (first + i) + half) * rows, held)
        for wanted in range(2):

            @pl.when(half == wanted)
            def _():
                outs[2 * wanted][:, head_lanes(0, i)] = value[:piece]
                outs[2 * wanted + 1][:, head_lanes(0, i)] = value[piece:]

    each_half(outs[0].shape[1] // HEAD_DIM, body)


def home_kernel(mask, q, mixed, stats, r1, r2, r3, *rest):
    outs, held = rest[:4], rest[4]
    z = lax.axis_index("frame")
    near2 = mask[0, z ^ 2] == 1

    @pl.when(inner_frame())
    def _():
        finish_own(0, q, (mixed, stats), [(r1, 0, near2)], outs, held)

    @pl.when(jnp.logical_not(inner_frame()))
    def _():
        slots = [(r2, 0, near2), (r3, 0, mask[0, z ^ 3] == 1)]
        finish_own(0, q, (mixed, stats), slots, outs, held)


def guest_kernel(q, mixed, stats, n1m, n2m, n2o, r1, out, held):
    rows = r1.shape[0]
    z = lax.axis_index("frame")

    def told(ref, group):
        return ref[rows : rows + 1, group * 128 : (group + 1) * 128][:, :1].astype(jnp.float32)

    @pl.when(inner_frame())
    def _():
        near2 = jnp.where(z == 1, told(n1m, 2), told(n1m, 1)) > 0.5
        near1 = jnp.where(z == 1, told(n1m, 3), told(n1m, 0)) > 0.5
        picked = told(n2m, 4) == (lax.axis_index("head") // 2).astype(jnp.float32)
        slots = [(n2m, HOME, near2 & picked), (n2o, HOME, near2 & jnp.logical_not(picked)), (r1, 0, near1)]

        def body(i, half):
            value = add_far(guest_queries((q,), half, i), (mixed, stats), slots, i, (2 * i + half) * rows, held)
            out[pl.ds(pl.multiple_of(half * rows, rows), rows), head_lanes(0, i)] = value

        each_half(out.shape[1] // HEAD_DIM, body)


def rest_kernel(mask, q, mixed, stats, r1, back, *rest):
    outs, held = rest[:4], rest[4]
    z = lax.axis_index("frame")

    @pl.when(inner_frame())
    def _():
        finish_own(HOME, q, (mixed, stats), [(r1, 0, mask[0, z ^ 2] == 1)], outs, held)

    @pl.when(jnp.logical_not(inner_frame()))
    def _():
        for d, out in enumerate(outs):
            out[...] = back[d * out.shape[0] : (d + 1) * out.shape[0]]


def pass_kernel(done, x, out):
    out[...] = x[...]


def passed(x, done):
    return pl.pallas_call(
        pass_kernel,
        in_specs=[pl.BlockSpec(memory_space=pltpu.VMEM)] * 2,
        out_specs=pl.BlockSpec(memory_space=pltpu.VMEM),
        out_shape=jax.ShapeDtypeStruct(x.shape, x.dtype),
        compiler_params=pltpu.CompilerParams(vmem_limit_bytes=4 * 1024 * 1024),
    )(done, x)


def run_kernel(kernel, mask, arrays, outs, rooms, flops):
    scalars = [] if mask is None else [mask]
    return pl.pallas_call(
        kernel,
        in_specs=[pl.BlockSpec(memory_space=pltpu.SMEM)] * len(scalars)
        + [pl.BlockSpec(memory_space=pltpu.VMEM)] * len(arrays),
        out_specs=[pl.BlockSpec(memory_space=pltpu.VMEM)] * len(outs),
        out_shape=[jax.ShapeDtypeStruct(shape, dtype) for shape, dtype in outs],
        scratch_shapes=[pltpu.VMEM(rooms[1], jnp.float32)] * rooms[0],
        compiler_params=pltpu.CompilerParams(vmem_limit_bytes=10 * 1024 * 1024),
        cost_estimate=pl.CostEstimate(
            flops=flops, bytes_accessed=sum(x.size * 2 for x in arrays), transcendentals=flops // (4 * HEAD_DIM)
        ),
    )(*scalars, *arrays)


def pack_kernel(copies, width, mask, offset, *refs):
    ins, outs, sems = refs[:3], refs[3:-1], refs[-1]
    h = lax.axis_index("head")
    started = []
    for n, (operand, d, begin, result, at, lanes) in enumerate(copies):
        source = ins[operand].at[:, pl.ds(pl.multiple_of((h ^ d) * width + begin, HEAD_DIM), lanes)]
        copy = pltpu.make_async_copy(source, outs[result].at[:, at : at + lanes], sems.at[n])
        copy.start()
        started.append(copy)
    if len(outs) > 1 + max(copy[3] for copy in copies):
        told = outs[-1]
        for group in range(told.shape[1] // 128):
            value = mask[0, group] if group < 4 else offset[0]
            rows = jnp.full((told.shape[0], 128), value, jnp.int32).astype(jnp.float32)
            told[:, group * 128 : (group + 1) * 128] = rows.astype(told.dtype)
    for copy in started:
        copy.wait()


def packed(operands, mask, offset, results, width, told):
    rows = operands[0].shape[0]
    copies, shapes = [], []
    for n, parts in enumerate(results):
        at = 0
        for operand, d, begin, lanes in parts:
            copies.append((operand, d, begin, n, at, lanes))
            at += lanes
        shapes.append(jax.ShapeDtypeStruct((rows, at), jnp.bfloat16))
    if told:
        shapes.append(jax.ShapeDtypeStruct((INFO_ROWS, told), jnp.bfloat16))
    return pl.pallas_call(
        functools.partial(pack_kernel, copies, width),
        in_specs=[pl.BlockSpec(memory_space=pltpu.SMEM)] * 2 + [pl.BlockSpec(memory_space=pltpu.HBM)] * 3,
        out_specs=[pl.BlockSpec(memory_space=pltpu.VMEM)] * len(shapes),
        out_shape=shapes,
        scratch_shapes=[pltpu.SemaphoreType.DMA((len(copies),))],
        compiler_params=pltpu.CompilerParams(vmem_limit_bytes=4 * 1024 * 1024),
    )(mask, offset, *operands)


def relayed_kernel(parts, mine, other, *outs):
    tile = other.shape[0]
    half = other.shape[1] // 2
    offset = jnp.max(mine[tile : tile + INFO_ROWS, 4 * 128 : 5 * 128].astype(jnp.float32))
    here = offset == (lax.axis_index("head") // 2).astype(jnp.float32)

    def take(ref):
        for (begin, end), out in zip(parts, outs):
            out[:, : end - begin] = ref[:tile, begin:end]
            out[:, end - begin :] = ref[:tile, half + begin : half + end]

    @pl.when(here)
    def _():
        take(mine)

    @pl.when(jnp.logical_not(here))
    def _():
        take(other)


def relayed(mine, other, parts):
    return pl.pallas_call(
        functools.partial(relayed_kernel, parts),
        in_specs=[pl.BlockSpec(memory_space=pltpu.VMEM)] * 2,
        out_specs=[pl.BlockSpec(memory_space=pltpu.VMEM)] * len(parts),
        out_shape=[jax.ShapeDtypeStruct((other.shape[0], 2 * (end - begin)), other.dtype) for begin, end in parts],
        compiler_params=pltpu.CompilerParams(vmem_limit_bytes=4 * 1024 * 1024),
    )(mine, other)


def swap_kernel(mine, other, q, out):
    cut = HOME * HEAD_DIM

    @pl.when(inner_frame())
    def _():
        relayed_kernel([(0, cut)], mine, other, out)

    @pl.when(jnp.logical_not(inner_frame()))
    def _():
        rows, count = out.shape[0], q.shape[1] - cut
        out[...] = jnp.zeros_like(out)
        out[:, :count] = q[:rows, cut:]
        out[:, cut : cut + count] = q[rows:, cut:]


def swapped(mine, other, q):
    return pl.pallas_call(
        swap_kernel,
        in_specs=[pl.BlockSpec(memory_space=pltpu.VMEM)] * 3,
        out_specs=pl.BlockSpec(memory_space=pltpu.VMEM),
        out_shape=jax.ShapeDtypeStruct((other.shape[0], 2 * HOME * HEAD_DIM), other.dtype),
        compiler_params=pltpu.CompilerParams(vmem_limit_bytes=4 * 1024 * 1024),
    )(mine, other, q)


def four_frames(queries, keys, values, pair_mask, tile_offset):
    h = lax.axis_index("head")
    rows, features = queries.shape
    width = features // 4
    heads = width // HEAD_DIM

    def columns(array, d):
        return lax.dynamic_slice_in_dim(array, (h ^ d) * width, width, axis=1)

    def beside(*arrays):
        return jnp.concatenate(arrays, axis=1)

    def below(*arrays):
        return jnp.concatenate(arrays, axis=0)

    def to_head(array, d):
        return lax.ppermute(array, "head", [(i, i ^ d) for i in range(4)])

    def along(array, pairs):
        return lax.ppermute(array, "frame", pairs)

    def across(array):
        pairs = [(4 * z + j, 4 * (3 - z) + j if z in (1, 2) else 4 * z + (j ^ 1)) for z in range(4) for j in range(4)]
        return lax.ppermute(array, ("frame", "head"), pairs)

    def after(array, earlier):
        return lax.optimization_barrier((array, earlier))[0]

    kv = [[columns(array, d) for array in (keys, values)] for d in range(4)]
    kv = lax.optimization_barrier(kv)
    got = to_head(beside(*kv[1], *kv[3]), 1)
    pay, q_own, q_far, told = packed(
        (queries, keys, values),
        pair_mask,
        tile_offset,
        [[(0, 1, 0, width), (0, 3, 0, width)], [(0, 0, 0, width)], [(0, 2, 0, width)]],
        width,
        2 * width,
    )
    mine = below(beside(*kv[0]), got[:, : 2 * width], told)
    other = to_head(below(beside(*kv[2]), got[:, 2 * width :]), 2)
    n1m = along(mine, OUTER)
    n2m = across(mine)
    n1o = along(other, OUTER)
    n2o = across(other)

    got = to_head(after(pay, got), 1)
    q = below(q_own, got[:, :width], to_head(after(below(q_far, got[:, width:]), other), 2))

    tile = 2 * rows
    cut = HOME * HEAD_DIM
    guests = heads - HOME
    r1_home, r1_rest = after(relayed(n1m, n1o, [(0, cut), (cut, width)]), n2m)
    r1_home = across(r1_home)
    swap = along(swapped(n2m, n2o, q), OUTER)
    r1_rest = across(after(r1_rest, n2o))

    def state(count):
        return [((count * 2 * tile, HEAD_DIM), jnp.float32)] * 2 + [((8, 128), jnp.float32)]

    def flops(chunks, tiles):
        return 4 * chunks * tiles * tile * tile * HEAD_DIM

    bf16 = jnp.bfloat16
    *near, done = run_kernel(
        functools.partial(near_kernel, 0, ((6, heads), (4, HOME)), own_queries, 1),
        None,
        [q, mine, other, n1m, n1o, n2m, n2o],
        state(heads),
        (2, (tile, 6 * tile)),
        flops(2 * heads, 6),
    )
    r3 = along(after(passed(r1_home, done), swap), OUTER)
    *guest_near, _ = run_kernel(
        functools.partial(near_kernel, HOME, ((4, guests), (0, 0)), guest_queries, 1),
        None,
        [swap, mine, other, n1m, n1o],
        state(guests),
        (2, (tile, 4 * tile)),
        flops(2 * guests, 4),
    )
    (back,) = run_kernel(
        guest_kernel,
        None,
        [swap, *guest_near, n1m, n2m, n2o, r1_rest],
        [((2 * tile, width - cut), bf16)],
        (1, (tile, 3 * tile)),
        flops(2 * guests, 3),
    )
    back = along(back, OUTER)
    out = run_kernel(
        home_kernel,
        pair_mask,
        [q, *near, r1_home, swap, r3],
        [((rows, cut), bf16)] * 4,
        (1, (tile, 2 * tile)),
        flops(2 * HOME, 2),
    )
    pieces = [(to_head(out[d], d) if d else out[0], d, 0) for d in range(4)]
    out = run_kernel(
        rest_kernel,
        pair_mask,
        [q, *near, r1_rest, after(back, out[1])],
        [((rows, width - cut), bf16)] * 4,
        (1, (tile, tile)),
        flops(2 * guests, 1),
    )
    pieces += [(to_head(out[d], d) if d else out[0], d, cut) for d in range(4)]
    result = jnp.zeros((rows, features), jnp.bfloat16)
    for piece, d, begin in pieces:
        result = lax.dynamic_update_slice_in_dim(result, piece, (h ^ d) * width + begin, axis=1)
    return result


def solution(mesh):
    sizes = dict(mesh.shape)
    per_device = four_frames if sizes["frame"] == 4 and sizes["head"] == 4 else general
    return jax.shard_map(
        per_device,
        mesh=mesh,
        in_specs=(
            P(("parts", "frame", "head"), None),
            P(("parts", "frame", "head"), None),
            P(("parts", "frame", "head"), None),
            P(("parts", "frame"), None),
            P(("parts", "frame")),
        ),
        out_specs=P(("parts", "frame", "head"), None),
        check_vma=False,
    )
```

```python
import functools
import math

import jax
import jax.numpy as jnp
from jax import lax
from jax.experimental import pallas as pl
from jax.experimental.pallas import tpu as pltpu
from jax.sharding import PartitionSpec as P

HEAD_DIM = 128
SCALE = 1.0 / HEAD_DIM**0.5
LOG2E = math.log2(math.e)


def padded(x, sides, width):
    for axis, dim in sides:
        peers, length = (lax.axis_size(axis), x.shape[dim])
        up = [(i, (i + 1) % peers) for i in range(peers - 1)]
        down = [(j, i) for i, j in up]
        last = lax.slice_in_dim(x, length - width, length, axis=dim)
        leading = lax.slice_in_dim(x, 0, width, axis=dim)
        before = lax.ppermute(last, axis, up)
        after = lax.ppermute(leading, axis, down)
        x = jnp.concatenate([before, x, after], axis=dim)
    return x


def from_partner(x, axis, bit):
    return lax.ppermute(x, axis, [(i, i ^ 1 << bit) for i in range(lax.axis_size(axis))])


def subsample(frame_rows, offset, level, tiles, tile):
    step = 2**level
    width = frame_rows.shape[-1]
    grouped = frame_rows.reshape(tiles // step, step, tile, width)
    picked = lax.dynamic_index_in_dim(grouped, offset % step, 1, keepdims=False)
    return picked.reshape(-1, width)


def attend(query_rows, key_rows, value_rows, valid):
    count = query_rows.shape[0]
    heads = query_rows.shape[1] // HEAD_DIM
    q_three = query_rows.reshape(count, heads, HEAD_DIM).transpose(1, 0, 2)
    k_three = key_rows.reshape(-1, heads, HEAD_DIM).transpose(1, 0, 2)
    v_three = value_rows.reshape(-1, heads, HEAD_DIM).transpose(1, 0, 2)

    def one_head(operands):
        q_head, k_head, v_head = operands
        scores = jnp.dot(q_head, k_head.T, preferred_element_type=jnp.float32) * SCALE
        scores = jnp.where(valid[None, :] > 0, scores, -1e30)
        top = jnp.max(scores, axis=1, keepdims=True)
        weights = jnp.exp(scores - top) * valid[None, :]
        total = jnp.sum(weights, axis=1, keepdims=True)
        mixed = jnp.dot(weights.astype(jnp.bfloat16), v_head, preferred_element_type=jnp.float32)
        return mixed / total

    outcome = lax.map(one_head, (q_three, k_three, v_three))
    return outcome.transpose(1, 0, 2).reshape(count, heads * HEAD_DIM).astype(jnp.bfloat16)


def ordered(mine, theirs, upper):
    return jnp.where(upper == 1, jnp.concatenate([theirs, mine]), jnp.concatenate([mine, theirs]))


def general(queries, keys, values, pair_mask, tile_offset):
    frames_n = lax.axis_size("frame")
    current = lax.axis_index("frame")
    q_rows, k_rows, v_rows = (
        lax.all_to_all(queries, "head", split_axis=1, concat_axis=0, tiled=True),
        lax.all_to_all(keys, "head", split_axis=1, concat_axis=0, tiled=True),
        lax.all_to_all(values, "head", split_axis=1, concat_axis=0, tiled=True),
    )
    count = q_rows.shape[0]
    width = q_rows.shape[1]
    tiles = frames_n // 2
    tile = count // tiles
    depth = frames_n.bit_length() - 1
    stacked = jnp.stack([k_rows, v_rows])
    near = padded(stacked, (("frame", 1),), count)
    near_index = current - 1 + jnp.arange(3, dtype=jnp.int32)
    near_good = ((near_index >= 0) & (near_index < frames_n)).astype(jnp.float32)
    key_parts = [near[0]]
    value_parts = [near[1]]
    valid_parts = [jnp.repeat(near_good, count)]
    mask_row = pair_mask[0]
    offset = tile_offset[0]
    k_tiles = k_rows.reshape(tiles, tile, width)
    v_tiles = v_rows.reshape(tiles, tile, width)
    own = {}
    for level in range(1, depth):
        own[level] = (
            subsample(k_tiles, offset, level, tiles, tile)[None],
            subsample(v_tiles, offset, level, tiles, tile)[None],
        )
    sibling = {}
    cut = max(1, depth - 2)
    upper_levels = [level for level in range(1, depth) if level >= cut]
    k_pack = jnp.concatenate([own[level][0].reshape(-1, width) for level in upper_levels])
    v_pack = jnp.concatenate([own[level][1].reshape(-1, width) for level in upper_levels])
    k_every, v_every = (
        lax.all_gather(k_pack, "frame", axis=0, tiled=True),
        lax.all_gather(v_pack, "frame", axis=0, tiled=True),
    )
    k_every = k_every.reshape(frames_n, -1, width)
    v_every = v_every.reshape(frames_n, -1, width)
    position = 0
    for level in upper_levels:
        step = 2**level
        rows = count // step
        start = jnp.bitwise_xor(current // step, 1) * step
        block_k = lax.dynamic_slice_in_dim(k_every[:, position : position + rows], start, step, 0)
        block_v = lax.dynamic_slice_in_dim(v_every[:, position : position + rows], start, step, 0)
        sibling[level] = (block_k, block_v)
        position = position + rows
    swap_levels = [level for level in range(1, depth) if level < cut]
    growing = {level: own[level] for level in swap_levels}
    sections = cut if swap_levels else 0
    for bit in range(sections):
        active = [level for level in swap_levels if level >= bit]
        k_pack = jnp.concatenate([growing[level][0].reshape(-1, width) for level in active])
        v_pack = jnp.concatenate([growing[level][1].reshape(-1, width) for level in active])
        k_in, v_in = (from_partner(k_pack, "frame", bit), from_partner(v_pack, "frame", bit))
        upper = current // 2**bit % 2
        position = 0
        for level in active:
            shape = growing[level][0].shape
            size = shape[0] * shape[1]
            theirs_k = k_in[position : position + size].reshape(shape)
            theirs_v = v_in[position : position + size].reshape(shape)
            position = position + size
            if level == bit:
                sibling[level] = (theirs_k, theirs_v)
            else:
                growing[level] = (
                    ordered(growing[level][0], theirs_k, upper),
                    ordered(growing[level][1], theirs_v, upper),
                )
    for level in range(1, depth):
        step = 2**level
        start = jnp.bitwise_xor(current // step, 1) * step
        frame_ids = start + jnp.arange(step, dtype=jnp.int32)
        allowed = lax.dynamic_slice_in_dim(mask_row, start, step, 0)
        good = ((jnp.abs(frame_ids - current) >= 2) & (allowed == 1)).astype(jnp.float32)
        block_k, block_v = sibling[level]
        key_parts.append(block_k.reshape(-1, width))
        value_parts.append(block_v.reshape(-1, width))
        valid_parts.append(jnp.repeat(good, block_k.shape[1]))
    result = attend(
        q_rows,
        jnp.concatenate(key_parts),
        jnp.concatenate(value_parts),
        jnp.concatenate(valid_parts),
    )
    return lax.all_to_all(result, "head", split_axis=0, concat_axis=1, tiled=True)


HOME = 3
INFO_ROWS = 16
OUTER = [(0, 1), (1, 0), (2, 3), (3, 2)]
FACTOR = SCALE * LOG2E


def inner_frame():
    z = lax.axis_index("frame")
    return (z == 1) | (z == 2)


def head_lanes(first, i):
    return pl.ds(pl.multiple_of((first + i) * HEAD_DIM, HEAD_DIM), HEAD_DIM)


def keys_of(ref, first, i, rows):
    return ref[:rows, head_lanes(first, i)]


def values_of(ref, first, i, rows):
    return ref[:rows, head_lanes(ref.shape[1] // (2 * HEAD_DIM) + first, i)]


def dot_keys(q, k):
    return lax.dot_general(q, k, (((1,), (1,)), ((), ())), preferred_element_type=jnp.float32)


def fold(x, op):
    result = x[:, :128]
    for at in range(128, x.shape[1], 128):
        result = op(result, x[:, at : at + 128])
    return result


def near_kernel(first, counts, queries_of, carries, *refs):
    n_outs = 5 if carries else 4
    ins, outs, rooms = refs[: -2 - n_outs], refs[-2 - n_outs : -2], refs[-2:]
    queries, tiles = ins[0], ins[1:]
    mixed_out, tops, totals, done = outs[:4]
    rows = rooms[0].shape[0]
    done[...] = jnp.zeros_like(done)
    if carries:
        outs[4][...] = ins[-1][...]

    def one_head(used, i):
        found = []
        for half, held in enumerate(rooms):
            q = queries_of(queries, half, i)
            best = None
            for at, ref in enumerate(used):
                s = dot_keys(q, keys_of(ref, first, i, rows))
                held[:, at * rows : (at + 1) * rows] = s
                part = fold(s, jnp.maximum)
                best = part if best is None else jnp.maximum(best, part)
            found.append(jnp.max(best, axis=1, keepdims=True))
        for half, (top, held) in enumerate(zip(found, rooms)):
            total, mixed = None, None
            for at, ref in enumerate(used):
                w = jnp.exp2((held[:, at * rows : (at + 1) * rows] - top) * FACTOR)
                mix = jnp.dot(w.astype(jnp.bfloat16), values_of(ref, first, i, rows), preferred_element_type=jnp.float32)
                part = fold(w, jnp.add)
                mixed = mix if mixed is None else mixed + mix
                total = part if total is None else total + part
            span = pl.ds(pl.multiple_of((2 * i + half) * rows, rows), rows)
            mixed_out[span] = mixed
            tops[span] = jnp.broadcast_to(top, (rows, HEAD_DIM))
            totals[span] = jnp.broadcast_to(jnp.sum(total, axis=1, keepdims=True), (rows, HEAD_DIM))

    for wanted, (n_tiles, n_heads) in zip((True, False), counts):
        if n_heads:

            @pl.when(inner_frame() == wanted)
            def _():
                def step(i, carry):
                    one_head(tiles[:n_tiles], i)
                    return carry

                lax.fori_loop(0, n_heads, step, 0)


def own_queries(ref, half, i):
    rows = ref.shape[0] // 2
    return ref[half * rows : (half + 1) * rows, head_lanes(0, i)]


def guest_queries(ref, half, i):
    return ref[:, head_lanes(half * HOME, i)]


def add_far(q, state, slots, i, begin, held):
    rows = q.shape[0]
    span = pl.ds(pl.multiple_of(begin, rows), rows)
    near_top = state[1][span]
    top = near_top
    for at, (ref, first, valid) in enumerate(slots):
        s = dot_keys(q, keys_of(ref, first, i, rows))
        held[:, at * rows : (at + 1) * rows] = s
        best = jnp.broadcast_to(jnp.max(fold(s, jnp.maximum), axis=1, keepdims=True), near_top.shape)
        top = jnp.maximum(top, jnp.where(valid, best, -1e30))
    shrink = jnp.exp2((near_top - top) * FACTOR)
    mixed = state[0][span] * shrink
    total = None
    for at, (ref, first, valid) in enumerate(slots):
        level = jnp.where(valid, top, 1e30)
        parts = []
        for lane in range(at * rows, (at + 1) * rows, HEAD_DIM):
            part = jnp.exp2((held[:, lane : lane + HEAD_DIM] - level) * FACTOR)
            total = part if total is None else total + part
            parts.append(part.astype(jnp.bfloat16))
        w = jnp.concatenate(parts, axis=1)
        mixed += jnp.dot(w, values_of(ref, first, i, rows), preferred_element_type=jnp.float32)
    total = jnp.broadcast_to(jnp.sum(total, axis=1, keepdims=True), near_top.shape) + state[2][span] * shrink
    return (mixed * (1.0 / total)).astype(jnp.bfloat16)


def each_head(heads, body):
    def step(i, carry):
        body(i)
        return carry

    lax.fori_loop(0, heads, step, 0)


def finish_own(first, queries, state, slots, outs, rooms):
    piece = outs[0].shape[0]
    rows = 2 * piece

    def body(i):
        for half, held in enumerate(rooms):
            q = queries[half * rows : (half + 1) * rows, head_lanes(first, i)]
            value = add_far(q, state, slots, i, (2 * (first + i) + half) * rows, held)
            outs[2 * half][:, head_lanes(0, i)] = value[:piece]
            outs[2 * half + 1][:, head_lanes(0, i)] = value[piece:]

    each_head(outs[0].shape[1] // HEAD_DIM, body)


def home_kernel(mask, q, mixed, tops, totals, r1, r2, r3, *rest):
    outs, rooms, got, sems = rest[:4], rest[4:6], rest[6:8], rest[8]
    z = lax.axis_index("frame")
    near2 = mask[0, z ^ 2] == 1

    def body(far, valid):
        copies = [pltpu.make_async_copy(ref, room, sems.at[n]) for n, (ref, room) in enumerate(zip(far, got))]
        for copy in copies:
            copy.start()
        for copy in copies:
            copy.wait()
        slots = [(room, 0, ok) for room, ok in zip(got, valid)]
        finish_own(0, q, (mixed, tops, totals), slots, outs, rooms)

    @pl.when(inner_frame())
    def _():
        body([r1], [near2])

    @pl.when(jnp.logical_not(inner_frame()))
    def _():
        body([r2, r3], [near2, mask[0, z ^ 3] == 1])


def guest_kernel(q, mixed, tops, totals, n1m, n2m, n2o, r1, out, *rooms):
    rows = r1.shape[0]
    z = lax.axis_index("frame")

    def told(ref, group):
        return ref[rows : rows + 1, group * 128 : (group + 1) * 128].astype(jnp.float32)

    @pl.when(inner_frame())
    def _():
        near2 = jnp.where(z == 1, told(n1m, 2), told(n1m, 1)) > 0.5
        near1 = jnp.where(z == 1, told(n1m, 3), told(n1m, 0)) > 0.5
        picked = told(n2m, 4) == (lax.axis_index("head") // 2).astype(jnp.float32)
        slots = [(n2m, HOME, near2 & picked), (n2o, HOME, near2 & jnp.logical_not(picked)), (r1, 0, near1)]

        def body(i):
            for half, held in enumerate(rooms):
                value = add_far(guest_queries(q, half, i), (mixed, tops, totals), slots, i, (2 * i + half) * rows, held)
                out[half * rows : (half + 1) * rows, head_lanes(0, i)] = value

        each_head(out.shape[1] // HEAD_DIM, body)


def rest_kernel(mask, q, mixed, tops, totals, r1, back, *rest):
    outs, rooms = rest[:4], rest[4:]
    z = lax.axis_index("frame")

    @pl.when(inner_frame())
    def _():
        finish_own(HOME, q, (mixed, tops, totals), [(r1, 0, mask[0, z ^ 2] == 1)], outs, rooms)

    @pl.when(jnp.logical_not(inner_frame()))
    def _():
        for d, out in enumerate(outs):
            out[...] = back[d * out.shape[0] : (d + 1) * out.shape[0]]


def pass_kernel(done, x, out):
    out[...] = x[...]


def passed(x, done):
    return pl.pallas_call(
        pass_kernel,
        in_specs=[pl.BlockSpec(memory_space=pltpu.VMEM)] * 2,
        out_specs=pl.BlockSpec(memory_space=pltpu.VMEM),
        out_shape=jax.ShapeDtypeStruct(x.shape, x.dtype),
        compiler_params=pltpu.CompilerParams(vmem_limit_bytes=4 * 1024 * 1024),
    )(done, x)


def run_kernel(kernel, mask, arrays, outs, room, flops, loose=()):
    scalars = [] if mask is None else [mask]
    scratch = [pltpu.VMEM(room, jnp.float32)] * 2
    if loose:
        scratch += [pltpu.VMEM(loose[0].shape, loose[0].dtype)] * 2 + [pltpu.SemaphoreType.DMA((2,))]
    return pl.pallas_call(
        kernel,
        in_specs=[pl.BlockSpec(memory_space=pltpu.SMEM)] * len(scalars)
        + [pl.BlockSpec(memory_space=pltpu.VMEM)] * len(arrays)
        + [pl.BlockSpec(memory_space=pl.ANY)] * len(loose),
        out_specs=[pl.BlockSpec(memory_space=pltpu.VMEM)] * len(outs),
        out_shape=[jax.ShapeDtypeStruct(shape, dtype) for shape, dtype in outs],
        scratch_shapes=scratch,
        compiler_params=pltpu.CompilerParams(vmem_limit_bytes=10 * 1024 * 1024),
        cost_estimate=pl.CostEstimate(
            flops=flops, bytes_accessed=sum(x.size * 2 for x in arrays), transcendentals=flops // (4 * HEAD_DIM)
        ),
    )(*scalars, *arrays, *loose)


def pack_kernel(copies, width, mask, offset, *refs):
    ins, outs, sems = refs[:3], refs[3:-1], refs[-1]
    h = lax.axis_index("head")
    started = []
    for n, (operand, d, begin, result, at, lanes) in enumerate(copies):
        source = ins[operand].at[:, pl.ds(pl.multiple_of((h ^ d) * width + begin, HEAD_DIM), lanes)]
        copy = pltpu.make_async_copy(source, outs[result].at[:, at : at + lanes], sems.at[n])
        copy.start()
        started.append(copy)
    if len(outs) > 1 + max(copy[3] for copy in copies):
        told = outs[-1]
        for group in range(told.shape[1] // 128):
            value = mask[0, group] if group < 4 else offset[0]
            rows = jnp.full((told.shape[0], 128), value, jnp.int32).astype(jnp.float32)
            told[:, group * 128 : (group + 1) * 128] = rows.astype(told.dtype)
    for copy in started:
        copy.wait()


def packed(operands, mask, offset, results, width, told):
    rows = operands[0].shape[0]
    copies, shapes = [], []
    for n, parts in enumerate(results):
        at = 0
        for operand, d, begin, lanes in parts:
            copies.append((operand, d, begin, n, at, lanes))
            at += lanes
        shapes.append(jax.ShapeDtypeStruct((rows, at), jnp.bfloat16))
    if told:
        shapes.append(jax.ShapeDtypeStruct((INFO_ROWS, told), jnp.bfloat16))
    return pl.pallas_call(
        functools.partial(pack_kernel, copies, width),
        in_specs=[pl.BlockSpec(memory_space=pltpu.SMEM)] * 2 + [pl.BlockSpec(memory_space=pltpu.HBM)] * 3,
        out_specs=[pl.BlockSpec(memory_space=pltpu.VMEM)] * len(shapes),
        out_shape=shapes,
        scratch_shapes=[pltpu.SemaphoreType.DMA((len(copies),))],
        compiler_params=pltpu.CompilerParams(vmem_limit_bytes=4 * 1024 * 1024),
    )(mask, offset, *operands)


def relayed_kernel(parts, mine, other, *outs):
    tile = other.shape[0]
    half = other.shape[1] // 2
    offset = jnp.max(mine[tile : tile + INFO_ROWS, 4 * 128 : 5 * 128].astype(jnp.float32))
    here = offset == (lax.axis_index("head") // 2).astype(jnp.float32)

    def take(ref):
        for (begin, end), out in zip(parts, outs):
            out[:, : end - begin] = ref[:tile, begin:end]
            out[:, end - begin :] = ref[:tile, half + begin : half + end]

    @pl.when(here)
    def _():
        take(mine)

    @pl.when(jnp.logical_not(here))
    def _():
        take(other)


def relayed(mine, other, parts):
    return pl.pallas_call(
        functools.partial(relayed_kernel, parts),
        in_specs=[pl.BlockSpec(memory_space=pltpu.VMEM)] * 2,
        out_specs=[pl.BlockSpec(memory_space=pltpu.VMEM)] * len(parts),
        out_shape=[jax.ShapeDtypeStruct((other.shape[0], 2 * (end - begin)), other.dtype) for begin, end in parts],
        compiler_params=pltpu.CompilerParams(vmem_limit_bytes=4 * 1024 * 1024),
    )(mine, other)


def swap_kernel(mine, other, q, out):
    cut = HOME * HEAD_DIM

    @pl.when(inner_frame())
    def _():
        relayed_kernel([(0, cut)], mine, other, out)

    @pl.when(jnp.logical_not(inner_frame()))
    def _():
        rows, count = out.shape[0], q.shape[1] - cut
        out[...] = jnp.zeros_like(out)
        out[:, :count] = q[:rows, cut:]
        out[:, cut : cut + count] = q[rows:, cut:]


def swapped(mine, other, q):
    return pl.pallas_call(
        swap_kernel,
        in_specs=[pl.BlockSpec(memory_space=pltpu.VMEM)] * 3,
        out_specs=pl.BlockSpec(memory_space=pltpu.VMEM),
        out_shape=jax.ShapeDtypeStruct((other.shape[0], 2 * HOME * HEAD_DIM), other.dtype),
        compiler_params=pltpu.CompilerParams(vmem_limit_bytes=4 * 1024 * 1024),
    )(mine, other, q)


def four_frames(queries, keys, values, pair_mask, tile_offset):
    h = lax.axis_index("head")
    rows, features = queries.shape
    width = features // 4
    heads = width // HEAD_DIM

    def columns(array, d):
        return lax.dynamic_slice_in_dim(array, (h ^ d) * width, width, axis=1)

    def beside(*arrays):
        return jnp.concatenate(arrays, axis=1)

    def below(*arrays):
        return jnp.concatenate(arrays, axis=0)

    def to_head(array, d):
        return lax.ppermute(array, "head", [(i, i ^ d) for i in range(4)])

    def along(array, pairs):
        return lax.ppermute(array, "frame", pairs)

    def across(array):
        pairs = [(4 * z + j, 4 * (3 - z) + j if z in (1, 2) else 4 * z + (j ^ 1)) for z in range(4) for j in range(4)]
        return lax.ppermute(array, ("frame", "head"), pairs)

    def after(array, earlier):
        return lax.optimization_barrier((array, earlier))[0]

    kv = [[columns(array, d) for array in (keys, values)] for d in range(4)]
    kv = lax.optimization_barrier(kv)
    got = to_head(beside(*kv[1], *kv[3]), 1)
    pay, q_own, q_far, told = packed(
        (queries, keys, values),
        pair_mask,
        tile_offset,
        [[(0, 1, 0, width), (0, 3, 0, width)], [(0, 0, 0, width)], [(0, 2, 0, width)]],
        width,
        2 * width,
    )
    mine = below(beside(*kv[0]), got[:, : 2 * width], told)
    other = to_head(below(beside(*kv[2]), got[:, 2 * width :]), 2)
    n1m = along(mine, OUTER)
    n2m = across(mine)
    n1o = along(other, OUTER)
    n2o = across(other)

    got = to_head(after(pay, got), 1)
    q = below(q_own, got[:, :width], to_head(after(below(q_far, got[:, width:]), other), 2))

    tile = 2 * rows
    cut = HOME * HEAD_DIM
    guests = heads - HOME
    r1_home, r1_rest = after(relayed(n1m, n1o, [(0, cut), (cut, width)]), n2m)
    r1_home = across(r1_home)
    swap = along(swapped(n2m, n2o, q), OUTER)

    def state(count):
        return [((count * 2 * tile, HEAD_DIM), jnp.float32)] * 3 + [((8, 128), jnp.float32)]

    def flops(chunks, tiles):
        return 4 * chunks * tiles * tile * tile * HEAD_DIM

    bf16 = jnp.bfloat16
    *near, done, r1_rest = run_kernel(
        functools.partial(near_kernel, 0, ((6, heads), (4, HOME)), own_queries, True),
        None,
        [q, mine, other, n1m, n1o, n2m, n2o, r1_rest],
        state(heads) + [(r1_rest.shape, bf16)],
        (tile, 6 * tile),
        flops(2 * heads, 6),
    )
    r1_rest = across(r1_rest)
    r3 = along(after(passed(r1_home, done), swap), OUTER)
    *guest_near, _ = run_kernel(
        functools.partial(near_kernel, HOME, ((4, guests), (0, 0)), guest_queries, False),
        None,
        [swap, mine, other, n1m, n1o],
        state(guests),
        (tile, 4 * tile),
        flops(2 * guests, 4),
    )
    (back,) = run_kernel(
        guest_kernel,
        None,
        [swap, *guest_near, n1m, n2m, n2o, r1_rest],
        [((2 * tile, width - cut), bf16)],
        (tile, 3 * tile),
        flops(2 * guests, 3),
    )
    back = along(back, OUTER)
    out = run_kernel(
        home_kernel,
        pair_mask,
        [q, *near],
        [((rows, cut), bf16)] * 4,
        (tile, 2 * tile),
        flops(2 * HOME, 2),
        loose=(r1_home, swap, r3),
    )
    pieces = [(to_head(out[d], d) if d else out[0], d, 0) for d in range(4)]
    out = run_kernel(
        rest_kernel,
        pair_mask,
        [q, *near, r1_rest, after(back, out[1])],
        [((rows, width - cut), bf16)] * 4,
        (tile, tile),
        flops(2 * guests, 1),
    )
    pieces += [(to_head(out[d], d) if d else out[0], d, cut) for d in range(4)]
    result = jnp.zeros((rows, features), jnp.bfloat16)
    for piece, d, begin in pieces:
        result = lax.dynamic_update_slice_in_dim(result, piece, (h ^ d) * width + begin, axis=1)
    return result


def solution(mesh):
    sizes = dict(mesh.shape)
    per_device = four_frames if sizes["frame"] == 4 and sizes["head"] == 4 else general
    return jax.shard_map(
        per_device,
        mesh=mesh,
        in_specs=(
            P(("parts", "frame", "head"), None),
            P(("parts", "frame", "head"), None),
            P(("parts", "frame", "head"), None),
            P(("parts", "frame"), None),
            P(("parts", "frame")),
        ),
        out_specs=P(("parts", "frame", "head"), None),
        check_vma=False,
    )
```

```python
import functools
import math

import jax
import jax.numpy as jnp
from jax import lax
from jax.experimental import pallas as pl
from jax.experimental.pallas import tpu as pltpu
from jax.sharding import PartitionSpec as P

HEAD_DIM = 128
SCALE = 1.0 / HEAD_DIM**0.5
LOG2E = math.log2(math.e)


def padded(x, sides, width):
    for axis, dim in sides:
        peers, length = (lax.axis_size(axis), x.shape[dim])
        up = [(i, (i + 1) % peers) for i in range(peers - 1)]
        down = [(j, i) for i, j in up]
        last = lax.slice_in_dim(x, length - width, length, axis=dim)
        leading = lax.slice_in_dim(x, 0, width, axis=dim)
        before = lax.ppermute(last, axis, up)
        after = lax.ppermute(leading, axis, down)
        x = jnp.concatenate([before, x, after], axis=dim)
    return x


def from_partner(x, axis, bit):
    return lax.ppermute(x, axis, [(i, i ^ 1 << bit) for i in range(lax.axis_size(axis))])


def subsample(frame_rows, offset, level, tiles, tile):
    step = 2**level
    width = frame_rows.shape[-1]
    grouped = frame_rows.reshape(tiles // step, step, tile, width)
    picked = lax.dynamic_index_in_dim(grouped, offset % step, 1, keepdims=False)
    return picked.reshape(-1, width)


def attend(query_rows, key_rows, value_rows, valid):
    count = query_rows.shape[0]
    heads = query_rows.shape[1] // HEAD_DIM
    q_three = query_rows.reshape(count, heads, HEAD_DIM).transpose(1, 0, 2)
    k_three = key_rows.reshape(-1, heads, HEAD_DIM).transpose(1, 0, 2)
    v_three = value_rows.reshape(-1, heads, HEAD_DIM).transpose(1, 0, 2)

    def one_head(operands):
        q_head, k_head, v_head = operands
        scores = jnp.dot(q_head, k_head.T, preferred_element_type=jnp.float32) * SCALE
        scores = jnp.where(valid[None, :] > 0, scores, -1e30)
        top = jnp.max(scores, axis=1, keepdims=True)
        weights = jnp.exp(scores - top) * valid[None, :]
        total = jnp.sum(weights, axis=1, keepdims=True)
        mixed = jnp.dot(weights.astype(jnp.bfloat16), v_head, preferred_element_type=jnp.float32)
        return mixed / total

    outcome = lax.map(one_head, (q_three, k_three, v_three))
    return outcome.transpose(1, 0, 2).reshape(count, heads * HEAD_DIM).astype(jnp.bfloat16)


def ordered(mine, theirs, upper):
    return jnp.where(upper == 1, jnp.concatenate([theirs, mine]), jnp.concatenate([mine, theirs]))


def general(queries, keys, values, pair_mask, tile_offset):
    frames_n = lax.axis_size("frame")
    current = lax.axis_index("frame")
    q_rows, k_rows, v_rows = (
        lax.all_to_all(queries, "head", split_axis=1, concat_axis=0, tiled=True),
        lax.all_to_all(keys, "head", split_axis=1, concat_axis=0, tiled=True),
        lax.all_to_all(values, "head", split_axis=1, concat_axis=0, tiled=True),
    )
    count = q_rows.shape[0]
    width = q_rows.shape[1]
    tiles = frames_n // 2
    tile = count // tiles
    depth = frames_n.bit_length() - 1
    stacked = jnp.stack([k_rows, v_rows])
    near = padded(stacked, (("frame", 1),), count)
    near_index = current - 1 + jnp.arange(3, dtype=jnp.int32)
    near_good = ((near_index >= 0) & (near_index < frames_n)).astype(jnp.float32)
    key_parts = [near[0]]
    value_parts = [near[1]]
    valid_parts = [jnp.repeat(near_good, count)]
    mask_row = pair_mask[0]
    offset = tile_offset[0]
    k_tiles = k_rows.reshape(tiles, tile, width)
    v_tiles = v_rows.reshape(tiles, tile, width)
    own = {}
    for level in range(1, depth):
        own[level] = (
            subsample(k_tiles, offset, level, tiles, tile)[None],
            subsample(v_tiles, offset, level, tiles, tile)[None],
        )
    sibling = {}
    cut = max(1, depth - 2)
    upper_levels = [level for level in range(1, depth) if level >= cut]
    k_pack = jnp.concatenate([own[level][0].reshape(-1, width) for level in upper_levels])
    v_pack = jnp.concatenate([own[level][1].reshape(-1, width) for level in upper_levels])
    k_every, v_every = (
        lax.all_gather(k_pack, "frame", axis=0, tiled=True),
        lax.all_gather(v_pack, "frame", axis=0, tiled=True),
    )
    k_every = k_every.reshape(frames_n, -1, width)
    v_every = v_every.reshape(frames_n, -1, width)
    position = 0
    for level in upper_levels:
        step = 2**level
        rows = count // step
        start = jnp.bitwise_xor(current // step, 1) * step
        block_k = lax.dynamic_slice_in_dim(k_every[:, position : position + rows], start, step, 0)
        block_v = lax.dynamic_slice_in_dim(v_every[:, position : position + rows], start, step, 0)
        sibling[level] = (block_k, block_v)
        position = position + rows
    swap_levels = [level for level in range(1, depth) if level < cut]
    growing = {level: own[level] for level in swap_levels}
    sections = cut if swap_levels else 0
    for bit in range(sections):
        active = [level for level in swap_levels if level >= bit]
        k_pack = jnp.concatenate([growing[level][0].reshape(-1, width) for level in active])
        v_pack = jnp.concatenate([growing[level][1].reshape(-1, width) for level in active])
        k_in, v_in = (from_partner(k_pack, "frame", bit), from_partner(v_pack, "frame", bit))
        upper = current // 2**bit % 2
        position = 0
        for level in active:
            shape = growing[level][0].shape
            size = shape[0] * shape[1]
            theirs_k = k_in[position : position + size].reshape(shape)
            theirs_v = v_in[position : position + size].reshape(shape)
            position = position + size
            if level == bit:
                sibling[level] = (theirs_k, theirs_v)
            else:
                growing[level] = (
                    ordered(growing[level][0], theirs_k, upper),
                    ordered(growing[level][1], theirs_v, upper),
                )
    for level in range(1, depth):
        step = 2**level
        start = jnp.bitwise_xor(current // step, 1) * step
        frame_ids = start + jnp.arange(step, dtype=jnp.int32)
        allowed = lax.dynamic_slice_in_dim(mask_row, start, step, 0)
        good = ((jnp.abs(frame_ids - current) >= 2) & (allowed == 1)).astype(jnp.float32)
        block_k, block_v = sibling[level]
        key_parts.append(block_k.reshape(-1, width))
        value_parts.append(block_v.reshape(-1, width))
        valid_parts.append(jnp.repeat(good, block_k.shape[1]))
    result = attend(
        q_rows,
        jnp.concatenate(key_parts),
        jnp.concatenate(value_parts),
        jnp.concatenate(valid_parts),
    )
    return lax.all_to_all(result, "head", split_axis=0, concat_axis=1, tiled=True)


HOME = 3
INFO_ROWS = 16
OUTER = [(0, 1), (1, 0), (2, 3), (3, 2)]
FACTOR = SCALE * LOG2E


def inner_frame():
    z = lax.axis_index("frame")
    return (z == 1) | (z == 2)


def head_lanes(first, i):
    return pl.ds(pl.multiple_of((first + i) * HEAD_DIM, HEAD_DIM), HEAD_DIM)


def keys_of(ref, first, i, rows):
    return ref[:rows, head_lanes(first, i)]


def values_of(ref, first, i, rows):
    return ref[:rows, head_lanes(ref.shape[1] // (2 * HEAD_DIM) + first, i)]


def dot_keys(q, k):
    return lax.dot_general(q, k, (((1,), (1,)), ((), ())), preferred_element_type=jnp.float32)


def fold(x, op):
    result = x[:, :128]
    for at in range(128, x.shape[1], 128):
        result = op(result, x[:, at : at + 128])
    return result


def near_kernel(first, counts, queries_of, carries, *refs):
    n_outs = 4 if carries else 3
    ins, outs, rooms = refs[: -2 - n_outs], refs[-2 - n_outs : -2], refs[-2:]
    queries, tiles = ins[0], ins[1:]
    mixed_out, levels, done = outs[:3]
    rows = rooms[0].shape[0]
    done[...] = jnp.zeros_like(done)
    if carries:
        outs[3][...] = ins[-1][...]

    def one_head(used, i):
        found = []
        for half, held in enumerate(rooms):
            q = queries_of(queries, half, i)
            best = None
            for at, ref in enumerate(used):
                s = dot_keys(q, keys_of(ref, first, i, rows))
                held[:, at * rows : (at + 1) * rows] = s
                part = fold(s, jnp.maximum)
                best = part if best is None else jnp.maximum(best, part)
            found.append(jnp.max(best, axis=1, keepdims=True))
        for half, (top, held) in enumerate(zip(found, rooms)):
            total, mixed = None, None
            for at, ref in enumerate(used):
                w = jnp.exp2((held[:, at * rows : (at + 1) * rows] - top) * FACTOR)
                mix = jnp.dot(w.astype(jnp.bfloat16), values_of(ref, first, i, rows), preferred_element_type=jnp.float32)
                part = fold(w, jnp.add)
                mixed = mix if mixed is None else mixed + mix
                total = part if total is None else total + part
            span = pl.ds(pl.multiple_of((2 * i + half) * rows, rows), rows)
            total = jnp.broadcast_to(jnp.sum(total, axis=1, keepdims=True), (rows, HEAD_DIM))
            mixed_out[span] = mixed * (1.0 / total)
            levels[span] = jnp.broadcast_to(top, (rows, HEAD_DIM)) * FACTOR + jnp.log2(total)

    for wanted, (n_tiles, n_heads) in zip((True, False), counts):
        if n_heads:

            @pl.when(inner_frame() == wanted)
            def _():
                def step(i, carry):
                    one_head(tiles[:n_tiles], i)
                    return carry

                lax.fori_loop(0, n_heads, step, 0)


def own_queries(ref, half, i):
    rows = ref.shape[0] // 2
    return ref[half * rows : (half + 1) * rows, head_lanes(0, i)]


def guest_queries(ref, half, i):
    return ref[:, head_lanes(half * HOME, i)]


def far_tile(ref, first, valid):
    return functools.partial(keys_of, ref, first), functools.partial(values_of, ref, first), valid


def far_pair(keys, values, valid):
    return functools.partial(keys_of, keys, 0), functools.partial(keys_of, values, 0), valid


def add_far(q, state, slots, i, begin, held):
    rows = q.shape[0]
    span = pl.ds(pl.multiple_of(begin, rows), rows)
    near_level = state[1][span]
    level = near_level
    for at, (keys, _, valid) in enumerate(slots):
        s = dot_keys(q, keys(i, rows)) * FACTOR
        held[:, at * rows : (at + 1) * rows] = s
        best = jnp.broadcast_to(jnp.max(fold(s, jnp.maximum), axis=1, keepdims=True), near_level.shape)
        level = jnp.maximum(level, jnp.where(valid, best, -1e30))
    shrink = jnp.exp2(near_level - level)
    mixed = state[0][span] * shrink
    total = None
    for at, (_, values, valid) in enumerate(slots):
        used = jnp.where(valid, level, 1e30)
        parts = []
        for lane in range(at * rows, (at + 1) * rows, HEAD_DIM):
            part = jnp.exp2(held[:, lane : lane + HEAD_DIM] - used)
            total = part if total is None else total + part
            parts.append(part.astype(jnp.bfloat16))
        mixed += jnp.dot(jnp.concatenate(parts, axis=1), values(i, rows), preferred_element_type=jnp.float32)
    total = jnp.broadcast_to(jnp.sum(total, axis=1, keepdims=True), near_level.shape) + shrink
    return (mixed * (1.0 / total)).astype(jnp.bfloat16)


def each_head(heads, body):
    def step(i, carry):
        body(i)
        return carry

    lax.fori_loop(0, heads, step, 0)


def finish_own(first, queries, state, slots, outs, rooms):
    piece = outs[0].shape[0]
    rows = 2 * piece

    def body(i):
        for half, held in enumerate(rooms):
            q = queries[half * rows : (half + 1) * rows, head_lanes(first, i)]
            value = add_far(q, state, slots, i, (2 * (first + i) + half) * rows, held)
            outs[2 * half][:, head_lanes(0, i)] = value[:piece]
            outs[2 * half + 1][:, head_lanes(0, i)] = value[piece:]

    each_head(outs[0].shape[1] // HEAD_DIM, body)


def home_kernel(mask, q, mixed, levels, r1k, r1v, r2, r3k, r3v, *rest):
    outs, rooms = rest[:4], rest[4:]
    z = lax.axis_index("frame")
    near2 = mask[0, z ^ 2] == 1

    @pl.when(inner_frame())
    def _():
        finish_own(0, q, (mixed, levels), [far_pair(r1k, r1v, near2)], outs, rooms)

    @pl.when(jnp.logical_not(inner_frame()))
    def _():
        slots = [far_tile(r2, 0, near2), far_pair(r3k, r3v, mask[0, z ^ 3] == 1)]
        finish_own(0, q, (mixed, levels), slots, outs, rooms)


def guest_kernel(q, mixed, levels, n1m, n2m, n2o, r1, out, *rooms):
    rows = r1.shape[0]
    z = lax.axis_index("frame")

    def told(ref, group):
        return ref[rows : rows + 1, group * 128 : (group + 1) * 128].astype(jnp.float32)

    @pl.when(inner_frame())
    def _():
        near2 = jnp.where(z == 1, told(n1m, 2), told(n1m, 1)) > 0.5
        near1 = jnp.where(z == 1, told(n1m, 3), told(n1m, 0)) > 0.5
        picked = told(n2m, 4) == (lax.axis_index("head") // 2).astype(jnp.float32)
        slots = [
            far_tile(n2m, HOME, near2 & picked),
            far_tile(n2o, HOME, near2 & jnp.logical_not(picked)),
            far_tile(r1, 0, near1),
        ]

        def body(i):
            for half, held in enumerate(rooms):
                value = add_far(guest_queries(q, half, i), (mixed, levels), slots, i, (2 * i + half) * rows, held)
                out[half * rows : (half + 1) * rows, head_lanes(0, i)] = value

        each_head(out.shape[1] // HEAD_DIM, body)


def rest_kernel(mask, q, mixed, levels, r1, back, *rest):
    outs, rooms = rest[:4], rest[4:]
    z = lax.axis_index("frame")

    @pl.when(inner_frame())
    def _():
        finish_own(HOME, q, (mixed, levels), [far_tile(r1, 0, mask[0, z ^ 2] == 1)], outs, rooms)

    @pl.when(jnp.logical_not(inner_frame()))
    def _():
        for d, out in enumerate(outs):
            out[...] = back[d * out.shape[0] : (d + 1) * out.shape[0]]


def pass_kernel(done, *refs):
    half = len(refs) // 2
    for x, out in zip(refs[:half], refs[half:]):
        out[...] = x[...]


def passed(done, *arrays):
    return pl.pallas_call(
        pass_kernel,
        in_specs=[pl.BlockSpec(memory_space=pltpu.VMEM)] * (1 + len(arrays)),
        out_specs=[pl.BlockSpec(memory_space=pltpu.VMEM)] * len(arrays),
        out_shape=[jax.ShapeDtypeStruct(x.shape, x.dtype) for x in arrays],
        compiler_params=pltpu.CompilerParams(vmem_limit_bytes=4 * 1024 * 1024),
    )(done, *arrays)


def run_kernel(kernel, mask, arrays, outs, room, flops, grant):
    scalars = [] if mask is None else [mask]
    return pl.pallas_call(
        kernel,
        in_specs=[pl.BlockSpec(memory_space=pltpu.SMEM)] * len(scalars)
        + [pl.BlockSpec(memory_space=pltpu.VMEM)] * len(arrays),
        out_specs=[pl.BlockSpec(memory_space=pltpu.VMEM)] * len(outs),
        out_shape=[jax.ShapeDtypeStruct(shape, dtype) for shape, dtype in outs],
        scratch_shapes=[pltpu.VMEM(room, jnp.float32)] * 2,
        compiler_params=pltpu.CompilerParams(vmem_limit_bytes=grant * 1024 * 1024),
        cost_estimate=pl.CostEstimate(
            flops=flops, bytes_accessed=sum(x.size * 2 for x in arrays), transcendentals=flops // (4 * HEAD_DIM)
        ),
    )(*scalars, *arrays)


def pack_kernel(copies, width, mask, offset, *refs):
    ins, outs, sems = refs[:3], refs[3:-1], refs[-1]
    h = lax.axis_index("head")
    started = []
    for n, (operand, d, begin, result, at, lanes) in enumerate(copies):
        source = ins[operand].at[:, pl.ds(pl.multiple_of((h ^ d) * width + begin, HEAD_DIM), lanes)]
        copy = pltpu.make_async_copy(source, outs[result].at[:, at : at + lanes], sems.at[n])
        copy.start()
        started.append(copy)
    if len(outs) > 1 + max(copy[3] for copy in copies):
        told = outs[-1]
        for group in range(told.shape[1] // 128):
            value = mask[0, group] if group < 4 else offset[0]
            rows = jnp.full((told.shape[0], 128), value, jnp.int32).astype(jnp.float32)
            told[:, group * 128 : (group + 1) * 128] = rows.astype(told.dtype)
    for copy in started:
        copy.wait()


def packed(operands, mask, offset, results, width, told):
    rows = operands[0].shape[0]
    copies, shapes = [], []
    for n, parts in enumerate(results):
        at = 0
        for operand, d, begin, lanes in parts:
            copies.append((operand, d, begin, n, at, lanes))
            at += lanes
        shapes.append(jax.ShapeDtypeStruct((rows, at), jnp.bfloat16))
    if told:
        shapes.append(jax.ShapeDtypeStruct((INFO_ROWS, told), jnp.bfloat16))
    return pl.pallas_call(
        functools.partial(pack_kernel, copies, width),
        in_specs=[pl.BlockSpec(memory_space=pltpu.SMEM)] * 2 + [pl.BlockSpec(memory_space=pltpu.HBM)] * 3,
        out_specs=[pl.BlockSpec(memory_space=pltpu.VMEM)] * len(shapes),
        out_shape=shapes,
        scratch_shapes=[pltpu.SemaphoreType.DMA((len(copies),))],
        compiler_params=pltpu.CompilerParams(vmem_limit_bytes=4 * 1024 * 1024),
    )(mask, offset, *operands)


def relayed_kernel(parts, mine, other, *outs):
    tile = other.shape[0]
    offset = jnp.max(mine[tile : tile + INFO_ROWS, 4 * 128 : 5 * 128].astype(jnp.float32))
    here = offset == (lax.axis_index("head") // 2).astype(jnp.float32)

    def take(ref):
        for spans, out in zip(parts, outs):
            at = 0
            for begin, end in spans:
                out[:, at : at + end - begin] = ref[:tile, begin:end]
                at += end - begin

    @pl.when(here)
    def _():
        take(mine)

    @pl.when(jnp.logical_not(here))
    def _():
        take(other)


def relayed(mine, other, parts):
    widths = [sum(end - begin for begin, end in spans) for spans in parts]
    return pl.pallas_call(
        functools.partial(relayed_kernel, parts),
        in_specs=[pl.BlockSpec(memory_space=pltpu.VMEM)] * 2,
        out_specs=[pl.BlockSpec(memory_space=pltpu.VMEM)] * len(parts),
        out_shape=[jax.ShapeDtypeStruct((other.shape[0], width), other.dtype) for width in widths],
        compiler_params=pltpu.CompilerParams(vmem_limit_bytes=4 * 1024 * 1024),
    )(mine, other)


def swap_kernel(mine, other, q, out):
    cut = HOME * HEAD_DIM

    @pl.when(inner_frame())
    def _():
        half = other.shape[1] // 2
        relayed_kernel([[(0, cut), (half, half + cut)]], mine, other, out)

    @pl.when(jnp.logical_not(inner_frame()))
    def _():
        rows, count = out.shape[0], q.shape[1] - cut
        out[...] = jnp.zeros_like(out)
        out[:, :count] = q[:rows, cut:]
        out[:, cut : cut + count] = q[rows:, cut:]


def swapped(mine, other, q):
    return pl.pallas_call(
        swap_kernel,
        in_specs=[pl.BlockSpec(memory_space=pltpu.VMEM)] * 3,
        out_specs=pl.BlockSpec(memory_space=pltpu.VMEM),
        out_shape=jax.ShapeDtypeStruct((other.shape[0], 2 * HOME * HEAD_DIM), other.dtype),
        compiler_params=pltpu.CompilerParams(vmem_limit_bytes=4 * 1024 * 1024),
    )(mine, other, q)


def four_frames(queries, keys, values, pair_mask, tile_offset):
    h = lax.axis_index("head")
    rows, features = queries.shape
    width = features // 4
    heads = width // HEAD_DIM

    def columns(array, d):
        return lax.dynamic_slice_in_dim(array, (h ^ d) * width, width, axis=1)

    def beside(*arrays):
        return jnp.concatenate(arrays, axis=1)

    def below(*arrays):
        return jnp.concatenate(arrays, axis=0)

    def to_head(array, d):
        return lax.ppermute(array, "head", [(i, i ^ d) for i in range(4)])

    def along(array, pairs):
        return lax.ppermute(array, "frame", pairs)

    def across(array):
        pairs = [(4 * z + j, 4 * (3 - z) + j if z in (1, 2) else 4 * z + (j ^ 1)) for z in range(4) for j in range(4)]
        return lax.ppermute(array, ("frame", "head"), pairs)

    def after(array, earlier):
        return lax.optimization_barrier((array, earlier))[0]

    kv = [[columns(array, d) for array in (keys, values)] for d in range(4)]
    kv = lax.optimization_barrier(kv)
    got = to_head(beside(*kv[1], *kv[3]), 1)
    pay, q_own, q_far, told = packed(
        (queries, keys, values),
        pair_mask,
        tile_offset,
        [[(0, 1, 0, width), (0, 3, 0, width)], [(0, 0, 0, width)], [(0, 2, 0, width)]],
        width,
        2 * width,
    )
    mine = below(beside(*kv[0]), got[:, : 2 * width], told)
    other = to_head(below(beside(*kv[2]), got[:, 2 * width :]), 2)
    n1m = along(mine, OUTER)
    n2m = across(mine)
    n1o = along(other, OUTER)
    n2o = across(other)

    got = to_head(after(pay, got), 1)
    q = below(q_own, got[:, :width], to_head(after(below(q_far, got[:, width:]), other), 2))

    tile = 2 * rows
    cut = HOME * HEAD_DIM
    guests = heads - HOME
    r1k, r1v, r1_rest = after(
        relayed(n1m, n1o, [[(0, cut)], [(width, width + cut)], [(cut, width), (width + cut, 2 * width)]]), n2m
    )
    r1k = across(r1k)
    swap = along(swapped(n2m, n2o, q), OUTER)
    r1v = across(after(r1v, n2o))

    def state(count):
        return [((count * 2 * tile, HEAD_DIM), jnp.float32)] * 2 + [((8, 128), jnp.float32)]

    def flops(chunks, tiles):
        return 4 * chunks * tiles * tile * tile * HEAD_DIM

    bf16 = jnp.bfloat16
    *near, done = run_kernel(
        functools.partial(near_kernel, 0, ((6, heads), (4, HOME)), own_queries, False),
        None,
        [q, mine, other, n1m, n1o, n2m, n2o],
        state(heads),
        (tile, 6 * tile),
        flops(2 * heads, 6),
        8,
    )
    r3k, r1_rest = passed(done, r1k, r1_rest)
    r3k = along(r3k, OUTER)
    r1_rest = across(r1_rest)
    r3v = along(after(r1v, swap), OUTER)
    *guest_near, _ = run_kernel(
        functools.partial(near_kernel, HOME, ((4, guests), (0, 0)), guest_queries, False),
        None,
        [swap, mine, other, n1m, n1o],
        state(guests),
        (tile, 4 * tile),
        flops(2 * guests, 4),
        6,
    )
    (back,) = run_kernel(
        guest_kernel,
        None,
        [swap, *guest_near, n1m, n2m, n2o, r1_rest],
        [((2 * tile, width - cut), bf16)],
        (tile, 3 * tile),
        flops(2 * guests, 3),
        6,
    )
    back = along(back, OUTER)
    out = run_kernel(
        home_kernel,
        pair_mask,
        [q, *near, r1k, r1v, swap, r3k, r3v],
        [((rows, cut), bf16)] * 4,
        (tile, 2 * tile),
        flops(2 * HOME, 2),
        6,
    )
    pieces = [(to_head(out[d], d) if d else out[0], d, 0) for d in range(4)]
    out = run_kernel(
        rest_kernel,
        pair_mask,
        [q, *near, r1_rest, after(back, out[1])],
        [((rows, width - cut), bf16)] * 4,
        (tile, tile),
        flops(2 * guests, 1),
        6,
    )
    pieces += [(to_head(out[d], d) if d else out[0], d, cut) for d in range(4)]
    result = jnp.zeros((rows, features), jnp.bfloat16)
    for piece, d, begin in pieces:
        result = lax.dynamic_update_slice_in_dim(result, piece, (h ^ d) * width + begin, axis=1)
    return result


def solution(mesh):
    sizes = dict(mesh.shape)
    per_device = four_frames if sizes["frame"] == 4 and sizes["head"] == 4 else general
    return jax.shard_map(
        per_device,
        mesh=mesh,
        in_specs=(
            P(("parts", "frame", "head"), None),
            P(("parts", "frame", "head"), None),
            P(("parts", "frame", "head"), None),
            P(("parts", "frame"), None),
            P(("parts", "frame")),
        ),
        out_specs=P(("parts", "frame", "head"), None),
        check_vma=False,
    )
```

```python
import functools
import math

import jax
import jax.numpy as jnp
from jax import lax
from jax.experimental import pallas as pl
from jax.experimental.pallas import tpu as pltpu
from jax.sharding import PartitionSpec as P

HEAD_DIM = 128
SCALE = 1.0 / HEAD_DIM**0.5
LOG2E = math.log2(math.e)


def padded(x, sides, width):
    for axis, dim in sides:
        peers, length = (lax.axis_size(axis), x.shape[dim])
        up = [(i, (i + 1) % peers) for i in range(peers - 1)]
        down = [(j, i) for i, j in up]
        last = lax.slice_in_dim(x, length - width, length, axis=dim)
        leading = lax.slice_in_dim(x, 0, width, axis=dim)
        before = lax.ppermute(last, axis, up)
        after = lax.ppermute(leading, axis, down)
        x = jnp.concatenate([before, x, after], axis=dim)
    return x


def from_partner(x, axis, bit):
    return lax.ppermute(x, axis, [(i, i ^ 1 << bit) for i in range(lax.axis_size(axis))])


def subsample(frame_rows, offset, level, tiles, tile):
    step = 2**level
    width = frame_rows.shape[-1]
    grouped = frame_rows.reshape(tiles // step, step, tile, width)
    picked = lax.dynamic_index_in_dim(grouped, offset % step, 1, keepdims=False)
    return picked.reshape(-1, width)


def attend(query_rows, key_rows, value_rows, valid):
    count = query_rows.shape[0]
    heads = query_rows.shape[1] // HEAD_DIM
    q_three = query_rows.reshape(count, heads, HEAD_DIM).transpose(1, 0, 2)
    k_three = key_rows.reshape(-1, heads, HEAD_DIM).transpose(1, 0, 2)
    v_three = value_rows.reshape(-1, heads, HEAD_DIM).transpose(1, 0, 2)

    def one_head(operands):
        q_head, k_head, v_head = operands
        scores = jnp.dot(q_head, k_head.T, preferred_element_type=jnp.float32) * SCALE
        scores = jnp.where(valid[None, :] > 0, scores, -1e30)
        top = jnp.max(scores, axis=1, keepdims=True)
        weights = jnp.exp(scores - top) * valid[None, :]
        total = jnp.sum(weights, axis=1, keepdims=True)
        mixed = jnp.dot(weights.astype(jnp.bfloat16), v_head, preferred_element_type=jnp.float32)
        return mixed / total

    outcome = lax.map(one_head, (q_three, k_three, v_three))
    return outcome.transpose(1, 0, 2).reshape(count, heads * HEAD_DIM).astype(jnp.bfloat16)


def ordered(mine, theirs, upper):
    return jnp.where(upper == 1, jnp.concatenate([theirs, mine]), jnp.concatenate([mine, theirs]))


def general(queries, keys, values, pair_mask, tile_offset):
    frames_n = lax.axis_size("frame")
    current = lax.axis_index("frame")
    q_rows, k_rows, v_rows = (
        lax.all_to_all(queries, "head", split_axis=1, concat_axis=0, tiled=True),
        lax.all_to_all(keys, "head", split_axis=1, concat_axis=0, tiled=True),
        lax.all_to_all(values, "head", split_axis=1, concat_axis=0, tiled=True),
    )
    count = q_rows.shape[0]
    width = q_rows.shape[1]
    tiles = frames_n // 2
    tile = count // tiles
    depth = frames_n.bit_length() - 1
    stacked = jnp.stack([k_rows, v_rows])
    near = padded(stacked, (("frame", 1),), count)
    near_index = current - 1 + jnp.arange(3, dtype=jnp.int32)
    near_good = ((near_index >= 0) & (near_index < frames_n)).astype(jnp.float32)
    key_parts = [near[0]]
    value_parts = [near[1]]
    valid_parts = [jnp.repeat(near_good, count)]
    mask_row = pair_mask[0]
    offset = tile_offset[0]
    k_tiles = k_rows.reshape(tiles, tile, width)
    v_tiles = v_rows.reshape(tiles, tile, width)
    own = {}
    for level in range(1, depth):
        own[level] = (
            subsample(k_tiles, offset, level, tiles, tile)[None],
            subsample(v_tiles, offset, level, tiles, tile)[None],
        )
    sibling = {}
    cut = max(1, depth - 2)
    upper_levels = [level for level in range(1, depth) if level >= cut]
    k_pack = jnp.concatenate([own[level][0].reshape(-1, width) for level in upper_levels])
    v_pack = jnp.concatenate([own[level][1].reshape(-1, width) for level in upper_levels])
    k_every, v_every = (
        lax.all_gather(k_pack, "frame", axis=0, tiled=True),
        lax.all_gather(v_pack, "frame", axis=0, tiled=True),
    )
    k_every = k_every.reshape(frames_n, -1, width)
    v_every = v_every.reshape(frames_n, -1, width)
    position = 0
    for level in upper_levels:
        step = 2**level
        rows = count // step
        start = jnp.bitwise_xor(current // step, 1) * step
        block_k = lax.dynamic_slice_in_dim(k_every[:, position : position + rows], start, step, 0)
        block_v = lax.dynamic_slice_in_dim(v_every[:, position : position + rows], start, step, 0)
        sibling[level] = (block_k, block_v)
        position = position + rows
    swap_levels = [level for level in range(1, depth) if level < cut]
    growing = {level: own[level] for level in swap_levels}
    sections = cut if swap_levels else 0
    for bit in range(sections):
        active = [level for level in swap_levels if level >= bit]
        k_pack = jnp.concatenate([growing[level][0].reshape(-1, width) for level in active])
        v_pack = jnp.concatenate([growing[level][1].reshape(-1, width) for level in active])
        k_in, v_in = (from_partner(k_pack, "frame", bit), from_partner(v_pack, "frame", bit))
        upper = current // 2**bit % 2
        position = 0
        for level in active:
            shape = growing[level][0].shape
            size = shape[0] * shape[1]
            theirs_k = k_in[position : position + size].reshape(shape)
            theirs_v = v_in[position : position + size].reshape(shape)
            position = position + size
            if level == bit:
                sibling[level] = (theirs_k, theirs_v)
            else:
                growing[level] = (
                    ordered(growing[level][0], theirs_k, upper),
                    ordered(growing[level][1], theirs_v, upper),
                )
    for level in range(1, depth):
        step = 2**level
        start = jnp.bitwise_xor(current // step, 1) * step
        frame_ids = start + jnp.arange(step, dtype=jnp.int32)
        allowed = lax.dynamic_slice_in_dim(mask_row, start, step, 0)
        good = ((jnp.abs(frame_ids - current) >= 2) & (allowed == 1)).astype(jnp.float32)
        block_k, block_v = sibling[level]
        key_parts.append(block_k.reshape(-1, width))
        value_parts.append(block_v.reshape(-1, width))
        valid_parts.append(jnp.repeat(good, block_k.shape[1]))
    result = attend(
        q_rows,
        jnp.concatenate(key_parts),
        jnp.concatenate(value_parts),
        jnp.concatenate(valid_parts),
    )
    return lax.all_to_all(result, "head", split_axis=0, concat_axis=1, tiled=True)


HOME = 3
INFO_ROWS = 16
OUTER = [(0, 1), (1, 0), (2, 3), (3, 2)]
FACTOR = SCALE * LOG2E


def inner_frame():
    z = lax.axis_index("frame")
    return (z == 1) | (z == 2)


def head_lanes(first, i):
    return pl.ds(pl.multiple_of((first + i) * HEAD_DIM, HEAD_DIM), HEAD_DIM)


def keys_of(ref, first, i, rows):
    return ref[:rows, head_lanes(first, i)]


def values_of(ref, first, i, rows):
    return ref[:rows, head_lanes(ref.shape[1] // (2 * HEAD_DIM) + first, i)]


def dot_keys(q, k):
    return lax.dot_general(q, k, (((1,), (1,)), ((), ())), preferred_element_type=jnp.float32)


def fold(x, op):
    result = x[:, :128]
    for at in range(128, x.shape[1], 128):
        result = op(result, x[:, at : at + 128])
    return result


def near_kernel(first, counts, queries_of, carries, *refs):
    n_outs = 4 if carries else 3
    ins, outs, rooms = refs[: -2 - n_outs], refs[-2 - n_outs : -2], refs[-2:]
    queries, tiles = ins[0], ins[1:]
    mixed_out, levels, done = outs[:3]
    rows = rooms[0].shape[0]
    done[...] = jnp.zeros_like(done)
    if carries:
        outs[3][...] = ins[-1][...]

    def one_head(used, i):
        found = []
        for half, held in enumerate(rooms):
            q = queries_of(queries, half, i)
            best = None
            for at, ref in enumerate(used):
                s = dot_keys(q, keys_of(ref, first, i, rows))
                held[:, at * rows : (at + 1) * rows] = s
                part = fold(s, jnp.maximum)
                best = part if best is None else jnp.maximum(best, part)
            found.append(jnp.max(best, axis=1, keepdims=True))
        for half, (top, held) in enumerate(zip(found, rooms)):
            total, mixed = None, None
            for at, ref in enumerate(used):
                w = jnp.exp2((held[:, at * rows : (at + 1) * rows] - top) * FACTOR)
                mix = jnp.dot(w.astype(jnp.bfloat16), values_of(ref, first, i, rows), preferred_element_type=jnp.float32)
                part = fold(w, jnp.add)
                mixed = mix if mixed is None else mixed + mix
                total = part if total is None else total + part
            span = pl.ds(pl.multiple_of((2 * i + half) * rows, rows), rows)
            total = jnp.broadcast_to(jnp.sum(total, axis=1, keepdims=True), (rows, HEAD_DIM))
            mixed_out[span] = mixed * (1.0 / total)
            levels[span] = jnp.broadcast_to(top, (rows, HEAD_DIM)) * FACTOR + jnp.log2(total)

    for wanted, (n_tiles, n_heads) in zip((True, False), counts):
        if n_heads:

            @pl.when(inner_frame() == wanted)
            def _():
                def step(i, carry):
                    one_head(tiles[:n_tiles], i)
                    return carry

                lax.fori_loop(0, n_heads, step, 0)


def own_queries(ref, half, i):
    rows = ref.shape[0] // 2
    return ref[half * rows : (half + 1) * rows, head_lanes(0, i)]


def guest_queries(ref, half, i):
    return ref[:, head_lanes(half * HOME, i)]


def far_tile(ref, first, valid):
    return functools.partial(keys_of, ref, first), functools.partial(values_of, ref, first), valid


def far_pair(keys, values, valid):
    return functools.partial(keys_of, keys, 0), functools.partial(keys_of, values, 0), valid


def add_far(q, state, slots, i, begin, held):
    rows = q.shape[0]
    span = pl.ds(pl.multiple_of(begin, rows), rows)
    near_level = state[1][span]
    level = near_level
    for at, (keys, _, valid) in enumerate(slots):
        s = dot_keys(q, keys(i, rows)) * FACTOR
        held[:, at * rows : (at + 1) * rows] = s
        best = jnp.broadcast_to(jnp.max(fold(s, jnp.maximum), axis=1, keepdims=True), near_level.shape)
        level = jnp.maximum(level, jnp.where(valid, best, -1e30))
    shrink = jnp.exp2(near_level - level)
    mixed = state[0][span] * shrink
    total = None
    for at, (_, values, valid) in enumerate(slots):
        used = jnp.where(valid, level, 1e30)
        parts = []
        for lane in range(at * rows, (at + 1) * rows, HEAD_DIM):
            part = jnp.exp2(held[:, lane : lane + HEAD_DIM] - used)
            total = part if total is None else total + part
            parts.append(part.astype(jnp.bfloat16))
        mixed += jnp.dot(jnp.concatenate(parts, axis=1), values(i, rows), preferred_element_type=jnp.float32)
    total = jnp.broadcast_to(jnp.sum(total, axis=1, keepdims=True), near_level.shape) + shrink
    return (mixed * (1.0 / total)).astype(jnp.bfloat16)


def each_head(heads, body):
    def step(i, carry):
        body(i)
        return carry

    lax.fori_loop(0, heads, step, 0)


def finish_own(first, queries, state, slots, outs, rooms):
    piece = outs[0].shape[0]
    rows = 2 * piece

    def body(i):
        for half, held in enumerate(rooms):
            q = queries[half * rows : (half + 1) * rows, head_lanes(first, i)]
            value = add_far(q, state, slots, i, (2 * (first + i) + half) * rows, held)
            outs[2 * half][:, head_lanes(0, i)] = value[:piece]
            outs[2 * half + 1][:, head_lanes(0, i)] = value[piece:]

    each_head(outs[0].shape[1] // HEAD_DIM, body)


def home_kernel(mask, q, mixed, levels, r1k, r1v, r2, r3k, r3v, *rest):
    outs, rooms = rest[:4], rest[4:]
    z = lax.axis_index("frame")
    near2 = mask[0, z ^ 2] == 1

    @pl.when(inner_frame())
    def _():
        finish_own(0, q, (mixed, levels), [far_pair(r1k, r1v, near2)], outs, rooms)

    @pl.when(jnp.logical_not(inner_frame()))
    def _():
        slots = [far_tile(r2, 0, near2), far_pair(r3k, r3v, mask[0, z ^ 3] == 1)]
        finish_own(0, q, (mixed, levels), slots, outs, rooms)


def guest_kernel(q, mixed, levels, n1m, n2m, n2o, r1, out, *rooms):
    rows = r1.shape[0]
    z = lax.axis_index("frame")

    def told(ref, group):
        return ref[rows : rows + 1, group * 128 : (group + 1) * 128].astype(jnp.float32)

    @pl.when(inner_frame())
    def _():
        near2 = jnp.where(z == 1, told(n1m, 2), told(n1m, 1)) > 0.5
        near1 = jnp.where(z == 1, told(n1m, 3), told(n1m, 0)) > 0.5
        picked = told(n2m, 4) == (lax.axis_index("head") // 2).astype(jnp.float32)
        slots = [
            far_tile(n2m, HOME, near2 & picked),
            far_tile(n2o, HOME, near2 & jnp.logical_not(picked)),
            far_tile(r1, 0, near1),
        ]

        def body(i):
            for half, held in enumerate(rooms):
                value = add_far(guest_queries(q, half, i), (mixed, levels), slots, i, (2 * i + half) * rows, held)
                out[half * rows : (half + 1) * rows, head_lanes(0, i)] = value

        each_head(out.shape[1] // HEAD_DIM, body)


def rest_kernel(mask, q, mixed, levels, r1, back, *rest):
    outs, rooms = rest[:4], rest[4:]
    z = lax.axis_index("frame")

    @pl.when(inner_frame())
    def _():
        finish_own(HOME, q, (mixed, levels), [far_tile(r1, 0, mask[0, z ^ 2] == 1)], outs, rooms)

    @pl.when(jnp.logical_not(inner_frame()))
    def _():
        for d, out in enumerate(outs):
            out[...] = back[d * out.shape[0] : (d + 1) * out.shape[0]]


def pass_kernel(done, *refs):
    half = len(refs) // 2
    for x, out in zip(refs[:half], refs[half:]):
        out[...] = x[...]


def passed(done, *arrays):
    return pl.pallas_call(
        pass_kernel,
        in_specs=[pl.BlockSpec(memory_space=pltpu.VMEM)] * (1 + len(arrays)),
        out_specs=[pl.BlockSpec(memory_space=pltpu.VMEM)] * len(arrays),
        out_shape=[jax.ShapeDtypeStruct(x.shape, x.dtype) for x in arrays],
        compiler_params=pltpu.CompilerParams(vmem_limit_bytes=4 * 1024 * 1024),
    )(done, *arrays)


def run_kernel(kernel, mask, arrays, outs, room, flops, grant):
    scalars = [] if mask is None else [mask]
    return pl.pallas_call(
        kernel,
        in_specs=[pl.BlockSpec(memory_space=pltpu.SMEM)] * len(scalars)
        + [pl.BlockSpec(memory_space=pltpu.VMEM)] * len(arrays),
        out_specs=[pl.BlockSpec(memory_space=pltpu.VMEM)] * len(outs),
        out_shape=[jax.ShapeDtypeStruct(shape, dtype) for shape, dtype in outs],
        scratch_shapes=[pltpu.VMEM(room, jnp.float32)] * 2,
        compiler_params=pltpu.CompilerParams(vmem_limit_bytes=grant * 1024 * 1024),
        cost_estimate=pl.CostEstimate(
            flops=flops, bytes_accessed=sum(x.size * 2 for x in arrays), transcendentals=flops // (4 * HEAD_DIM)
        ),
    )(*scalars, *arrays)


def pack_kernel(copies, width, mask, offset, *refs):
    ins, outs, sems = refs[:3], refs[3:-1], refs[-1]
    h = lax.axis_index("head")
    started = []
    for n, (operand, d, begin, result, at, lanes) in enumerate(copies):
        source = ins[operand].at[:, pl.ds(pl.multiple_of((h ^ d) * width + begin, HEAD_DIM), lanes)]
        copy = pltpu.make_async_copy(source, outs[result].at[:, at : at + lanes], sems.at[n])
        copy.start()
        started.append(copy)
    if len(outs) > 1 + max(copy[3] for copy in copies):
        told = outs[-1]
        for group in range(told.shape[1] // 128):
            value = mask[0, group] if group < 4 else offset[0]
            rows = jnp.full((told.shape[0], 128), value, jnp.int32).astype(jnp.float32)
            told[:, group * 128 : (group + 1) * 128] = rows.astype(told.dtype)
    for copy in started:
        copy.wait()


def packed(operands, mask, offset, results, width, told):
    rows = operands[0].shape[0]
    copies, shapes = [], []
    for n, parts in enumerate(results):
        at = 0
        for operand, d, begin, lanes in parts:
            copies.append((operand, d, begin, n, at, lanes))
            at += lanes
        shapes.append(jax.ShapeDtypeStruct((rows, at), jnp.bfloat16))
    if told:
        shapes.append(jax.ShapeDtypeStruct((INFO_ROWS, told), jnp.bfloat16))
    return pl.pallas_call(
        functools.partial(pack_kernel, copies, width),
        in_specs=[pl.BlockSpec(memory_space=pltpu.SMEM)] * 2 + [pl.BlockSpec(memory_space=pltpu.HBM)] * 3,
        out_specs=[pl.BlockSpec(memory_space=pltpu.VMEM)] * len(shapes),
        out_shape=shapes,
        scratch_shapes=[pltpu.SemaphoreType.DMA((len(copies),))],
        compiler_params=pltpu.CompilerParams(vmem_limit_bytes=4 * 1024 * 1024),
    )(mask, offset, *operands)


def relayed_kernel(parts, mine, other, *outs):
    tile = other.shape[0]
    offset = jnp.max(mine[tile : tile + INFO_ROWS, 4 * 128 : 5 * 128].astype(jnp.float32))
    here = offset == (lax.axis_index("head") // 2).astype(jnp.float32)

    def take(ref):
        for spans, out in zip(parts, outs):
            at = 0
            for begin, end in spans:
                out[:, at : at + end - begin] = ref[:tile, begin:end]
                at += end - begin

    @pl.when(here)
    def _():
        take(mine)

    @pl.when(jnp.logical_not(here))
    def _():
        take(other)


def relayed(mine, other, parts):
    widths = [sum(end - begin for begin, end in spans) for spans in parts]
    return pl.pallas_call(
        functools.partial(relayed_kernel, parts),
        in_specs=[pl.BlockSpec(memory_space=pltpu.VMEM)] * 2,
        out_specs=[pl.BlockSpec(memory_space=pltpu.VMEM)] * len(parts),
        out_shape=[jax.ShapeDtypeStruct((other.shape[0], width), other.dtype) for width in widths],
        compiler_params=pltpu.CompilerParams(vmem_limit_bytes=4 * 1024 * 1024),
    )(mine, other)


def swap_kernel(mine, other, q, out):
    cut = HOME * HEAD_DIM

    @pl.when(inner_frame())
    def _():
        half = other.shape[1] // 2
        relayed_kernel([[(0, cut), (half, half + cut)]], mine, other, out)

    @pl.when(jnp.logical_not(inner_frame()))
    def _():
        rows, count = out.shape[0], q.shape[1] - cut
        out[...] = jnp.zeros_like(out)
        out[:, :count] = q[:rows, cut:]
        out[:, cut : cut + count] = q[rows:, cut:]


def swapped(mine, other, q):
    return pl.pallas_call(
        swap_kernel,
        in_specs=[pl.BlockSpec(memory_space=pltpu.VMEM)] * 3,
        out_specs=pl.BlockSpec(memory_space=pltpu.VMEM),
        out_shape=jax.ShapeDtypeStruct((other.shape[0], 2 * HOME * HEAD_DIM), other.dtype),
        compiler_params=pltpu.CompilerParams(vmem_limit_bytes=4 * 1024 * 1024),
    )(mine, other, q)


def four_frames(queries, keys, values, pair_mask, tile_offset):
    h = lax.axis_index("head")
    rows, features = queries.shape
    width = features // 4
    heads = width // HEAD_DIM

    def columns(array, d):
        return lax.dynamic_slice_in_dim(array, (h ^ d) * width, width, axis=1)

    def beside(*arrays):
        return jnp.concatenate(arrays, axis=1)

    def below(*arrays):
        return jnp.concatenate(arrays, axis=0)

    def to_head(array, d):
        return lax.ppermute(array, "head", [(i, i ^ d) for i in range(4)])

    def along(array, pairs):
        return lax.ppermute(array, "frame", pairs)

    def across(array):
        pairs = [(4 * z + j, 4 * (3 - z) + j if z in (1, 2) else 4 * z + (j ^ 1)) for z in range(4) for j in range(4)]
        return lax.ppermute(array, ("frame", "head"), pairs)

    def after(array, earlier):
        return lax.optimization_barrier((array, earlier))[0]

    kv = [[columns(array, d) for array in (keys, values)] for d in range(4)]
    kv = lax.optimization_barrier(kv)
    got = to_head(beside(*kv[1], *kv[3]), 1)
    pay, q_own, q_far, told = packed(
        (queries, keys, values),
        pair_mask,
        tile_offset,
        [[(0, 1, 0, width), (0, 3, 0, width)], [(0, 0, 0, width)], [(0, 2, 0, width)]],
        width,
        2 * width,
    )
    mine = below(beside(*kv[0]), got[:, : 2 * width], told)
    other = to_head(below(beside(*kv[2]), got[:, 2 * width :]), 2)
    n1m = along(mine, OUTER)
    n2m = across(mine)
    n1o = along(other, OUTER)
    n2o = across(other)

    got = to_head(after(pay, got), 1)
    q = below(q_own, got[:, :width], to_head(after(below(q_far, got[:, width:]), other), 2))

    tile = 2 * rows
    cut = HOME * HEAD_DIM
    guests = heads - HOME
    r1k, r1v, r1_rest = after(
        relayed(n1m, n1o, [[(0, cut)], [(width, width + cut)], [(cut, width), (width + cut, 2 * width)]]), n2m
    )
    r1k = across(r1k)
    swap = along(swapped(n2m, n2o, q), OUTER)
    r1v = across(after(r1v, n2o))

    def state(count):
        return [((count * 2 * tile, HEAD_DIM), jnp.float32)] * 2 + [((8, 128), jnp.float32)]

    def flops(chunks, tiles):
        return 4 * chunks * tiles * tile * tile * HEAD_DIM

    bf16 = jnp.bfloat16
    *near, done = run_kernel(
        functools.partial(near_kernel, 0, ((6, heads), (4, HOME)), own_queries, False),
        None,
        [q, mine, other, n1m, n1o, n2m, n2o],
        state(heads),
        (tile, 6 * tile),
        flops(2 * heads, 6),
        10,
    )
    r3k, r1_rest = passed(done, r1k, r1_rest)
    r3k = along(r3k, OUTER)
    r1_rest = across(r1_rest)
    r3v = along(after(r1v, swap), OUTER)
    *guest_near, _ = run_kernel(
        functools.partial(near_kernel, HOME, ((4, guests), (0, 0)), guest_queries, False),
        None,
        [swap, mine, other, n1m, n1o],
        state(guests),
        (tile, 4 * tile),
        flops(2 * guests, 4),
        10,
    )
    (back,) = run_kernel(
        guest_kernel,
        None,
        [swap, *guest_near, n1m, n2m, n2o, r1_rest],
        [((2 * tile, width - cut), bf16)],
        (tile, 3 * tile),
        flops(2 * guests, 3),
        10,
    )
    back = along(back, OUTER)
    out = run_kernel(
        home_kernel,
        pair_mask,
        [q, *near, r1k, r1v, swap, r3k, r3v],
        [((rows, cut), bf16)] * 4,
        (tile, 2 * tile),
        flops(2 * HOME, 2),
        10,
    )
    pieces = [(to_head(out[d], d) if d else out[0], d, 0) for d in range(4)]
    out = run_kernel(
        rest_kernel,
        pair_mask,
        [q, *near, r1_rest, after(back, out[1])],
        [((rows, width - cut), bf16)] * 4,
        (tile, tile),
        flops(2 * guests, 1),
        10,
    )
    moved = [out[0]] + [to_head(out[d], d) for d in (1, 2, 3)]
    pieces = [(after(piece, moved[1] if d == 3 else out[1]) if d > 1 else piece, d, at) for piece, d, at in pieces]
    pieces += [(piece, d, cut) for d, piece in enumerate(moved)]
    result = jnp.zeros((rows, features), jnp.bfloat16)
    for piece, d, begin in pieces:
        result = lax.dynamic_update_slice_in_dim(result, piece, (h ^ d) * width + begin, axis=1)
    return result


def solution(mesh):
    sizes = dict(mesh.shape)
    per_device = four_frames if sizes["frame"] == 4 and sizes["head"] == 4 else general
    return jax.shard_map(
        per_device,
        mesh=mesh,
        in_specs=(
            P(("parts", "frame", "head"), None),
            P(("parts", "frame", "head"), None),
            P(("parts", "frame", "head"), None),
            P(("parts", "frame"), None),
            P(("parts", "frame")),
        ),
        out_specs=P(("parts", "frame", "head"), None),
        check_vma=False,
    )
```

```python
import functools
import math

import jax
import jax.numpy as jnp
from jax import lax
from jax.experimental import pallas as pl
from jax.experimental.pallas import tpu as pltpu
from jax.sharding import PartitionSpec as P

HEAD_DIM = 128
SCALE = 1.0 / HEAD_DIM**0.5
LOG2E = math.log2(math.e)


def padded(x, sides, width):
    for axis, dim in sides:
        peers, length = (lax.axis_size(axis), x.shape[dim])
        up = [(i, (i + 1) % peers) for i in range(peers - 1)]
        down = [(j, i) for i, j in up]
        last = lax.slice_in_dim(x, length - width, length, axis=dim)
        leading = lax.slice_in_dim(x, 0, width, axis=dim)
        before = lax.ppermute(last, axis, up)
        after = lax.ppermute(leading, axis, down)
        x = jnp.concatenate([before, x, after], axis=dim)
    return x


def from_partner(x, axis, bit):
    return lax.ppermute(x, axis, [(i, i ^ 1 << bit) for i in range(lax.axis_size(axis))])


def subsample(frame_rows, offset, level, tiles, tile):
    step = 2**level
    width = frame_rows.shape[-1]
    grouped = frame_rows.reshape(tiles // step, step, tile, width)
    picked = lax.dynamic_index_in_dim(grouped, offset % step, 1, keepdims=False)
    return picked.reshape(-1, width)


def attend(query_rows, key_rows, value_rows, valid):
    count = query_rows.shape[0]
    heads = query_rows.shape[1] // HEAD_DIM
    q_three = query_rows.reshape(count, heads, HEAD_DIM).transpose(1, 0, 2)
    k_three = key_rows.reshape(-1, heads, HEAD_DIM).transpose(1, 0, 2)
    v_three = value_rows.reshape(-1, heads, HEAD_DIM).transpose(1, 0, 2)

    def one_head(operands):
        q_head, k_head, v_head = operands
        scores = jnp.dot(q_head, k_head.T, preferred_element_type=jnp.float32) * SCALE
        scores = jnp.where(valid[None, :] > 0, scores, -1e30)
        top = jnp.max(scores, axis=1, keepdims=True)
        weights = jnp.exp(scores - top) * valid[None, :]
        total = jnp.sum(weights, axis=1, keepdims=True)
        mixed = jnp.dot(weights.astype(jnp.bfloat16), v_head, preferred_element_type=jnp.float32)
        return mixed / total

    outcome = lax.map(one_head, (q_three, k_three, v_three))
    return outcome.transpose(1, 0, 2).reshape(count, heads * HEAD_DIM).astype(jnp.bfloat16)


def ordered(mine, theirs, upper):
    return jnp.where(upper == 1, jnp.concatenate([theirs, mine]), jnp.concatenate([mine, theirs]))


def general(queries, keys, values, pair_mask, tile_offset):
    frames_n = lax.axis_size("frame")
    current = lax.axis_index("frame")
    q_rows, k_rows, v_rows = (
        lax.all_to_all(queries, "head", split_axis=1, concat_axis=0, tiled=True),
        lax.all_to_all(keys, "head", split_axis=1, concat_axis=0, tiled=True),
        lax.all_to_all(values, "head", split_axis=1, concat_axis=0, tiled=True),
    )
    count = q_rows.shape[0]
    width = q_rows.shape[1]
    tiles = frames_n // 2
    tile = count // tiles
    depth = frames_n.bit_length() - 1
    stacked = jnp.stack([k_rows, v_rows])
    near = padded(stacked, (("frame", 1),), count)
    near_index = current - 1 + jnp.arange(3, dtype=jnp.int32)
    near_good = ((near_index >= 0) & (near_index < frames_n)).astype(jnp.float32)
    key_parts = [near[0]]
    value_parts = [near[1]]
    valid_parts = [jnp.repeat(near_good, count)]
    mask_row = pair_mask[0]
    offset = tile_offset[0]
    k_tiles = k_rows.reshape(tiles, tile, width)
    v_tiles = v_rows.reshape(tiles, tile, width)
    own = {}
    for level in range(1, depth):
        own[level] = (
            subsample(k_tiles, offset, level, tiles, tile)[None],
            subsample(v_tiles, offset, level, tiles, tile)[None],
        )
    sibling = {}
    cut = max(1, depth - 2)
    upper_levels = [level for level in range(1, depth) if level >= cut]
    k_pack = jnp.concatenate([own[level][0].reshape(-1, width) for level in upper_levels])
    v_pack = jnp.concatenate([own[level][1].reshape(-1, width) for level in upper_levels])
    k_every, v_every = (
        lax.all_gather(k_pack, "frame", axis=0, tiled=True),
        lax.all_gather(v_pack, "frame", axis=0, tiled=True),
    )
    k_every = k_every.reshape(frames_n, -1, width)
    v_every = v_every.reshape(frames_n, -1, width)
    position = 0
    for level in upper_levels:
        step = 2**level
        rows = count // step
        start = jnp.bitwise_xor(current // step, 1) * step
        block_k = lax.dynamic_slice_in_dim(k_every[:, position : position + rows], start, step, 0)
        block_v = lax.dynamic_slice_in_dim(v_every[:, position : position + rows], start, step, 0)
        sibling[level] = (block_k, block_v)
        position = position + rows
    swap_levels = [level for level in range(1, depth) if level < cut]
    growing = {level: own[level] for level in swap_levels}
    sections = cut if swap_levels else 0
    for bit in range(sections):
        active = [level for level in swap_levels if level >= bit]
        k_pack = jnp.concatenate([growing[level][0].reshape(-1, width) for level in active])
        v_pack = jnp.concatenate([growing[level][1].reshape(-1, width) for level in active])
        k_in, v_in = (from_partner(k_pack, "frame", bit), from_partner(v_pack, "frame", bit))
        upper = current // 2**bit % 2
        position = 0
        for level in active:
            shape = growing[level][0].shape
            size = shape[0] * shape[1]
            theirs_k = k_in[position : position + size].reshape(shape)
            theirs_v = v_in[position : position + size].reshape(shape)
            position = position + size
            if level == bit:
                sibling[level] = (theirs_k, theirs_v)
            else:
                growing[level] = (
                    ordered(growing[level][0], theirs_k, upper),
                    ordered(growing[level][1], theirs_v, upper),
                )
    for level in range(1, depth):
        step = 2**level
        start = jnp.bitwise_xor(current // step, 1) * step
        frame_ids = start + jnp.arange(step, dtype=jnp.int32)
        allowed = lax.dynamic_slice_in_dim(mask_row, start, step, 0)
        good = ((jnp.abs(frame_ids - current) >= 2) & (allowed == 1)).astype(jnp.float32)
        block_k, block_v = sibling[level]
        key_parts.append(block_k.reshape(-1, width))
        value_parts.append(block_v.reshape(-1, width))
        valid_parts.append(jnp.repeat(good, block_k.shape[1]))
    result = attend(
        q_rows,
        jnp.concatenate(key_parts),
        jnp.concatenate(value_parts),
        jnp.concatenate(valid_parts),
    )
    return lax.all_to_all(result, "head", split_axis=0, concat_axis=1, tiled=True)


HOME = 3
INFO_ROWS = 16
OUTER = [(0, 1), (1, 0), (2, 3), (3, 2)]
FACTOR = SCALE * LOG2E


def inner_frame():
    z = lax.axis_index("frame")
    return (z == 1) | (z == 2)


def head_lanes(first, i):
    return pl.ds(pl.multiple_of((first + i) * HEAD_DIM, HEAD_DIM), HEAD_DIM)


def keys_of(ref, first, i, rows):
    return ref[:rows, head_lanes(first, i)]


def values_of(ref, first, i, rows):
    return ref[:rows, head_lanes(ref.shape[1] // (2 * HEAD_DIM) + first, i)]


def dot_keys(q, k):
    return lax.dot_general(q, k, (((1,), (1,)), ((), ())), preferred_element_type=jnp.float32)


def fold(x, op):
    result = x[:, :128]
    for at in range(128, x.shape[1], 128):
        result = op(result, x[:, at : at + 128])
    return result


def near_kernel(first, counts, queries_of, extra, *refs):
    n_outs = 3 + extra
    ins, outs, rooms = refs[: -2 - n_outs], refs[-2 - n_outs : -2], refs[-2:]
    queries, tiles = ins[0], ins[1:]
    mixed_out, levels, done = outs[:3]
    rows = rooms[0].shape[0]
    done[...] = jnp.zeros_like(done)
    if extra:

        @pl.when(inner_frame())
        def _():
            for ref, out in zip(tiles, outs[3:-1]):
                half, count = ref.shape[1] // 2, out.shape[1] // 2
                out[:, :count] = ref[:rows, half - count : half]
                out[:, count:] = ref[:rows, 2 * half - count :]
            info = outs[-1]
            info[:INFO_ROWS] = tiles[2][rows:, : info.shape[1]]
            info[INFO_ROWS:] = tiles[4][rows:, : info.shape[1]]

    def one_head(used, i):
        found = []
        for half, held in enumerate(rooms):
            q = queries_of(queries, half, i)
            best = None
            for at, ref in enumerate(used):
                s = dot_keys(q, keys_of(ref, first, i, rows))
                held[:, at * rows : (at + 1) * rows] = s
                part = fold(s, jnp.maximum)
                best = part if best is None else jnp.maximum(best, part)
            found.append(jnp.max(best, axis=1, keepdims=True))
        for half, (top, held) in enumerate(zip(found, rooms)):
            total, mixed = None, None
            for at, ref in enumerate(used):
                w = jnp.exp2((held[:, at * rows : (at + 1) * rows] - top) * FACTOR)
                mix = jnp.dot(w.astype(jnp.bfloat16), values_of(ref, first, i, rows), preferred_element_type=jnp.float32)
                part = fold(w, jnp.add)
                mixed = mix if mixed is None else mixed + mix
                total = part if total is None else total + part
            span = pl.ds(pl.multiple_of((2 * i + half) * rows, rows), rows)
            total = jnp.broadcast_to(jnp.sum(total, axis=1, keepdims=True), (rows, HEAD_DIM))
            mixed_out[span] = mixed * (1.0 / total)
            levels[span] = jnp.broadcast_to(top, (rows, HEAD_DIM)) * FACTOR + jnp.log2(total)

    for wanted, (n_tiles, n_heads) in zip((True, False), counts):
        if n_heads:

            @pl.when(inner_frame() == wanted)
            def _():
                def step(i, carry):
                    one_head(tiles[:n_tiles], i)
                    return carry

                lax.fori_loop(0, n_heads, step, 0)


def own_queries(ref, half, i):
    rows = ref.shape[0] // 2
    return ref[half * rows : (half + 1) * rows, head_lanes(0, i)]


def guest_queries(ref, half, i):
    return ref[:, head_lanes(half * HOME, i)]


def far_tile(ref, first, valid):
    return functools.partial(keys_of, ref, first), functools.partial(values_of, ref, first), valid


def far_pair(keys, values, valid):
    return functools.partial(keys_of, keys, 0), functools.partial(keys_of, values, 0), valid


def add_far(q, state, slots, i, begin, held):
    rows = q.shape[0]
    span = pl.ds(pl.multiple_of(begin, rows), rows)
    near_level = state[1][span]
    level = near_level
    for at, (keys, _, valid) in enumerate(slots):
        s = dot_keys(q, keys(i, rows)) * FACTOR
        held[:, at * rows : (at + 1) * rows] = s
        best = jnp.broadcast_to(jnp.max(fold(s, jnp.maximum), axis=1, keepdims=True), near_level.shape)
        level = jnp.maximum(level, jnp.where(valid, best, -1e30))
    shrink = jnp.exp2(near_level - level)
    mixed = state[0][span] * shrink
    total = None
    for at, (_, values, valid) in enumerate(slots):
        used = jnp.where(valid, level, 1e30)
        parts = []
        for lane in range(at * rows, (at + 1) * rows, HEAD_DIM):
            part = jnp.exp2(held[:, lane : lane + HEAD_DIM] - used)
            total = part if total is None else total + part
            parts.append(part.astype(jnp.bfloat16))
        mixed += jnp.dot(jnp.concatenate(parts, axis=1), values(i, rows), preferred_element_type=jnp.float32)
    total = jnp.broadcast_to(jnp.sum(total, axis=1, keepdims=True), near_level.shape) + shrink
    return (mixed * (1.0 / total)).astype(jnp.bfloat16)


def each_head(heads, body):
    def step(i, carry):
        body(i)
        return carry

    lax.fori_loop(0, heads, step, 0)


def finish_own(first, queries, state, slots, outs, rooms):
    piece = outs[0].shape[0]
    rows = 2 * piece

    def body(i):
        for half, held in enumerate(rooms):
            q = queries[half * rows : (half + 1) * rows, head_lanes(first, i)]
            value = add_far(q, state, slots, i, (2 * (first + i) + half) * rows, held)
            outs[2 * half][:, head_lanes(0, i)] = value[:piece]
            outs[2 * half + 1][:, head_lanes(0, i)] = value[piece:]

    each_head(outs[0].shape[1] // HEAD_DIM, body)


def home_kernel(mask, q, mixed, levels, r1k, r1v, r2, r3k, r3v, *rest):
    outs, rooms = rest[:4], rest[4:]
    z = lax.axis_index("frame")
    near2 = mask[0, z ^ 2] == 1

    @pl.when(inner_frame())
    def _():
        finish_own(0, q, (mixed, levels), [far_pair(r1k, r1v, near2)], outs, rooms)

    @pl.when(jnp.logical_not(inner_frame()))
    def _():
        slots = [far_tile(r2, 0, near2), far_pair(r3k, r3v, mask[0, z ^ 3] == 1)]
        finish_own(0, q, (mixed, levels), slots, outs, rooms)


def guest_kernel(q, mixed, levels, info, n2m, n2o, r1, out, *rooms):
    rows = r1.shape[0]
    z = lax.axis_index("frame")

    def told(row, group):
        return info[row : row + 1, group * 128 : (group + 1) * 128].astype(jnp.float32)

    @pl.when(inner_frame())
    def _():
        near2 = jnp.where(z == 1, told(0, 2), told(0, 1)) > 0.5
        near1 = jnp.where(z == 1, told(0, 3), told(0, 0)) > 0.5
        picked = told(INFO_ROWS, 4) == (lax.axis_index("head") // 2).astype(jnp.float32)
        slots = [
            far_tile(n2m, 0, near2 & picked),
            far_tile(n2o, 0, near2 & jnp.logical_not(picked)),
            far_tile(r1, 0, near1),
        ]

        def body(i):
            for half, held in enumerate(rooms):
                value = add_far(guest_queries(q, half, i), (mixed, levels), slots, i, (2 * i + half) * rows, held)
                out[half * rows : (half + 1) * rows, head_lanes(0, i)] = value

        each_head(out.shape[1] // HEAD_DIM, body)


def rest_kernel(mask, q, mixed, levels, r1, back, *rest):
    outs, rooms = rest[:4], rest[4:]
    z = lax.axis_index("frame")

    @pl.when(inner_frame())
    def _():
        finish_own(HOME, q, (mixed, levels), [far_tile(r1, 0, mask[0, z ^ 2] == 1)], outs, rooms)

    @pl.when(jnp.logical_not(inner_frame()))
    def _():
        for d, out in enumerate(outs):
            out[...] = back[d * out.shape[0] : (d + 1) * out.shape[0]]


def pass_kernel(done, *refs):
    half = len(refs) // 2
    for x, out in zip(refs[:half], refs[half:]):
        out[...] = x[...]


def passed(done, *arrays):
    return pl.pallas_call(
        pass_kernel,
        in_specs=[pl.BlockSpec(memory_space=pltpu.VMEM)] * (1 + len(arrays)),
        out_specs=[pl.BlockSpec(memory_space=pltpu.VMEM)] * len(arrays),
        out_shape=[jax.ShapeDtypeStruct(x.shape, x.dtype) for x in arrays],
        compiler_params=pltpu.CompilerParams(vmem_limit_bytes=4 * 1024 * 1024),
    )(done, *arrays)


def run_kernel(kernel, mask, arrays, outs, room, flops, grant):
    scalars = [] if mask is None else [mask]
    return pl.pallas_call(
        kernel,
        in_specs=[pl.BlockSpec(memory_space=pltpu.SMEM)] * len(scalars)
        + [pl.BlockSpec(memory_space=pltpu.VMEM)] * len(arrays),
        out_specs=[pl.BlockSpec(memory_space=pltpu.VMEM)] * len(outs),
        out_shape=[jax.ShapeDtypeStruct(shape, dtype) for shape, dtype in outs],
        scratch_shapes=[pltpu.VMEM(room, jnp.float32)] * 2,
        compiler_params=pltpu.CompilerParams(vmem_limit_bytes=grant * 1024 * 1024),
        cost_estimate=pl.CostEstimate(
            flops=flops, bytes_accessed=sum(x.size * 2 for x in arrays), transcendentals=flops // (4 * HEAD_DIM)
        ),
    )(*scalars, *arrays)


def pack_kernel(copies, width, mask, offset, *refs):
    ins, outs, sems = refs[:3], refs[3:-1], refs[-1]
    h = lax.axis_index("head")
    started = []
    for n, (operand, d, begin, result, at, lanes) in enumerate(copies):
        source = ins[operand].at[:, pl.ds(pl.multiple_of((h ^ d) * width + begin, HEAD_DIM), lanes)]
        copy = pltpu.make_async_copy(source, outs[result].at[:, at : at + lanes], sems.at[n])
        copy.start()
        started.append(copy)
    if len(outs) > 1 + max(copy[3] for copy in copies):
        told = outs[-1]
        for group in range(told.shape[1] // 128):
            value = mask[0, group] if group < 4 else offset[0]
            rows = jnp.full((told.shape[0], 128), value, jnp.int32).astype(jnp.float32)
            told[:, group * 128 : (group + 1) * 128] = rows.astype(told.dtype)
    for copy in started:
        copy.wait()


def packed(operands, mask, offset, results, width, told):
    rows = operands[0].shape[0]
    copies, shapes = [], []
    for n, parts in enumerate(results):
        at = 0
        for operand, d, begin, lanes in parts:
            copies.append((operand, d, begin, n, at, lanes))
            at += lanes
        shapes.append(jax.ShapeDtypeStruct((rows, at), jnp.bfloat16))
    if told:
        shapes.append(jax.ShapeDtypeStruct((INFO_ROWS, told), jnp.bfloat16))
    return pl.pallas_call(
        functools.partial(pack_kernel, copies, width),
        in_specs=[pl.BlockSpec(memory_space=pltpu.SMEM)] * 2 + [pl.BlockSpec(memory_space=pltpu.HBM)] * 3,
        out_specs=[pl.BlockSpec(memory_space=pltpu.VMEM)] * len(shapes),
        out_shape=shapes,
        scratch_shapes=[pltpu.SemaphoreType.DMA((len(copies),))],
        compiler_params=pltpu.CompilerParams(vmem_limit_bytes=4 * 1024 * 1024),
    )(mask, offset, *operands)


def relayed_kernel(parts, mine, other, *outs):
    tile = other.shape[0]
    offset = jnp.max(mine[tile : tile + INFO_ROWS, 4 * 128 : 5 * 128].astype(jnp.float32))
    here = offset == (lax.axis_index("head") // 2).astype(jnp.float32)

    def take(ref):
        for spans, out in zip(parts, outs):
            at = 0
            for begin, end in spans:
                out[:, at : at + end - begin] = ref[:tile, begin:end]
                at += end - begin

    @pl.when(here)
    def _():
        take(mine)

    @pl.when(jnp.logical_not(here))
    def _():
        take(other)


def relayed(mine, other, parts):
    widths = [sum(end - begin for begin, end in spans) for spans in parts]
    return pl.pallas_call(
        functools.partial(relayed_kernel, parts),
        in_specs=[pl.BlockSpec(memory_space=pltpu.VMEM)] * 2,
        out_specs=[pl.BlockSpec(memory_space=pltpu.VMEM)] * len(parts),
        out_shape=[jax.ShapeDtypeStruct((other.shape[0], width), other.dtype) for width in widths],
        compiler_params=pltpu.CompilerParams(vmem_limit_bytes=4 * 1024 * 1024),
    )(mine, other)


def swap_kernel(mine, other, q, out):
    cut = HOME * HEAD_DIM

    @pl.when(inner_frame())
    def _():
        half = other.shape[1] // 2
        relayed_kernel([[(0, cut), (half, half + cut)]], mine, other, out)

    @pl.when(jnp.logical_not(inner_frame()))
    def _():
        rows, count = out.shape[0], q.shape[1] - cut
        out[...] = jnp.zeros_like(out)
        out[:, :count] = q[:rows, cut:]
        out[:, cut : cut + count] = q[rows:, cut:]


def swapped(mine, other, q):
    return pl.pallas_call(
        swap_kernel,
        in_specs=[pl.BlockSpec(memory_space=pltpu.VMEM)] * 3,
        out_specs=pl.BlockSpec(memory_space=pltpu.VMEM),
        out_shape=jax.ShapeDtypeStruct((other.shape[0], 2 * HOME * HEAD_DIM), other.dtype),
        compiler_params=pltpu.CompilerParams(vmem_limit_bytes=4 * 1024 * 1024),
    )(mine, other, q)


def four_frames(queries, keys, values, pair_mask, tile_offset):
    h = lax.axis_index("head")
    rows, features = queries.shape
    width = features // 4
    heads = width // HEAD_DIM

    def columns(array, d):
        return lax.dynamic_slice_in_dim(array, (h ^ d) * width, width, axis=1)

    def beside(*arrays):
        return jnp.concatenate(arrays, axis=1)

    def below(*arrays):
        return jnp.concatenate(arrays, axis=0)

    def to_head(array, d):
        return lax.ppermute(array, "head", [(i, i ^ d) for i in range(4)])

    def along(array, pairs):
        return lax.ppermute(array, "frame", pairs)

    def across(array):
        pairs = [(4 * z + j, 4 * (3 - z) + j if z in (1, 2) else 4 * z + (j ^ 1)) for z in range(4) for j in range(4)]
        return lax.ppermute(array, ("frame", "head"), pairs)

    def after(array, earlier):
        return lax.optimization_barrier((array, earlier))[0]

    kv = [[columns(array, d) for array in (keys, values)] for d in range(4)]
    kv = lax.optimization_barrier(kv)
    got = to_head(beside(*kv[1], *kv[3]), 1)
    pay, q_own, q_far, told = packed(
        (queries, keys, values),
        pair_mask,
        tile_offset,
        [[(0, 1, 0, width), (0, 3, 0, width)], [(0, 0, 0, width)], [(0, 2, 0, width)]],
        width,
        2 * width,
    )
    mine = below(beside(*kv[0]), got[:, : 2 * width], told)
    other = to_head(below(beside(*kv[2]), got[:, 2 * width :]), 2)
    n1m = along(mine, OUTER)
    n2m = across(mine)
    n1o = along(other, OUTER)
    n2o = across(other)

    got = to_head(after(pay, got), 1)
    q = below(q_own, got[:, :width], to_head(after(below(q_far, got[:, width:]), other), 2))

    tile = 2 * rows
    cut = HOME * HEAD_DIM
    guests = heads - HOME
    r1k, r1v, r1_rest = after(
        relayed(n1m, n1o, [[(0, cut)], [(width, width + cut)], [(cut, width), (width + cut, 2 * width)]]), n2m
    )
    r1k = across(r1k)
    swap = along(swapped(n2m, n2o, q), OUTER)
    r1v = across(after(r1v, n2o))

    def state(count):
        return [((count * 2 * tile, HEAD_DIM), jnp.float32)] * 2 + [((8, 128), jnp.float32)]

    def flops(chunks, tiles):
        return 4 * chunks * tiles * tile * tile * HEAD_DIM

    bf16 = jnp.bfloat16
    near_mixed, near_levels, done, *kept, info = run_kernel(
        functools.partial(near_kernel, 0, ((6, heads), (4, HOME)), own_queries, 7),
        None,
        [q, mine, other, n1m, n1o, n2m, n2o],
        state(heads) + [((tile, 2 * (width - cut)), bf16)] * 6 + [((2 * INFO_ROWS, 5 * 128), bf16)],
        (tile, 6 * tile),
        flops(2 * heads, 6),
        10,
    )
    near = [near_mixed, near_levels]
    r3k, r1_rest = passed(done, r1k, r1_rest)
    r3k = along(r3k, OUTER)
    r1_rest = across(r1_rest)
    r3v = along(after(r1v, swap), OUTER)
    *guest_near, _ = run_kernel(
        functools.partial(near_kernel, 0, ((4, guests), (0, 0)), guest_queries, 0),
        None,
        [swap, *kept[:4]],
        state(guests),
        (tile, 4 * tile),
        flops(2 * guests, 4),
        10,
    )
    (back,) = run_kernel(
        guest_kernel,
        None,
        [swap, *guest_near, info, *kept[4:], r1_rest],
        [((2 * tile, width - cut), bf16)],
        (tile, 3 * tile),
        flops(2 * guests, 3),
        10,
    )
    back = along(back, OUTER)
    out = run_kernel(
        home_kernel,
        pair_mask,
        [q, *near, r1k, r1v, swap, r3k, r3v],
        [((rows, cut), bf16)] * 4,
        (tile, 2 * tile),
        flops(2 * HOME, 2),
        10,
    )
    pieces = [(to_head(out[d], d) if d else out[0], d, 0) for d in range(4)]
    out = run_kernel(
        rest_kernel,
        pair_mask,
        [q, *near, r1_rest, after(back, out[1])],
        [((rows, width - cut), bf16)] * 4,
        (tile, tile),
        flops(2 * guests, 1),
        10,
    )
    moved = [out[0]] + [to_head(out[d], d) for d in (1, 2, 3)]
    pieces = [(after(piece, moved[1] if d == 3 else out[1]) if d > 1 else piece, d, at) for piece, d, at in pieces]
    pieces += [(piece, d, cut) for d, piece in enumerate(moved)]
    result = jnp.zeros((rows, features), jnp.bfloat16)
    for piece, d, begin in pieces:
        result = lax.dynamic_update_slice_in_dim(result, piece, (h ^ d) * width + begin, axis=1)
    return result


def solution(mesh):
    sizes = dict(mesh.shape)
    per_device = four_frames if sizes["frame"] == 4 and sizes["head"] == 4 else general
    return jax.shard_map(
        per_device,
        mesh=mesh,
        in_specs=(
            P(("parts", "frame", "head"), None),
            P(("parts", "frame", "head"), None),
            P(("parts", "frame", "head"), None),
            P(("parts", "frame"), None),
            P(("parts", "frame")),
        ),
        out_specs=P(("parts", "frame", "head"), None),
        check_vma=False,
    )
```

```python
import functools
import math

import jax
import jax.numpy as jnp
from jax import lax
from jax.experimental import pallas as pl
from jax.experimental.pallas import tpu as pltpu
from jax.sharding import PartitionSpec as P

HEAD_DIM = 128
SCALE = 1.0 / HEAD_DIM**0.5
LOG2E = math.log2(math.e)


def padded(x, sides, width):
    for axis, dim in sides:
        peers, length = (lax.axis_size(axis), x.shape[dim])
        up = [(i, (i + 1) % peers) for i in range(peers - 1)]
        down = [(j, i) for i, j in up]
        last = lax.slice_in_dim(x, length - width, length, axis=dim)
        leading = lax.slice_in_dim(x, 0, width, axis=dim)
        before = lax.ppermute(last, axis, up)
        after = lax.ppermute(leading, axis, down)
        x = jnp.concatenate([before, x, after], axis=dim)
    return x


def from_partner(x, axis, bit):
    return lax.ppermute(x, axis, [(i, i ^ 1 << bit) for i in range(lax.axis_size(axis))])


def subsample(frame_rows, offset, level, tiles, tile):
    step = 2**level
    width = frame_rows.shape[-1]
    grouped = frame_rows.reshape(tiles // step, step, tile, width)
    picked = lax.dynamic_index_in_dim(grouped, offset % step, 1, keepdims=False)
    return picked.reshape(-1, width)


def attend(query_rows, key_rows, value_rows, valid):
    count = query_rows.shape[0]
    heads = query_rows.shape[1] // HEAD_DIM
    q_three = query_rows.reshape(count, heads, HEAD_DIM).transpose(1, 0, 2)
    k_three = key_rows.reshape(-1, heads, HEAD_DIM).transpose(1, 0, 2)
    v_three = value_rows.reshape(-1, heads, HEAD_DIM).transpose(1, 0, 2)

    def one_head(operands):
        q_head, k_head, v_head = operands
        scores = jnp.dot(q_head, k_head.T, preferred_element_type=jnp.float32) * SCALE
        scores = jnp.where(valid[None, :] > 0, scores, -1e30)
        top = jnp.max(scores, axis=1, keepdims=True)
        weights = jnp.exp(scores - top) * valid[None, :]
        total = jnp.sum(weights, axis=1, keepdims=True)
        mixed = jnp.dot(weights.astype(jnp.bfloat16), v_head, preferred_element_type=jnp.float32)
        return mixed / total

    outcome = lax.map(one_head, (q_three, k_three, v_three))
    return outcome.transpose(1, 0, 2).reshape(count, heads * HEAD_DIM).astype(jnp.bfloat16)


def ordered(mine, theirs, upper):
    return jnp.where(upper == 1, jnp.concatenate([theirs, mine]), jnp.concatenate([mine, theirs]))


def general(queries, keys, values, pair_mask, tile_offset):
    frames_n = lax.axis_size("frame")
    current = lax.axis_index("frame")
    q_rows, k_rows, v_rows = (
        lax.all_to_all(queries, "head", split_axis=1, concat_axis=0, tiled=True),
        lax.all_to_all(keys, "head", split_axis=1, concat_axis=0, tiled=True),
        lax.all_to_all(values, "head", split_axis=1, concat_axis=0, tiled=True),
    )
    count = q_rows.shape[0]
    width = q_rows.shape[1]
    tiles = frames_n // 2
    tile = count // tiles
    depth = frames_n.bit_length() - 1
    stacked = jnp.stack([k_rows, v_rows])
    near = padded(stacked, (("frame", 1),), count)
    near_index = current - 1 + jnp.arange(3, dtype=jnp.int32)
    near_good = ((near_index >= 0) & (near_index < frames_n)).astype(jnp.float32)
    key_parts = [near[0]]
    value_parts = [near[1]]
    valid_parts = [jnp.repeat(near_good, count)]
    mask_row = pair_mask[0]
    offset = tile_offset[0]
    k_tiles = k_rows.reshape(tiles, tile, width)
    v_tiles = v_rows.reshape(tiles, tile, width)
    own = {}
    for level in range(1, depth):
        own[level] = (
            subsample(k_tiles, offset, level, tiles, tile)[None],
            subsample(v_tiles, offset, level, tiles, tile)[None],
        )
    sibling = {}
    cut = max(1, depth - 2)
    upper_levels = [level for level in range(1, depth) if level >= cut]
    k_pack = jnp.concatenate([own[level][0].reshape(-1, width) for level in upper_levels])
    v_pack = jnp.concatenate([own[level][1].reshape(-1, width) for level in upper_levels])
    k_every, v_every = (
        lax.all_gather(k_pack, "frame", axis=0, tiled=True),
        lax.all_gather(v_pack, "frame", axis=0, tiled=True),
    )
    k_every = k_every.reshape(frames_n, -1, width)
    v_every = v_every.reshape(frames_n, -1, width)
    position = 0
    for level in upper_levels:
        step = 2**level
        rows = count // step
        start = jnp.bitwise_xor(current // step, 1) * step
        block_k = lax.dynamic_slice_in_dim(k_every[:, position : position + rows], start, step, 0)
        block_v = lax.dynamic_slice_in_dim(v_every[:, position : position + rows], start, step, 0)
        sibling[level] = (block_k, block_v)
        position = position + rows
    swap_levels = [level for level in range(1, depth) if level < cut]
    growing = {level: own[level] for level in swap_levels}
    sections = cut if swap_levels else 0
    for bit in range(sections):
        active = [level for level in swap_levels if level >= bit]
        k_pack = jnp.concatenate([growing[level][0].reshape(-1, width) for level in active])
        v_pack = jnp.concatenate([growing[level][1].reshape(-1, width) for level in active])
        k_in, v_in = (from_partner(k_pack, "frame", bit), from_partner(v_pack, "frame", bit))
        upper = current // 2**bit % 2
        position = 0
        for level in active:
            shape = growing[level][0].shape
            size = shape[0] * shape[1]
            theirs_k = k_in[position : position + size].reshape(shape)
            theirs_v = v_in[position : position + size].reshape(shape)
            position = position + size
            if level == bit:
                sibling[level] = (theirs_k, theirs_v)
            else:
                growing[level] = (
                    ordered(growing[level][0], theirs_k, upper),
                    ordered(growing[level][1], theirs_v, upper),
                )
    for level in range(1, depth):
        step = 2**level
        start = jnp.bitwise_xor(current // step, 1) * step
        frame_ids = start + jnp.arange(step, dtype=jnp.int32)
        allowed = lax.dynamic_slice_in_dim(mask_row, start, step, 0)
        good = ((jnp.abs(frame_ids - current) >= 2) & (allowed == 1)).astype(jnp.float32)
        block_k, block_v = sibling[level]
        key_parts.append(block_k.reshape(-1, width))
        value_parts.append(block_v.reshape(-1, width))
        valid_parts.append(jnp.repeat(good, block_k.shape[1]))
    result = attend(
        q_rows,
        jnp.concatenate(key_parts),
        jnp.concatenate(value_parts),
        jnp.concatenate(valid_parts),
    )
    return lax.all_to_all(result, "head", split_axis=0, concat_axis=1, tiled=True)


HOME = 3
INFO_ROWS = 16
OUTER = [(0, 1), (1, 0), (2, 3), (3, 2)]
FACTOR = SCALE * LOG2E


def inner_frame():
    z = lax.axis_index("frame")
    return (z == 1) | (z == 2)


def head_lanes(first, i):
    return pl.ds(pl.multiple_of((first + i) * HEAD_DIM, HEAD_DIM), HEAD_DIM)


def keys_of(ref, first, i, rows):
    return ref[:rows, head_lanes(first, i)]


def values_of(ref, first, i, rows):
    return ref[:rows, head_lanes(ref.shape[1] // (2 * HEAD_DIM) + first, i)]


def dot_keys(q, k):
    return lax.dot_general(q, k, (((1,), (1,)), ((), ())), preferred_element_type=jnp.float32)


def fold(x, op):
    result = x[:, :128]
    for at in range(128, x.shape[1], 128):
        result = op(result, x[:, at : at + 128])
    return result


def near_kernel(first, counts, queries_of, carries, *refs):
    n_outs = 4 if carries else 3
    ins, outs, rooms = refs[: -2 - n_outs], refs[-2 - n_outs : -2], refs[-2:]
    queries, tiles = ins[0], ins[1:]
    mixed_out, levels, done = outs[:3]
    rows = rooms[0].shape[0]
    done[...] = jnp.zeros_like(done)
    if carries:
        outs[3][...] = ins[-1][...]

    def one_head(used, i):
        found = []
        for half, held in enumerate(rooms):
            q = queries_of(queries, half, i)
            best = None
            for at, ref in enumerate(used):
                s = dot_keys(q, keys_of(ref, first, i, rows))
                held[:, at * rows : (at + 1) * rows] = s
                part = fold(s, jnp.maximum)
                best = part if best is None else jnp.maximum(best, part)
            found.append(jnp.max(best, axis=1, keepdims=True))
        for half, (top, held) in enumerate(zip(found, rooms)):
            total, mixed = None, None
            for at, ref in enumerate(used):
                w = jnp.exp2((held[:, at * rows : (at + 1) * rows] - top) * FACTOR)
                mix = jnp.dot(w.astype(jnp.bfloat16), values_of(ref, first, i, rows), preferred_element_type=jnp.float32)
                part = fold(w, jnp.add)
                mixed = mix if mixed is None else mixed + mix
                total = part if total is None else total + part
            span = pl.ds(pl.multiple_of((2 * i + half) * rows, rows), rows)
            total = jnp.broadcast_to(jnp.sum(total, axis=1, keepdims=True), (rows, HEAD_DIM))
            mixed_out[span] = mixed * (1.0 / total)
            levels[span] = jnp.broadcast_to(top, (rows, HEAD_DIM)) * FACTOR + jnp.log2(total)

    for wanted, (n_tiles, n_heads) in zip((True, False), counts):
        if n_heads:

            @pl.when(inner_frame() == wanted)
            def _():
                def step(i, carry):
                    one_head(tiles[:n_tiles], i)
                    return carry

                lax.fori_loop(0, n_heads, step, 0)


def own_queries(ref, half, i):
    rows = ref.shape[0] // 2
    return ref[half * rows : (half + 1) * rows, head_lanes(0, i)]


def guest_queries(ref, half, i):
    return ref[:, head_lanes(half * HOME, i)]


def far_tile(ref, first, valid):
    return functools.partial(keys_of, ref, first), functools.partial(values_of, ref, first), valid


def far_pair(keys, values, valid):
    return functools.partial(keys_of, keys, 0), functools.partial(keys_of, values, 0), valid


def add_far(q, state, slots, i, begin, held):
    rows = q.shape[0]
    span = pl.ds(pl.multiple_of(begin, rows), rows)
    near_level = state[1][span]
    level = near_level
    for at, (keys, _, valid) in enumerate(slots):
        s = dot_keys(q, keys(i, rows)) * FACTOR
        held[:, at * rows : (at + 1) * rows] = s
        best = jnp.broadcast_to(jnp.max(fold(s, jnp.maximum), axis=1, keepdims=True), near_level.shape)
        level = jnp.maximum(level, jnp.where(valid, best, -1e30))
    shrink = jnp.exp2(near_level - level)
    mixed = state[0][span] * shrink
    total = None
    for at, (_, values, valid) in enumerate(slots):
        used = jnp.where(valid, level, 1e30)
        parts = []
        for lane in range(at * rows, (at + 1) * rows, HEAD_DIM):
            part = jnp.exp2(held[:, lane : lane + HEAD_DIM] - used)
            total = part if total is None else total + part
            parts.append(part.astype(jnp.bfloat16))
        mixed += jnp.dot(jnp.concatenate(parts, axis=1), values(i, rows), preferred_element_type=jnp.float32)
    total = jnp.broadcast_to(jnp.sum(total, axis=1, keepdims=True), near_level.shape) + shrink
    return (mixed * (1.0 / total)).astype(jnp.bfloat16)


def each_head(heads, body):
    def step(i, carry):
        body(i)
        return carry

    lax.fori_loop(0, heads, step, 0)


def finish_own(first, queries, state, slots, outs, rooms):
    piece = outs[0].shape[0]
    rows = 2 * piece

    def body(i):
        for half, held in enumerate(rooms):
            q = queries[half * rows : (half + 1) * rows, head_lanes(first, i)]
            value = add_far(q, state, slots, i, (2 * (first + i) + half) * rows, held)
            outs[2 * half][:, head_lanes(0, i)] = value[:piece]
            outs[2 * half + 1][:, head_lanes(0, i)] = value[piece:]

    each_head(outs[0].shape[1] // HEAD_DIM, body)


def home_kernel(mask, q, mixed, levels, r1k, r1v, r2, r3k, r3v, *rest):
    outs, rooms = rest[:4], rest[4:]
    z = lax.axis_index("frame")
    near2 = mask[0, z ^ 2] == 1

    @pl.when(inner_frame())
    def _():
        finish_own(0, q, (mixed, levels), [far_pair(r1k, r1v, near2)], outs, rooms)

    @pl.when(jnp.logical_not(inner_frame()))
    def _():
        slots = [far_tile(r2, 0, near2), far_pair(r3k, r3v, mask[0, z ^ 3] == 1)]
        finish_own(0, q, (mixed, levels), slots, outs, rooms)


def guest_kernel(q, mixed, levels, n1m, n2m, n2o, r1, out, *rooms):
    rows = r1.shape[0]
    z = lax.axis_index("frame")

    def told(ref, group):
        return ref[rows : rows + 1, group * 128 : (group + 1) * 128].astype(jnp.float32)

    @pl.when(inner_frame())
    def _():
        near2 = jnp.where(z == 1, told(n1m, 2), told(n1m, 1)) > 0.5
        near1 = jnp.where(z == 1, told(n1m, 3), told(n1m, 0)) > 0.5
        picked = told(n2m, 4) == (lax.axis_index("head") // 2).astype(jnp.float32)
        slots = [
            far_tile(n2m, HOME, near2 & picked),
            far_tile(n2o, HOME, near2 & jnp.logical_not(picked)),
            far_tile(r1, 0, near1),
        ]

        def body(i):
            for half, held in enumerate(rooms):
                value = add_far(guest_queries(q, half, i), (mixed, levels), slots, i, (2 * i + half) * rows, held)
                out[half * rows : (half + 1) * rows, head_lanes(0, i)] = value

        each_head(out.shape[1] // HEAD_DIM, body)


def rest_kernel(mask, q, mixed, levels, r1, back, *rest):
    outs, rooms = rest[:4], rest[4:]
    z = lax.axis_index("frame")

    @pl.when(inner_frame())
    def _():
        finish_own(HOME, q, (mixed, levels), [far_tile(r1, 0, mask[0, z ^ 2] == 1)], outs, rooms)

    @pl.when(jnp.logical_not(inner_frame()))
    def _():
        for d, out in enumerate(outs):
            out[...] = back[d * out.shape[0] : (d + 1) * out.shape[0]]


def pass_kernel(done, *refs):
    half = len(refs) // 2
    for x, out in zip(refs[:half], refs[half:]):
        out[...] = x[...]


def passed(done, *arrays):
    return pl.pallas_call(
        pass_kernel,
        in_specs=[pl.BlockSpec(memory_space=pltpu.VMEM)] * (1 + len(arrays)),
        out_specs=[pl.BlockSpec(memory_space=pltpu.VMEM)] * len(arrays),
        out_shape=[jax.ShapeDtypeStruct(x.shape, x.dtype) for x in arrays],
        compiler_params=pltpu.CompilerParams(vmem_limit_bytes=4 * 1024 * 1024),
    )(done, *arrays)


def run_kernel(kernel, mask, arrays, outs, room, flops, grant):
    scalars = [] if mask is None else [mask]
    return pl.pallas_call(
        kernel,
        in_specs=[pl.BlockSpec(memory_space=pltpu.SMEM)] * len(scalars)
        + [pl.BlockSpec(memory_space=pltpu.VMEM)] * len(arrays),
        out_specs=[pl.BlockSpec(memory_space=pltpu.VMEM)] * len(outs),
        out_shape=[jax.ShapeDtypeStruct(shape, dtype) for shape, dtype in outs],
        scratch_shapes=[pltpu.VMEM(room, jnp.float32)] * 2,
        compiler_params=pltpu.CompilerParams(vmem_limit_bytes=grant * 1024 * 1024),
        cost_estimate=pl.CostEstimate(
            flops=flops, bytes_accessed=sum(x.size * 2 for x in arrays), transcendentals=flops // (4 * HEAD_DIM)
        ),
    )(*scalars, *arrays)


def pack_kernel(copies, width, mask, offset, *refs):
    ins, outs, sems = refs[:3], refs[3:-1], refs[-1]
    h = lax.axis_index("head")
    started = []
    for n, (operand, d, begin, result, at, lanes) in enumerate(copies):
        source = ins[operand].at[:, pl.ds(pl.multiple_of((h ^ d) * width + begin, HEAD_DIM), lanes)]
        copy = pltpu.make_async_copy(source, outs[result].at[:, at : at + lanes], sems.at[n])
        copy.start()
        started.append(copy)
    if len(outs) > 1 + max(copy[3] for copy in copies):
        told = outs[-1]
        for group in range(told.shape[1] // 128):
            value = mask[0, group] if group < 4 else offset[0]
            rows = jnp.full((told.shape[0], 128), value, jnp.int32).astype(jnp.float32)
            told[:, group * 128 : (group + 1) * 128] = rows.astype(told.dtype)
    for copy in started:
        copy.wait()


def packed(operands, mask, offset, results, width, told):
    rows = operands[0].shape[0]
    copies, shapes = [], []
    for n, parts in enumerate(results):
        at = 0
        for operand, d, begin, lanes in parts:
            copies.append((operand, d, begin, n, at, lanes))
            at += lanes
        shapes.append(jax.ShapeDtypeStruct((rows, at), jnp.bfloat16))
    if told:
        shapes.append(jax.ShapeDtypeStruct((INFO_ROWS, told), jnp.bfloat16))
    return pl.pallas_call(
        functools.partial(pack_kernel, copies, width),
        in_specs=[pl.BlockSpec(memory_space=pltpu.SMEM)] * 2 + [pl.BlockSpec(memory_space=pltpu.HBM)] * 3,
        out_specs=[pl.BlockSpec(memory_space=pltpu.VMEM)] * len(shapes),
        out_shape=shapes,
        scratch_shapes=[pltpu.SemaphoreType.DMA((len(copies),))],
        compiler_params=pltpu.CompilerParams(vmem_limit_bytes=4 * 1024 * 1024),
    )(mask, offset, *operands)


def relayed_kernel(parts, mine, other, *outs):
    tile = other.shape[0]
    offset = jnp.max(mine[tile : tile + INFO_ROWS, 4 * 128 : 5 * 128].astype(jnp.float32))
    here = offset == (lax.axis_index("head") // 2).astype(jnp.float32)

    def take(ref):
        for spans, out in zip(parts, outs):
            at = 0
            for begin, end in spans:
                out[:, at : at + end - begin] = ref[:tile, begin:end]
                at += end - begin

    @pl.when(here)
    def _():
        take(mine)

    @pl.when(jnp.logical_not(here))
    def _():
        take(other)


def relayed(mine, other, parts):
    widths = [sum(end - begin for begin, end in spans) for spans in parts]
    return pl.pallas_call(
        functools.partial(relayed_kernel, parts),
        in_specs=[pl.BlockSpec(memory_space=pltpu.VMEM)] * 2,
        out_specs=[pl.BlockSpec(memory_space=pltpu.VMEM)] * len(parts),
        out_shape=[jax.ShapeDtypeStruct((other.shape[0], width), other.dtype) for width in widths],
        compiler_params=pltpu.CompilerParams(vmem_limit_bytes=4 * 1024 * 1024),
    )(mine, other)


def swap_kernel(mine, other, q, out):
    cut = HOME * HEAD_DIM

    @pl.when(inner_frame())
    def _():
        half = other.shape[1] // 2
        relayed_kernel([[(0, cut), (half, half + cut)]], mine, other, out)

    @pl.when(jnp.logical_not(inner_frame()))
    def _():
        rows, count = out.shape[0], q.shape[1] - cut
        out[...] = jnp.zeros_like(out)
        out[:, :count] = q[:rows, cut:]
        out[:, cut : cut + count] = q[rows:, cut:]


def swapped(mine, other, q):
    return pl.pallas_call(
        swap_kernel,
        in_specs=[pl.BlockSpec(memory_space=pltpu.VMEM)] * 3,
        out_specs=pl.BlockSpec(memory_space=pltpu.VMEM),
        out_shape=jax.ShapeDtypeStruct((other.shape[0], 2 * HOME * HEAD_DIM), other.dtype),
        compiler_params=pltpu.CompilerParams(vmem_limit_bytes=4 * 1024 * 1024),
    )(mine, other, q)


def four_frames(queries, keys, values, pair_mask, tile_offset):
    h = lax.axis_index("head")
    rows, features = queries.shape
    width = features // 4
    heads = width // HEAD_DIM

    def columns(array, d):
        return lax.dynamic_slice_in_dim(array, (h ^ d) * width, width, axis=1)

    def beside(*arrays):
        return jnp.concatenate(arrays, axis=1)

    def below(*arrays):
        return jnp.concatenate(arrays, axis=0)

    def to_head(array, d):
        return lax.ppermute(array, "head", [(i, i ^ d) for i in range(4)])

    def along(array, pairs):
        return lax.ppermute(array, "frame", pairs)

    def across(array):
        pairs = [(4 * z + j, 4 * (3 - z) + j if z in (1, 2) else 4 * z + (j ^ 1)) for z in range(4) for j in range(4)]
        return lax.ppermute(array, ("frame", "head"), pairs)

    def after(array, earlier):
        return lax.optimization_barrier((array, earlier))[0]

    kv = [[columns(array, d) for array in (keys, values)] for d in range(4)]
    kv = lax.optimization_barrier(kv)
    got = to_head(beside(*kv[1], *kv[3]), 1)
    pay, q_own, q_far, told = packed(
        (queries, keys, values),
        pair_mask,
        tile_offset,
        [[(0, 1, 0, width), (0, 3, 0, width)], [(0, 0, 0, width)], [(0, 2, 0, width)]],
        width,
        2 * width,
    )
    mine = below(beside(*kv[0]), got[:, : 2 * width], told)
    other = to_head(below(beside(*kv[2]), got[:, 2 * width :]), 2)
    n1m = along(mine, OUTER)
    n2m = across(mine)
    n1o = along(other, OUTER)
    n2o = across(other)

    got = to_head(after(pay, got), 1)
    q = below(q_own, got[:, :width], to_head(after(below(q_far, got[:, width:]), other), 2))

    tile = 2 * rows
    cut = HOME * HEAD_DIM
    guests = heads - HOME
    r1k, r1v, r1_rest = after(
        relayed(n1m, n1o, [[(0, cut)], [(width, width + cut)], [(cut, width), (width + cut, 2 * width)]]), n2m
    )
    r1k = across(r1k)
    swap = along(swapped(n2m, n2o, q), OUTER)
    r1v = across(after(r1v, n2o))

    def state(count):
        return [((count * 2 * tile, HEAD_DIM), jnp.float32)] * 2 + [((8, 128), jnp.float32)]

    def flops(chunks, tiles):
        return 4 * chunks * tiles * tile * tile * HEAD_DIM

    bf16 = jnp.bfloat16
    *near, done = run_kernel(
        functools.partial(near_kernel, 0, ((6, heads), (4, HOME)), own_queries, False),
        None,
        [q, mine, other, n1m, n1o, n2m, n2o],
        state(heads),
        (tile, 6 * tile),
        flops(2 * heads, 6),
        16,
    )
    r3k, r1_rest = passed(done, r1k, r1_rest)
    r3k = along(r3k, OUTER)
    r1_rest = across(r1_rest)
    r3v = along(after(r1v, swap), OUTER)
    *guest_near, _ = run_kernel(
        functools.partial(near_kernel, HOME, ((4, guests), (0, 0)), guest_queries, False),
        None,
        [swap, mine, other, n1m, n1o],
        state(guests),
        (tile, 4 * tile),
        flops(2 * guests, 4),
        16,
    )
    (back,) = run_kernel(
        guest_kernel,
        None,
        [swap, *guest_near, n1m, n2m, n2o, r1_rest],
        [((2 * tile, width - cut), bf16)],
        (tile, 3 * tile),
        flops(2 * guests, 3),
        16,
    )
    back = along(back, OUTER)
    out = run_kernel(
        home_kernel,
        pair_mask,
        [q, *near, r1k, r1v, swap, r3k, r3v],
        [((rows, cut), bf16)] * 4,
        (tile, 2 * tile),
        flops(2 * HOME, 2),
        16,
    )
    pieces = [(to_head(out[d], d) if d else out[0], d, 0) for d in range(4)]
    out = run_kernel(
        rest_kernel,
        pair_mask,
        [q, *near, r1_rest, after(back, out[1])],
        [((rows, width - cut), bf16)] * 4,
        (tile, tile),
        flops(2 * guests, 1),
        16,
    )
    moved = [out[0]] + [to_head(out[d], d) for d in (1, 2, 3)]
    pieces = [(after(piece, moved[1] if d == 3 else out[1]) if d > 1 else piece, d, at) for piece, d, at in pieces]
    pieces += [(piece, d, cut) for d, piece in enumerate(moved)]
    result = jnp.zeros((rows, features), jnp.bfloat16)
    for piece, d, begin in pieces:
        result = lax.dynamic_update_slice_in_dim(result, piece, (h ^ d) * width + begin, axis=1)
    return result


def solution(mesh):
    sizes = dict(mesh.shape)
    per_device = four_frames if sizes["frame"] == 4 and sizes["head"] == 4 else general
    return jax.shard_map(
        per_device,
        mesh=mesh,
        in_specs=(
            P(("parts", "frame", "head"), None),
            P(("parts", "frame", "head"), None),
            P(("parts", "frame", "head"), None),
            P(("parts", "frame"), None),
            P(("parts", "frame")),
        ),
        out_specs=P(("parts", "frame", "head"), None),
        check_vma=False,
    )
```

```python
import functools
import math

import jax
import jax.numpy as jnp
from jax import lax
from jax.experimental import pallas as pl
from jax.experimental.pallas import tpu as pltpu
from jax.sharding import PartitionSpec as P

HEAD_DIM = 128
SCALE = 1.0 / HEAD_DIM**0.5
LOG2E = math.log2(math.e)


def padded(x, sides, width):
    for axis, dim in sides:
        peers, length = (lax.axis_size(axis), x.shape[dim])
        up = [(i, (i + 1) % peers) for i in range(peers - 1)]
        down = [(j, i) for i, j in up]
        last = lax.slice_in_dim(x, length - width, length, axis=dim)
        leading = lax.slice_in_dim(x, 0, width, axis=dim)
        before = lax.ppermute(last, axis, up)
        after = lax.ppermute(leading, axis, down)
        x = jnp.concatenate([before, x, after], axis=dim)
    return x


def from_partner(x, axis, bit):
    return lax.ppermute(x, axis, [(i, i ^ 1 << bit) for i in range(lax.axis_size(axis))])


def subsample(frame_rows, offset, level, tiles, tile):
    step = 2**level
    width = frame_rows.shape[-1]
    grouped = frame_rows.reshape(tiles // step, step, tile, width)
    picked = lax.dynamic_index_in_dim(grouped, offset % step, 1, keepdims=False)
    return picked.reshape(-1, width)


def attend(query_rows, key_rows, value_rows, valid):
    count = query_rows.shape[0]
    heads = query_rows.shape[1] // HEAD_DIM
    q_three = query_rows.reshape(count, heads, HEAD_DIM).transpose(1, 0, 2)
    k_three = key_rows.reshape(-1, heads, HEAD_DIM).transpose(1, 0, 2)
    v_three = value_rows.reshape(-1, heads, HEAD_DIM).transpose(1, 0, 2)

    def one_head(operands):
        q_head, k_head, v_head = operands
        scores = jnp.dot(q_head, k_head.T, preferred_element_type=jnp.float32) * SCALE
        scores = jnp.where(valid[None, :] > 0, scores, -1e30)
        top = jnp.max(scores, axis=1, keepdims=True)
        weights = jnp.exp(scores - top) * valid[None, :]
        total = jnp.sum(weights, axis=1, keepdims=True)
        mixed = jnp.dot(weights.astype(jnp.bfloat16), v_head, preferred_element_type=jnp.float32)
        return mixed / total

    outcome = lax.map(one_head, (q_three, k_three, v_three))
    return outcome.transpose(1, 0, 2).reshape(count, heads * HEAD_DIM).astype(jnp.bfloat16)


def ordered(mine, theirs, upper):
    return jnp.where(upper == 1, jnp.concatenate([theirs, mine]), jnp.concatenate([mine, theirs]))


def general(queries, keys, values, pair_mask, tile_offset):
    frames_n = lax.axis_size("frame")
    current = lax.axis_index("frame")
    q_rows, k_rows, v_rows = (
        lax.all_to_all(queries, "head", split_axis=1, concat_axis=0, tiled=True),
        lax.all_to_all(keys, "head", split_axis=1, concat_axis=0, tiled=True),
        lax.all_to_all(values, "head", split_axis=1, concat_axis=0, tiled=True),
    )
    count = q_rows.shape[0]
    width = q_rows.shape[1]
    tiles = frames_n // 2
    tile = count // tiles
    depth = frames_n.bit_length() - 1
    stacked = jnp.stack([k_rows, v_rows])
    near = padded(stacked, (("frame", 1),), count)
    near_index = current - 1 + jnp.arange(3, dtype=jnp.int32)
    near_good = ((near_index >= 0) & (near_index < frames_n)).astype(jnp.float32)
    key_parts = [near[0]]
    value_parts = [near[1]]
    valid_parts = [jnp.repeat(near_good, count)]
    mask_row = pair_mask[0]
    offset = tile_offset[0]
    k_tiles = k_rows.reshape(tiles, tile, width)
    v_tiles = v_rows.reshape(tiles, tile, width)
    own = {}
    for level in range(1, depth):
        own[level] = (
            subsample(k_tiles, offset, level, tiles, tile)[None],
            subsample(v_tiles, offset, level, tiles, tile)[None],
        )
    sibling = {}
    cut = max(1, depth - 2)
    upper_levels = [level for level in range(1, depth) if level >= cut]
    k_pack = jnp.concatenate([own[level][0].reshape(-1, width) for level in upper_levels])
    v_pack = jnp.concatenate([own[level][1].reshape(-1, width) for level in upper_levels])
    k_every, v_every = (
        lax.all_gather(k_pack, "frame", axis=0, tiled=True),
        lax.all_gather(v_pack, "frame", axis=0, tiled=True),
    )
    k_every = k_every.reshape(frames_n, -1, width)
    v_every = v_every.reshape(frames_n, -1, width)
    position = 0
    for level in upper_levels:
        step = 2**level
        rows = count // step
        start = jnp.bitwise_xor(current // step, 1) * step
        block_k = lax.dynamic_slice_in_dim(k_every[:, position : position + rows], start, step, 0)
        block_v = lax.dynamic_slice_in_dim(v_every[:, position : position + rows], start, step, 0)
        sibling[level] = (block_k, block_v)
        position = position + rows
    swap_levels = [level for level in range(1, depth) if level < cut]
    growing = {level: own[level] for level in swap_levels}
    sections = cut if swap_levels else 0
    for bit in range(sections):
        active = [level for level in swap_levels if level >= bit]
        k_pack = jnp.concatenate([growing[level][0].reshape(-1, width) for level in active])
        v_pack = jnp.concatenate([growing[level][1].reshape(-1, width) for level in active])
        k_in, v_in = (from_partner(k_pack, "frame", bit), from_partner(v_pack, "frame", bit))
        upper = current // 2**bit % 2
        position = 0
        for level in active:
            shape = growing[level][0].shape
            size = shape[0] * shape[1]
            theirs_k = k_in[position : position + size].reshape(shape)
            theirs_v = v_in[position : position + size].reshape(shape)
            position = position + size
            if level == bit:
                sibling[level] = (theirs_k, theirs_v)
            else:
                growing[level] = (
                    ordered(growing[level][0], theirs_k, upper),
                    ordered(growing[level][1], theirs_v, upper),
                )
    for level in range(1, depth):
        step = 2**level
        start = jnp.bitwise_xor(current // step, 1) * step
        frame_ids = start + jnp.arange(step, dtype=jnp.int32)
        allowed = lax.dynamic_slice_in_dim(mask_row, start, step, 0)
        good = ((jnp.abs(frame_ids - current) >= 2) & (allowed == 1)).astype(jnp.float32)
        block_k, block_v = sibling[level]
        key_parts.append(block_k.reshape(-1, width))
        value_parts.append(block_v.reshape(-1, width))
        valid_parts.append(jnp.repeat(good, block_k.shape[1]))
    result = attend(
        q_rows,
        jnp.concatenate(key_parts),
        jnp.concatenate(value_parts),
        jnp.concatenate(valid_parts),
    )
    return lax.all_to_all(result, "head", split_axis=0, concat_axis=1, tiled=True)


HOME = 4
INFO_ROWS = 16
OUTER = [(0, 1), (1, 0), (2, 3), (3, 2)]
FACTOR = SCALE * LOG2E


def inner_frame():
    z = lax.axis_index("frame")
    return (z == 1) | (z == 2)


def head_lanes(first, i):
    return pl.ds(pl.multiple_of((first + i) * HEAD_DIM, HEAD_DIM), HEAD_DIM)


def keys_of(ref, first, i, rows):
    return ref[:rows, head_lanes(first, i)]


def values_of(ref, first, i, rows):
    return ref[:rows, head_lanes(ref.shape[1] // (2 * HEAD_DIM) + first, i)]


def dot_keys(q, k):
    return lax.dot_general(q, k, (((1,), (1,)), ((), ())), preferred_element_type=jnp.float32)


def fold(x, op):
    result = x[:, :128]
    for at in range(128, x.shape[1], 128):
        result = op(result, x[:, at : at + 128])
    return result


def near_kernel(first, counts, queries_of, carries, *refs):
    n_outs = 4 if carries else 3
    ins, outs, rooms = refs[: -2 - n_outs], refs[-2 - n_outs : -2], refs[-2:]
    queries, tiles = ins[0], ins[1:]
    mixed_out, levels, done = outs[:3]
    rows = rooms[0].shape[0]
    done[...] = jnp.zeros_like(done)
    if carries:
        outs[3][...] = ins[-1][...]

    def one_head(used, i):
        found = []
        for half, held in enumerate(rooms):
            q = queries_of(queries, half, i)
            best = None
            for at, ref in enumerate(used):
                s = dot_keys(q, keys_of(ref, first, i, rows))
                held[:, at * rows : (at + 1) * rows] = s
                part = fold(s, jnp.maximum)
                best = part if best is None else jnp.maximum(best, part)
            found.append(jnp.max(best, axis=1, keepdims=True))
        for half, (top, held) in enumerate(zip(found, rooms)):
            total, mixed = None, None
            for at, ref in enumerate(used):
                w = jnp.exp2((held[:, at * rows : (at + 1) * rows] - top) * FACTOR)
                mix = jnp.dot(w.astype(jnp.bfloat16), values_of(ref, first, i, rows), preferred_element_type=jnp.float32)
                part = fold(w, jnp.add)
                mixed = mix if mixed is None else mixed + mix
                total = part if total is None else total + part
            span = pl.ds(pl.multiple_of((2 * i + half) * rows, rows), rows)
            total = jnp.broadcast_to(jnp.sum(total, axis=1, keepdims=True), (rows, HEAD_DIM))
            mixed_out[span] = mixed * (1.0 / total)
            levels[span] = jnp.broadcast_to(top, (rows, HEAD_DIM)) * FACTOR + jnp.log2(total)

    for wanted, (n_tiles, n_heads) in zip((True, False), counts):
        if n_heads:

            @pl.when(inner_frame() == wanted)
            def _():
                def step(i, carry):
                    one_head(tiles[:n_tiles], i)
                    return carry

                lax.fori_loop(0, n_heads, step, 0)


def own_queries(ref, half, i):
    rows = ref.shape[0] // 2
    return ref[half * rows : (half + 1) * rows, head_lanes(0, i)]


def guest_queries(ref, half, i):
    return ref[:, head_lanes(half * HOME, i)]


def far_tile(ref, first, valid):
    return functools.partial(keys_of, ref, first), functools.partial(values_of, ref, first), valid


def far_pair(keys, values, valid):
    return functools.partial(keys_of, keys, 0), functools.partial(keys_of, values, 0), valid


def add_far(q, state, slots, i, begin, held):
    rows = q.shape[0]
    span = pl.ds(pl.multiple_of(begin, rows), rows)
    near_level = state[1][span]
    level = near_level
    for at, (keys, _, valid) in enumerate(slots):
        s = dot_keys(q, keys(i, rows)) * FACTOR
        held[:, at * rows : (at + 1) * rows] = s
        best = jnp.broadcast_to(jnp.max(fold(s, jnp.maximum), axis=1, keepdims=True), near_level.shape)
        level = jnp.maximum(level, jnp.where(valid, best, -1e30))
    shrink = jnp.exp2(near_level - level)
    mixed = state[0][span] * shrink
    total = None
    for at, (_, values, valid) in enumerate(slots):
        used = jnp.where(valid, level, 1e30)
        parts = []
        for lane in range(at * rows, (at + 1) * rows, HEAD_DIM):
            part = jnp.exp2(held[:, lane : lane + HEAD_DIM] - used)
            total = part if total is None else total + part
            parts.append(part.astype(jnp.bfloat16))
        mixed += jnp.dot(jnp.concatenate(parts, axis=1), values(i, rows), preferred_element_type=jnp.float32)
    total = jnp.broadcast_to(jnp.sum(total, axis=1, keepdims=True), near_level.shape) + shrink
    return (mixed * (1.0 / total)).astype(jnp.bfloat16)


def each_head(heads, body):
    def step(i, carry):
        body(i)
        return carry

    lax.fori_loop(0, heads, step, 0)


def finish_own(first, queries, state, slots, outs, rooms):
    piece = outs[0].shape[0]
    rows = 2 * piece

    def body(i):
        for half, held in enumerate(rooms):
            q = queries[half * rows : (half + 1) * rows, head_lanes(first, i)]
            value = add_far(q, state, slots, i, (2 * (first + i) + half) * rows, held)
            outs[2 * half][:, head_lanes(0, i)] = value[:piece]
            outs[2 * half + 1][:, head_lanes(0, i)] = value[piece:]

    each_head(outs[0].shape[1] // HEAD_DIM, body)


def home_kernel(mask, q, mixed, levels, r1k, r1v, r2, r3k, r3v, *rest):
    outs, rooms = rest[:4], rest[4:]
    z = lax.axis_index("frame")
    near2 = mask[0, z ^ 2] == 1

    @pl.when(inner_frame())
    def _():
        finish_own(0, q, (mixed, levels), [far_pair(r1k, r1v, near2)], outs, rooms)

    @pl.when(jnp.logical_not(inner_frame()))
    def _():
        slots = [far_tile(r2, 0, near2), far_pair(r3k, r3v, mask[0, z ^ 3] == 1)]
        finish_own(0, q, (mixed, levels), slots, outs, rooms)


def guest_kernel(q, mixed, levels, n1m, n2m, n2o, r1, out, *rooms):
    rows = r1.shape[0]
    z = lax.axis_index("frame")

    def told(ref, group):
        return ref[rows : rows + 1, group * 128 : (group + 1) * 128].astype(jnp.float32)

    @pl.when(inner_frame())
    def _():
        near2 = jnp.where(z == 1, told(n1m, 2), told(n1m, 1)) > 0.5
        near1 = jnp.where(z == 1, told(n1m, 3), told(n1m, 0)) > 0.5
        picked = told(n2m, 4) == (lax.axis_index("head") // 2).astype(jnp.float32)
        slots = [
            far_tile(n2m, HOME, near2 & picked),
            far_tile(n2o, HOME, near2 & jnp.logical_not(picked)),
            far_tile(r1, 0, near1),
        ]

        def body(i):
            for half, held in enumerate(rooms):
                value = add_far(guest_queries(q, half, i), (mixed, levels), slots, i, (2 * i + half) * rows, held)
                out[half * rows : (half + 1) * rows, head_lanes(0, i)] = value

        each_head(out.shape[1] // HEAD_DIM, body)


def rest_kernel(mask, q, mixed, levels, r1, back, *rest):
    outs, rooms = rest[:4], rest[4:]
    z = lax.axis_index("frame")

    @pl.when(inner_frame())
    def _():
        finish_own(HOME, q, (mixed, levels), [far_tile(r1, 0, mask[0, z ^ 2] == 1)], outs, rooms)

    @pl.when(jnp.logical_not(inner_frame()))
    def _():
        for d, out in enumerate(outs):
            out[...] = back[d * out.shape[0] : (d + 1) * out.shape[0]]


def pass_kernel(done, *refs):
    half = len(refs) // 2
    for x, out in zip(refs[:half], refs[half:]):
        out[...] = x[...]


def passed(done, *arrays):
    return pl.pallas_call(
        pass_kernel,
        in_specs=[pl.BlockSpec(memory_space=pltpu.VMEM)] * (1 + len(arrays)),
        out_specs=[pl.BlockSpec(memory_space=pltpu.VMEM)] * len(arrays),
        out_shape=[jax.ShapeDtypeStruct(x.shape, x.dtype) for x in arrays],
        compiler_params=pltpu.CompilerParams(vmem_limit_bytes=4 * 1024 * 1024),
    )(done, *arrays)


def run_kernel(kernel, mask, arrays, outs, room, flops, grant):
    scalars = [] if mask is None else [mask]
    return pl.pallas_call(
        kernel,
        in_specs=[pl.BlockSpec(memory_space=pltpu.SMEM)] * len(scalars)
        + [pl.BlockSpec(memory_space=pltpu.VMEM)] * len(arrays),
        out_specs=[pl.BlockSpec(memory_space=pltpu.VMEM)] * len(outs),
        out_shape=[jax.ShapeDtypeStruct(shape, dtype) for shape, dtype in outs],
        scratch_shapes=[pltpu.VMEM(room, jnp.float32)] * 2,
        compiler_params=pltpu.CompilerParams(vmem_limit_bytes=grant * 1024 * 1024),
        cost_estimate=pl.CostEstimate(
            flops=flops, bytes_accessed=sum(x.size * 2 for x in arrays), transcendentals=flops // (4 * HEAD_DIM)
        ),
    )(*scalars, *arrays)


def pack_kernel(copies, width, mask, offset, *refs):
    ins, outs, sems = refs[:3], refs[3:-1], refs[-1]
    h = lax.axis_index("head")
    started = []
    for n, (operand, d, begin, result, at, lanes) in enumerate(copies):
        source = ins[operand].at[:, pl.ds(pl.multiple_of((h ^ d) * width + begin, HEAD_DIM), lanes)]
        copy = pltpu.make_async_copy(source, outs[result].at[:, at : at + lanes], sems.at[n])
        copy.start()
        started.append(copy)
    if len(outs) > 1 + max(copy[3] for copy in copies):
        told = outs[-1]
        for group in range(told.shape[1] // 128):
            value = mask[0, group] if group < 4 else offset[0]
            rows = jnp.full((told.shape[0], 128), value, jnp.int32).astype(jnp.float32)
            told[:, group * 128 : (group + 1) * 128] = rows.astype(told.dtype)
    for copy in started:
        copy.wait()


def packed(operands, mask, offset, results, width, told):
    rows = operands[0].shape[0]
    copies, shapes = [], []
    for n, parts in enumerate(results):
        at = 0
        for operand, d, begin, lanes in parts:
            copies.append((operand, d, begin, n, at, lanes))
            at += lanes
        shapes.append(jax.ShapeDtypeStruct((rows, at), jnp.bfloat16))
    if told:
        shapes.append(jax.ShapeDtypeStruct((INFO_ROWS, told), jnp.bfloat16))
    return pl.pallas_call(
        functools.partial(pack_kernel, copies, width),
        in_specs=[pl.BlockSpec(memory_space=pltpu.SMEM)] * 2 + [pl.BlockSpec(memory_space=pltpu.HBM)] * 3,
        out_specs=[pl.BlockSpec(memory_space=pltpu.VMEM)] * len(shapes),
        out_shape=shapes,
        scratch_shapes=[pltpu.SemaphoreType.DMA((len(copies),))],
        compiler_params=pltpu.CompilerParams(vmem_limit_bytes=4 * 1024 * 1024),
    )(mask, offset, *operands)


def relayed_kernel(parts, mine, other, *outs):
    tile = other.shape[0]
    offset = jnp.max(mine[tile : tile + INFO_ROWS, 4 * 128 : 5 * 128].astype(jnp.float32))
    here = offset == (lax.axis_index("head") // 2).astype(jnp.float32)

    def take(ref):
        for spans, out in zip(parts, outs):
            at = 0
            for begin, end in spans:
                out[:, at : at + end - begin] = ref[:tile, begin:end]
                at += end - begin

    @pl.when(here)
    def _():
        take(mine)

    @pl.when(jnp.logical_not(here))
    def _():
        take(other)


def relayed(mine, other, parts):
    widths = [sum(end - begin for begin, end in spans) for spans in parts]
    return pl.pallas_call(
        functools.partial(relayed_kernel, parts),
        in_specs=[pl.BlockSpec(memory_space=pltpu.VMEM)] * 2,
        out_specs=[pl.BlockSpec(memory_space=pltpu.VMEM)] * len(parts),
        out_shape=[jax.ShapeDtypeStruct((other.shape[0], width), other.dtype) for width in widths],
        compiler_params=pltpu.CompilerParams(vmem_limit_bytes=4 * 1024 * 1024),
    )(mine, other)


def swap_kernel(mine, other, q, out):
    cut = HOME * HEAD_DIM

    @pl.when(inner_frame())
    def _():
        half = other.shape[1] // 2
        relayed_kernel([[(0, cut), (half, half + cut)]], mine, other, out)

    @pl.when(jnp.logical_not(inner_frame()))
    def _():
        rows, count = out.shape[0], q.shape[1] - cut
        out[...] = jnp.zeros_like(out)
        out[:, :count] = q[:rows, cut:]
        out[:, cut : cut + count] = q[rows:, cut:]


def swapped(mine, other, q):
    return pl.pallas_call(
        swap_kernel,
        in_specs=[pl.BlockSpec(memory_space=pltpu.VMEM)] * 3,
        out_specs=pl.BlockSpec(memory_space=pltpu.VMEM),
        out_shape=jax.ShapeDtypeStruct((other.shape[0], 2 * HOME * HEAD_DIM), other.dtype),
        compiler_params=pltpu.CompilerParams(vmem_limit_bytes=4 * 1024 * 1024),
    )(mine, other, q)


def four_frames(queries, keys, values, pair_mask, tile_offset):
    h = lax.axis_index("head")
    rows, features = queries.shape
    width = features // 4
    heads = width // HEAD_DIM

    def columns(array, d):
        return lax.dynamic_slice_in_dim(array, (h ^ d) * width, width, axis=1)

    def beside(*arrays):
        return jnp.concatenate(arrays, axis=1)

    def below(*arrays):
        return jnp.concatenate(arrays, axis=0)

    def to_head(array, d):
        return lax.ppermute(array, "head", [(i, i ^ d) for i in range(4)])

    def along(array, pairs):
        return lax.ppermute(array, "frame", pairs)

    def across(array):
        pairs = [(4 * z + j, 4 * (3 - z) + j if z in (1, 2) else 4 * z + (j ^ 1)) for z in range(4) for j in range(4)]
        return lax.ppermute(array, ("frame", "head"), pairs)

    def after(array, earlier):
        return lax.optimization_barrier((array, earlier))[0]

    kv = [[columns(array, d) for array in (keys, values)] for d in range(4)]
    kv = lax.optimization_barrier(kv)
    got = to_head(beside(*kv[1], *kv[3]), 1)
    pay, q_own, q_far, told = packed(
        (queries, keys, values),
        pair_mask,
        tile_offset,
        [[(0, 1, 0, width), (0, 3, 0, width)], [(0, 0, 0, width)], [(0, 2, 0, width)]],
        width,
        2 * width,
    )
    mine = below(beside(*kv[0]), got[:, : 2 * width], told)
    other = to_head(below(beside(*kv[2]), got[:, 2 * width :]), 2)
    n1m = along(mine, OUTER)
    n2m = across(mine)
    n1o = along(other, OUTER)
    n2o = across(other)

    got = to_head(after(pay, got), 1)
    q = below(q_own, got[:, :width], to_head(after(below(q_far, got[:, width:]), other), 2))

    tile = 2 * rows
    cut = HOME * HEAD_DIM
    guests = heads - HOME
    r1k, r1v, r1_rest = after(
        relayed(n1m, n1o, [[(0, cut)], [(width, width + cut)], [(cut, width), (width + cut, 2 * width)]]), n2m
    )
    r1k = across(r1k)
    swap = along(swapped(n2m, n2o, q), OUTER)
    r1v = across(after(r1v, n2o))

    def state(count):
        return [((count * 2 * tile, HEAD_DIM), jnp.float32)] * 2 + [((8, 128), jnp.float32)]

    def flops(chunks, tiles):
        return 4 * chunks * tiles * tile * tile * HEAD_DIM

    bf16 = jnp.bfloat16
    *near, done = run_kernel(
        functools.partial(near_kernel, 0, ((6, heads), (4, HOME)), own_queries, False),
        None,
        [q, mine, other, n1m, n1o, n2m, n2o],
        state(heads),
        (tile, 6 * tile),
        flops(2 * heads, 6),
        16,
    )
    r3k, r1_rest = passed(done, r1k, r1_rest)
    r3k = along(r3k, OUTER)
    r1_rest = across(r1_rest)
    r3v = along(after(r1v, swap), OUTER)
    *guest_near, _ = run_kernel(
        functools.partial(near_kernel, HOME, ((4, guests), (0, 0)), guest_queries, False),
        None,
        [swap, mine, other, n1m, n1o],
        state(guests),
        (tile, 4 * tile),
        flops(2 * guests, 4),
        16,
    )
    (back,) = run_kernel(
        guest_kernel,
        None,
        [swap, *guest_near, n1m, n2m, n2o, r1_rest],
        [((2 * tile, width - cut), bf16)],
        (tile, 3 * tile),
        flops(2 * guests, 3),
        16,
    )
    back = along(back, OUTER)
    out = run_kernel(
        home_kernel,
        pair_mask,
        [q, *near, r1k, r1v, swap, r3k, r3v],
        [((rows, cut), bf16)] * 4,
        (tile, 2 * tile),
        flops(2 * HOME, 2),
        16,
    )
    pieces = [(to_head(out[d], d) if d else out[0], d, 0) for d in range(4)]
    out = run_kernel(
        rest_kernel,
        pair_mask,
        [q, *near, r1_rest, after(back, out[1])],
        [((rows, width - cut), bf16)] * 4,
        (tile, tile),
        flops(2 * guests, 1),
        16,
    )
    moved = [out[0]] + [to_head(out[d], d) for d in (1, 2, 3)]
    pieces = [(after(piece, moved[1] if d == 3 else out[1]) if d > 1 else piece, d, at) for piece, d, at in pieces]
    pieces += [(piece, d, cut) for d, piece in enumerate(moved)]
    result = jnp.zeros((rows, features), jnp.bfloat16)
    for piece, d, begin in pieces:
        result = lax.dynamic_update_slice_in_dim(result, piece, (h ^ d) * width + begin, axis=1)
    return result


def solution(mesh):
    sizes = dict(mesh.shape)
    per_device = four_frames if sizes["frame"] == 4 and sizes["head"] == 4 else general
    return jax.shard_map(
        per_device,
        mesh=mesh,
        in_specs=(
            P(("parts", "frame", "head"), None),
            P(("parts", "frame", "head"), None),
            P(("parts", "frame", "head"), None),
            P(("parts", "frame"), None),
            P(("parts", "frame")),
        ),
        out_specs=P(("parts", "frame", "head"), None),
        check_vma=False,
    )
```
